32 devices in a mesh: grp: 2 (over x), head: 2 (over y), blk: 8 (over z, core).
Axes of the slice: x: 2, y: 2, z: 4, core: 2. Of those that a mesh axis runs over, the one named last changes fastest.
Arguments:
- tokens_in: bfloat16 [4096, 768], P(('grp', 'head', 'blk')), may hold values from -6 to 6
- norm_gains: bfloat16 [2, 768], P(None, ('grp', 'head')), may hold values from 0.5 to 1.5
- attn_qkv: bfloat16 [768, 2304], P(None, ('grp', 'head')), may hold values from -0.21875 to 0.21875
- attn_proj: bfloat16 [768, 768], P(None, ('grp', 'head')), may hold values from -0.875 to 0.875
- router_rows: bfloat16 [16, 768], P(None, ('grp', 'head')), may hold values from -0.15917969 to 0.15917969
- shared_gate_up: bfloat16 [768, 4096], P(None, ('grp', 'head')), may hold values from -0.21875 to 0.21875
- shared_down: bfloat16 [2048, 768], P(None, ('grp', 'head')), may hold values from -0.1875 to 0.1875
- expert_gate_up: bfloat16 [2, 768, 32768], P(None, ('grp', 'head'), 'blk'), may hold values from -0.21875 to 0.21875
- expert_down: bfloat16 [32768, 768], P('blk', ('grp', 'head')), may hold values from -1 to 1
- routes: int32 [4096, 2], P(('grp', 'head', 'blk')), may hold values from 0 to 15, all different within a row; in each aligned block of 128 rows (0 to 127, 128 to 255, ...) at most 20 rows name the same one
- out_grad: bfloat16 [4096, 768], P(('grp', 'head', 'blk')), may hold values from -6 to 6
Outputs:
- layer_out: bfloat16 [4096, 768], P(('grp', 'head', 'blk'))
- grad_tokens: float32 [4096, 768], P(('grp', 'head', 'blk'))
- grad_gains: float32 [2, 768], P(None, ('grp', 'head'))
- grad_qkv: float32 [768, 2304], P(None, ('grp', 'head'))
- grad_proj: float32 [768, 768], P(None, ('grp', 'head'))
- grad_router: float32 [16, 768], P(None, ('grp', 'head'))
- grad_shared_gate_up: float32 [768, 4096], P(None, ('grp', 'head'))
- grad_shared_down: float32 [2048, 768], P(None, ('grp', 'head'))
- grad_expert_gate_up: float32 [2, 768, 32768], P(None, ('grp', 'head'), 'blk')
- grad_expert_down: float32 [32768, 768], P('blk', ('grp', 'head'))
The draws below stay inside these ranges and needn't reach their ends.
Inputs may be any that keep to these rules, and one draw needn't show every extreme that they name: `routes`: each row names two different experts; among the rows of one device (aligned blocks of 128 rows) no expert is named more than 20 times, a bound that some block reaches.
All inputs are finite; a program needn't handle non-finite values.
Results may differ from the reference program's by a relative error of at most 0.018.
Values may be sent and summed in bfloat16 or wider, within the bound.
No kernel may reach another device: no remote copies, remote signals or barrier semaphores. Data moves between devices by JAX's collectives and lax.ppermute only.
A program may use at most 192 MiB of HBM per device.

```python
import math
import jax
import jax.numpy as jnp
import numpy as np
from jax import lax

D = 768
HEADS = 12
DH = 64
EXPERTS = 16
FF = 2048
SFF = 2048
TOK_DEV = 128
PROMPT_DEV = 64
PROMPT = 1024
CONT = 128
CAP = 20
TOKENS = 4096
N_GRP = 2
N_HEAD = 2
N_BLK = 8
DEVICES = 32


def levels(rng, shape, pieces, low, top_value):
    factor_of, own = 1.0, jax.random.fold_in(rng, 6)
    for position, shards_of in pieces:
        heights = jnp.exp(jax.random.uniform(jax.random.fold_in(own, position), (shards_of,), jnp.float32, low / len(pieces), top_value / len(pieces)))
        factor_of = factor_of * jnp.repeat(heights, shape[position] // shards_of).reshape([-1 if axis == position else 1 for axis in range(len(shape))])
    return factor_of


def shared_out(rng, own, number, rows, amount, top, limit, slope):
    order = jax.random.permutation(rng, amount)
    crowded, usual = portions_of(amount, rows * top, limit, slope, True), portions_of(amount, rows * top, limit, slope, False)
    places = jnp.arange(amount)

    def named(sizes, rotation):
        used = int((sizes > 0).sum())
        fixed = max(1, used // 4)
        passed = fixed + (places - fixed + rotation * (used - fixed)) % max(1, amount - fixed)
        return jnp.zeros((amount,), jnp.int32).at[order[jnp.where(places < fixed, places, passed)]].set(jnp.asarray(sizes, jnp.int32))

    sizes = jnp.where(number % 4 == 0, named(crowded, number // 4), named(usual, number - number // 4 - 1))
    mixed = jax.random.permutation(jax.random.fold_in(own, 3), amount)
    giver, sink = mixed[0:amount // 2 * 2:2], mixed[1:amount // 2 * 2:2]
    slack = jnp.minimum(sizes[giver] - 1, limit - sizes[sink]) // 2
    slack = jnp.where((giver == order[0]) | (sink == order[0]) | (sizes[sink] == 0), 0, jnp.maximum(slack, 0))
    passed = jax.random.randint(jax.random.fold_in(own, 4), (amount // 2,), 0, 1 << 20) % (slack + 1)
    sizes = sizes.at[giver].add(-passed).at[sink].add(passed)
    members = jnp.searchsorted(jnp.cumsum(sizes), jnp.arange(rows * top), side="right").astype(jnp.int32)
    listing = members.reshape(top, rows).T
    listing = listing[jax.random.permutation(jax.random.fold_in(own, 1), rows)]
    rotation = jax.random.randint(jax.random.fold_in(own, 2), (rows, 1), 0, top)
    return jnp.take_along_axis(listing, (jnp.arange(top)[None, :] + rotation) % top, axis=1)


def portions_of(count, total, bound, skew, full):
    portions = [(1 << 20) // math.isqrt(grade ** skew) + 1 for grade in range(1, count + 1)]
    largest = bound if full else min(bound, max(-(-total // count), total * portions[0] // sum(portions)))
    least = 1 if total - largest >= count - 1 else 0
    holding, rest = [largest] + [least] * (count - 1), total - largest - least * (count - 1)
    while rest > 0:
        movable = [i for i in range(1, count) if holding[i] < largest] or [i for i in range(1, count) if holding[i] < bound]
        mass, remaining = sum([portions[i] for i in movable]), rest
        for i in movable:
            addition = min(bound - holding[i], max(1, remaining * portions[i] // mass), rest)
            holding[i] = holding[i] + addition
            rest = rest - addition
    return np.array(holding)


def noise(key, extent, width, bound, split=(), kind=jnp.bfloat16):
    result = jax.random.normal(key, extent, jnp.float32) * width
    if len(split) > 0:
        result = levels(key, extent, split, -0.22, 0.18) * result
    return jnp.clip(result, min=-bound, max=bound).astype(kind)


def setup_inputs(seed: int = 0) -> dict:
    seeds = jax.random.split(jax.random.key(seed), 12)
    tokens_in = noise(seeds[0], (TOKENS, D), 1.0, 6.0, ((0, 32),))
    norm_gains = jnp.clip(1.0 + 0.1 * jax.random.normal(seeds[1], (2, D), jnp.float32), 0.5, 1.5).astype(jnp.bfloat16)
    attn_qkv = noise(seeds[2], (D, 3 * D), D ** -0.5, 0.21875, ((1, 4),))
    attn_proj = noise(seeds[3], (D, D), (D // 16) ** -0.5, 0.875, ((1, 4),))
    router_rows = noise(seeds[4], (EXPERTS, D), 0.027, 0.15917969, ((1, 4),))
    shared_gate_up = noise(seeds[5], (D, 2 * SFF), D ** -0.5, 0.21875, ((1, 4),))
    shared_down = noise(seeds[6], (SFF, D), (SFF // 2) ** -0.5, 0.1875, ((1, 4),))
    expert_gate_up = noise(seeds[7], (2, D, EXPERTS * FF), D ** -0.5, 0.21875, ((1, 4), (2, 8)))
    expert_down = noise(seeds[8], (EXPERTS * FF, D), (FF // 64) ** -0.5, 1.0, ((0, 8), (1, 4)))
    routes_keys = jax.random.split(jax.random.fold_in(seeds[9], 1), TOKENS // TOK_DEV)
    routes_turns = jax.random.permutation(jax.random.fold_in(seeds[9], 3), TOKENS // TOK_DEV)
    routes = jax.vmap(lambda own, number: shared_out(jax.random.fold_in(seeds[9], 2), own, number, TOK_DEV, EXPERTS, 2, CAP, 1))(routes_keys, routes_turns).reshape((TOKENS, 2))
    out_grad = noise(seeds[10], (TOKENS, D), 1.0, 6.0, ((0, 32),))
    return {"tokens_in": tokens_in, "norm_gains": norm_gains, "attn_qkv": attn_qkv, "attn_proj": attn_proj, "router_rows": router_rows, "shared_gate_up": shared_gate_up, "shared_down": shared_down, "expert_gate_up": expert_gate_up, "expert_down": expert_down, "routes": routes, "out_grad": out_grad}


@jax.custom_vjp
def low(v):
    return lax.optimization_barrier(v.astype(jnp.bfloat16)).astype(jnp.float32)

@jax.custom_vjp
def low_back(v):
    return v

def low_keep(v):
    return (low(v), None)

def low_pass(kept, grad):
    return (grad,)

def back_keep(v):
    return (v, None)

def back_low(kept, grad):
    return (low(grad),)
low.defvjp(low_keep, low_pass)
low_back.defvjp(back_keep, back_low)
EPSILON = 1e-06
NEGATIVE = -1e+30
HIGHEST = lax.Precision.HIGHEST

def product(left, right):
    return jnp.dot(left, right, precision=HIGHEST, preferred_element_type=jnp.float32)

def norm_rows(values, gain):
    inverse = lax.rsqrt(lax.optimization_barrier(jnp.mean(values * values, axis=-1, keepdims=True)) + EPSILON)
    return values * inverse * gain

def angle_tables(positions):
    step_index = jnp.arange(DH // 2, dtype=jnp.float32)
    freq_rates = 10000.0 ** (-2.0 * step_index / DH)
    angles = positions.astype(jnp.float32)[:, None] * freq_rates[None, :]
    return (jnp.cos(angles)[:, None, :], jnp.sin(angles)[:, None, :])

def rotate(values, cosine, sine_table):
    half_size = values.shape[-1] // 2
    first_half = values[..., :half_size]
    second = values[..., half_size:]
    return jnp.concatenate([first_half * cosine - second * sine_table, second * cosine + first_half * sine_table], axis=-1)

def token_positions():
    flat_index = jnp.arange(TOKENS, dtype=jnp.int32)
    device = flat_index // TOK_DEV
    within = flat_index % TOK_DEV
    head_part = device // N_BLK % N_HEAD
    block_index = device % N_BLK
    prompt_index = (block_index * N_HEAD + head_part) * PROMPT_DEV + within
    cont_index = PROMPT + head_part * (TOK_DEV - PROMPT_DEV) + within - PROMPT_DEV
    return jnp.where(within < PROMPT_DEV, prompt_index, cont_index)

def attend(queries, key_rows, value_rows, visible):
    scores = low_back(jnp.einsum('qhd,khd->hqk', queries, key_rows, precision=HIGHEST) * DH ** (-0.5))
    masked = jnp.where(visible[None], scores, NEGATIVE)
    row_peak = lax.optimization_barrier(jnp.max(masked, axis=-1, keepdims=True))
    weights = jnp.where(visible[None], jnp.exp(masked - row_peak), 0.0)
    soft_weights = weights / lax.optimization_barrier(jnp.sum(weights, axis=-1, keepdims=True))
    return jnp.einsum('hqk,khd->qhd', low(soft_weights), value_rows, precision=HIGHEST)

def prompt_attention(queries, key_rows, value_rows):
    order_index = jnp.arange(PROMPT, dtype=jnp.int32)
    return attend(queries, key_rows, value_rows, order_index[None, :] <= order_index[:, None])

def cont_attention(queries, key_rows, value_rows, prompt_keys, prompt_values):
    order_index = jnp.arange(CONT, dtype=jnp.int32)
    visible = jnp.concatenate([jnp.ones((CONT, PROMPT), dtype=jnp.bool_), order_index[None, :] <= order_index[:, None]], axis=1)
    return attend(queries, jnp.concatenate([prompt_keys, key_rows], axis=0), jnp.concatenate([prompt_values, value_rows], axis=0), visible)

def group_attention(group_data):
    prompt_q, prompt_k, prompt_v, cont_q, cont_k, cont_v = group_data
    prompt_out = jax.checkpoint(prompt_attention)(prompt_q, prompt_k, prompt_v)

    def one_cont(member):
        return jax.checkpoint(cont_attention)(member[0], member[1], member[2], prompt_k, prompt_v)
    return (prompt_out, lax.map(one_cont, (cont_q, cont_k, cont_v)))

def split_layout(values):
    cube = values.reshape(N_GRP, N_HEAD, N_BLK, TOK_DEV, HEADS, DH)
    prompt_part = jnp.transpose(cube[:, :, :, :PROMPT_DEV], (0, 2, 1, 3, 4, 5)).reshape(N_GRP, PROMPT, HEADS, DH)
    cont_part = jnp.transpose(cube[:, :, :, PROMPT_DEV:], (0, 2, 1, 3, 4, 5)).reshape(N_GRP, N_BLK, CONT, HEADS, DH)
    return (prompt_part, cont_part)

def join_layout(prompt_part, cont_part):
    prompt_cube = jnp.transpose(prompt_part.reshape(N_GRP, N_BLK, N_HEAD, PROMPT_DEV, HEADS, DH), (0, 2, 1, 3, 4, 5))
    cont_cube = jnp.transpose(cont_part.reshape(N_GRP, N_BLK, N_HEAD, TOK_DEV - PROMPT_DEV, HEADS, DH), (0, 2, 1, 3, 4, 5))
    return jnp.concatenate([prompt_cube, cont_cube], axis=3).reshape(TOKENS, HEADS * DH)

def expert_branch(member):
    rows_in, gate_weight, up_weight, down_w = member
    gate_value = low_back(product(rows_in, gate_weight))
    up_value = low_back(product(rows_in, up_weight))
    return low_back(product(low(jax.nn.silu(gate_value) * up_value), down_w))

def forward(tokens, gain_rows, qkv_w, proj_w, router_w, shared_w, shared_out_w, expert_w, expert_out_w, routes, expert_of, slot_of, slot_token, cosine, sine_table):
    normed = low(norm_rows(tokens, gain_rows[0]))
    mixed_qkv = product(normed, qkv_w)
    query_pre = low_back(mixed_qkv[:, :D]).reshape(TOKENS, HEADS, DH)
    key_pre = low_back(mixed_qkv[:, D:2 * D]).reshape(TOKENS, HEADS, DH)
    queries = low(rotate(query_pre, cosine, sine_table))
    key_rows = low(rotate(key_pre, cosine, sine_table))
    value_rows = low(low_back(mixed_qkv[:, 2 * D:])).reshape(TOKENS, HEADS, DH)
    prompt_q, cont_q = split_layout(queries)
    prompt_k, cont_k = split_layout(key_rows)
    prompt_v, cont_v = split_layout(value_rows)
    prompt_out, cont_out = lax.map(group_attention, (prompt_q, prompt_k, prompt_v, cont_q, cont_k, cont_v))
    attn_out = low(low_back(join_layout(prompt_out, cont_out)))
    residual = tokens + low_back(product(attn_out, proj_w))
    hidden = low(norm_rows(residual, gain_rows[1]))
    logits = low_back(product(hidden, router_w.T))
    soft_route = jax.nn.softmax(logits, axis=-1)
    gate_values = jnp.take_along_axis(soft_route, routes, axis=1)
    shared_gate = low_back(product(hidden, shared_w[:, :SFF]))
    shared_up = low_back(product(hidden, shared_w[:, SFF:]))
    shared = low_back(product(low(jax.nn.silu(shared_gate) * shared_up), shared_out_w))
    padded = jnp.concatenate([hidden, jnp.zeros((1, D), jnp.float32)], axis=0)
    gate_weight = jnp.transpose(expert_w[0].reshape(D, EXPERTS, FF), (1, 0, 2))
    up_weight = jnp.transpose(expert_w[1].reshape(D, EXPERTS, FF), (1, 0, 2))
    down_w = expert_out_w.reshape(EXPERTS, FF, D)
    expert_out = lax.map(jax.checkpoint(expert_branch), (padded[slot_token], gate_weight, up_weight, down_w))
    chosen = expert_out[expert_of, slot_of].reshape(TOKENS, 2, D)
    experts = lax.optimization_barrier(jnp.sum(gate_values[:, :, None] * chosen, axis=1))
    return residual + shared + experts

def reference(tokens_in, norm_gains, attn_qkv, attn_proj, router_rows, shared_gate_up, shared_down, expert_gate_up, expert_down, routes, out_grad):
    pair_rows = routes.reshape(DEVICES, 2 * TOK_DEV)
    onehot_table = (pair_rows[:, :, None] == jnp.arange(EXPERTS, dtype=jnp.int32)[None, None, :]).astype(jnp.int32)
    rank_in_block = lax.optimization_barrier(jnp.sum(jnp.cumsum(onehot_table, axis=1) * onehot_table, axis=2)) - 1
    slot_of = (jnp.arange(DEVICES, dtype=jnp.int32)[:, None] * CAP + rank_in_block).reshape(-1)
    expert_of = pair_rows.reshape(-1)
    slot_owner = jnp.arange(2 * TOKENS, dtype=jnp.int32) // 2
    slot_token = jnp.full((EXPERTS, DEVICES * CAP), TOKENS, dtype=jnp.int32).at[expert_of, slot_of].set(slot_owner)
    cosine, sine_table = angle_tables(token_positions())
    floats = [source.astype(jnp.float32) for source in (tokens_in, norm_gains, attn_qkv, attn_proj, router_rows, shared_gate_up, shared_down, expert_gate_up, expert_down)]

    def run_layer(*weights):
        return forward(*weights, routes, expert_of, slot_of, slot_token, cosine, sine_table)
    layer_out, pull_back = jax.vjp(run_layer, *floats)
    grads = pull_back(out_grad.astype(jnp.float32))
    return (layer_out.astype(jnp.bfloat16), grads[0], grads[1], grads[2], grads[3], grads[4], grads[5], grads[6], grads[7], grads[8])
```

```python
import jax
import jax.numpy as jnp
from jax import lax
from jax.experimental import pallas as pl
from jax.experimental.pallas import tpu as pltpu
from jax.sharding import PartitionSpec as P

HEADS = 12
DH = 64
EXPERTS = 16
FF = 2048
SFF = 2048
PROMPT_ROWS = 64
PROMPT_LEAST = 1024


EPSILON = 1e-06
NEGATIVE = -1e30


def norm_rows(values, gain):
    inverse = lax.rsqrt(jnp.mean(values * values, axis=-1, keepdims=True) + EPSILON)
    return (values * inverse * gain, inverse)


def norm_back(values, inverse, gain, upstream):
    scaled = upstream * gain
    inner_mean = jnp.mean(scaled * values, axis=-1, keepdims=True)
    return (
        inverse * scaled - values * inverse**3 * inner_mean,
        jnp.sum(upstream * values * inverse, axis=0),
    )


def angle_tables(positions):
    step_index = jnp.arange(DH // 2, dtype=jnp.float32)
    freq_rates = 10000.0 ** (-2.0 * step_index / DH)
    angles = positions.astype(jnp.float32)[:, None] * freq_rates[None, :]
    return (jnp.cos(angles)[:, None, :], jnp.sin(angles)[:, None, :])


def rotate(values, cosine, sine_table):
    half_size = values.shape[-1] // 2
    first_half = values[..., :half_size]
    second = values[..., half_size:]
    return jnp.concatenate(
        [first_half * cosine - second * sine_table, second * cosine + first_half * sine_table],
        axis=-1,
    )


def swish_parts(gate_value):
    sigmoid = jax.nn.sigmoid(gate_value)
    return (gate_value * sigmoid, sigmoid * (1.0 + gate_value * (1.0 - sigmoid)))


def row_layout(head_part, within, block_index, heads_axis, blocks_axis, row_count, prompt_dev):
    prompt_all = prompt_dev * heads_axis * blocks_axis
    is_prompt = within < prompt_dev
    prompt_index = (block_index * heads_axis + head_part) * prompt_dev + within
    cont_index = head_part * (row_count - prompt_dev) + within - prompt_dev
    positions = jnp.where(is_prompt, prompt_index, prompt_all + cont_index)
    return (is_prompt, prompt_index, cont_index, positions)


def fetch_weights(
    norm_gains,
    attn_qkv,
    attn_proj,
    router_rows,
    shared_gate_up,
    shared_down,
    expert_gate_up,
    expert_down,
):
    return (
        lax.all_gather(norm_gains, ("grp", "head"), axis=1, tiled=True),
        lax.all_gather(attn_qkv, ("grp", "head"), axis=1, tiled=True),
        lax.all_gather(attn_proj, ("grp", "head"), axis=1, tiled=True),
        lax.all_gather(router_rows, ("grp", "head"), axis=1, tiled=True),
        lax.all_gather(shared_gate_up, ("grp", "head"), axis=1, tiled=True),
        lax.all_gather(shared_down, ("grp", "head"), axis=1, tiled=True),
        lax.all_gather(expert_gate_up, ("grp", "head"), axis=1, tiled=True),
        lax.all_gather(expert_down, ("grp", "head"), axis=1, tiled=True),
    )


def masked_scores(queries, key_rows, visible):
    scores = jnp.einsum(
        "qhd,khd->hqk", queries, key_rows, preferred_element_type=jnp.float32
    ) * DH ** (-0.5)
    return jnp.where(visible[None], scores, NEGATIVE)


def add_stats(carry, scores, visible):
    row_peak, row_total = carry
    new_peak = jnp.maximum(row_peak, jnp.max(scores, axis=-1))
    terms = jnp.where(visible[None], jnp.exp(scores - new_peak[:, :, None]), 0.0)
    return (new_peak, row_total * jnp.exp(row_peak - new_peak) + jnp.sum(terms, axis=-1))


def block_probs(scores, visible, log_total):
    return jnp.where(visible[None], jnp.exp(scores - log_total[:, :, None]), 0.0)


def grad_block(queries, grad_out, log_total, delta, key_rows, value_rows, visible):
    scale_factor = DH ** (-0.5)
    soft_weights = block_probs(masked_scores(queries, key_rows, visible), visible, log_total)
    grad_weights = jnp.einsum(
        "qhd,khd->hqk", grad_out, value_rows, preferred_element_type=jnp.float32
    )
    grad_scores = (soft_weights * (grad_weights - delta[:, :, None])).astype(jnp.bfloat16)
    grad_query = (
        jnp.einsum("hqk,khd->qhd", grad_scores, key_rows, preferred_element_type=jnp.float32)
        * scale_factor
    )
    grad_key = (
        jnp.einsum("hqk,qhd->khd", grad_scores, queries, preferred_element_type=jnp.float32)
        * scale_factor
    )
    grad_value = jnp.einsum(
        "hqk,qhd->khd",
        soft_weights.astype(jnp.bfloat16),
        grad_out,
        preferred_element_type=jnp.float32,
    )
    return (grad_query, grad_key, grad_value)


def body(
    tokens_in,
    norm_gains,
    attn_qkv,
    attn_proj,
    router_rows,
    shared_gate_up,
    shared_down,
    expert_gate_up,
    expert_down,
    routes,
    out_grad,
):
    heads_axis = lax.axis_size("head")
    blocks_axis = lax.axis_size("blk")
    row_count = tokens_in.shape[0]
    width_all = tokens_in.shape[1]
    prompt_dev = max(PROMPT_ROWS, PROMPT_LEAST // (heads_axis * blocks_axis))
    prompt_all = prompt_dev * heads_axis * blocks_axis
    local_heads = HEADS // heads_axis
    query_rows = heads_axis * row_count
    key_block = min(512, prompt_all)
    block_count = prompt_all // key_block
    head_me = lax.axis_index("head")
    block_me = lax.axis_index("blk")
    gain_rows, qkv_w, proj_w, router_w, shared_w, shared_out_w, expert_w, expert_out_w = (
        fetch_weights(
            norm_gains,
            attn_qkv,
            attn_proj,
            router_rows,
            shared_gate_up,
            shared_down,
            expert_gate_up,
            expert_down,
        )
    )
    tokens = tokens_in.astype(jnp.float32)
    first_gain = gain_rows[0].astype(jnp.float32)
    second_gain = gain_rows[1].astype(jnp.float32)
    normed_f, first_inverse = norm_rows(tokens, first_gain)
    normed = normed_f.astype(jnp.bfloat16)
    mixed_qkv = jnp.dot(normed, qkv_w, preferred_element_type=jnp.float32)
    token_row = jnp.arange(row_count, dtype=jnp.int32)
    token_pos = row_layout(
        head_me, token_row, block_me, heads_axis, blocks_axis, row_count, prompt_dev
    )[3]
    token_cos, token_sin = angle_tables(token_pos)
    query_tok = (
        rotate(mixed_qkv[:, :width_all].reshape(row_count, HEADS, DH), token_cos, token_sin)
        .reshape(row_count, width_all)
        .astype(jnp.bfloat16)
    )
    key_tok = (
        rotate(
            mixed_qkv[:, width_all : 2 * width_all].reshape(row_count, HEADS, DH),
            token_cos,
            token_sin,
        )
        .reshape(row_count, width_all)
        .astype(jnp.bfloat16)
    )
    value_tok = mixed_qkv[:, 2 * width_all :].astype(jnp.bfloat16)
    query_head, key_head, value_head = (
        lax.all_to_all(query_tok, "head", split_axis=1, concat_axis=0, tiled=True),
        lax.all_to_all(key_tok, "head", split_axis=1, concat_axis=0, tiled=True),
        lax.all_to_all(value_tok, "head", split_axis=1, concat_axis=0, tiled=True),
    )
    local_index = jnp.arange(query_rows, dtype=jnp.int32)
    is_prompt, prompt_index, cont_index, head_pos = row_layout(
        local_index // row_count,
        local_index % row_count,
        block_me,
        heads_axis,
        blocks_axis,
        row_count,
        prompt_dev,
    )
    is_cont = jnp.logical_not(is_prompt)
    local_visible = (
        is_cont[:, None] & is_cont[None, :] & (cont_index[None, :] <= cont_index[:, None])
    )
    queries = query_head.reshape(query_rows, local_heads, DH)
    key_local = key_head.reshape(query_rows, local_heads, DH)
    value_local = value_head.reshape(query_rows, local_heads, DH)
    prompt_keys, prompt_values = (
        lax.all_gather(
            key_head.reshape(heads_axis, row_count, -1)[:, :prompt_dev].reshape(
                heads_axis * prompt_dev, -1
            ),
            "blk",
            axis=0,
            tiled=True,
        ),
        lax.all_gather(
            value_head.reshape(heads_axis, row_count, -1)[:, :prompt_dev].reshape(
                heads_axis * prompt_dev, -1
            ),
            "blk",
            axis=0,
            tiled=True,
        ),
    )
    key_blocks = prompt_keys.reshape(block_count, key_block, local_heads, DH)
    value_blocks = prompt_values.reshape(block_count, key_block, local_heads, DH)
    block_starts = jnp.arange(block_count, dtype=jnp.int32) * key_block
    key_offsets = jnp.arange(key_block, dtype=jnp.int32)

    def prompt_visible(start):
        return is_cont[:, None] | (start + key_offsets[None, :] <= prompt_index[:, None])

    def stats_step(carry, member):
        visible = prompt_visible(member[1])
        return (add_stats(carry, masked_scores(queries, member[0], visible), visible), None)

    start_stats = (
        jnp.full((local_heads, query_rows), NEGATIVE, jnp.float32),
        jnp.zeros((local_heads, query_rows), jnp.float32),
    )
    stats = lax.scan(stats_step, start_stats, (key_blocks, block_starts))[0]
    row_peak, row_total = add_stats(
        stats, masked_scores(queries, key_local, local_visible), local_visible
    )
    log_total = row_peak + jnp.log(row_total)

    def output_step(total_out, member):
        visible = prompt_visible(member[2])
        soft_weights = block_probs(
            masked_scores(queries, member[0], visible), visible, log_total
        ).astype(jnp.bfloat16)
        return (
            total_out
            + jnp.einsum(
                "hqk,khd->qhd", soft_weights, member[1], preferred_element_type=jnp.float32
            ),
            None,
        )

    attn_heads = lax.scan(
        output_step,
        jnp.zeros((query_rows, local_heads, DH), jnp.float32),
        (key_blocks, value_blocks, block_starts),
    )[0]
    local_weights = block_probs(
        masked_scores(queries, key_local, local_visible), local_visible, log_total
    ).astype(jnp.bfloat16)
    attn_heads = attn_heads + jnp.einsum(
        "hqk,khd->qhd", local_weights, value_local, preferred_element_type=jnp.float32
    )
    attn_tok = lax.all_to_all(
        attn_heads.reshape(query_rows, -1).astype(jnp.bfloat16),
        "head",
        split_axis=0,
        concat_axis=1,
        tiled=True,
    )
    residual = tokens + jnp.dot(attn_tok, proj_w, preferred_element_type=jnp.float32)
    hidden_f, second_inverse = norm_rows(residual, second_gain)
    hidden = hidden_f.astype(jnp.bfloat16)
    logits = jnp.einsum("td,ed->te", hidden, router_w, preferred_element_type=jnp.float32)
    soft_route = jax.nn.softmax(logits, axis=-1)
    expert_ids = jnp.arange(EXPERTS, dtype=jnp.int32)
    route_match = routes[:, :, None] == expert_ids[None, None, :]
    gate_values = jnp.sum(jnp.where(route_match, soft_route[:, None, :], 0.0), axis=-1)
    shared_pre = jnp.dot(hidden, shared_w, preferred_element_type=jnp.float32)
    shared_act, shared_slope = swish_parts(shared_pre[:, :SFF])
    shared_up = shared_pre[:, SFF:]
    shared_mid = (shared_act * shared_up).astype(jnp.bfloat16)
    shared_out = jnp.dot(shared_mid, shared_out_w, preferred_element_type=jnp.float32)
    unit_count = expert_w.shape[2]
    per_device = max(1, unit_count // FF)
    spread = max(1, FF // unit_count)
    unit_width = unit_count // per_device
    capacity = max(2, 5 * row_count // (2 * EXPERTS))
    slot_count = blocks_axis * per_device * capacity
    pair_expert = routes.reshape(-1)
    pair_match = route_match.reshape(2 * row_count, EXPERTS).astype(jnp.int32)
    pair_rank = jnp.sum(jnp.cumsum(pair_match, axis=0) * pair_match, axis=1) - 1
    slot_base = (
        pair_expert // per_device * spread * per_device * capacity
        + pair_expert % per_device * capacity
        + pair_rank
    )
    slot_index = (
        slot_base[None, :] + (jnp.arange(spread, dtype=jnp.int32) * per_device * capacity)[:, None]
    )
    pair_ids = jnp.arange(2 * row_count, dtype=jnp.int32)
    slot_pair = (
        jnp.full((slot_count,), 2 * row_count, jnp.int32)
        .at[slot_index.reshape(-1)]
        .set(jnp.tile(pair_ids, spread))
    )
    slot_token = slot_pair // 2
    hidden_pad = jnp.concatenate([hidden, jnp.zeros((1, width_all), jnp.bfloat16)], axis=0)
    send_rows = hidden_pad[slot_token].reshape(blocks_axis, per_device, capacity, width_all)
    received_rows = lax.all_to_all(send_rows, "blk", split_axis=0, concat_axis=0, tiled=True)
    gate_weight = expert_w[0].reshape(width_all, per_device, unit_width)
    up_weight = expert_w[1].reshape(width_all, per_device, unit_width)
    down_w = expert_out_w.reshape(per_device, unit_width, width_all)
    expert_gate = jnp.einsum(
        "tfoa,afw->tfow", received_rows, gate_weight, preferred_element_type=jnp.float32
    )
    expert_up_projection = jnp.einsum(
        "tfoa,afw->tfow", received_rows, up_weight, preferred_element_type=jnp.float32
    )
    expert_activation, expert_slope = swish_parts(expert_gate)
    expert_mid = (expert_activation * expert_up_projection).astype(jnp.bfloat16)
    expert_part = jnp.einsum(
        "secm,emd->secd", expert_mid, down_w, preferred_element_type=jnp.float32
    )
    returned = (
        lax.all_to_all(
            expert_part.astype(jnp.bfloat16), "blk", split_axis=0, concat_axis=0, tiled=True
        )
        .astype(expert_part.dtype)
        .reshape(slot_count, width_all)
    )
    pair_out = jnp.sum(returned[slot_index], axis=0).reshape(row_count, 2, width_all)
    expert_sum = jnp.sum(gate_values[:, :, None] * pair_out, axis=1)
    layer_out = (residual + shared_out + expert_sum).astype(jnp.bfloat16)
    gain_rows, qkv_w, proj_w, router_w, shared_w, shared_out_w, expert_w, expert_out_w = (
        fetch_weights(
            norm_gains,
            attn_qkv,
            attn_proj,
            router_rows,
            shared_gate_up,
            shared_down,
            expert_gate_up,
            expert_down,
        )
    )
    gate_weight = expert_w[0].reshape(width_all, per_device, unit_width)
    up_weight = expert_w[1].reshape(width_all, per_device, unit_width)
    down_w = expert_out_w.reshape(per_device, unit_width, width_all)
    grad_layer = out_grad.astype(jnp.float32)
    grad_smid = jnp.einsum("td,fd->tf", out_grad, shared_out_w, preferred_element_type=jnp.float32)
    shared_grads = jnp.concatenate(
        [grad_smid * shared_up * shared_slope, grad_smid * shared_act], axis=1
    ).astype(jnp.bfloat16)
    grad_hidden = jnp.einsum(
        "tf,df->td", shared_grads, shared_w, preferred_element_type=jnp.float32
    )
    grad_shared_w = jnp.einsum(
        "td,tf->df", hidden, shared_grads, preferred_element_type=jnp.float32
    )
    grad_shared_out = jnp.einsum(
        "tf,td->fd", shared_mid, out_grad, preferred_element_type=jnp.float32
    )
    grad_gates = jnp.sum(grad_layer[:, None, :] * pair_out, axis=-1)
    grad_pairs = (
        (gate_values[:, :, None] * grad_layer[:, None, :])
        .reshape(2 * row_count, width_all)
        .astype(jnp.bfloat16)
    )
    grad_pad = jnp.concatenate([grad_pairs, jnp.zeros((1, width_all), jnp.bfloat16)], axis=0)
    grad_recv = lax.all_to_all(
        grad_pad[slot_pair].reshape(blocks_axis, per_device, capacity, width_all),
        "blk",
        split_axis=0,
        concat_axis=0,
        tiled=True,
    )
    grad_expert_middle = jnp.einsum(
        "secd,emd->secm", grad_recv, down_w, preferred_element_type=jnp.float32
    )
    grad_expert_gate_branch = (grad_expert_middle * expert_up_projection * expert_slope).astype(
        jnp.bfloat16
    )
    grad_expert_up_branch = (grad_expert_middle * expert_activation).astype(jnp.bfloat16)
    grad_rows = jnp.einsum(
        "auwj,buj->auwb", grad_expert_gate_branch, gate_weight, preferred_element_type=jnp.float32
    ) + jnp.einsum(
        "auwj,buj->auwb", grad_expert_up_branch, up_weight, preferred_element_type=jnp.float32
    )
    grad_expert_w = jnp.stack(
        [
            jnp.einsum(
                "jgki,jgkt->igt",
                received_rows,
                grad_expert_gate_branch,
                preferred_element_type=jnp.float32,
            ).reshape(width_all, unit_count),
            jnp.einsum(
                "jgki,jgkt->igt",
                received_rows,
                grad_expert_up_branch,
                preferred_element_type=jnp.float32,
            ).reshape(width_all, unit_count),
        ]
    )
    grad_expert_out = jnp.einsum(
        "secm,secd->emd", expert_mid, grad_recv, preferred_element_type=jnp.float32
    ).reshape(unit_count, width_all)
    grad_back = (
        lax.all_to_all(
            grad_rows.astype(jnp.bfloat16), "blk", split_axis=0, concat_axis=0, tiled=True
        )
        .astype(grad_rows.dtype)
        .reshape(slot_count, width_all)
    )
    grad_hidden = grad_hidden + jnp.sum(
        jnp.sum(grad_back[slot_index], axis=0).reshape(row_count, 2, width_all), axis=1
    )
    grad_soft = jnp.sum(jnp.where(route_match, grad_gates[:, :, None], 0.0), axis=1)
    grad_logits = (
        soft_route * (grad_soft - jnp.sum(soft_route * grad_soft, axis=-1, keepdims=True))
    ).astype(jnp.bfloat16)
    grad_hidden = grad_hidden + jnp.einsum(
        "te,ed->td", grad_logits, router_w, preferred_element_type=jnp.float32
    )
    grad_router = jnp.einsum("te,td->ed", grad_logits, hidden, preferred_element_type=jnp.float32)
    grad_norm_two, grad_second_gain = norm_back(residual, second_inverse, second_gain, grad_hidden)
    grad_resid = grad_layer + grad_norm_two
    grad_branch = grad_resid.astype(jnp.bfloat16)
    grad_proj = jnp.einsum("td,te->de", attn_tok, grad_branch, preferred_element_type=jnp.float32)
    grad_attn_tok = jnp.einsum(
        "te,de->td", grad_branch, proj_w, preferred_element_type=jnp.float32
    ).astype(jnp.bfloat16)
    grad_heads = lax.all_to_all(
        grad_attn_tok, "head", split_axis=1, concat_axis=0, tiled=True
    ).reshape(query_rows, local_heads, DH)
    delta = jnp.transpose(jnp.sum(grad_heads * attn_heads, axis=-1))

    def back_step(grad_acc, member):
        visible = prompt_visible(member[2])
        step_query, step_key, step_value = grad_block(
            queries, grad_heads, log_total, delta, member[0], member[1], visible
        )
        return (grad_acc + step_query, (step_key, step_value))

    grad_query, prompt_grads = lax.scan(
        back_step,
        jnp.zeros((query_rows, local_heads, DH), jnp.float32),
        (key_blocks, value_blocks, block_starts),
    )
    local_query, local_key, local_value = grad_block(
        queries, grad_heads, log_total, delta, key_local, value_local, local_visible
    )
    grad_query = grad_query + local_query
    key_share, value_share = (
        lax.psum_scatter(
            prompt_grads[0].reshape(prompt_all, -1), "blk", scatter_dimension=0, tiled=True
        ),
        lax.psum_scatter(
            prompt_grads[1].reshape(prompt_all, -1), "blk", scatter_dimension=0, tiled=True
        ),
    )
    grad_key = (
        local_key.reshape(heads_axis, row_count, -1)
        .at[:, :prompt_dev]
        .add(key_share.reshape(heads_axis, prompt_dev, -1))
        .reshape(query_rows, local_heads, DH)
    )
    grad_value = (
        local_value.reshape(heads_axis, row_count, -1)
        .at[:, :prompt_dev]
        .add(value_share.reshape(heads_axis, prompt_dev, -1))
    )
    head_cos, head_sin = angle_tables(head_pos)
    grad_query = (
        rotate(grad_query, head_cos, -head_sin).reshape(query_rows, -1).astype(jnp.bfloat16)
    )
    grad_key = rotate(grad_key, head_cos, -head_sin).reshape(query_rows, -1).astype(jnp.bfloat16)
    grad_value = grad_value.reshape(query_rows, -1).astype(jnp.bfloat16)
    grad_q_tok, grad_k_tok, grad_v_tok = (
        lax.all_to_all(grad_query, "head", split_axis=0, concat_axis=1, tiled=True),
        lax.all_to_all(grad_key, "head", split_axis=0, concat_axis=1, tiled=True),
        lax.all_to_all(grad_value, "head", split_axis=0, concat_axis=1, tiled=True),
    )
    grad_qkv_rows = jnp.concatenate([grad_q_tok, grad_k_tok, grad_v_tok], axis=1)
    grad_normed = jnp.einsum("tf,df->td", grad_qkv_rows, qkv_w, preferred_element_type=jnp.float32)
    grad_qkv = jnp.einsum("td,tf->df", normed, grad_qkv_rows, preferred_element_type=jnp.float32)
    grad_norm_one, grad_first_gain = norm_back(tokens, first_inverse, first_gain, grad_normed)
    grad_tokens = grad_resid + grad_norm_one
    owned = (
        lax.psum_scatter(
            jnp.stack([grad_first_gain, grad_second_gain]).astype(jnp.bfloat16),
            ("grp", "head"),
            scatter_dimension=1,
            tiled=True,
        ).astype(jnp.float32),
        lax.psum_scatter(
            grad_qkv.astype(jnp.bfloat16), ("grp", "head"), scatter_dimension=1, tiled=True
        ).astype(jnp.float32),
        lax.psum_scatter(
            grad_proj.astype(jnp.bfloat16), ("grp", "head"), scatter_dimension=1, tiled=True
        ).astype(jnp.float32),
        lax.psum_scatter(
            grad_router.astype(jnp.bfloat16), ("grp", "head"), scatter_dimension=1, tiled=True
        ).astype(jnp.float32),
        lax.psum_scatter(
            grad_shared_w.astype(jnp.bfloat16), ("grp", "head"), scatter_dimension=1, tiled=True
        ).astype(jnp.float32),
        lax.psum_scatter(
            grad_shared_out.astype(jnp.bfloat16), ("grp", "head"), scatter_dimension=1, tiled=True
        ).astype(jnp.float32),
        lax.psum_scatter(
            grad_expert_w.astype(jnp.bfloat16), ("grp", "head"), scatter_dimension=1, tiled=True
        ).astype(jnp.float32),
        lax.psum_scatter(
            grad_expert_out.astype(jnp.bfloat16), ("grp", "head"), scatter_dimension=1, tiled=True
        ).astype(jnp.float32),
    )
    summed = lax.psum((owned[0], owned[1], owned[2], owned[3], owned[4], owned[5]), "blk")
    return (
        layer_out,
        grad_tokens,
        summed[0],
        summed[1],
        summed[2],
        summed[3],
        summed[4],
        summed[5],
        owned[6],
        owned[7],
    )


TRANSPOSED = (((1,), (1,)), ((), ()))
PLAIN = (((1,), (0,)), ((), ()))
FIRST = (((0,), (0,)), ((), ()))
KERNEL_VMEM = 56 * 1024 * 1024


def mm(left, right, dims=PLAIN):
    return lax.dot_general(left, right, dims, preferred_element_type=jnp.float32)


def assemble(rows_ref, cut, parts, prompt_to, cont_to):
    sources = rows_ref.shape[0]
    blocks = sources // 2
    half = rows_ref.shape[1]
    for head_part in range(2):
        for block in range(blocks):
            piece = rows_ref[head_part * blocks + block]
            place = (block * 2 + head_part) * half
            for order in range(parts):
                prompt_to[order][place : place + half, :] = piece[
                    :, order * cut : (order + 1) * cut
                ]
                cont_to[order][place : place + half, :] = piece[
                    :, (parts + order) * cut : (parts + order + 1) * cut
                ]


def spread_out(target, prompt_parts, cont_parts, cut):
    sources = target.shape[0]
    blocks = sources // 2
    half = target.shape[1]
    for head_part in range(2):
        for block in range(blocks):
            place = (block * 2 + head_part) * half
            pieces = [part[place : place + half, :] for part in prompt_parts]
            pieces += [part[place : place + half, :] for part in cont_parts]
            target[head_part * blocks + block] = jnp.concatenate(pieces, axis=1).astype(
                target.dtype
            )


def causal_mask(rows):
    keys = lax.broadcasted_iota(jnp.int32, (rows, rows), 0)
    query = lax.broadcasted_iota(jnp.int32, (rows, rows), 1)
    return keys <= query


def cont_mask(rows, cont):
    keys = lax.broadcasted_iota(jnp.int32, (rows, rows), 0)
    query = lax.broadcasted_iota(jnp.int32, (rows, rows), 1)
    return (keys // cont == query // cont) & (keys <= query)


def attention_parts(step, block):
    if step is None:
        return None
    return (0, step * block)


def masked_block(keys, queries, mask):
    scores = mm(keys, queries, TRANSPOSED) * DH ** (-0.5)
    if mask is None:
        return scores
    return jnp.where(mask, scores, NEGATIVE)


def attention_kernel(rows_ref, out_ref, qp, kp, vp, qc, kc, vc, op, oc):
    block = 256
    prompt = qp.shape[0]
    assemble(rows_ref, DH, 3, (qp, kp, vp), (qc, kc, vc))
    cont = 2 * rows_ref.shape[1]
    for is_cont in range(2):
        source_q, source_k, source_v, result = (
            (qc, kc, vc, oc) if is_cont else (qp, kp, vp, op)
        )
        mask = cont_mask(block, cont) if is_cont else causal_mask(block)
        for step in range(prompt // block):
            rows = slice(step * block, (step + 1) * block)
            queries = source_q[rows, :]
            own = masked_block(source_k[rows, :], queries, mask)
            seen = prompt if is_cont else step * block
            peak = jnp.max(own, axis=0, keepdims=True)
            if seen:
                past = masked_block(kp[0:seen, :], queries, None)
                peak = jnp.maximum(peak, jnp.max(past, axis=0, keepdims=True))
            own = jnp.exp(own - peak)
            total = jnp.sum(own, axis=0, keepdims=True)
            gathered = mm(source_v[rows, :], own.astype(jnp.bfloat16), FIRST)
            if seen:
                past = jnp.exp(past - peak)
                total = total + jnp.sum(past, axis=0, keepdims=True)
                gathered = gathered + mm(vp[0:seen, :], past.astype(jnp.bfloat16), FIRST)
            result[rows, :] = jnp.transpose(gathered / total)
    spread_out(out_ref, (op,), (oc,), DH)


def attention_forward(rows):
    sources, half, _ = rows.shape
    prompt = sources * half
    small = pltpu.VMEM((prompt, DH), jnp.bfloat16)
    wide = pltpu.VMEM((prompt, DH), jnp.float32)
    return pl.pallas_call(
        attention_kernel,
        out_shape=jax.ShapeDtypeStruct((sources, half, 2 * DH), jnp.bfloat16),
        in_specs=[pl.BlockSpec(memory_space=pltpu.VMEM)],
        out_specs=pl.BlockSpec(memory_space=pltpu.VMEM),
        scratch_shapes=[small] * 6 + [wide] * 2,
        compiler_params=pltpu.CompilerParams(vmem_limit_bytes=KERNEL_VMEM),
        cost_estimate=pl.CostEstimate(
            flops=4 * 2 * prompt * prompt * DH, bytes_accessed=4 * 2**20, transcendentals=2**21
        ),
        name="attention_forward",
    )(rows)


def turn_back(values, cosine, sine):
    half = DH // 2
    first, second = values[:, :half], values[:, half:]
    return jnp.concatenate(
        [first * cosine + second * sine, second * cosine - first * sine], axis=1
    )


def attention_back_kernel(
    rows_ref, grad_ref, cos_ref, sin_ref, out_ref,
    qp, kp, vp, qc, kc, vc, gp, gc, dqp, dkp, dvp, dqc, dkc, dvc,
):
    block = 256
    prompt = qp.shape[0]
    scale = DH ** (-0.5)
    assemble(rows_ref, DH, 3, (qp, kp, vp), (qc, kc, vc))
    assemble(grad_ref, DH, 1, (gp,), (gc,))
    cont = 2 * rows_ref.shape[1]
    dkp[...] = jnp.zeros_like(dkp)
    dvp[...] = jnp.zeros_like(dvp)
    for is_cont in range(2):
        source_q, source_k, source_v, source_g = (
            (qc, kc, vc, gc) if is_cont else (qp, kp, vp, gp)
        )
        to_q, to_k, to_v = (dqc, dkc, dvc) if is_cont else (dqp, dkp, dvp)
        mask = cont_mask(block, cont) if is_cont else causal_mask(block)
        for step in range(prompt // block):
            rows = slice(step * block, (step + 1) * block)
            queries = source_q[rows, :]
            grads = source_g[rows, :]
            own_keys = source_k[rows, :]
            own = masked_block(own_keys, queries, mask)
            seen = prompt if is_cont else step * block
            peak = jnp.max(own, axis=0, keepdims=True)
            if seen:
                past = masked_block(kp[0:seen, :], queries, None)
                peak = jnp.maximum(peak, jnp.max(past, axis=0, keepdims=True))
            own = jnp.exp(own - peak)
            total = jnp.sum(own, axis=0, keepdims=True)
            if seen:
                past = jnp.exp(past - peak)
                total = total + jnp.sum(past, axis=0, keepdims=True)
            inverse = 1.0 / total
            own = own * inverse
            own_grad = mm(source_v[rows, :], grads, TRANSPOSED)
            delta = jnp.sum(own * own_grad, axis=0, keepdims=True)
            if seen:
                past = past * inverse
                past_grad = mm(vp[0:seen, :], grads, TRANSPOSED)
                delta = delta + jnp.sum(past * past_grad, axis=0, keepdims=True)
            own_scores = (own * (own_grad - delta)).astype(jnp.bfloat16)
            own_dv = mm(own.astype(jnp.bfloat16), grads)
            own_dk = mm(own_scores, queries) * scale
            turned = mm(own_keys, own_scores, FIRST)
            if is_cont:
                to_v[rows, :] = own_dv
                to_k[rows, :] = own_dk
            else:
                to_v[rows, :] += own_dv
                to_k[rows, :] += own_dk
            if seen:
                past_scores = (past * (past_grad - delta)).astype(jnp.bfloat16)
                dvp[0:seen, :] += mm(past.astype(jnp.bfloat16), grads)
                dkp[0:seen, :] += mm(past_scores, queries) * scale
                turned = turned + mm(kp[0:seen, :], past_scores, FIRST)
            to_q[rows, :] = jnp.transpose(turned) * scale
    cos_p, sin_p = cos_ref[0:prompt, :], sin_ref[0:prompt, :]
    dqp[...] = turn_back(dqp[...], cos_p, sin_p)
    dkp[...] = turn_back(dkp[...], cos_p, sin_p)
    for step in range(prompt // cont):
        rows = slice(step * cont, (step + 1) * cont)
        cos_c, sin_c = cos_ref[prompt : prompt + cont, :], sin_ref[prompt : prompt + cont, :]
        dqc[rows, :] = turn_back(dqc[rows, :], cos_c, sin_c)
        dkc[rows, :] = turn_back(dkc[rows, :], cos_c, sin_c)
    spread_out(out_ref, (dqp, dkp, dvp), (dqc, dkc, dvc), DH)


def attention_backward(rows, grads, cosine, sine):
    sources, half, wide = rows.shape
    prompt = sources * half
    small = pltpu.VMEM((prompt, DH), jnp.bfloat16)
    large = pltpu.VMEM((prompt, DH), jnp.float32)
    return pl.pallas_call(
        attention_back_kernel,
        out_shape=jax.ShapeDtypeStruct((sources, half, wide), jnp.bfloat16),
        in_specs=[pl.BlockSpec(memory_space=pltpu.VMEM)] * 4,
        out_specs=pl.BlockSpec(memory_space=pltpu.VMEM),
        scratch_shapes=[small] * 8 + [large] * 6,
        compiler_params=pltpu.CompilerParams(vmem_limit_bytes=KERNEL_VMEM),
        cost_estimate=pl.CostEstimate(
            flops=10 * 2 * prompt * prompt * DH, bytes_accessed=8 * 2**20, transcendentals=2**21
        ),
        name="attention_backward",
    )(rows, grads, cosine, sine)


def exchange(values, axis, mask):
    return lax.ppermute(values, axis, [(i, i ^ mask) for i in range(lax.axis_size(axis))])


def line_sum(values):
    place = lax.axis_index("blk")
    rows = values.shape[0]
    masks = []
    mask = 2
    while mask < lax.axis_size("blk"):
        masks.append(mask)
        mask *= 2
    part = values
    for mask in masks:
        half = part.shape[0] // 2
        upper = (place // mask) % 2
        kept = lax.dynamic_slice_in_dim(part, upper * half, half, 0)
        given = lax.dynamic_slice_in_dim(part, (1 - upper) * half, half, 0)
        part = kept + exchange(given.astype(jnp.bfloat16), "blk", mask).astype(jnp.float32)
    part = part.astype(jnp.bfloat16)
    for mask in reversed(masks):
        upper = (place // mask) % 2 == 1
        other = exchange(part, "blk", mask)
        part = jnp.concatenate(
            [jnp.where(upper, other, part), jnp.where(upper, part, other)], axis=0
        )
    return part


def pair_order(own, other, core):
    return jnp.where(core == 0, own, other), jnp.where(core == 0, other, own)


def quick_body(
    tokens_in,
    norm_gains,
    attn_qkv,
    attn_proj,
    router_rows,
    shared_gate_up,
    shared_down,
    expert_gate_up,
    expert_down,
    routes,
    out_grad,
):
    quad = ("grp", "head")
    line = ("head", "blk")
    blocks = lax.axis_size("blk")
    rows, width = tokens_in.shape
    grp, head, blk = lax.axis_index("grp"), lax.axis_index("head"), lax.axis_index("blk")
    core = blk % 2
    quarter = width // 4
    prompt_dev = max(PROMPT_ROWS, PROMPT_LEAST // (2 * blocks))
    prompt = prompt_dev * 2 * blocks
    cont = 2 * (rows - prompt_dev)
    halves = width // 2
    bf16, f32 = jnp.bfloat16, jnp.float32

    few = jnp.concatenate([norm_gains, router_rows], axis=0)
    few = jnp.pad(few, ((0, 20 - few.shape[0]), (0, 0)))
    few = jnp.concatenate([few[5 * i : 5 * i + 5] for i in range(4)], axis=1)
    few = jnp.pad(few, ((0, 3), (0, 0)))
    half_rows = lax.dynamic_slice_in_dim(
        jnp.concatenate([attn_qkv, attn_proj], axis=1), core * halves, halves, 0
    )
    own_w = lax.all_gather(jnp.concatenate([half_rows, few], axis=0), quad, axis=0)
    other_w = exchange(own_w, "blk", 1)
    few = own_w[:, halves : halves + 5].reshape(4, 5, 4, quarter)
    few = jnp.transpose(few, (2, 1, 0, 3)).reshape(20, width)
    gains = few[0:2].astype(f32)
    router_w = few[2 : 2 + EXPERTS]

    units = expert_gate_up.shape[2] // 4
    gate_send = jnp.transpose(expert_gate_up[0].reshape(quarter, 4, units), (1, 0, 2))
    up_send = jnp.transpose(expert_gate_up[1].reshape(quarter, 4, units), (1, 0, 2))
    down_send = jnp.transpose(expert_down.reshape(4, units, quarter), (0, 2, 1))
    gate_w = lax.all_to_all(gate_send, quad, 0, 0, tiled=True).reshape(width, units)
    up_w = lax.all_to_all(up_send, quad, 0, 0, tiled=True).reshape(width, units)
    down_w = lax.all_to_all(down_send, quad, 0, 0, tiled=True).reshape(width, units)

    span = SFF // 4
    shared_half = lax.dynamic_slice_in_dim(shared_gate_up, core * span, span, 1)
    shared_w = lax.all_gather(shared_half, quad, axis=0)
    down_half = jnp.concatenate(
        [
            lax.dynamic_slice_in_dim(shared_down, core * span, span, 0),
            lax.dynamic_slice_in_dim(shared_down, 2 * span + core * span, span, 0),
        ],
        axis=0,
    )
    shared_out_w = lax.all_gather(jnp.transpose(down_half), quad, axis=0).reshape(width, 2 * span)

    expert_ids = jnp.arange(EXPERTS, dtype=jnp.int32)
    match = (routes[:, :, None] == expert_ids).astype(jnp.int32)
    flat = match.reshape(2 * rows, EXPERTS)
    rank = (jnp.sum(jnp.cumsum(flat, axis=0) * flat, axis=1) - 1).reshape(rows, 2)
    capacity = 5 * rows // (2 * EXPERTS)
    slots = (routes // 2) * (2 * capacity) + (routes % 2 ^ grp) * capacity + rank
    slot_ids = jnp.arange(2 * capacity * blocks, dtype=jnp.int32)[:, None]
    pick = ((slot_ids == slots[:, 0]) | (slot_ids == slots[:, 1])).astype(bf16)

    def dispatch(values):
        sent = mm(pick, values).astype(bf16).reshape(blocks, 2 * capacity, width)
        got = lax.all_to_all(sent, "blk", 0, 0, tiled=True)
        kept = got[:, :capacity].reshape(blocks * capacity, width)
        given = got[:, capacity:].reshape(blocks * capacity, width)
        mine = jnp.concatenate([kept, exchange(given, "grp", 1)], axis=0)
        return jnp.concatenate([mine, exchange(mine, "head", 1)], axis=0)

    def bring_back(values):
        half = values.shape[0] // 2
        other = exchange(values[half:].astype(bf16), "head", 1)
        mine = (values[:half] + other.astype(f32)).astype(bf16)
        kept = mine[: half // 2].reshape(blocks, capacity, width)
        given = exchange(mine[half // 2 :], "grp", 1).reshape(blocks, capacity, width)
        got = lax.all_to_all(
            jnp.concatenate([kept, given], axis=1), "blk", 0, 0, tiled=True
        ).reshape(2 * capacity * blocks, width)
        return mm(pick, got, FIRST)

    grad_rows_in = dispatch(out_grad)
    grad_two = jnp.concatenate([out_grad, exchange(out_grad, "blk", 1)], axis=0)

    tokens = tokens_in.astype(f32)
    normed_f, first_inverse = norm_rows(tokens, gains[0])
    normed = normed_f.astype(bf16)
    normed_own = lax.dynamic_slice_in_dim(normed, core * halves, halves, 1)
    normed_other = lax.dynamic_slice_in_dim(normed, (1 - core) * halves, halves, 1)
    third = attn_qkv.shape[1]
    mixed = jnp.concatenate(
        [
            mm(normed_own, own_w[i, :halves, :third]) + mm(normed_other, other_w[i, :halves, :third])
            for i in range(4)
        ],
        axis=1,
    )
    token_row = jnp.arange(rows, dtype=jnp.int32)
    token_pos = row_layout(head, token_row, blk, 2, blocks, rows, prompt_dev)[3]
    token_cos, token_sin = angle_tables(token_pos)
    cubes = mixed.reshape(rows, 3, HEADS, DH)
    query_tok = rotate(cubes[:, 0], token_cos, token_sin)
    key_tok = rotate(cubes[:, 1], token_cos, token_sin)
    cubes = jnp.stack([query_tok, key_tok, cubes[:, 2]], axis=1).astype(bf16)

    def to_heads(values):
        count = values.shape[1]
        parts = values.reshape(2, prompt_dev, count, HEADS, DH)
        parts = jnp.transpose(parts, (3, 1, 0, 2, 4)).reshape(
            2, HEADS // 2, prompt_dev, 2 * count * DH
        )
        parts = jnp.pad(parts, ((0, 0), (0, blocks - HEADS // 2), (0, 0), (0, 0)))
        parts = parts.reshape(2 * blocks, prompt_dev, 2 * count * DH)
        return lax.all_to_all(parts, line, 0, 0, tiled=True)

    def to_tokens(values, count):
        got = lax.all_to_all(values, line, 0, 0, tiled=True)
        got = got.reshape(2, blocks, prompt_dev, 2, count, DH)[:, : HEADS // 2]
        return jnp.transpose(got, (3, 2, 4, 0, 1, 5)).reshape(rows, count * width)

    head_rows = to_heads(cubes)
    attn_tok = to_tokens(attention_forward(head_rows), 1)

    attn_own = lax.dynamic_slice_in_dim(attn_tok, core * halves, halves, 1)
    attn_other = lax.dynamic_slice_in_dim(attn_tok, (1 - core) * halves, halves, 1)
    residual = tokens + jnp.concatenate(
        [
            mm(attn_own, own_w[i, :halves, third:]) + mm(attn_other, other_w[i, :halves, third:])
            for i in range(4)
        ],
        axis=1,
    )
    hidden_f, second_inverse = norm_rows(residual, gains[1])
    hidden = hidden_f.astype(bf16)

    got_rows = dispatch(hidden)
    soft = jax.nn.softmax(mm(got_rows, router_w, TRANSPOSED), axis=-1)
    is_mine = (expert_ids == 2 * blk + grp).astype(f32)
    gate = jnp.sum(soft * is_mine, axis=1, keepdims=True)
    e_gate = mm(got_rows, gate_w)
    e_up = mm(got_rows, up_w)
    e_act, e_slope = swish_parts(e_gate)
    e_mid_f = e_act * e_up
    e_mid = e_mid_f.astype(bf16)
    e_grad = mm(grad_rows_in, down_w)
    g_gate = jnp.sum(e_mid_f * e_grad, axis=1, keepdims=True)
    g_mid = e_grad * gate
    g_egate = (g_mid * e_up * e_slope).astype(bf16)
    g_eup = (g_mid * e_act).astype(bf16)
    g_logits = (g_gate * soft * (is_mine - gate)).astype(bf16)
    g_rows = (
        mm(g_egate, gate_w, TRANSPOSED) + mm(g_eup, up_w, TRANSPOSED) + mm(g_logits, router_w)
    )
    g_hidden = bring_back(g_rows)
    g_eout = (gate * grad_rows_in.astype(f32)).astype(bf16)
    expert_sum = bring_back(gate * mm(e_mid, down_w, TRANSPOSED))
    g_router = mm(g_logits, got_rows, FIRST)

    def units_back(values):
        got = lax.all_to_all(
            values.astype(bf16).reshape(4, quarter, units), quad, 0, 0, tiled=True
        )
        return got

    g_gate_w = units_back(mm(got_rows, g_egate, FIRST))
    g_up_w = units_back(mm(got_rows, g_eup, FIRST))
    g_down_w = units_back(mm(g_eout, e_mid, FIRST))
    grad_expert_w = jnp.stack(
        [
            jnp.transpose(part, (1, 0, 2)).reshape(quarter, 4 * units).astype(f32)
            for part in (g_gate_w, g_up_w)
        ]
    )
    grad_expert_out = jnp.transpose(g_down_w, (0, 2, 1)).reshape(4 * units, quarter).astype(f32)

    hidden_two = jnp.concatenate([hidden, exchange(hidden, "blk", 1)], axis=0)
    s_gate = jnp.concatenate([mm(hidden_two, shared_w[0]), mm(hidden_two, shared_w[1])], axis=1)
    s_up = jnp.concatenate([mm(hidden_two, shared_w[2]), mm(hidden_two, shared_w[3])], axis=1)
    s_act, s_slope = swish_parts(s_gate)
    s_mid = (s_act * s_up).astype(bf16)

    def over_cores(values):
        return values[:rows] + exchange(values[rows:].astype(bf16), "blk", 1).astype(f32)

    shared_out = over_cores(mm(s_mid, shared_out_w, TRANSPOSED))
    layer_out = (residual + shared_out + expert_sum).astype(bf16)
    g_smid = mm(grad_two, shared_out_w)
    g_sgate = (g_smid * s_up * s_slope).astype(bf16)
    g_sup = (g_smid * s_act).astype(bf16)
    g_shared = [g_sgate[:, :span], g_sgate[:, span:], g_sup[:, :span], g_sup[:, span:]]
    g_hidden = g_hidden + over_cores(
        sum(mm(g_shared[i], shared_w[i], TRANSPOSED) for i in range(4))
    )
    g_shared_w = jnp.stack([mm(hidden_two, part, FIRST) for part in g_shared]).astype(bf16)
    g_shared_w = lax.psum_scatter(g_shared_w, quad, scatter_dimension=0)
    g_shared_out = mm(grad_two, s_mid, FIRST).astype(bf16).reshape(4, quarter, 2 * span)
    g_shared_out = lax.psum_scatter(g_shared_out, quad, scatter_dimension=0)
    g_shared_sum = line_sum(
        jnp.concatenate(
            [g_shared_w, g_shared_out[:, :span], g_shared_out[:, span:]], axis=0
        ).astype(f32)
    )
    first, second = pair_order(g_shared_sum, exchange(g_shared_sum, "blk", 1), core)
    grad_shared_w = jnp.concatenate([first[:width], second[:width]], axis=1).astype(f32)
    low_part, high_part = first[width:], second[width:]
    grad_shared_out = jnp.transpose(
        jnp.concatenate(
            [low_part[:quarter], high_part[:quarter], low_part[quarter:], high_part[quarter:]],
            axis=1,
        )
    ).astype(f32)

    g_norm_two, g_second_gain = norm_back(residual, second_inverse, gains[1], g_hidden)
    g_resid = out_grad.astype(f32) + g_norm_two
    g_branch = g_resid.astype(bf16)
    g_branch_parts = [g_branch[:, i * quarter : (i + 1) * quarter] for i in range(4)]
    g_attn_own = sum(mm(g_branch_parts[i], own_w[i, :halves, third:], TRANSPOSED) for i in range(4))
    g_attn_other = sum(
        mm(g_branch_parts[i], other_w[i, :halves, third:], TRANSPOSED) for i in range(4)
    )
    g_attn = jnp.concatenate(pair_order(g_attn_own, g_attn_other, core), axis=1).astype(bf16)
    grad_heads = to_heads(g_attn.reshape(rows, 1, HEADS, DH))
    all_cos, all_sin = angle_tables(jnp.arange(prompt + cont, dtype=jnp.int32))
    g_head_rows = attention_backward(head_rows, grad_heads, all_cos[:, 0], all_sin[:, 0])
    g_qkv = to_tokens(g_head_rows, 3)

    g_qkv_parts = [g_qkv[:, i * third : (i + 1) * third] for i in range(4)]
    g_normed_own = sum(mm(g_qkv_parts[i], own_w[i, :halves, :third], TRANSPOSED) for i in range(4))
    g_normed_other = sum(
        mm(g_qkv_parts[i], other_w[i, :halves, :third], TRANSPOSED) for i in range(4)
    )
    g_normed = jnp.concatenate(pair_order(g_normed_own, g_normed_other, core), axis=1)
    g_norm_one, g_first_gain = norm_back(tokens, first_inverse, gains[0], g_normed)
    grad_tokens = g_resid + g_norm_one

    def both_cores(own, whole):
        mine = lax.dynamic_slice_in_dim(own, core * halves, halves, 1)
        theirs = exchange(lax.dynamic_slice_in_dim(own, (1 - core) * halves, halves, 1), "blk", 1)
        return mm(mine, whole, FIRST) + mm(theirs, exchange(whole, "blk", 1), FIRST)

    g_qkv_half = both_cores(normed, g_qkv)
    g_proj_half = both_cores(attn_tok, g_branch)
    few = jnp.concatenate([g_first_gain[None], g_second_gain[None], g_router], axis=0)
    few = few + exchange(few, "blk", 1)
    few = jnp.transpose(
        jnp.pad(few, ((0, 2), (0, 0))).reshape(4, 5, 4, quarter), (2, 1, 0, 3)
    ).reshape(4, 5, width)
    few = jnp.pad(few, ((0, 0), (0, 3), (0, 0)))
    halved = jnp.concatenate(
        [
            jnp.transpose(g_qkv_half.reshape(halves, 4, third), (1, 0, 2)),
            jnp.transpose(g_proj_half.reshape(halves, 4, quarter), (1, 0, 2)),
        ],
        axis=2,
    )
    halved = jnp.concatenate([halved, few], axis=1).astype(bf16)
    halved = lax.psum_scatter(halved, quad, scatter_dimension=0)
    halved = jnp.pad(halved.astype(f32), ((0, 8), (0, 0)))
    halved = line_sum(halved)
    first, second = pair_order(halved, exchange(halved, "blk", 1), core)
    both = jnp.concatenate([first[:halves], second[:halves]], axis=0).astype(f32)
    few = first[halves : halves + 5].reshape(5, 4, quarter)
    few = jnp.transpose(few, (1, 0, 2)).reshape(20, quarter).astype(f32)
    return (
        layer_out,
        grad_tokens,
        few[0:2],
        both[:, :third],
        both[:, third:],
        few[2 : 2 + EXPERTS],
        grad_shared_w,
        grad_shared_out,
        grad_expert_w,
        grad_expert_out,
    )


def solution(mesh):
    whole = P(("grp", "head", "blk"), None)
    split = P(None, ("grp", "head"))
    sizes = dict(mesh.shape)
    quick = sizes["grp"] == 2 and sizes["head"] == 2 and sizes["blk"] * 2 == EXPERTS
    return jax.shard_map(
        quick_body if quick else body,
        mesh=mesh,
        in_specs=(
            whole, split, split, split, split, split, split,
            P(None, ("grp", "head"), "blk"), P("blk", ("grp", "head")), whole, whole,
        ),
        out_specs=(
            whole, whole, split, split, split, split, split, split,
            P(None, ("grp", "head"), "blk"), P("blk", ("grp", "head")),
        ),
        check_vma=False,
    )
```

```python
import jax
import jax.numpy as jnp
from jax import lax
from jax.experimental import pallas as pl
from jax.experimental.pallas import tpu as pltpu
from jax.sharding import PartitionSpec as P

HEADS = 12
DH = 64
EXPERTS = 16
FF = 2048
SFF = 2048
PROMPT_ROWS = 64
PROMPT_LEAST = 1024


EPSILON = 1e-06
NEGATIVE = -1e30


def norm_rows(values, gain):
    inverse = lax.rsqrt(jnp.mean(values * values, axis=-1, keepdims=True) + EPSILON)
    return (values * inverse * gain, inverse)


def norm_back(values, inverse, gain, upstream):
    scaled = upstream * gain
    inner_mean = jnp.mean(scaled * values, axis=-1, keepdims=True)
    return (
        inverse * scaled - values * inverse**3 * inner_mean,
        jnp.sum(upstream * values * inverse, axis=0),
    )


def angle_tables(positions):
    step_index = jnp.arange(DH // 2, dtype=jnp.float32)
    freq_rates = 10000.0 ** (-2.0 * step_index / DH)
    angles = positions.astype(jnp.float32)[:, None] * freq_rates[None, :]
    return (jnp.cos(angles)[:, None, :], jnp.sin(angles)[:, None, :])


def rotate(values, cosine, sine_table):
    half_size = values.shape[-1] // 2
    first_half = values[..., :half_size]
    second = values[..., half_size:]
    return jnp.concatenate(
        [first_half * cosine - second * sine_table, second * cosine + first_half * sine_table],
        axis=-1,
    )


def swish_parts(gate_value):
    sigmoid = jax.nn.sigmoid(gate_value)
    return (gate_value * sigmoid, sigmoid * (1.0 + gate_value * (1.0 - sigmoid)))


def row_layout(head_part, within, block_index, heads_axis, blocks_axis, row_count, prompt_dev):
    prompt_all = prompt_dev * heads_axis * blocks_axis
    is_prompt = within < prompt_dev
    prompt_index = (block_index * heads_axis + head_part) * prompt_dev + within
    cont_index = head_part * (row_count - prompt_dev) + within - prompt_dev
    positions = jnp.where(is_prompt, prompt_index, prompt_all + cont_index)
    return (is_prompt, prompt_index, cont_index, positions)


def fetch_weights(
    norm_gains,
    attn_qkv,
    attn_proj,
    router_rows,
    shared_gate_up,
    shared_down,
    expert_gate_up,
    expert_down,
):
    return (
        lax.all_gather(norm_gains, ("grp", "head"), axis=1, tiled=True),
        lax.all_gather(attn_qkv, ("grp", "head"), axis=1, tiled=True),
        lax.all_gather(attn_proj, ("grp", "head"), axis=1, tiled=True),
        lax.all_gather(router_rows, ("grp", "head"), axis=1, tiled=True),
        lax.all_gather(shared_gate_up, ("grp", "head"), axis=1, tiled=True),
        lax.all_gather(shared_down, ("grp", "head"), axis=1, tiled=True),
        lax.all_gather(expert_gate_up, ("grp", "head"), axis=1, tiled=True),
        lax.all_gather(expert_down, ("grp", "head"), axis=1, tiled=True),
    )


def masked_scores(queries, key_rows, visible):
    scores = jnp.einsum(
        "qhd,khd->hqk", queries, key_rows, preferred_element_type=jnp.float32
    ) * DH ** (-0.5)
    return jnp.where(visible[None], scores, NEGATIVE)


def add_stats(carry, scores, visible):
    row_peak, row_total = carry
    new_peak = jnp.maximum(row_peak, jnp.max(scores, axis=-1))
    terms = jnp.where(visible[None], jnp.exp(scores - new_peak[:, :, None]), 0.0)
    return (new_peak, row_total * jnp.exp(row_peak - new_peak) + jnp.sum(terms, axis=-1))


def block_probs(scores, visible, log_total):
    return jnp.where(visible[None], jnp.exp(scores - log_total[:, :, None]), 0.0)


def grad_block(queries, grad_out, log_total, delta, key_rows, value_rows, visible):
    scale_factor = DH ** (-0.5)
    soft_weights = block_probs(masked_scores(queries, key_rows, visible), visible, log_total)
    grad_weights = jnp.einsum(
        "qhd,khd->hqk", grad_out, value_rows, preferred_element_type=jnp.float32
    )
    grad_scores = (soft_weights * (grad_weights - delta[:, :, None])).astype(jnp.bfloat16)
    grad_query = (
        jnp.einsum("hqk,khd->qhd", grad_scores, key_rows, preferred_element_type=jnp.float32)
        * scale_factor
    )
    grad_key = (
        jnp.einsum("hqk,qhd->khd", grad_scores, queries, preferred_element_type=jnp.float32)
        * scale_factor
    )
    grad_value = jnp.einsum(
        "hqk,qhd->khd",
        soft_weights.astype(jnp.bfloat16),
        grad_out,
        preferred_element_type=jnp.float32,
    )
    return (grad_query, grad_key, grad_value)


def body(
    tokens_in,
    norm_gains,
    attn_qkv,
    attn_proj,
    router_rows,
    shared_gate_up,
    shared_down,
    expert_gate_up,
    expert_down,
    routes,
    out_grad,
):
    heads_axis = lax.axis_size("head")
    blocks_axis = lax.axis_size("blk")
    row_count = tokens_in.shape[0]
    width_all = tokens_in.shape[1]
    prompt_dev = max(PROMPT_ROWS, PROMPT_LEAST // (heads_axis * blocks_axis))
    prompt_all = prompt_dev * heads_axis * blocks_axis
    local_heads = HEADS // heads_axis
    query_rows = heads_axis * row_count
    key_block = min(512, prompt_all)
    block_count = prompt_all // key_block
    head_me = lax.axis_index("head")
    block_me = lax.axis_index("blk")
    gain_rows, qkv_w, proj_w, router_w, shared_w, shared_out_w, expert_w, expert_out_w = (
        fetch_weights(
            norm_gains,
            attn_qkv,
            attn_proj,
            router_rows,
            shared_gate_up,
            shared_down,
            expert_gate_up,
            expert_down,
        )
    )
    tokens = tokens_in.astype(jnp.float32)
    first_gain = gain_rows[0].astype(jnp.float32)
    second_gain = gain_rows[1].astype(jnp.float32)
    normed_f, first_inverse = norm_rows(tokens, first_gain)
    normed = normed_f.astype(jnp.bfloat16)
    mixed_qkv = jnp.dot(normed, qkv_w, preferred_element_type=jnp.float32)
    token_row = jnp.arange(row_count, dtype=jnp.int32)
    token_pos = row_layout(
        head_me, token_row, block_me, heads_axis, blocks_axis, row_count, prompt_dev
    )[3]
    token_cos, token_sin = angle_tables(token_pos)
    query_tok = (
        rotate(mixed_qkv[:, :width_all].reshape(row_count, HEADS, DH), token_cos, token_sin)
        .reshape(row_count, width_all)
        .astype(jnp.bfloat16)
    )
    key_tok = (
        rotate(
            mixed_qkv[:, width_all : 2 * width_all].reshape(row_count, HEADS, DH),
            token_cos,
            token_sin,
        )
        .reshape(row_count, width_all)
        .astype(jnp.bfloat16)
    )
    value_tok = mixed_qkv[:, 2 * width_all :].astype(jnp.bfloat16)
    query_head, key_head, value_head = (
        lax.all_to_all(query_tok, "head", split_axis=1, concat_axis=0, tiled=True),
        lax.all_to_all(key_tok, "head", split_axis=1, concat_axis=0, tiled=True),
        lax.all_to_all(value_tok, "head", split_axis=1, concat_axis=0, tiled=True),
    )
    local_index = jnp.arange(query_rows, dtype=jnp.int32)
    is_prompt, prompt_index, cont_index, head_pos = row_layout(
        local_index // row_count,
        local_index % row_count,
        block_me,
        heads_axis,
        blocks_axis,
        row_count,
        prompt_dev,
    )
    is_cont = jnp.logical_not(is_prompt)
    local_visible = (
        is_cont[:, None] & is_cont[None, :] & (cont_index[None, :] <= cont_index[:, None])
    )
    queries = query_head.reshape(query_rows, local_heads, DH)
    key_local = key_head.reshape(query_rows, local_heads, DH)
    value_local = value_head.reshape(query_rows, local_heads, DH)
    prompt_keys, prompt_values = (
        lax.all_gather(
            key_head.reshape(heads_axis, row_count, -1)[:, :prompt_dev].reshape(
                heads_axis * prompt_dev, -1
            ),
            "blk",
            axis=0,
            tiled=True,
        ),
        lax.all_gather(
            value_head.reshape(heads_axis, row_count, -1)[:, :prompt_dev].reshape(
                heads_axis * prompt_dev, -1
            ),
            "blk",
            axis=0,
            tiled=True,
        ),
    )
    key_blocks = prompt_keys.reshape(block_count, key_block, local_heads, DH)
    value_blocks = prompt_values.reshape(block_count, key_block, local_heads, DH)
    block_starts = jnp.arange(block_count, dtype=jnp.int32) * key_block
    key_offsets = jnp.arange(key_block, dtype=jnp.int32)

    def prompt_visible(start):
        return is_cont[:, None] | (start + key_offsets[None, :] <= prompt_index[:, None])

    def stats_step(carry, member):
        visible = prompt_visible(member[1])
        return (add_stats(carry, masked_scores(queries, member[0], visible), visible), None)

    start_stats = (
        jnp.full((local_heads, query_rows), NEGATIVE, jnp.float32),
        jnp.zeros((local_heads, query_rows), jnp.float32),
    )
    stats = lax.scan(stats_step, start_stats, (key_blocks, block_starts))[0]
    row_peak, row_total = add_stats(
        stats, masked_scores(queries, key_local, local_visible), local_visible
    )
    log_total = row_peak + jnp.log(row_total)

    def output_step(total_out, member):
        visible = prompt_visible(member[2])
        soft_weights = block_probs(
            masked_scores(queries, member[0], visible), visible, log_total
        ).astype(jnp.bfloat16)
        return (
            total_out
            + jnp.einsum(
                "hqk,khd->qhd", soft_weights, member[1], preferred_element_type=jnp.float32
            ),
            None,
        )

    attn_heads = lax.scan(
        output_step,
        jnp.zeros((query_rows, local_heads, DH), jnp.float32),
        (key_blocks, value_blocks, block_starts),
    )[0]
    local_weights = block_probs(
        masked_scores(queries, key_local, local_visible), local_visible, log_total
    ).astype(jnp.bfloat16)
    attn_heads = attn_heads + jnp.einsum(
        "hqk,khd->qhd", local_weights, value_local, preferred_element_type=jnp.float32
    )
    attn_tok = lax.all_to_all(
        attn_heads.reshape(query_rows, -1).astype(jnp.bfloat16),
        "head",
        split_axis=0,
        concat_axis=1,
        tiled=True,
    )
    residual = tokens + jnp.dot(attn_tok, proj_w, preferred_element_type=jnp.float32)
    hidden_f, second_inverse = norm_rows(residual, second_gain)
    hidden = hidden_f.astype(jnp.bfloat16)
    logits = jnp.einsum("td,ed->te", hidden, router_w, preferred_element_type=jnp.float32)
    soft_route = jax.nn.softmax(logits, axis=-1)
    expert_ids = jnp.arange(EXPERTS, dtype=jnp.int32)
    route_match = routes[:, :, None] == expert_ids[None, None, :]
    gate_values = jnp.sum(jnp.where(route_match, soft_route[:, None, :], 0.0), axis=-1)
    shared_pre = jnp.dot(hidden, shared_w, preferred_element_type=jnp.float32)
    shared_act, shared_slope = swish_parts(shared_pre[:, :SFF])
    shared_up = shared_pre[:, SFF:]
    shared_mid = (shared_act * shared_up).astype(jnp.bfloat16)
    shared_out = jnp.dot(shared_mid, shared_out_w, preferred_element_type=jnp.float32)
    unit_count = expert_w.shape[2]
    per_device = max(1, unit_count // FF)
    spread = max(1, FF // unit_count)
    unit_width = unit_count // per_device
    capacity = max(2, 5 * row_count // (2 * EXPERTS))
    slot_count = blocks_axis * per_device * capacity
    pair_expert = routes.reshape(-1)
    pair_match = route_match.reshape(2 * row_count, EXPERTS).astype(jnp.int32)
    pair_rank = jnp.sum(jnp.cumsum(pair_match, axis=0) * pair_match, axis=1) - 1
    slot_base = (
        pair_expert // per_device * spread * per_device * capacity
        + pair_expert % per_device * capacity
        + pair_rank
    )
    slot_index = (
        slot_base[None, :] + (jnp.arange(spread, dtype=jnp.int32) * per_device * capacity)[:, None]
    )
    pair_ids = jnp.arange(2 * row_count, dtype=jnp.int32)
    slot_pair = (
        jnp.full((slot_count,), 2 * row_count, jnp.int32)
        .at[slot_index.reshape(-1)]
        .set(jnp.tile(pair_ids, spread))
    )
    slot_token = slot_pair // 2
    hidden_pad = jnp.concatenate([hidden, jnp.zeros((1, width_all), jnp.bfloat16)], axis=0)
    send_rows = hidden_pad[slot_token].reshape(blocks_axis, per_device, capacity, width_all)
    received_rows = lax.all_to_all(send_rows, "blk", split_axis=0, concat_axis=0, tiled=True)
    gate_weight = expert_w[0].reshape(width_all, per_device, unit_width)
    up_weight = expert_w[1].reshape(width_all, per_device, unit_width)
    down_w = expert_out_w.reshape(per_device, unit_width, width_all)
    expert_gate = jnp.einsum(
        "tfoa,afw->tfow", received_rows, gate_weight, preferred_element_type=jnp.float32
    )
    expert_up_projection = jnp.einsum(
        "tfoa,afw->tfow", received_rows, up_weight, preferred_element_type=jnp.float32
    )
    expert_activation, expert_slope = swish_parts(expert_gate)
    expert_mid = (expert_activation * expert_up_projection).astype(jnp.bfloat16)
    expert_part = jnp.einsum(
        "secm,emd->secd", expert_mid, down_w, preferred_element_type=jnp.float32
    )
    returned = (
        lax.all_to_all(
            expert_part.astype(jnp.bfloat16), "blk", split_axis=0, concat_axis=0, tiled=True
        )
        .astype(expert_part.dtype)
        .reshape(slot_count, width_all)
    )
    pair_out = jnp.sum(returned[slot_index], axis=0).reshape(row_count, 2, width_all)
    expert_sum = jnp.sum(gate_values[:, :, None] * pair_out, axis=1)
    layer_out = (residual + shared_out + expert_sum).astype(jnp.bfloat16)
    gain_rows, qkv_w, proj_w, router_w, shared_w, shared_out_w, expert_w, expert_out_w = (
        fetch_weights(
            norm_gains,
            attn_qkv,
            attn_proj,
            router_rows,
            shared_gate_up,
            shared_down,
            expert_gate_up,
            expert_down,
        )
    )
    gate_weight = expert_w[0].reshape(width_all, per_device, unit_width)
    up_weight = expert_w[1].reshape(width_all, per_device, unit_width)
    down_w = expert_out_w.reshape(per_device, unit_width, width_all)
    grad_layer = out_grad.astype(jnp.float32)
    grad_smid = jnp.einsum("td,fd->tf", out_grad, shared_out_w, preferred_element_type=jnp.float32)
    shared_grads = jnp.concatenate(
        [grad_smid * shared_up * shared_slope, grad_smid * shared_act], axis=1
    ).astype(jnp.bfloat16)
    grad_hidden = jnp.einsum(
        "tf,df->td", shared_grads, shared_w, preferred_element_type=jnp.float32
    )
    grad_shared_w = jnp.einsum(
        "td,tf->df", hidden, shared_grads, preferred_element_type=jnp.float32
    )
    grad_shared_out = jnp.einsum(
        "tf,td->fd", shared_mid, out_grad, preferred_element_type=jnp.float32
    )
    grad_gates = jnp.sum(grad_layer[:, None, :] * pair_out, axis=-1)
    grad_pairs = (
        (gate_values[:, :, None] * grad_layer[:, None, :])
        .reshape(2 * row_count, width_all)
        .astype(jnp.bfloat16)
    )
    grad_pad = jnp.concatenate([grad_pairs, jnp.zeros((1, width_all), jnp.bfloat16)], axis=0)
    grad_recv = lax.all_to_all(
        grad_pad[slot_pair].reshape(blocks_axis, per_device, capacity, width_all),
        "blk",
        split_axis=0,
        concat_axis=0,
        tiled=True,
    )
    grad_expert_middle = jnp.einsum(
        "secd,emd->secm", grad_recv, down_w, preferred_element_type=jnp.float32
    )
    grad_expert_gate_branch = (grad_expert_middle * expert_up_projection * expert_slope).astype(
        jnp.bfloat16
    )
    grad_expert_up_branch = (grad_expert_middle * expert_activation).astype(jnp.bfloat16)
    grad_rows = jnp.einsum(
        "auwj,buj->auwb", grad_expert_gate_branch, gate_weight, preferred_element_type=jnp.float32
    ) + jnp.einsum(
        "auwj,buj->auwb", grad_expert_up_branch, up_weight, preferred_element_type=jnp.float32
    )
    grad_expert_w = jnp.stack(
        [
            jnp.einsum(
                "jgki,jgkt->igt",
                received_rows,
                grad_expert_gate_branch,
                preferred_element_type=jnp.float32,
            ).reshape(width_all, unit_count),
            jnp.einsum(
                "jgki,jgkt->igt",
                received_rows,
                grad_expert_up_branch,
                preferred_element_type=jnp.float32,
            ).reshape(width_all, unit_count),
        ]
    )
    grad_expert_out = jnp.einsum(
        "secm,secd->emd", expert_mid, grad_recv, preferred_element_type=jnp.float32
    ).reshape(unit_count, width_all)
    grad_back = (
        lax.all_to_all(
            grad_rows.astype(jnp.bfloat16), "blk", split_axis=0, concat_axis=0, tiled=True
        )
        .astype(grad_rows.dtype)
        .reshape(slot_count, width_all)
    )
    grad_hidden = grad_hidden + jnp.sum(
        jnp.sum(grad_back[slot_index], axis=0).reshape(row_count, 2, width_all), axis=1
    )
    grad_soft = jnp.sum(jnp.where(route_match, grad_gates[:, :, None], 0.0), axis=1)
    grad_logits = (
        soft_route * (grad_soft - jnp.sum(soft_route * grad_soft, axis=-1, keepdims=True))
    ).astype(jnp.bfloat16)
    grad_hidden = grad_hidden + jnp.einsum(
        "te,ed->td", grad_logits, router_w, preferred_element_type=jnp.float32
    )
    grad_router = jnp.einsum("te,td->ed", grad_logits, hidden, preferred_element_type=jnp.float32)
    grad_norm_two, grad_second_gain = norm_back(residual, second_inverse, second_gain, grad_hidden)
    grad_resid = grad_layer + grad_norm_two
    grad_branch = grad_resid.astype(jnp.bfloat16)
    grad_proj = jnp.einsum("td,te->de", attn_tok, grad_branch, preferred_element_type=jnp.float32)
    grad_attn_tok = jnp.einsum(
        "te,de->td", grad_branch, proj_w, preferred_element_type=jnp.float32
    ).astype(jnp.bfloat16)
    grad_heads = lax.all_to_all(
        grad_attn_tok, "head", split_axis=1, concat_axis=0, tiled=True
    ).reshape(query_rows, local_heads, DH)
    delta = jnp.transpose(jnp.sum(grad_heads * attn_heads, axis=-1))

    def back_step(grad_acc, member):
        visible = prompt_visible(member[2])
        step_query, step_key, step_value = grad_block(
            queries, grad_heads, log_total, delta, member[0], member[1], visible
        )
        return (grad_acc + step_query, (step_key, step_value))

    grad_query, prompt_grads = lax.scan(
        back_step,
        jnp.zeros((query_rows, local_heads, DH), jnp.float32),
        (key_blocks, value_blocks, block_starts),
    )
    local_query, local_key, local_value = grad_block(
        queries, grad_heads, log_total, delta, key_local, value_local, local_visible
    )
    grad_query = grad_query + local_query
    key_share, value_share = (
        lax.psum_scatter(
            prompt_grads[0].reshape(prompt_all, -1), "blk", scatter_dimension=0, tiled=True
        ),
        lax.psum_scatter(
            prompt_grads[1].reshape(prompt_all, -1), "blk", scatter_dimension=0, tiled=True
        ),
    )
    grad_key = (
        local_key.reshape(heads_axis, row_count, -1)
        .at[:, :prompt_dev]
        .add(key_share.reshape(heads_axis, prompt_dev, -1))
        .reshape(query_rows, local_heads, DH)
    )
    grad_value = (
        local_value.reshape(heads_axis, row_count, -1)
        .at[:, :prompt_dev]
        .add(value_share.reshape(heads_axis, prompt_dev, -1))
    )
    head_cos, head_sin = angle_tables(head_pos)
    grad_query = (
        rotate(grad_query, head_cos, -head_sin).reshape(query_rows, -1).astype(jnp.bfloat16)
    )
    grad_key = rotate(grad_key, head_cos, -head_sin).reshape(query_rows, -1).astype(jnp.bfloat16)
    grad_value = grad_value.reshape(query_rows, -1).astype(jnp.bfloat16)
    grad_q_tok, grad_k_tok, grad_v_tok = (
        lax.all_to_all(grad_query, "head", split_axis=0, concat_axis=1, tiled=True),
        lax.all_to_all(grad_key, "head", split_axis=0, concat_axis=1, tiled=True),
        lax.all_to_all(grad_value, "head", split_axis=0, concat_axis=1, tiled=True),
    )
    grad_qkv_rows = jnp.concatenate([grad_q_tok, grad_k_tok, grad_v_tok], axis=1)
    grad_normed = jnp.einsum("tf,df->td", grad_qkv_rows, qkv_w, preferred_element_type=jnp.float32)
    grad_qkv = jnp.einsum("td,tf->df", normed, grad_qkv_rows, preferred_element_type=jnp.float32)
    grad_norm_one, grad_first_gain = norm_back(tokens, first_inverse, first_gain, grad_normed)
    grad_tokens = grad_resid + grad_norm_one
    owned = (
        lax.psum_scatter(
            jnp.stack([grad_first_gain, grad_second_gain]).astype(jnp.bfloat16),
            ("grp", "head"),
            scatter_dimension=1,
            tiled=True,
        ).astype(jnp.float32),
        lax.psum_scatter(
            grad_qkv.astype(jnp.bfloat16), ("grp", "head"), scatter_dimension=1, tiled=True
        ).astype(jnp.float32),
        lax.psum_scatter(
            grad_proj.astype(jnp.bfloat16), ("grp", "head"), scatter_dimension=1, tiled=True
        ).astype(jnp.float32),
        lax.psum_scatter(
            grad_router.astype(jnp.bfloat16), ("grp", "head"), scatter_dimension=1, tiled=True
        ).astype(jnp.float32),
        lax.psum_scatter(
            grad_shared_w.astype(jnp.bfloat16), ("grp", "head"), scatter_dimension=1, tiled=True
        ).astype(jnp.float32),
        lax.psum_scatter(
            grad_shared_out.astype(jnp.bfloat16), ("grp", "head"), scatter_dimension=1, tiled=True
        ).astype(jnp.float32),
        lax.psum_scatter(
            grad_expert_w.astype(jnp.bfloat16), ("grp", "head"), scatter_dimension=1, tiled=True
        ).astype(jnp.float32),
        lax.psum_scatter(
            grad_expert_out.astype(jnp.bfloat16), ("grp", "head"), scatter_dimension=1, tiled=True
        ).astype(jnp.float32),
    )
    summed = lax.psum((owned[0], owned[1], owned[2], owned[3], owned[4], owned[5]), "blk")
    return (
        layer_out,
        grad_tokens,
        summed[0],
        summed[1],
        summed[2],
        summed[3],
        summed[4],
        summed[5],
        owned[6],
        owned[7],
    )


TRANSPOSED = (((1,), (1,)), ((), ()))
PLAIN = (((1,), (0,)), ((), ()))
FIRST = (((0,), (0,)), ((), ()))
KERNEL_VMEM = 56 * 1024 * 1024
FEW = 32


def mm(left, right, dims=PLAIN):
    return lax.dot_general(left, right, dims, preferred_element_type=jnp.float32)


def assemble(rows_ref, cut, parts, prompt_to, cont_to):
    sources = rows_ref.shape[0]
    blocks = sources // 2
    half = rows_ref.shape[1]
    for head_part in range(2):
        for block in range(blocks):
            piece = rows_ref[head_part * blocks + block]
            place = (block * 2 + head_part) * half
            for order in range(parts):
                prompt_to[order][place : place + half, :] = piece[
                    :, order * cut : (order + 1) * cut
                ]
                cont_to[order][place : place + half, :] = piece[
                    :, (parts + order) * cut : (parts + order + 1) * cut
                ]


def spread_out(target, prompt_parts, cont_parts, cut):
    sources = target.shape[0]
    blocks = sources // 2
    half = target.shape[1]
    for head_part in range(2):
        for block in range(blocks):
            place = (block * 2 + head_part) * half
            pieces = [part[place : place + half, :] for part in prompt_parts]
            pieces += [part[place : place + half, :] for part in cont_parts]
            target[head_part * blocks + block] = jnp.concatenate(pieces, axis=1).astype(
                target.dtype
            )


def causal_mask(rows):
    keys = lax.broadcasted_iota(jnp.int32, (rows, rows), 0)
    query = lax.broadcasted_iota(jnp.int32, (rows, rows), 1)
    return keys <= query


def cont_mask(rows, cont):
    keys = lax.broadcasted_iota(jnp.int32, (rows, rows), 0)
    query = lax.broadcasted_iota(jnp.int32, (rows, rows), 1)
    return (keys // cont == query // cont) & (keys <= query)


def attention_parts(step, block):
    if step is None:
        return None
    return (0, step * block)


def masked_block(keys, queries, mask):
    scores = mm(keys, queries, TRANSPOSED) * DH ** (-0.5)
    if mask is None:
        return scores
    return jnp.where(mask, scores, NEGATIVE)


def attention_kernel(rows_ref, out_ref, qp, kp, vp, qc, kc, vc, op, oc):
    block = 256
    prompt = qp.shape[0]
    assemble(rows_ref, DH, 3, (qp, kp, vp), (qc, kc, vc))
    cont = 2 * rows_ref.shape[1]
    for is_cont in range(2):
        source_q, source_k, source_v, result = (
            (qc, kc, vc, oc) if is_cont else (qp, kp, vp, op)
        )
        mask = cont_mask(block, cont) if is_cont else causal_mask(block)
        for step in range(prompt // block):
            rows = slice(step * block, (step + 1) * block)
            queries = source_q[rows, :]
            own = masked_block(source_k[rows, :], queries, mask)
            seen = prompt if is_cont else step * block
            peak = jnp.max(own, axis=0, keepdims=True)
            if seen:
                past = masked_block(kp[0:seen, :], queries, None)
                peak = jnp.maximum(peak, jnp.max(past, axis=0, keepdims=True))
            own = jnp.exp(own - peak)
            total = jnp.sum(own, axis=0, keepdims=True)
            gathered = mm(source_v[rows, :], own.astype(jnp.bfloat16), FIRST)
            if seen:
                past = jnp.exp(past - peak)
                total = total + jnp.sum(past, axis=0, keepdims=True)
                gathered = gathered + mm(vp[0:seen, :], past.astype(jnp.bfloat16), FIRST)
            result[rows, :] = jnp.transpose(gathered / total)
    spread_out(out_ref, (op,), (oc,), DH)


def attention_forward(rows):
    sources, half, _ = rows.shape
    prompt = sources * half
    small = pltpu.VMEM((prompt, DH), jnp.bfloat16)
    wide = pltpu.VMEM((prompt, DH), jnp.float32)
    return pl.pallas_call(
        attention_kernel,
        out_shape=jax.ShapeDtypeStruct((sources, half, 2 * DH), jnp.bfloat16),
        in_specs=[pl.BlockSpec(memory_space=pltpu.VMEM)],
        out_specs=pl.BlockSpec(memory_space=pltpu.VMEM),
        scratch_shapes=[small] * 6 + [wide] * 2,
        compiler_params=pltpu.CompilerParams(vmem_limit_bytes=KERNEL_VMEM),
        cost_estimate=pl.CostEstimate(
            flops=2**20, bytes_accessed=2**16, transcendentals=0
        ),
        name="attention_forward",
    )(rows)


def turn_back(values, cosine, sine):
    half = DH // 2
    first, second = values[:, :half], values[:, half:]
    return jnp.concatenate(
        [first * cosine + second * sine, second * cosine - first * sine], axis=1
    )


def attention_back_kernel(
    rows_ref, grad_ref, cos_ref, sin_ref, out_ref,
    qp, kp, vp, qc, kc, vc, gp, gc, dqp, dkp, dvp, dqc, dkc, dvc,
):
    block = 256
    prompt = qp.shape[0]
    scale = DH ** (-0.5)
    assemble(rows_ref, DH, 3, (qp, kp, vp), (qc, kc, vc))
    assemble(grad_ref, DH, 1, (gp,), (gc,))
    cont = 2 * rows_ref.shape[1]
    dkp[...] = jnp.zeros_like(dkp)
    dvp[...] = jnp.zeros_like(dvp)
    for is_cont in range(2):
        source_q, source_k, source_v, source_g = (
            (qc, kc, vc, gc) if is_cont else (qp, kp, vp, gp)
        )
        to_q, to_k, to_v = (dqc, dkc, dvc) if is_cont else (dqp, dkp, dvp)
        mask = cont_mask(block, cont) if is_cont else causal_mask(block)
        for step in range(prompt // block):
            rows = slice(step * block, (step + 1) * block)
            queries = source_q[rows, :]
            grads = source_g[rows, :]
            own_keys = source_k[rows, :]
            own = masked_block(own_keys, queries, mask)
            seen = prompt if is_cont else step * block
            peak = jnp.max(own, axis=0, keepdims=True)
            if seen:
                past = masked_block(kp[0:seen, :], queries, None)
                peak = jnp.maximum(peak, jnp.max(past, axis=0, keepdims=True))
            own = jnp.exp(own - peak)
            total = jnp.sum(own, axis=0, keepdims=True)
            if seen:
                past = jnp.exp(past - peak)
                total = total + jnp.sum(past, axis=0, keepdims=True)
            inverse = 1.0 / total
            own = own * inverse
            own_grad = mm(source_v[rows, :], grads, TRANSPOSED)
            delta = jnp.sum(own * own_grad, axis=0, keepdims=True)
            if seen:
                past = past * inverse
                past_grad = mm(vp[0:seen, :], grads, TRANSPOSED)
                delta = delta + jnp.sum(past * past_grad, axis=0, keepdims=True)
            own_scores = (own * (own_grad - delta)).astype(jnp.bfloat16)
            own_dv = mm(own.astype(jnp.bfloat16), grads)
            own_dk = mm(own_scores, queries) * scale
            turned = mm(own_keys, own_scores, FIRST)
            if is_cont:
                to_v[rows, :] = own_dv
                to_k[rows, :] = own_dk
            else:
                to_v[rows, :] += own_dv
                to_k[rows, :] += own_dk
            if seen:
                past_scores = (past * (past_grad - delta)).astype(jnp.bfloat16)
                dvp[0:seen, :] += mm(past.astype(jnp.bfloat16), grads)
                dkp[0:seen, :] += mm(past_scores, queries) * scale
                turned = turned + mm(kp[0:seen, :], past_scores, FIRST)
            to_q[rows, :] = jnp.transpose(turned) * scale
    cos_p, sin_p = cos_ref[0:prompt, :], sin_ref[0:prompt, :]
    dqp[...] = turn_back(dqp[...], cos_p, sin_p)
    dkp[...] = turn_back(dkp[...], cos_p, sin_p)
    for step in range(prompt // cont):
        rows = slice(step * cont, (step + 1) * cont)
        cos_c, sin_c = cos_ref[prompt : prompt + cont, :], sin_ref[prompt : prompt + cont, :]
        dqc[rows, :] = turn_back(dqc[rows, :], cos_c, sin_c)
        dkc[rows, :] = turn_back(dkc[rows, :], cos_c, sin_c)
    spread_out(out_ref, (dqp, dkp, dvp), (dqc, dkc, dvc), DH)


def attention_backward(rows, grads, cosine, sine):
    sources, half, wide = rows.shape
    prompt = sources * half
    small = pltpu.VMEM((prompt, DH), jnp.bfloat16)
    large = pltpu.VMEM((prompt, DH), jnp.float32)
    return pl.pallas_call(
        attention_back_kernel,
        out_shape=jax.ShapeDtypeStruct((sources, half, wide), jnp.bfloat16),
        in_specs=[pl.BlockSpec(memory_space=pltpu.VMEM)] * 4,
        out_specs=pl.BlockSpec(memory_space=pltpu.VMEM),
        scratch_shapes=[small] * 8 + [large] * 6,
        compiler_params=pltpu.CompilerParams(vmem_limit_bytes=KERNEL_VMEM),
        cost_estimate=pl.CostEstimate(
            flops=2**20, bytes_accessed=2**16, transcendentals=0
        ),
        name="attention_backward",
    )(rows, grads, cosine, sine)


def exchange(values, axis, mask):
    return lax.ppermute(values, axis, [(i, i ^ mask) for i in range(lax.axis_size(axis))])


def to_member(values, number):
    if number == 2:
        return exchange(values, "grp", 1)
    if number == 1:
        return exchange(values, "head", 1)
    return lax.ppermute(values, ("grp", "head"), [(i, i ^ number) for i in range(4)])


def tie(values, *after):
    return lax.optimization_barrier((values, *after))[0]


def kernel_call(body_of, outs, scratch, name, *inputs):
    spec = pl.BlockSpec(memory_space=pltpu.VMEM)
    return pl.pallas_call(
        body_of,
        out_shape=[jax.ShapeDtypeStruct(*out) for out in outs],
        in_specs=[
            pl.BlockSpec(memory_space=pltpu.SMEM) if one.dtype == jnp.int32 else spec
            for one in inputs
        ],
        out_specs=[spec] * len(outs),
        scratch_shapes=[pltpu.VMEM(*one) for one in scratch],
        compiler_params=pltpu.CompilerParams(vmem_limit_bytes=KERNEL_VMEM),
        cost_estimate=pl.CostEstimate(flops=2**20, bytes_accessed=2**16, transcendentals=0),
        name=name,
    )(*inputs)


def head_slot(head_number, slots):
    return head_number // (HEADS // 2) * (slots // 2) + head_number % (HEADS // 2)


def qkv_kernel(place, tokens_ref, cos_ref, sin_ref, *refs):
    own, other = refs[0:4], refs[4:8]
    normed_ref, rows_ref, gains_ref, router_ref, qkv_ref, proj_ref, few = refs[8:]
    quad_me, core = place[0], place[1]
    rows, width = tokens_ref.shape
    quarter = width // 4
    per_qkv, per_proj = qkv_ref.shape[1], proj_ref.shape[1]
    for j in range(4):
        few[quad_me ^ j] = own[j][per_qkv + per_proj : per_qkv + per_proj + 16, :].astype(jnp.float32)
        for where, source in ((core, own[j]), (1 - core, other[j])):
            qkv_ref[(quad_me ^ j) * 2 + where] = source[0:per_qkv, :]
            proj_ref[(quad_me ^ j) * 2 + where] = source[per_qkv : per_qkv + per_proj, :]

    def few_row(number):
        part, row = divmod(number, 5)
        return jnp.concatenate(
            [few[k, row : row + 1, part * quarter : (part + 1) * quarter] for k in range(4)],
            axis=1,
        )

    gains = jnp.concatenate([few_row(0), few_row(1)], axis=0)
    gains_ref[...] = gains
    router_ref[...] = jnp.concatenate(
        [few_row(2 + e) for e in range(EXPERTS)], axis=0
    ).astype(jnp.bfloat16)
    tokens = tokens_ref[...].astype(jnp.float32)
    normed = norm_rows(tokens, gains[0:1])[0].astype(jnp.bfloat16)
    normed_ref[...] = normed
    mixed = mm(normed, qkv_ref[...].reshape(3 * width, width), TRANSPOSED)
    cosine, sine = cos_ref[...], sin_ref[...]

    def chunk(number):
        return mixed[:, number * DH : (number + 1) * DH]

    slots = rows_ref.shape[0]
    rows_ref[...] = jnp.zeros_like(rows_ref)
    for one in range(HEADS):
        pieces = [
            turn_back(chunk(one), cosine, -sine),
            turn_back(chunk(HEADS + one), cosine, -sine),
            chunk(2 * HEADS + one),
        ]
        rows_ref[head_slot(one, slots)] = jnp.concatenate(
            [piece[: rows // 2] for piece in pieces] + [piece[rows // 2 :] for piece in pieces],
            axis=1,
        ).astype(jnp.bfloat16)


def hidden_kernel(
    got_ref, tokens_ref, gains_ref, pick_ref, proj_ref,
    residual_ref, hidden_ref, attn_ref, sent_ref, attn,
):
    rows, width = tokens_ref.shape
    slots = got_ref.shape[0]
    for one in range(HEADS):
        piece = got_ref[head_slot(one, slots)]
        attn[0 : rows // 2, one * DH : (one + 1) * DH] = piece[:, 0:DH]
        attn[rows // 2 : rows, one * DH : (one + 1) * DH] = piece[:, DH : 2 * DH]
    attn_ref[...] = attn[...]
    residual = tokens_ref[...].astype(jnp.float32) + mm(
        attn[...], proj_ref[...].reshape(width, width), TRANSPOSED
    )
    residual_ref[...] = residual
    hidden = norm_rows(residual, gains_ref[1:2, :])[0].astype(jnp.bfloat16)
    hidden_ref[...] = hidden
    sent_ref[...] = mm(pick_ref[...], hidden).astype(jnp.bfloat16)


def expert_kernel(place, rows_ref, grad_ref, router_ref, *refs):
    gates, ups, downs = refs[0:4], refs[4:8], refs[8:12]
    (
        g_own, g_part, e_own, e_part, egate_ref, eup_ref, mid_ref, eout_ref, g_router_ref,
        gate_w, up_w, down_w,
    ) = refs[12:]
    quad_me, expert_me = place[0], place[2]
    quarter = gates[0].shape[0]
    for j in range(4):
        at = pl.ds(pl.multiple_of((quad_me ^ j) * quarter, 64), quarter)
        gate_w[at, :] = gates[j][...]
        up_w[at, :] = ups[j][...]
        down_w[at, :] = downs[j][...]
    count = rows_ref.shape[0]
    block = count // 4
    router = router_ref[...]
    mine = lax.broadcasted_iota(jnp.int32, (block, EXPERTS), 1) == expert_me
    mine = mine.astype(jnp.float32)
    g_router = jnp.zeros_like(g_router_ref)
    for step in range(4):
        at = slice(step * block, (step + 1) * block)
        rows, grads = rows_ref[at, :], grad_ref[at, :]
        logits = mm(rows, router, TRANSPOSED)
        logits = jnp.exp(logits - jnp.max(logits, axis=1, keepdims=True))
        soft = logits / jnp.sum(logits, axis=1, keepdims=True)
        gate = jnp.sum(soft * mine, axis=1, keepdims=True)
        e_up = mm(rows, up_w[...])
        e_act, e_slope = swish_parts(mm(rows, gate_w[...]))
        e_mid = e_act * e_up
        e_grad = mm(grads, down_w[...])
        g_gate = jnp.sum(e_mid * e_grad, axis=1, keepdims=True)
        g_mid = e_grad * gate
        egate = (g_mid * e_up * e_slope).astype(jnp.bfloat16)
        eup = (g_mid * e_act).astype(jnp.bfloat16)
        e_mid = e_mid.astype(jnp.bfloat16)
        g_logits = (g_gate * soft * (mine - gate)).astype(jnp.bfloat16)
        g_rows = (
            mm(egate, gate_w[...], TRANSPOSED)
            + mm(eup, up_w[...], TRANSPOSED)
            + mm(g_logits, router)
        )
        e_rows = gate * mm(e_mid, down_w[...], TRANSPOSED)
        if step < 2:
            g_own[at, :] = g_rows
            e_own[at, :] = e_rows
        else:
            there = slice((step - 2) * block, (step - 1) * block)
            g_part[there, :] = g_rows.astype(jnp.bfloat16)
            e_part[there, :] = e_rows.astype(jnp.bfloat16)
        egate_ref[at, :] = egate
        eup_ref[at, :] = eup
        mid_ref[at, :] = e_mid
        eout_ref[at, :] = (gate * grads.astype(jnp.float32)).astype(jnp.bfloat16)
        g_router = g_router + mm(g_logits, rows, FIRST)
    g_router_ref[...] = g_router


def branch_kernel(
    back_ref, pick_ref, shared_ref, residual_ref, gains_ref, grad_ref, proj_ref,
    resid_ref, branch_ref, rows_ref, gain_ref,
):
    rows, width = grad_ref.shape
    g_hidden = mm(pick_ref[...], back_ref[...], FIRST) + shared_ref[...].astype(jnp.float32)
    residual = residual_ref[...]
    gain = gains_ref[1:2, :]
    inverse = norm_rows(residual, gain)[1]
    g_norm, g_gain = norm_back(residual, inverse, gain, g_hidden)
    gain_ref[...] = g_gain[None]
    g_resid = grad_ref[...].astype(jnp.float32) + g_norm
    resid_ref[...] = g_resid
    branch = g_resid.astype(jnp.bfloat16)
    branch_ref[...] = branch
    attn = mm(branch, proj_ref[...].reshape(width, width)).astype(jnp.bfloat16)
    slots = rows_ref.shape[0]
    rows_ref[...] = jnp.zeros_like(rows_ref)
    for one in range(HEADS):
        piece = attn[:, one * DH : (one + 1) * DH]
        rows_ref[head_slot(one, slots)] = jnp.concatenate(
            [piece[: rows // 2], piece[rows // 2 :]], axis=1
        )


def tokens_kernel(
    got_ref, tokens_ref, gains_ref, resid_ref, qkv_ref, out_ref, gain_ref, parts
):
    rows, width = tokens_ref.shape
    slots = got_ref.shape[0]
    for one in range(HEADS):
        piece = got_ref[head_slot(one, slots)]
        for kind in range(3):
            at = (kind * HEADS + one) * DH
            parts[0 : rows // 2, at : at + DH] = piece[:, kind * DH : (kind + 1) * DH]
            parts[rows // 2 : rows, at : at + DH] = piece[:, (3 + kind) * DH : (4 + kind) * DH]
    g_normed = mm(parts[...], qkv_ref[...].reshape(3 * width, width))
    tokens = tokens_ref[...].astype(jnp.float32)
    gain = gains_ref[0:1, :]
    inverse = norm_rows(tokens, gain)[1]
    g_norm, g_gain = norm_back(tokens, inverse, gain, g_normed)
    gain_ref[...] = g_gain[None]
    out_ref[...] = resid_ref[...] + g_norm


def head_weight_kernel(rows_ref, normed_ref, out_ref, left):
    sources, half, wide = rows_ref.shape
    for source in range(sources):
        at = source * 2 * half
        left[at : at + half, :] = rows_ref[source, :, 0 : wide // 2]
        left[at + half : at + 2 * half, :] = rows_ref[source, :, wide // 2 : wide]
    right = normed_ref[...].reshape(2 * half * sources, normed_ref.shape[2])
    out_ref[...] = mm(left[...], right, FIRST).astype(jnp.bfloat16)


def chunk_kernel(order, got_ref, out_ref, few_ref):
    few = jnp.zeros_like(few_ref)
    for source in range(got_ref.shape[0]):
        few = few + got_ref[source, 2 * DH : 2 * DH + FEW, :].astype(jnp.float32)
    few_ref[...] = few
    for number in range(order.shape[0]):
        which = order[number]
        at = pl.ds(pl.multiple_of(which % 2 * DH, DH), DH)
        out_ref[number * DH : (number + 1) * DH, :] = got_ref[which // 2, at, :].astype(
            jnp.float32
        )


def shared_kernel(place, *refs):
    hidden_refs, grads_refs, pieces = refs[0:4], refs[4:8], refs[8:12]
    out_ref, back_ref = refs[12:14]
    given = refs[14:18]
    both_w, down_w, g_both, g_down = refs[18:]
    quad_me = place[0]
    width, span = both_w.shape[0], both_w.shape[1] // 4
    quarter = width // 4
    block = hidden_refs[0].shape[0]
    for j in range(4):
        k = quad_me ^ j
        both_w[:, pl.ds(pl.multiple_of(k * span, 128), span)] = pieces[j][0:width, :]
        at = pl.ds(pl.multiple_of(k * quarter, 64), quarter)
        down_w[at, 0:span] = pieces[j][width : width + quarter, :]
        down_w[at, span : 2 * span] = pieces[j][width + quarter : width + 2 * quarter, :]
    for step in range(2):
        rows = slice(step * 2 * block, (step + 1) * 2 * block)
        hidden = jnp.concatenate([hidden_refs[2 * step][...], hidden_refs[2 * step + 1][...]])
        grads = jnp.concatenate([grads_refs[2 * step][...], grads_refs[2 * step + 1][...]])
        pre = mm(hidden, both_w[...])
        act, slope = swish_parts(pre[:, : 2 * span])
        up = pre[:, 2 * span :]
        mid = (act * up).astype(jnp.bfloat16)
        out_ref[rows, :] = mm(mid, down_w[...], TRANSPOSED).astype(jnp.bfloat16)
        g_mid = mm(grads, down_w[...])
        g_pre = jnp.concatenate([g_mid * up * slope, g_mid * act], axis=1).astype(jnp.bfloat16)
        back_ref[rows, :] = mm(g_pre, both_w[...], TRANSPOSED).astype(jnp.bfloat16)
        new_both = mm(hidden, g_pre, FIRST)
        new_down = mm(grads, mid, FIRST)
        if step == 0:
            g_both[...] = new_both
            g_down[...] = new_down
        else:
            g_both[...] += new_both
            g_down[...] += new_down
    for j in range(4):
        k = quad_me ^ j
        at = pl.ds(pl.multiple_of(k * quarter, 64), quarter)
        given[j][0:width, :] = g_both[:, pl.ds(pl.multiple_of(k * span, 128), span)].astype(
            jnp.bfloat16
        )
        given[j][width : width + quarter, :] = g_down[at, 0:span].astype(jnp.bfloat16)
        given[j][width + quarter : width + 2 * quarter, :] = g_down[at, span : 2 * span].astype(
            jnp.bfloat16
        )


def shared_out_kernel(place, *refs):
    parts, wide_ref, down_ref, proj_ref = refs[0:4], refs[4], refs[5], refs[6]
    width, span = wide_ref.shape[0], parts[0].shape[1]
    quarter = down_ref.shape[0]
    last, per = width + 2 * quarter, quarter // 4
    for j in range(4):
        k = (place[3] % 4) ^ j
        at = pl.ds(pl.multiple_of(k * span, 128), span)
        wide_ref[:, at] = parts[j][0:width, :].astype(jnp.float32)
        down_ref[:, at] = parts[j][width : width + quarter, :].astype(jnp.float32)
        at = pl.ds(pl.multiple_of((4 + k) * span, 128), span)
        down_ref[:, at] = parts[j][width + quarter : last, :].astype(jnp.float32)
        at = pl.ds(pl.multiple_of(k * per, 16), per)
        for i in range(width // span):
            proj_ref[at, i * span : (i + 1) * span] = parts[j][
                last + i * per : last + (i + 1) * per, :
            ].astype(jnp.float32)


def units_out_kernel(place, *refs):
    sets, out_ref = refs[:-1], refs[-1]
    units = sets[0].shape[1]
    for number, part in enumerate(sets):
        at = pl.ds(pl.multiple_of((place[0] ^ number % 4) * units, 128), units)
        out_ref[number // 4, :, at] = part[...].astype(jnp.float32)


def quick_body(
    tokens_in,
    norm_gains,
    attn_qkv,
    attn_proj,
    router_rows,
    shared_gate_up,
    shared_down,
    expert_gate_up,
    expert_down,
    routes,
    out_grad,
):
    quad = ("grp", "head")
    line = ("head", "blk")
    blocks = lax.axis_size("blk")
    rows, width = tokens_in.shape
    grp, head, blk = lax.axis_index("grp"), lax.axis_index("head"), lax.axis_index("blk")
    core = blk % 2
    quarter = width // 4
    prompt_dev = max(PROMPT_ROWS, PROMPT_LEAST // (2 * blocks))
    prompt = prompt_dev * 2 * blocks
    cont = 2 * (rows - prompt_dev)
    halves = width // 2
    bf16, f32 = jnp.bfloat16, jnp.float32

    member = 2 * grp + head
    place = jnp.stack([member, core, 2 * blk + grp, blk])
    third = attn_qkv.shape[1]
    few = jnp.concatenate([norm_gains, router_rows], axis=0)
    few = jnp.pad(few, ((0, 20 - few.shape[0]), (0, 0)))
    few = jnp.concatenate([few[5 * i : 5 * i + 5] for i in range(4)], axis=1)
    few = jnp.pad(few, ((0, 11), (0, 0)))
    half_rows = jnp.concatenate(
        [
            lax.dynamic_slice_in_dim(attn_qkv.T, core * (third // 2), third // 2, 0),
            lax.dynamic_slice_in_dim(attn_proj.T, core * (quarter // 2), quarter // 2, 0),
            few,
        ],
        axis=0,
    )
    own_w = [half_rows] + [to_member(half_rows, j) for j in (1, 2, 3)]
    other_w = [exchange(part, "blk", 1) for part in own_w]

    span = SFF // 2 // 4
    four = blk % 4
    down_t = shared_down.T
    piece = jnp.concatenate(
        [
            lax.dynamic_slice_in_dim(shared_gate_up, four * span, span, 1),
            lax.dynamic_slice_in_dim(down_t, four * span, span, 1),
            lax.dynamic_slice_in_dim(down_t, SFF // 2 + four * span, span, 1),
        ],
        axis=0,
    )

    def of_four(values):
        far = exchange(values, "blk", 2)
        return [values, exchange(values, "blk", 1), far, exchange(far, "blk", 1)]

    def sum_of_four(parts):
        near = exchange(jnp.stack([parts[1], parts[3]]), "blk", 1)
        far = (parts[2].astype(f32) + near[1].astype(f32)).astype(bf16)
        return parts[0].astype(f32) + near[0].astype(f32) + exchange(far, "blk", 2).astype(f32)

    units = expert_gate_up.shape[2] // 4
    down_all = expert_down.T

    def unit_part(values, j):
        return lax.dynamic_slice_in_dim(values, (member ^ j) * units, units, 1)

    gate_send = [unit_part(expert_gate_up[0], j) for j in range(4)]
    up_send = [unit_part(expert_gate_up[1], j) for j in range(4)]
    down_send = [unit_part(down_all, j) for j in range(4)]

    def fetched(parts, after, *numbers):
        for j in numbers:
            parts[j] = to_member(tie(parts[j], after), j)

    expert_ids = jnp.arange(EXPERTS, dtype=jnp.int32)
    match = (routes[:, :, None] == expert_ids).astype(jnp.int32)
    flat = match.reshape(2 * rows, EXPERTS)
    rank = (jnp.sum(jnp.cumsum(flat, axis=0) * flat, axis=1) - 1).reshape(rows, 2)
    capacity = 5 * rows // (2 * EXPERTS)
    slots = (routes // 2) * (2 * capacity) + (routes % 2 ^ grp) * capacity + rank
    slot_ids = jnp.arange(2 * capacity * blocks, dtype=jnp.int32)[:, None]
    pick = ((slot_ids == slots[:, 0]) | (slot_ids == slots[:, 1])).astype(bf16)

    def over_line(sent):
        got = lax.all_to_all(
            sent.reshape(blocks, 2 * capacity, width), "blk", 0, 0, tiled=True
        )
        kept = got[:, :capacity].reshape(blocks * capacity, width)
        given = got[:, capacity:].reshape(blocks * capacity, width)
        return kept, given

    grad_kept, grad_given = over_line(mm(pick, out_grad).astype(bf16))
    four_grads = of_four(out_grad)

    wait = lax.optimization_barrier
    own_w, gate_send, up_send, down_send, piece = wait(
        (own_w, gate_send, up_send, down_send, piece)
    )
    token_row = jnp.arange(rows, dtype=jnp.int32)
    token_pos = row_layout(head, token_row, blk, 2, blocks, rows, prompt_dev)[3]
    token_cos, token_sin = angle_tables(token_pos)
    slots_all = 2 * blocks
    normed, head_send, gains, router_w, qkv_w, proj_w = kernel_call(
        qkv_kernel,
        [
            ((rows, width), bf16),
            ((slots_all, prompt_dev, 6 * DH), bf16),
            ((2, width), f32),
            ((EXPERTS, width), bf16),
            ((8, third // 2, width), bf16),
            ((8, quarter // 2, width), bf16),
        ],
        [((4, 16, width), f32)],
        "qkv_rows",
        place, tokens_in, token_cos[:, 0], token_sin[:, 0], *own_w, *other_w,
    )
    fetched(gate_send, own_w[3], 1, 2)
    head_send, gate_send = wait((head_send, gate_send))
    head_rows = lax.all_to_all(head_send, line, 0, 0, tiled=True)
    fetched(gate_send, head_send, 3)
    fetched(up_send, head_send, 1, 2)
    head_rows, gate_send, up_send = wait((head_rows, gate_send, up_send))
    all_normed = lax.all_gather(tie(normed, head_rows), line, axis=0)
    attn_heads = attention_forward(head_rows)
    fetched(up_send, head_rows, 3)
    attn_heads, up_send = wait((attn_heads, up_send))
    attn_got = lax.all_to_all(attn_heads, line, 0, 0, tiled=True)
    fetched(down_send, attn_heads, 1, 2)
    grad_given = exchange(tie(grad_given, attn_heads), "grp", 1)
    attn_got, down_send, grad_given = wait((attn_got, down_send, grad_given))
    residual, hidden, attn_tok, sent = kernel_call(
        hidden_kernel,
        [
            ((rows, width), f32),
            ((rows, width), bf16),
            ((rows, width), bf16),
            ((2 * capacity * blocks, width), bf16),
        ],
        [((rows, width), bf16)],
        "hidden_rows",
        attn_got, tokens_in, gains, pick, proj_w,
    )
    fetched(down_send, attn_got, 3)

    grad_mine = jnp.concatenate([grad_kept, grad_given], axis=0)
    grad_rows_in = jnp.concatenate(
        [grad_mine, exchange(tie(grad_mine, attn_got), "head", 1)], axis=0
    )
    kept, given = over_line(sent)
    kept, given, down_send, grad_rows_in = wait((kept, given, down_send, grad_rows_in))
    got_mine = jnp.concatenate([kept, exchange(given, "grp", 1)], axis=0)
    got_rows = jnp.concatenate([got_mine, exchange(got_mine, "head", 1)], axis=0)
    four_hidden = of_four(tie(hidden, given))
    shared_parts = [piece, piece, piece, piece]
    fetched(shared_parts, got_rows, 1, 2)
    count = got_rows.shape[0]
    g_own, g_part, e_own, e_part, egate, eup, e_mid, g_eout, g_router = kernel_call(
        expert_kernel,
        [
            ((count // 2, width), f32),
            ((count // 2, width), bf16),
            ((count // 2, width), f32),
            ((count // 2, width), bf16),
            ((count, units), bf16),
            ((count, units), bf16),
            ((count, units), bf16),
            ((count, width), bf16),
            ((EXPERTS, width), f32),
        ],
        [((width, units), bf16)] * 3,
        "expert_rows",
        place, got_rows, grad_rows_in, router_w, *gate_send, *up_send, *down_send,
    )
    g_part, shared_parts = wait((g_part, shared_parts))
    fetched(shared_parts, g_part, 3)

    shared_out, shared_back, *shared_given = kernel_call(
        shared_kernel,
        [((4 * rows, width), bf16)] * 2 + [((width + 2 * quarter, span), bf16)] * 4,
        [
            ((width, 4 * span), bf16),
            ((width, 2 * span), bf16),
            ((width, 4 * span), f32),
            ((width, 2 * span), f32),
        ],
        "shared_rows",
        place, *four_hidden, *four_grads, *shared_parts,
    )
    shared_back = sum_of_four([shared_back[i * rows : (i + 1) * rows] for i in range(4)])

    def features(left, right):
        whole = mm(left, right, FIRST).astype(bf16)
        return [
            lax.dynamic_slice_in_dim(whole, (member ^ j) * quarter, quarter, 0) for j in range(4)
        ]

    gate_out, up_out, down_out = (
        features(got_rows, egate), features(got_rows, eup), features(g_eout, e_mid)
    )

    def joined(own, part):
        return (own.astype(f32) + part.astype(f32)).astype(bf16)

    def over_line_back(mine, given):
        return lax.all_to_all(
            jnp.concatenate(
                [
                    mine.reshape(blocks, capacity, width),
                    given.reshape(blocks, capacity, width),
                ],
                axis=1,
            ),
            "blk", 0, 0, tiled=True,
        ).reshape(2 * capacity * blocks, width)

    per_line = blocks * capacity
    g_mine = joined(g_own, exchange(g_part, "head", 1))
    fetched(gate_out, g_part, 2)
    g_mine, gate_out[2] = wait((g_mine, gate_out[2]))
    g_given = exchange(g_mine[per_line:], "grp", 1)
    fetched(gate_out, g_mine, 1)
    g_given, gate_out[1] = wait((g_given, gate_out[1]))
    g_back = over_line_back(g_mine[:per_line], g_given)
    fetched(shared_given, g_given, 1, 2)
    g_back, shared_given = wait((g_back, shared_given))

    g_resid, g_branch, grad_send, g_second_gain = kernel_call(
        branch_kernel,
        [
            ((rows, width), f32),
            ((rows, width), bf16),
            ((slots_all, prompt_dev, 2 * DH), bf16),
            ((1, width), f32),
        ],
        [],
        "branch_rows",
        g_back, pick, shared_back, residual, gains, out_grad, proj_w,
    )
    grad_heads = lax.all_to_all(grad_send, line, 0, 0, tiled=True)
    fetched(shared_given, g_back, 3)
    g_proj = mm(g_branch, attn_tok, FIRST).astype(bf16).reshape(4, 4, quarter // 4, width)
    g_proj = sum_of_four(
        [
            lax.dynamic_index_in_dim(g_proj, four ^ j, 1, keepdims=False).reshape(quarter, width)
            for j in range(4)
        ]
    )
    g_proj = g_proj.astype(bf16).reshape(4, quarter // 4, width)
    proj_out = []
    for j in range(4):
        part = lax.dynamic_index_in_dim(g_proj, member ^ j, 0, keepdims=False)
        proj_out.append(
            jnp.concatenate([part[:, i * span : (i + 1) * span] for i in range(width // span)])
        )
    fetched(proj_out, grad_send, 1, 2, 3)
    shared_sum = jnp.concatenate(
        [sum(part.astype(f32) for part in parts) for parts in (shared_given, proj_out)]
    ).astype(bf16)
    grad_heads, shared_sum = wait((grad_heads, shared_sum))
    all_cos, all_sin = angle_tables(jnp.arange(prompt + cont, dtype=jnp.int32))
    g_head_rows = attention_backward(head_rows, grad_heads, all_cos[:, 0], all_sin[:, 0])
    cutting = shared_sum.shape[0] // 32 * 16
    upper = joined(shared_sum[:cutting], exchange(shared_sum[:cutting], "blk", 4))
    fetched(gate_out, grad_heads, 3)
    e_mine = joined(e_own, exchange(tie(e_part, grad_heads), "head", 1))
    g_head_rows, upper, gate_out, e_mine = wait((g_head_rows, upper, gate_out, e_mine))
    g_got = lax.all_to_all(g_head_rows, line, 0, 0, tiled=True)
    fetched(up_out, g_head_rows, 1, 2)
    e_given = exchange(tie(e_mine, g_head_rows)[per_line:], "grp", 1)
    g_got, up_out, e_given = wait((g_got, up_out, e_given))
    grad_tokens, g_first_gain = kernel_call(
        tokens_kernel,
        [((rows, width), f32), ((1, width), f32)],
        [((rows, 3 * width), bf16)],
        "token_grads",
        g_got, tokens_in, gains, g_resid, qkv_w,
    )

    head_w = kernel_call(
        head_weight_kernel,
        [((3 * DH, width), bf16)],
        [((2 * rows * blocks, 3 * DH), bf16)],
        "head_weights",
        tie(g_head_rows, g_got), all_normed,
    )[0].reshape(3, DH, width)

    def chunk_pair(side):
        kept_kind = 2 * side
        given_kind = jnp.where(head == 0, 1 + side, side)
        return jnp.stack([head_w[kept_kind], head_w[given_kind]])

    few = jnp.concatenate([g_first_gain, g_second_gain, g_router], axis=0)
    few = jnp.pad(few, ((0, FEW - few.shape[0]), (0, 0))).astype(bf16)
    own_pair = jnp.concatenate([*jnp.where(grp == 0, chunk_pair(0), chunk_pair(1)), few])
    other_pair = jnp.concatenate([*jnp.where(grp == 0, chunk_pair(1), chunk_pair(0)), few])
    own_pair = joined(own_pair.astype(f32), exchange(other_pair, "grp", 1))
    from_head = exchange(own_pair[DH:], "head", 1)
    own_pair = jnp.concatenate(
        [own_pair[:DH], from_head[:DH], joined(own_pair[2 * DH :].astype(f32), from_head[DH:])]
    )
    all_pairs = lax.all_gather(own_pair, "blk", axis=0)
    order = jnp.array(
        [
            [0, 2, 4, 6, 8, 10, 1, 3, 5],
            [6, 8, 10, 1, 3, 5, 7, 9, 11],
            [1, 3, 5, 7, 9, 11, 0, 2, 4],
            [7, 9, 11, 0, 2, 4, 6, 8, 10],
        ],
        jnp.int32,
    )[member]
    grad_qkv, few = kernel_call(
        chunk_kernel,
        [((third, width), f32), ((FEW, width), f32)],
        [],
        "chunk_rows",
        order, all_pairs,
    )
    grad_qkv = grad_qkv.T
    few = lax.dynamic_slice_in_dim(few, member * quarter, quarter, 1)

    shared_out = sum_of_four(
        [tie(shared_out, g_got)[i * rows : (i + 1) * rows] for i in range(4)]
    )
    fetched(up_out, g_got, 3)
    fetched(down_out, from_head, 1, 2, 3)
    lower = tie(shared_sum[cutting:], g_got)
    lower = joined(lower, exchange(lower, "blk", 4))
    four_shared = of_four(jnp.concatenate([upper, lower]))
    e_back = over_line_back(tie(e_mine, g_got)[:per_line], e_given)
    expert_sum = mm(pick, e_back, FIRST)
    layer_out = (residual + shared_out + expert_sum).astype(bf16)
    grad_expert_w = kernel_call(
        units_out_kernel,
        [((2, quarter, 4 * units), f32)],
        [],
        "units_out",
        place, *gate_out, *up_out,
    )[0]
    grad_expert_out = kernel_call(
        units_out_kernel, [((1, quarter, 4 * units), f32)], [], "down_out", place, *down_out
    )[0][0].T
    grad_shared_w, grad_shared_out, grad_proj = kernel_call(
        shared_out_kernel,
        [((width, 4 * span), f32), ((quarter, SFF), f32), ((quarter, width), f32)],
        [],
        "shared_grads",
        place, *four_shared,
    )
    grad_shared_out, grad_proj = grad_shared_out.T, grad_proj.T
    return (
        layer_out,
        grad_tokens,
        few[0:2],
        grad_qkv,
        grad_proj,
        few[2 : 2 + EXPERTS],
        grad_shared_w,
        grad_shared_out,
        grad_expert_w,
        grad_expert_out,
    )


def solution(mesh):
    whole = P(("grp", "head", "blk"), None)
    split = P(None, ("grp", "head"))
    sizes = dict(mesh.shape)
    quick = sizes["grp"] == 2 and sizes["head"] == 2 and sizes["blk"] == 8
    return jax.shard_map(
        quick_body if quick else body,
        mesh=mesh,
        in_specs=(
            whole, split, split, split, split, split, split,
            P(None, ("grp", "head"), "blk"), P("blk", ("grp", "head")), whole, whole,
        ),
        out_specs=(
            whole, whole, split, split, split, split, split, split,
            P(None, ("grp", "head"), "blk"), P("blk", ("grp", "head")),
        ),
        check_vma=False,
    )
```

```python
import math

import jax
import jax.numpy as jnp
import numpy as np
from jax import lax
from jax.experimental import pallas as pl
from jax.experimental.pallas import tpu as pltpu
from jax.sharding import PartitionSpec as P

HEADS = 12
DH = 64
EXPERTS = 16
FF = 2048
SFF = 2048
PROMPT_ROWS = 64
PROMPT_LEAST = 1024


EPSILON = 1e-06
NEGATIVE = -1e30


def norm_rows(values, gain):
    inverse = lax.rsqrt(jnp.mean(values * values, axis=-1, keepdims=True) + EPSILON)
    return (values * inverse * gain, inverse)


def norm_back(values, inverse, gain, upstream):
    scaled = upstream * gain
    inner_mean = jnp.mean(scaled * values, axis=-1, keepdims=True)
    return (
        inverse * scaled - values * inverse**3 * inner_mean,
        jnp.sum(upstream * values * inverse, axis=0),
    )


def angle_tables(positions):
    step_index = jnp.arange(DH // 2, dtype=jnp.float32)
    freq_rates = 10000.0 ** (-2.0 * step_index / DH)
    angles = positions.astype(jnp.float32)[:, None] * freq_rates[None, :]
    return (jnp.cos(angles)[:, None, :], jnp.sin(angles)[:, None, :])


def rotate(values, cosine, sine_table):
    half_size = values.shape[-1] // 2
    first_half = values[..., :half_size]
    second = values[..., half_size:]
    return jnp.concatenate(
        [first_half * cosine - second * sine_table, second * cosine + first_half * sine_table],
        axis=-1,
    )


def swish_parts(gate_value):
    sigmoid = jax.nn.sigmoid(gate_value)
    return (gate_value * sigmoid, sigmoid * (1.0 + gate_value * (1.0 - sigmoid)))


def row_layout(head_part, within, block_index, heads_axis, blocks_axis, row_count, prompt_dev):
    prompt_all = prompt_dev * heads_axis * blocks_axis
    is_prompt = within < prompt_dev
    prompt_index = (block_index * heads_axis + head_part) * prompt_dev + within
    cont_index = head_part * (row_count - prompt_dev) + within - prompt_dev
    positions = jnp.where(is_prompt, prompt_index, prompt_all + cont_index)
    return (is_prompt, prompt_index, cont_index, positions)


def fetch_weights(
    norm_gains,
    attn_qkv,
    attn_proj,
    router_rows,
    shared_gate_up,
    shared_down,
    expert_gate_up,
    expert_down,
):
    return (
        lax.all_gather(norm_gains, ("grp", "head"), axis=1, tiled=True),
        lax.all_gather(attn_qkv, ("grp", "head"), axis=1, tiled=True),
        lax.all_gather(attn_proj, ("grp", "head"), axis=1, tiled=True),
        lax.all_gather(router_rows, ("grp", "head"), axis=1, tiled=True),
        lax.all_gather(shared_gate_up, ("grp", "head"), axis=1, tiled=True),
        lax.all_gather(shared_down, ("grp", "head"), axis=1, tiled=True),
        lax.all_gather(expert_gate_up, ("grp", "head"), axis=1, tiled=True),
        lax.all_gather(expert_down, ("grp", "head"), axis=1, tiled=True),
    )


def masked_scores(queries, key_rows, visible):
    scores = jnp.einsum(
        "qhd,khd->hqk", queries, key_rows, preferred_element_type=jnp.float32
    ) * DH ** (-0.5)
    return jnp.where(visible[None], scores, NEGATIVE)


def add_stats(carry, scores, visible):
    row_peak, row_total = carry
    new_peak = jnp.maximum(row_peak, jnp.max(scores, axis=-1))
    terms = jnp.where(visible[None], jnp.exp(scores - new_peak[:, :, None]), 0.0)
    return (new_peak, row_total * jnp.exp(row_peak - new_peak) + jnp.sum(terms, axis=-1))


def block_probs(scores, visible, log_total):
    return jnp.where(visible[None], jnp.exp(scores - log_total[:, :, None]), 0.0)


def grad_block(queries, grad_out, log_total, delta, key_rows, value_rows, visible):
    scale_factor = DH ** (-0.5)
    soft_weights = block_probs(masked_scores(queries, key_rows, visible), visible, log_total)
    grad_weights = jnp.einsum(
        "qhd,khd->hqk", grad_out, value_rows, preferred_element_type=jnp.float32
    )
    grad_scores = (soft_weights * (grad_weights - delta[:, :, None])).astype(jnp.bfloat16)
    grad_query = (
        jnp.einsum("hqk,khd->qhd", grad_scores, key_rows, preferred_element_type=jnp.float32)
        * scale_factor
    )
    grad_key = (
        jnp.einsum("hqk,qhd->khd", grad_scores, queries, preferred_element_type=jnp.float32)
        * scale_factor
    )
    grad_value = jnp.einsum(
        "hqk,qhd->khd",
        soft_weights.astype(jnp.bfloat16),
        grad_out,
        preferred_element_type=jnp.float32,
    )
    return (grad_query, grad_key, grad_value)


def body(
    tokens_in,
    norm_gains,
    attn_qkv,
    attn_proj,
    router_rows,
    shared_gate_up,
    shared_down,
    expert_gate_up,
    expert_down,
    routes,
    out_grad,
):
    heads_axis = lax.axis_size("head")
    blocks_axis = lax.axis_size("blk")
    row_count = tokens_in.shape[0]
    width_all = tokens_in.shape[1]
    prompt_dev = max(PROMPT_ROWS, PROMPT_LEAST // (heads_axis * blocks_axis))
    prompt_all = prompt_dev * heads_axis * blocks_axis
    local_heads = HEADS // heads_axis
    query_rows = heads_axis * row_count
    key_block = min(512, prompt_all)
    block_count = prompt_all // key_block
    head_me = lax.axis_index("head")
    block_me = lax.axis_index("blk")
    gain_rows, qkv_w, proj_w, router_w, shared_w, shared_out_w, expert_w, expert_out_w = (
        fetch_weights(
            norm_gains,
            attn_qkv,
            attn_proj,
            router_rows,
            shared_gate_up,
            shared_down,
            expert_gate_up,
            expert_down,
        )
    )
    tokens = tokens_in.astype(jnp.float32)
    first_gain = gain_rows[0].astype(jnp.float32)
    second_gain = gain_rows[1].astype(jnp.float32)
    normed_f, first_inverse = norm_rows(tokens, first_gain)
    normed = normed_f.astype(jnp.bfloat16)
    mixed_qkv = jnp.dot(normed, qkv_w, preferred_element_type=jnp.float32)
    token_row = jnp.arange(row_count, dtype=jnp.int32)
    token_pos = row_layout(
        head_me, token_row, block_me, heads_axis, blocks_axis, row_count, prompt_dev
    )[3]
    token_cos, token_sin = angle_tables(token_pos)
    query_tok = (
        rotate(mixed_qkv[:, :width_all].reshape(row_count, HEADS, DH), token_cos, token_sin)
        .reshape(row_count, width_all)
        .astype(jnp.bfloat16)
    )
    key_tok = (
        rotate(
            mixed_qkv[:, width_all : 2 * width_all].reshape(row_count, HEADS, DH),
            token_cos,
            token_sin,
        )
        .reshape(row_count, width_all)
        .astype(jnp.bfloat16)
    )
    value_tok = mixed_qkv[:, 2 * width_all :].astype(jnp.bfloat16)
    query_head, key_head, value_head = (
        lax.all_to_all(query_tok, "head", split_axis=1, concat_axis=0, tiled=True),
        lax.all_to_all(key_tok, "head", split_axis=1, concat_axis=0, tiled=True),
        lax.all_to_all(value_tok, "head", split_axis=1, concat_axis=0, tiled=True),
    )
    local_index = jnp.arange(query_rows, dtype=jnp.int32)
    is_prompt, prompt_index, cont_index, head_pos = row_layout(
        local_index // row_count,
        local_index % row_count,
        block_me,
        heads_axis,
        blocks_axis,
        row_count,
        prompt_dev,
    )
    is_cont = jnp.logical_not(is_prompt)
    local_visible = (
        is_cont[:, None] & is_cont[None, :] & (cont_index[None, :] <= cont_index[:, None])
    )
    queries = query_head.reshape(query_rows, local_heads, DH)
    key_local = key_head.reshape(query_rows, local_heads, DH)
    value_local = value_head.reshape(query_rows, local_heads, DH)
    prompt_keys, prompt_values = (
        lax.all_gather(
            key_head.reshape(heads_axis, row_count, -1)[:, :prompt_dev].reshape(
                heads_axis * prompt_dev, -1
            ),
            "blk",
            axis=0,
            tiled=True,
        ),
        lax.all_gather(
            value_head.reshape(heads_axis, row_count, -1)[:, :prompt_dev].reshape(
                heads_axis * prompt_dev, -1
            ),
            "blk",
            axis=0,
            tiled=True,
        ),
    )
    key_blocks = prompt_keys.reshape(block_count, key_block, local_heads, DH)
    value_blocks = prompt_values.reshape(block_count, key_block, local_heads, DH)
    block_starts = jnp.arange(block_count, dtype=jnp.int32) * key_block
    key_offsets = jnp.arange(key_block, dtype=jnp.int32)

    def prompt_visible(start):
        return is_cont[:, None] | (start + key_offsets[None, :] <= prompt_index[:, None])

    def stats_step(carry, member):
        visible = prompt_visible(member[1])
        return (add_stats(carry, masked_scores(queries, member[0], visible), visible), None)

    start_stats = (
        jnp.full((local_heads, query_rows), NEGATIVE, jnp.float32),
        jnp.zeros((local_heads, query_rows), jnp.float32),
    )
    stats = lax.scan(stats_step, start_stats, (key_blocks, block_starts))[0]
    row_peak, row_total = add_stats(
        stats, masked_scores(queries, key_local, local_visible), local_visible
    )
    log_total = row_peak + jnp.log(row_total)

    def output_step(total_out, member):
        visible = prompt_visible(member[2])
        soft_weights = block_probs(
            masked_scores(queries, member[0], visible), visible, log_total
        ).astype(jnp.bfloat16)
        return (
            total_out
            + jnp.einsum(
                "hqk,khd->qhd", soft_weights, member[1], preferred_element_type=jnp.float32
            ),
            None,
        )

    attn_heads = lax.scan(
        output_step,
        jnp.zeros((query_rows, local_heads, DH), jnp.float32),
        (key_blocks, value_blocks, block_starts),
    )[0]
    local_weights = block_probs(
        masked_scores(queries, key_local, local_visible), local_visible, log_total
    ).astype(jnp.bfloat16)
    attn_heads = attn_heads + jnp.einsum(
        "hqk,khd->qhd", local_weights, value_local, preferred_element_type=jnp.float32
    )
    attn_tok = lax.all_to_all(
        attn_heads.reshape(query_rows, -1).astype(jnp.bfloat16),
        "head",
        split_axis=0,
        concat_axis=1,
        tiled=True,
    )
    residual = tokens + jnp.dot(attn_tok, proj_w, preferred_element_type=jnp.float32)
    hidden_f, second_inverse = norm_rows(residual, second_gain)
    hidden = hidden_f.astype(jnp.bfloat16)
    logits = jnp.einsum("td,ed->te", hidden, router_w, preferred_element_type=jnp.float32)
    soft_route = jax.nn.softmax(logits, axis=-1)
    expert_ids = jnp.arange(EXPERTS, dtype=jnp.int32)
    route_match = routes[:, :, None] == expert_ids[None, None, :]
    gate_values = jnp.sum(jnp.where(route_match, soft_route[:, None, :], 0.0), axis=-1)
    shared_pre = jnp.dot(hidden, shared_w, preferred_element_type=jnp.float32)
    shared_act, shared_slope = swish_parts(shared_pre[:, :SFF])
    shared_up = shared_pre[:, SFF:]
    shared_mid = (shared_act * shared_up).astype(jnp.bfloat16)
    shared_out = jnp.dot(shared_mid, shared_out_w, preferred_element_type=jnp.float32)
    unit_count = expert_w.shape[2]
    per_device = max(1, unit_count // FF)
    spread = max(1, FF // unit_count)
    unit_width = unit_count // per_device
    capacity = max(2, 5 * row_count // (2 * EXPERTS))
    slot_count = blocks_axis * per_device * capacity
    pair_expert = routes.reshape(-1)
    pair_match = route_match.reshape(2 * row_count, EXPERTS).astype(jnp.int32)
    pair_rank = jnp.sum(jnp.cumsum(pair_match, axis=0) * pair_match, axis=1) - 1
    slot_base = (
        pair_expert // per_device * spread * per_device * capacity
        + pair_expert % per_device * capacity
        + pair_rank
    )
    slot_index = (
        slot_base[None, :] + (jnp.arange(spread, dtype=jnp.int32) * per_device * capacity)[:, None]
    )
    pair_ids = jnp.arange(2 * row_count, dtype=jnp.int32)
    slot_pair = (
        jnp.full((slot_count,), 2 * row_count, jnp.int32)
        .at[slot_index.reshape(-1)]
        .set(jnp.tile(pair_ids, spread))
    )
    slot_token = slot_pair // 2
    hidden_pad = jnp.concatenate([hidden, jnp.zeros((1, width_all), jnp.bfloat16)], axis=0)
    send_rows = hidden_pad[slot_token].reshape(blocks_axis, per_device, capacity, width_all)
    received_rows = lax.all_to_all(send_rows, "blk", split_axis=0, concat_axis=0, tiled=True)
    gate_weight = expert_w[0].reshape(width_all, per_device, unit_width)
    up_weight = expert_w[1].reshape(width_all, per_device, unit_width)
    down_w = expert_out_w.reshape(per_device, unit_width, width_all)
    expert_gate = jnp.einsum(
        "tfoa,afw->tfow", received_rows, gate_weight, preferred_element_type=jnp.float32
    )
    expert_up_projection = jnp.einsum(
        "tfoa,afw->tfow", received_rows, up_weight, preferred_element_type=jnp.float32
    )
    expert_activation, expert_slope = swish_parts(expert_gate)
    expert_mid = (expert_activation * expert_up_projection).astype(jnp.bfloat16)
    expert_part = jnp.einsum(
        "secm,emd->secd", expert_mid, down_w, preferred_element_type=jnp.float32
    )
    returned = (
        lax.all_to_all(
            expert_part.astype(jnp.bfloat16), "blk", split_axis=0, concat_axis=0, tiled=True
        )
        .astype(expert_part.dtype)
        .reshape(slot_count, width_all)
    )
    pair_out = jnp.sum(returned[slot_index], axis=0).reshape(row_count, 2, width_all)
    expert_sum = jnp.sum(gate_values[:, :, None] * pair_out, axis=1)
    layer_out = (residual + shared_out + expert_sum).astype(jnp.bfloat16)
    gain_rows, qkv_w, proj_w, router_w, shared_w, shared_out_w, expert_w, expert_out_w = (
        fetch_weights(
            norm_gains,
            attn_qkv,
            attn_proj,
            router_rows,
            shared_gate_up,
            shared_down,
            expert_gate_up,
            expert_down,
        )
    )
    gate_weight = expert_w[0].reshape(width_all, per_device, unit_width)
    up_weight = expert_w[1].reshape(width_all, per_device, unit_width)
    down_w = expert_out_w.reshape(per_device, unit_width, width_all)
    grad_layer = out_grad.astype(jnp.float32)
    grad_smid = jnp.einsum("td,fd->tf", out_grad, shared_out_w, preferred_element_type=jnp.float32)
    shared_grads = jnp.concatenate(
        [grad_smid * shared_up * shared_slope, grad_smid * shared_act], axis=1
    ).astype(jnp.bfloat16)
    grad_hidden = jnp.einsum(
        "tf,df->td", shared_grads, shared_w, preferred_element_type=jnp.float32
    )
    grad_shared_w = jnp.einsum(
        "td,tf->df", hidden, shared_grads, preferred_element_type=jnp.float32
    )
    grad_shared_out = jnp.einsum(
        "tf,td->fd", shared_mid, out_grad, preferred_element_type=jnp.float32
    )
    grad_gates = jnp.sum(grad_layer[:, None, :] * pair_out, axis=-1)
    grad_pairs = (
        (gate_values[:, :, None] * grad_layer[:, None, :])
        .reshape(2 * row_count, width_all)
        .astype(jnp.bfloat16)
    )
    grad_pad = jnp.concatenate([grad_pairs, jnp.zeros((1, width_all), jnp.bfloat16)], axis=0)
    grad_recv = lax.all_to_all(
        grad_pad[slot_pair].reshape(blocks_axis, per_device, capacity, width_all),
        "blk",
        split_axis=0,
        concat_axis=0,
        tiled=True,
    )
    grad_expert_middle = jnp.einsum(
        "secd,emd->secm", grad_recv, down_w, preferred_element_type=jnp.float32
    )
    grad_expert_gate_branch = (grad_expert_middle * expert_up_projection * expert_slope).astype(
        jnp.bfloat16
    )
    grad_expert_up_branch = (grad_expert_middle * expert_activation).astype(jnp.bfloat16)
    grad_rows = jnp.einsum(
        "auwj,buj->auwb", grad_expert_gate_branch, gate_weight, preferred_element_type=jnp.float32
    ) + jnp.einsum(
        "auwj,buj->auwb", grad_expert_up_branch, up_weight, preferred_element_type=jnp.float32
    )
    grad_expert_w = jnp.stack(
        [
            jnp.einsum(
                "jgki,jgkt->igt",
                received_rows,
                grad_expert_gate_branch,
                preferred_element_type=jnp.float32,
            ).reshape(width_all, unit_count),
            jnp.einsum(
                "jgki,jgkt->igt",
                received_rows,
                grad_expert_up_branch,
                preferred_element_type=jnp.float32,
            ).reshape(width_all, unit_count),
        ]
    )
    grad_expert_out = jnp.einsum(
        "secm,secd->emd", expert_mid, grad_recv, preferred_element_type=jnp.float32
    ).reshape(unit_count, width_all)
    grad_back = (
        lax.all_to_all(
            grad_rows.astype(jnp.bfloat16), "blk", split_axis=0, concat_axis=0, tiled=True
        )
        .astype(grad_rows.dtype)
        .reshape(slot_count, width_all)
    )
    grad_hidden = grad_hidden + jnp.sum(
        jnp.sum(grad_back[slot_index], axis=0).reshape(row_count, 2, width_all), axis=1
    )
    grad_soft = jnp.sum(jnp.where(route_match, grad_gates[:, :, None], 0.0), axis=1)
    grad_logits = (
        soft_route * (grad_soft - jnp.sum(soft_route * grad_soft, axis=-1, keepdims=True))
    ).astype(jnp.bfloat16)
    grad_hidden = grad_hidden + jnp.einsum(
        "te,ed->td", grad_logits, router_w, preferred_element_type=jnp.float32
    )
    grad_router = jnp.einsum("te,td->ed", grad_logits, hidden, preferred_element_type=jnp.float32)
    grad_norm_two, grad_second_gain = norm_back(residual, second_inverse, second_gain, grad_hidden)
    grad_resid = grad_layer + grad_norm_two
    grad_branch = grad_resid.astype(jnp.bfloat16)
    grad_proj = jnp.einsum("td,te->de", attn_tok, grad_branch, preferred_element_type=jnp.float32)
    grad_attn_tok = jnp.einsum(
        "te,de->td", grad_branch, proj_w, preferred_element_type=jnp.float32
    ).astype(jnp.bfloat16)
    grad_heads = lax.all_to_all(
        grad_attn_tok, "head", split_axis=1, concat_axis=0, tiled=True
    ).reshape(query_rows, local_heads, DH)
    delta = jnp.transpose(jnp.sum(grad_heads * attn_heads, axis=-1))

    def back_step(grad_acc, member):
        visible = prompt_visible(member[2])
        step_query, step_key, step_value = grad_block(
            queries, grad_heads, log_total, delta, member[0], member[1], visible
        )
        return (grad_acc + step_query, (step_key, step_value))

    grad_query, prompt_grads = lax.scan(
        back_step,
        jnp.zeros((query_rows, local_heads, DH), jnp.float32),
        (key_blocks, value_blocks, block_starts),
    )
    local_query, local_key, local_value = grad_block(
        queries, grad_heads, log_total, delta, key_local, value_local, local_visible
    )
    grad_query = grad_query + local_query
    key_share, value_share = (
        lax.psum_scatter(
            prompt_grads[0].reshape(prompt_all, -1), "blk", scatter_dimension=0, tiled=True
        ),
        lax.psum_scatter(
            prompt_grads[1].reshape(prompt_all, -1), "blk", scatter_dimension=0, tiled=True
        ),
    )
    grad_key = (
        local_key.reshape(heads_axis, row_count, -1)
        .at[:, :prompt_dev]
        .add(key_share.reshape(heads_axis, prompt_dev, -1))
        .reshape(query_rows, local_heads, DH)
    )
    grad_value = (
        local_value.reshape(heads_axis, row_count, -1)
        .at[:, :prompt_dev]
        .add(value_share.reshape(heads_axis, prompt_dev, -1))
    )
    head_cos, head_sin = angle_tables(head_pos)
    grad_query = (
        rotate(grad_query, head_cos, -head_sin).reshape(query_rows, -1).astype(jnp.bfloat16)
    )
    grad_key = rotate(grad_key, head_cos, -head_sin).reshape(query_rows, -1).astype(jnp.bfloat16)
    grad_value = grad_value.reshape(query_rows, -1).astype(jnp.bfloat16)
    grad_q_tok, grad_k_tok, grad_v_tok = (
        lax.all_to_all(grad_query, "head", split_axis=0, concat_axis=1, tiled=True),
        lax.all_to_all(grad_key, "head", split_axis=0, concat_axis=1, tiled=True),
        lax.all_to_all(grad_value, "head", split_axis=0, concat_axis=1, tiled=True),
    )
    grad_qkv_rows = jnp.concatenate([grad_q_tok, grad_k_tok, grad_v_tok], axis=1)
    grad_normed = jnp.einsum("tf,df->td", grad_qkv_rows, qkv_w, preferred_element_type=jnp.float32)
    grad_qkv = jnp.einsum("td,tf->df", normed, grad_qkv_rows, preferred_element_type=jnp.float32)
    grad_norm_one, grad_first_gain = norm_back(tokens, first_inverse, first_gain, grad_normed)
    grad_tokens = grad_resid + grad_norm_one
    owned = (
        lax.psum_scatter(
            jnp.stack([grad_first_gain, grad_second_gain]).astype(jnp.bfloat16),
            ("grp", "head"),
            scatter_dimension=1,
            tiled=True,
        ).astype(jnp.float32),
        lax.psum_scatter(
            grad_qkv.astype(jnp.bfloat16), ("grp", "head"), scatter_dimension=1, tiled=True
        ).astype(jnp.float32),
        lax.psum_scatter(
            grad_proj.astype(jnp.bfloat16), ("grp", "head"), scatter_dimension=1, tiled=True
        ).astype(jnp.float32),
        lax.psum_scatter(
            grad_router.astype(jnp.bfloat16), ("grp", "head"), scatter_dimension=1, tiled=True
        ).astype(jnp.float32),
        lax.psum_scatter(
            grad_shared_w.astype(jnp.bfloat16), ("grp", "head"), scatter_dimension=1, tiled=True
        ).astype(jnp.float32),
        lax.psum_scatter(
            grad_shared_out.astype(jnp.bfloat16), ("grp", "head"), scatter_dimension=1, tiled=True
        ).astype(jnp.float32),
        lax.psum_scatter(
            grad_expert_w.astype(jnp.bfloat16), ("grp", "head"), scatter_dimension=1, tiled=True
        ).astype(jnp.float32),
        lax.psum_scatter(
            grad_expert_out.astype(jnp.bfloat16), ("grp", "head"), scatter_dimension=1, tiled=True
        ).astype(jnp.float32),
    )
    summed = lax.psum((owned[0], owned[1], owned[2], owned[3], owned[4], owned[5]), "blk")
    return (
        layer_out,
        grad_tokens,
        summed[0],
        summed[1],
        summed[2],
        summed[3],
        summed[4],
        summed[5],
        owned[6],
        owned[7],
    )


TRANSPOSED = (((1,), (1,)), ((), ()))
PLAIN = (((1,), (0,)), ((), ()))
FIRST = (((0,), (0,)), ((), ()))
FORWARD_VMEM = 20 * 1024 * 1024
BACKWARD_VMEM = 32 * 1024 * 1024
FEW = 32
UNIT_ORDER = (0, 2, 1, 3)


def mm(left, right, dims=PLAIN):
    return lax.dot_general(left, right, dims, preferred_element_type=jnp.float32)


def assemble(rows_ref, cut, parts, prompt_to, cont_to):
    blocks, half = rows_ref.shape[0], rows_ref.shape[1] // 2
    for block in range(blocks):
        for head_part in range(2):
            piece = rows_ref[block, head_part * half : (head_part + 1) * half, :]
            place = (block * 2 + head_part) * half
            for order in range(parts):
                prompt_to[order][place : place + half, :] = piece[
                    :, order * cut : (order + 1) * cut
                ]
                cont_to[order][place : place + half, :] = piece[
                    :, (parts + order) * cut : (parts + order + 1) * cut
                ]


def spread_out(target, prompt_parts, cont_parts, cut):
    blocks, half = target.shape[0], target.shape[1] // 2
    for block in range(blocks):
        for head_part in range(2):
            place = (block * 2 + head_part) * half
            pieces = [part[place : place + half, :] for part in prompt_parts]
            pieces += [part[place : place + half, :] for part in cont_parts]
            target[block, head_part * half : (head_part + 1) * half, :] = jnp.concatenate(
                pieces, axis=1
            ).astype(target.dtype)


def causal_mask(rows):
    keys = lax.broadcasted_iota(jnp.int32, (rows, rows), 0)
    query = lax.broadcasted_iota(jnp.int32, (rows, rows), 1)
    return keys <= query


def cont_mask(rows, cont):
    keys = lax.broadcasted_iota(jnp.int32, (rows, rows), 0)
    query = lax.broadcasted_iota(jnp.int32, (rows, rows), 1)
    return (keys // cont == query // cont) & (keys <= query)


def masked_block(keys, queries, mask):
    scores = mm(keys, queries, TRANSPOSED) * DH ** (-0.5)
    if mask is None:
        return scores
    return jnp.where(mask, scores, NEGATIVE)


def attention_kernel(rows_ref, out_ref, qp, kp, vp, qc, kc, vc, op, oc):
    block = 256
    prompt = qp.shape[0]
    assemble(rows_ref, DH, 3, (qp, kp, vp), (qc, kc, vc))
    cont = rows_ref.shape[1]
    for is_cont in range(2):
        source_q, source_k, source_v, result = (
            (qc, kc, vc, oc) if is_cont else (qp, kp, vp, op)
        )
        mask = cont_mask(block, cont) if is_cont else causal_mask(block)
        for step in range(prompt // block):
            rows = slice(step * block, (step + 1) * block)
            queries = source_q[rows, :]
            own = masked_block(source_k[rows, :], queries, mask)
            seen = prompt if is_cont else step * block
            peak = jnp.max(own, axis=0, keepdims=True)
            if seen:
                past = masked_block(kp[0:seen, :], queries, None)
                peak = jnp.maximum(peak, jnp.max(past, axis=0, keepdims=True))
            own = jnp.exp(own - peak)
            total = jnp.sum(own, axis=0, keepdims=True)
            gathered = mm(source_v[rows, :], own.astype(jnp.bfloat16), FIRST)
            if seen:
                past = jnp.exp(past - peak)
                total = total + jnp.sum(past, axis=0, keepdims=True)
                gathered = gathered + mm(vp[0:seen, :], past.astype(jnp.bfloat16), FIRST)
            result[rows, :] = jnp.transpose(gathered / total)
    spread_out(out_ref, (op,), (oc,), DH)


def attention_forward(rows):
    blocks, both, _ = rows.shape
    prompt = blocks * both
    small = pltpu.VMEM((prompt, DH), jnp.bfloat16)
    wide = pltpu.VMEM((prompt, DH), jnp.float32)
    return pl.pallas_call(
        attention_kernel,
        out_shape=jax.ShapeDtypeStruct((blocks, both, 2 * DH), jnp.bfloat16),
        in_specs=[pl.BlockSpec(memory_space=pltpu.VMEM)],
        out_specs=pl.BlockSpec(memory_space=pltpu.VMEM),
        scratch_shapes=[small] * 6 + [wide] * 2,
        compiler_params=pltpu.CompilerParams(vmem_limit_bytes=FORWARD_VMEM),
        cost_estimate=pl.CostEstimate(
            flops=2**20, bytes_accessed=2**16, transcendentals=0
        ),
        name="attention_forward",
    )(rows)


def turn_back(values, cosine, sine):
    half = DH // 2
    first, second = values[:, :half], values[:, half:]
    return jnp.concatenate(
        [first * cosine + second * sine, second * cosine - first * sine], axis=1
    )


def attention_back_kernel(
    rows_ref, grad_ref, table_ref, out_ref,
    qp, kp, vp, qc, kc, vc, gp, gc, dqp, dkp, dvp, dqc, dkc, dvc,
):
    block = 256
    prompt = qp.shape[0]
    scale = DH ** (-0.5)
    assemble(rows_ref, DH, 3, (qp, kp, vp), (qc, kc, vc))
    assemble(grad_ref, DH, 1, (gp,), (gc,))
    cont = rows_ref.shape[1]
    dkp[...] = jnp.zeros_like(dkp)
    dvp[...] = jnp.zeros_like(dvp)
    for is_cont in range(2):
        source_q, source_k, source_v, source_g = (
            (qc, kc, vc, gc) if is_cont else (qp, kp, vp, gp)
        )
        to_q, to_k, to_v = (dqc, dkc, dvc) if is_cont else (dqp, dkp, dvp)
        mask = cont_mask(block, cont) if is_cont else causal_mask(block)
        for step in range(prompt // block):
            rows = slice(step * block, (step + 1) * block)
            queries = source_q[rows, :]
            grads = source_g[rows, :]
            own_keys = source_k[rows, :]
            own = masked_block(own_keys, queries, mask)
            seen = prompt if is_cont else step * block
            peak = jnp.max(own, axis=0, keepdims=True)
            if seen:
                past = masked_block(kp[0:seen, :], queries, None)
                peak = jnp.maximum(peak, jnp.max(past, axis=0, keepdims=True))
            own = jnp.exp(own - peak)
            total = jnp.sum(own, axis=0, keepdims=True)
            if seen:
                past = jnp.exp(past - peak)
                total = total + jnp.sum(past, axis=0, keepdims=True)
            inverse = 1.0 / total
            own = own * inverse
            own_grad = mm(source_v[rows, :], grads, TRANSPOSED)
            delta = jnp.sum(own * own_grad, axis=0, keepdims=True)
            if seen:
                past = past * inverse
                past_grad = mm(vp[0:seen, :], grads, TRANSPOSED)
                delta = delta + jnp.sum(past * past_grad, axis=0, keepdims=True)
            own_scores = (own * (own_grad - delta)).astype(jnp.bfloat16)
            own_dv = mm(own.astype(jnp.bfloat16), grads)
            own_dk = mm(own_scores, queries) * scale
            turned = mm(own_keys, own_scores, FIRST)
            if is_cont:
                to_v[rows, :] = own_dv
                to_k[rows, :] = own_dk
            else:
                to_v[rows, :] += own_dv
                to_k[rows, :] += own_dk
            if seen:
                past_scores = (past * (past_grad - delta)).astype(jnp.bfloat16)
                dvp[0:seen, :] += mm(past.astype(jnp.bfloat16), grads)
                dkp[0:seen, :] += mm(past_scores, queries) * scale
                turned = turned + mm(kp[0:seen, :], past_scores, FIRST)
            to_q[rows, :] = jnp.transpose(turned) * scale
    turn = DH // 2
    cos_p, sin_p = table_ref[0:prompt, :turn], table_ref[0:prompt, turn:]
    dqp[...] = turn_back(dqp[...], cos_p, sin_p)
    dkp[...] = turn_back(dkp[...], cos_p, sin_p)
    for step in range(prompt // cont):
        rows = slice(step * cont, (step + 1) * cont)
        cos_c = table_ref[prompt : prompt + cont, :turn]
        sin_c = table_ref[prompt : prompt + cont, turn:]
        dqc[rows, :] = turn_back(dqc[rows, :], cos_c, sin_c)
        dkc[rows, :] = turn_back(dkc[rows, :], cos_c, sin_c)
    spread_out(out_ref, (dqp, dkp, dvp), (dqc, dkc, dvc), DH)


def attention_backward(rows, grads, table):
    blocks, both, wide = rows.shape
    prompt = blocks * both
    small = pltpu.VMEM((prompt, DH), jnp.bfloat16)
    large = pltpu.VMEM((prompt, DH), jnp.float32)
    return pl.pallas_call(
        attention_back_kernel,
        out_shape=jax.ShapeDtypeStruct((blocks, both, wide), jnp.bfloat16),
        in_specs=[pl.BlockSpec(memory_space=pltpu.VMEM)] * 3,
        out_specs=pl.BlockSpec(memory_space=pltpu.VMEM),
        scratch_shapes=[small] * 8 + [large] * 6,
        compiler_params=pltpu.CompilerParams(vmem_limit_bytes=BACKWARD_VMEM),
        cost_estimate=pl.CostEstimate(
            flops=2**20, bytes_accessed=2**16, transcendentals=0
        ),
        name="attention_backward",
    )(rows, grads, table)


def exchange(values, axis, mask):
    return lax.ppermute(values, axis, [(i, i ^ mask) for i in range(lax.axis_size(axis))])


def to_member(values, number):
    if number == 2:
        return exchange(values, "grp", 1)
    if number == 1:
        return exchange(values, "head", 1)
    return lax.ppermute(values, ("grp", "head"), [(i, i ^ number) for i in range(4)])


def tie(values, *after):
    return lax.optimization_barrier((values, *after))[0]


def padded_bytes(shape, kind):
    shape = (1,) * (2 - len(shape)) + tuple(shape)
    rows, lanes = -(-shape[-2] // 16) * 16, -(-shape[-1] // 128) * 128
    return math.prod(shape[:-2]) * rows * lanes * jnp.dtype(kind).itemsize


def kernel_call(body_of, outs, scratch, name, *inputs, room=6):
    held = [*outs, *scratch, *((one.shape, one.dtype) for one in inputs)]
    limit = sum(padded_bytes(*one) for one in held) + room * 2**20
    spec = pl.BlockSpec(memory_space=pltpu.VMEM)
    return pl.pallas_call(
        body_of,
        out_shape=[jax.ShapeDtypeStruct(*out) for out in outs],
        in_specs=[
            pl.BlockSpec(memory_space=pltpu.SMEM) if one.dtype == jnp.int32 else spec
            for one in inputs
        ],
        out_specs=[spec] * len(outs),
        scratch_shapes=[pltpu.VMEM(*one) for one in scratch],
        compiler_params=pltpu.CompilerParams(vmem_limit_bytes=limit),
        cost_estimate=pl.CostEstimate(flops=2**20, bytes_accessed=2**16, transcendentals=0),
        name=name,
    )(*inputs)


def packed(rows):
    count, width = rows.shape
    blocks = count // 20
    last = rows[16 * blocks :]
    half = width // 2
    return jnp.concatenate(
        [
            rows[: 8 * blocks].reshape(blocks, 8, width),
            rows[8 * blocks : 16 * blocks].reshape(blocks, 8, width),
            jnp.concatenate(
                [last[:, :half].reshape(blocks, 4, half), last[:, half:].reshape(blocks, 4, half)],
                axis=1,
            ),
        ],
        axis=2,
    )


def unpack_to(target, at, source_ref):
    blocks = source_ref.shape[0]
    width = target.shape[1]
    half = width // 2
    target[at : at + 8 * blocks, :] = source_ref[:, :, 0:width].reshape(8 * blocks, width)
    target[at + 8 * blocks : at + 16 * blocks, :] = source_ref[:, :, width : 2 * width].reshape(
        8 * blocks, width
    )
    for block in range(blocks):
        place = at + 16 * blocks + 4 * block
        last = source_ref[block, :, 2 * width :]
        target[place : place + 4, 0:half] = last[0:4]
        target[place : place + 4, half:width] = last[4:8]


def pack_kernel(rows_ref, out_ref):
    out_ref[...] = packed(rows_ref[...].astype(jnp.float32)).astype(jnp.bfloat16)


def join_kernel(own_ref, part_ref, out_ref):
    rows = own_ref[...] + part_ref[...].astype(jnp.float32)
    out_ref[...] = packed(rows).astype(jnp.bfloat16)


def layer_kernel(got_ref, pick_ref, residual_ref, shared_ref, out_ref, rows):
    unpack_to(rows, 0, got_ref)
    out_ref[...] = (
        residual_ref[...] + shared_ref[...] + mm(pick_ref[...], rows[...], FIRST)
    ).astype(jnp.bfloat16)


def qkv_kernel(place, tokens_ref, partner_ref, table_ref, window_ref, few_ref, *refs):
    got, passed = refs[0:3], refs[3:6]
    normed_ref, rows_ref, gains_ref, router_ref, weight_ref, window, few, both = refs[6:]
    quad_me, core, head = place[0], place[1], place[4]
    rows, width = tokens_ref.shape
    half, quarter = rows // 2, width // 4
    per = window.shape[1] // 2
    window[quad_me] = window_ref[...]
    few[quad_me] = few_ref[...].astype(jnp.float32)
    for j in (1, 2, 3):
        k = quad_me ^ j
        few[k] = got[j - 1][per : per + 16, :].astype(jnp.float32)
        window[k, pl.ds(pl.multiple_of(core * per, 64), per), :] = got[j - 1][0:per, :]
        window[k, pl.ds(pl.multiple_of((1 - core) * per, 64), per), :] = passed[j - 1][0:per, :]
    span = 2 * per

    @pl.when(head == 0)
    def _():
        weight_ref[0:span, :] = window[0]
        weight_ref[span : 2 * span, :] = window[1]
        weight_ref[2 * span : 2 * span + per, :] = window[2, per:span, :]
        weight_ref[2 * span + per : 3 * span, :] = window[3, 0:per, :]

    @pl.when(head == 1)
    def _():
        weight_ref[0:per, :] = window[0, per:span, :]
        weight_ref[per:span, :] = window[1, 0:per, :]
        weight_ref[span : 2 * span, :] = window[2]
        weight_ref[2 * span : 3 * span, :] = window[3]

    def few_row(number):
        part, row = divmod(number, 5)
        return jnp.concatenate(
            [few[k, row : row + 1, part * quarter : (part + 1) * quarter] for k in range(4)],
            axis=1,
        )

    gains = jnp.concatenate([few_row(0), few_row(1)], axis=0)
    gains_ref[...] = gains
    router_ref[...] = jnp.concatenate(
        [few_row(2 + e) for e in range(EXPERTS)], axis=0
    ).astype(jnp.bfloat16)
    for where, source in ((head, tokens_ref), (1 - head, partner_ref)):
        tokens = source[...].astype(jnp.float32)
        both[where] = norm_rows(tokens, gains[0:1])[0].astype(jnp.bfloat16)
    normed = both[...].reshape(2 * rows, width)
    normed_ref[...] = normed
    mixed = mm(normed, weight_ref[...], TRANSPOSED)
    turn = DH // 2
    table = []
    for part in range(2):
        table.append(table_ref[pl.ds(pl.multiple_of((2 * place[3] + part) * half, 64), half), :])
        at = table_ref.shape[0] - 2 * half + part * half
        table.append(table_ref[at : at + half, :])
    table = jnp.concatenate(table, axis=0)
    cosine, sine = table[:, :turn], table[:, turn:]
    heads = HEADS // 2

    def chunk(number):
        return mixed[:, number * DH : (number + 1) * DH]

    rows_ref[...] = jnp.zeros_like(rows_ref)
    for one in range(heads):
        pieces = [
            turn_back(chunk(one), cosine, -sine),
            turn_back(chunk(heads + one), cosine, -sine),
            chunk(2 * heads + one),
        ]
        for part in range(2):
            at = part * rows
            rows_ref[one, part * half : (part + 1) * half, :] = jnp.concatenate(
                [piece[at : at + half] for piece in pieces]
                + [piece[at + half : at + rows] for piece in pieces],
                axis=1,
            ).astype(jnp.bfloat16)


def hidden_kernel(place, got_ref, partner_ref, tokens_ref, gains_ref, pick_ref, *refs):
    own, other = refs[0:4], refs[4:8]
    residual_ref, hidden_ref, attn_ref, sent_ref, proj_ref, attn = refs[8:]
    head = place[4]
    rows, width = tokens_ref.shape
    half = rows // 2
    for j in range(4):
        for where, source in ((place[1], own[j]), (1 - place[1], other[j])):
            proj_ref[(place[0] ^ j) * 2 + where] = source[...]
    for one in range(HEADS // 2):
        at = slice(one * DH, (one + 1) * DH)
        mine = got_ref[one, pl.ds(pl.multiple_of(head * half, 64), half), :]
        for where, piece in ((head, mine), (1 - head, partner_ref[one])):
            attn[where, 0:half, at] = piece[:, 0:DH]
            attn[where, half:rows, at] = piece[:, DH : 2 * DH]
    attn_all = jnp.concatenate([attn[0], attn[1]], axis=1)
    attn_ref[...] = attn_all
    residual = tokens_ref[...].astype(jnp.float32) + mm(
        attn_all, proj_ref[...].reshape(width, width), TRANSPOSED
    )
    residual_ref[...] = residual
    hidden = norm_rows(residual, gains_ref[1:2, :])[0].astype(jnp.bfloat16)
    hidden_ref[...] = hidden
    sent_ref[...] = packed(mm(pick_ref[...], hidden)).astype(jnp.bfloat16)


def expert_kernel(place, own_ref, other_ref, own_grad, other_grad, router_ref, *refs):
    gates, ups, downs = refs[0:4], refs[4:8], refs[8:12]
    (
        g_own, g_part, e_own, e_part, egate_ref, eup_ref, mid_ref, eout_ref, g_router_ref,
        rows_ref, gate_w, up_w, down_w, grad_ref,
    ) = refs[12:]
    quad_me, expert_me = place[0], place[2]
    half_count = rows_ref.shape[0] // 2
    unpack_to(rows_ref, 0, own_ref)
    unpack_to(rows_ref, half_count, other_ref)
    unpack_to(grad_ref, 0, own_grad)
    unpack_to(grad_ref, half_count, other_grad)
    quarter = gates[0].shape[0]
    for j in range(4):
        at = pl.ds(pl.multiple_of((quad_me ^ j) * quarter, 64), quarter)
        gate_w[at, :] = gates[j][...]
        up_w[at, :] = ups[j][...]
        down_w[at, :] = downs[j][...]
    count = rows_ref.shape[0]
    block = count // 4
    router = router_ref[...]
    mine = lax.broadcasted_iota(jnp.int32, (block, EXPERTS), 1) == expert_me
    mine = mine.astype(jnp.float32)
    g_router = jnp.zeros_like(g_router_ref)
    for step in range(4):
        at = slice(step * block, (step + 1) * block)
        rows, grads = rows_ref[at, :], grad_ref[at, :]
        logits = mm(rows, router, TRANSPOSED)
        logits = jnp.exp(logits - jnp.max(logits, axis=1, keepdims=True))
        soft = logits / jnp.sum(logits, axis=1, keepdims=True)
        gate = jnp.sum(soft * mine, axis=1, keepdims=True)
        e_up = mm(rows, up_w[...])
        e_act, e_slope = swish_parts(mm(rows, gate_w[...]))
        e_mid = e_act * e_up
        e_grad = mm(grads, down_w[...])
        g_gate = jnp.sum(e_mid * e_grad, axis=1, keepdims=True)
        g_mid = e_grad * gate
        egate = (g_mid * e_up * e_slope).astype(jnp.bfloat16)
        eup = (g_mid * e_act).astype(jnp.bfloat16)
        e_mid = e_mid.astype(jnp.bfloat16)
        g_logits = (g_gate * soft * (mine - gate)).astype(jnp.bfloat16)
        g_rows = (
            mm(egate, gate_w[...], TRANSPOSED)
            + mm(eup, up_w[...], TRANSPOSED)
            + mm(g_logits, router)
        )
        e_rows = gate * mm(e_mid, down_w[...], TRANSPOSED)
        if step < 2:
            g_own[at, :] = g_rows
            e_own[at, :] = e_rows
        else:
            there = slice((step - 2) * block, (step - 1) * block)
            g_part[there, :] = g_rows.astype(jnp.bfloat16)
            e_part[there, :] = e_rows.astype(jnp.bfloat16)
        egate_ref[at, :] = egate
        eup_ref[at, :] = eup
        mid_ref[at, :] = e_mid
        eout_ref[at, :] = (gate * grads.astype(jnp.float32)).astype(jnp.bfloat16)
        g_router = g_router + mm(g_logits, rows, FIRST)
    g_router_ref[...] = g_router


def branch_kernel(
    place, got_ref, pick_ref, shared_ref, residual_ref, gains_ref, grad_ref, proj_ref,
    resid_ref, branch_ref, mine_ref, theirs_ref, gain_ref, back, heads,
):
    rows, width = grad_ref.shape
    unpack_to(back, 0, got_ref)
    g_hidden = mm(pick_ref[...], back[...], FIRST) + shared_ref[...].astype(jnp.float32)
    residual = residual_ref[...]
    gain = gains_ref[1:2, :]
    inverse = norm_rows(residual, gain)[1]
    g_norm, g_gain = norm_back(residual, inverse, gain, g_hidden)
    gain_ref[...] = g_gain[None]
    g_resid = grad_ref[...].astype(jnp.float32) + g_norm
    resid_ref[...] = g_resid
    branch = g_resid.astype(jnp.bfloat16)
    branch_ref[...] = branch
    attn = mm(branch, proj_ref[...].reshape(width, width)).astype(jnp.bfloat16)
    half = rows // 2
    for one in range(HEADS):
        piece = attn[:, one * DH : (one + 1) * DH]
        heads[one // (HEADS // 2), one % (HEADS // 2)] = jnp.concatenate(
            [piece[:half], piece[half:]], axis=1
        )
    mine_ref[...] = heads[place[4]]
    theirs_ref[...] = heads[1 - place[4]]


def tokens_kernel(
    place, got_ref, qkv_ref, tokens_ref, partner_ref, mine_ref, theirs_ref, gain_ref, parts, grads
):
    half = got_ref.shape[1] // 2
    rows = 2 * half
    heads = HEADS // 2
    for one in range(heads):
        for part in range(2):
            piece = got_ref[one, part * half : (part + 1) * half, :]
            at = part * rows
            for kind in range(3):
                there = slice((kind * heads + one) * DH, (kind * heads + one + 1) * DH)
                parts[at : at + half, there] = piece[:, kind * DH : (kind + 1) * DH]
                parts[at + half : at + rows, there] = piece[:, (3 + kind) * DH : (4 + kind) * DH]
    g_normed = mm(parts[...], qkv_ref[...])
    grads[0] = g_normed[:rows]
    grads[1] = g_normed[rows:]
    mine_ref[...] = grads[place[4]]
    theirs_ref[...] = grads[1 - place[4]].astype(jnp.bfloat16)
    gain = 0.0
    for source, where in ((tokens_ref, place[4]), (partner_ref, 1 - place[4])):
        tokens = source[...].astype(jnp.float32)
        inverse = norm_rows(tokens, 1.0)[1]
        gain = gain + jnp.sum(grads[where] * tokens * inverse, axis=0, keepdims=True)
    gain_ref[...] = gain


def tokens_out_kernel(mine_ref, partner_ref, tokens_ref, gains_ref, resid_ref, out_ref):
    g_normed = mine_ref[...] + partner_ref[...].astype(jnp.float32)
    tokens = tokens_ref[...].astype(jnp.float32)
    gain = gains_ref[0:1, :]
    inverse = norm_rows(tokens, gain)[1]
    out_ref[...] = resid_ref[...] + norm_back(tokens, inverse, gain, g_normed)[0]


def head_weight_kernel(rows_ref, normed_ref, out_ref, left):
    blocks, both, wide = rows_ref.shape
    half = both // 2
    for block in range(blocks):
        for part in range(2):
            at = (block * 2 + part) * both
            piece = rows_ref[block, part * half : (part + 1) * half, :]
            left[at : at + half, :] = piece[:, 0 : wide // 2]
            left[at + half : at + both, :] = piece[:, wide // 2 : wide]
    right = normed_ref[...].reshape(2 * both * blocks, normed_ref.shape[2])
    out_ref[...] = mm(left[...], right, FIRST).astype(jnp.bfloat16)


def chunk_kernel(order, got_ref, out_ref, few_ref):
    few = jnp.zeros_like(few_ref)
    for source in range(got_ref.shape[0]):
        few = few + got_ref[source, 2 * DH : 2 * DH + FEW, :].astype(jnp.float32)
    few_ref[...] = few
    for number in range(order.shape[0]):
        which = order[number]
        at = pl.ds(pl.multiple_of(which % 2 * DH, DH), DH)
        out_ref[number * DH : (number + 1) * DH, :] = got_ref[which // 2, at, :].astype(
            jnp.float32
        )


def shared_kernel(place, *refs):
    hidden_refs, grads_refs, pieces = refs[0:4], refs[4:8], refs[8:12]
    out_ref, back_ref = refs[12:14]
    given = refs[14:18]
    both_w, down_w, g_both, g_down = refs[18:]
    quad_me = place[0]
    width, span = both_w.shape[0], both_w.shape[1] // 4
    quarter = width // 4
    block = hidden_refs[0].shape[0]
    for j in range(4):
        k = quad_me ^ j
        both_w[:, pl.ds(pl.multiple_of(k * span, 128), span)] = pieces[j][0:width, :]
        at = pl.ds(pl.multiple_of(k * quarter, 64), quarter)
        down_w[at, 0:span] = pieces[j][width : width + quarter, :]
        down_w[at, span : 2 * span] = pieces[j][width + quarter : width + 2 * quarter, :]
    for step in range(2):
        rows = slice(step * 2 * block, (step + 1) * 2 * block)
        hidden = jnp.concatenate([hidden_refs[2 * step][...], hidden_refs[2 * step + 1][...]])
        grads = jnp.concatenate([grads_refs[2 * step][...], grads_refs[2 * step + 1][...]])
        pre = mm(hidden, both_w[...])
        act, slope = swish_parts(pre[:, : 2 * span])
        up = pre[:, 2 * span :]
        mid = (act * up).astype(jnp.bfloat16)
        out_ref[rows, :] = mm(mid, down_w[...], TRANSPOSED).astype(jnp.bfloat16)
        g_mid = mm(grads, down_w[...])
        g_pre = jnp.concatenate([g_mid * up * slope, g_mid * act], axis=1).astype(jnp.bfloat16)
        back_ref[rows, :] = mm(g_pre, both_w[...], TRANSPOSED).astype(jnp.bfloat16)
        new_both = mm(hidden, g_pre, FIRST)
        new_down = mm(grads, mid, FIRST)
        if step == 0:
            g_both[...] = new_both
            g_down[...] = new_down
        else:
            g_both[...] += new_both
            g_down[...] += new_down
    for j in range(4):
        k = quad_me ^ j
        at = pl.ds(pl.multiple_of(k * quarter, 64), quarter)
        given[j][0:width, :] = g_both[:, pl.ds(pl.multiple_of(k * span, 128), span)].astype(
            jnp.bfloat16
        )
        given[j][width : width + quarter, :] = g_down[at, 0:span].astype(jnp.bfloat16)
        given[j][width + quarter : width + 2 * quarter, :] = g_down[at, span : 2 * span].astype(
            jnp.bfloat16
        )


def shared_out_kernel(place, *refs):
    parts, projs, wide_ref, down_ref, proj_ref = refs[0:4], refs[4:8], refs[8], refs[9], refs[10]
    width, span = wide_ref.shape[0], parts[0].shape[1]
    quarter = down_ref.shape[0]
    per = quarter // 4
    for j in range(4):
        k = (place[3] % 4) ^ j
        at = pl.ds(pl.multiple_of(k * span, 128), span)
        wide_ref[:, at] = parts[j][0:width, :].astype(jnp.float32)
        down_ref[:, at] = parts[j][width : width + quarter, :].astype(jnp.float32)
        at = pl.ds(pl.multiple_of((4 + k) * span, 128), span)
        down_ref[:, at] = parts[j][width + quarter : width + 2 * quarter, :].astype(jnp.float32)
        at = pl.ds(pl.multiple_of(k * per, 16), per)
        for i in range(width // span):
            proj_ref[at, i * span : (i + 1) * span] = projs[j][i * per : (i + 1) * per, :].astype(
                jnp.float32
            )


def units_out_kernel(place, *refs):
    sets, out_ref = refs[:-1], refs[-1]
    units = sets[0].shape[1]
    for number, part in enumerate(sets):
        at = pl.ds(pl.multiple_of((place[6] ^ UNIT_ORDER[number % 4]) * units, 128), units)
        out_ref[number // 4, :, at] = part[...].astype(jnp.float32)


def quick_body(
    tokens_in,
    norm_gains,
    attn_qkv,
    attn_proj,
    router_rows,
    shared_gate_up,
    shared_down,
    expert_gate_up,
    expert_down,
    routes,
    out_grad,
):
    quad = ("grp", "head")
    line = ("head", "blk")
    blocks = lax.axis_size("blk")
    rows, width = tokens_in.shape
    grp, head, blk = lax.axis_index("grp"), lax.axis_index("head"), lax.axis_index("blk")
    core = blk % 2
    quarter = width // 4
    prompt_dev = max(PROMPT_ROWS, PROMPT_LEAST // (2 * blocks))
    prompt = prompt_dev * 2 * blocks
    cont = 2 * (rows - prompt_dev)
    bf16, f32 = jnp.bfloat16, jnp.float32

    member = 2 * grp + head
    unit_me = 2 * head + grp
    place = jnp.stack([member, core, 2 * blk + head, blk, head, grp, unit_me])
    third = attn_qkv.shape[1]
    few = jnp.concatenate([norm_gains, router_rows], axis=0)
    few = jnp.pad(few, ((0, 20 - few.shape[0]), (0, 0)))
    few = jnp.concatenate([few[5 * i : 5 * i + 5] for i in range(4)], axis=1)
    few = jnp.pad(few, ((0, 11), (0, 0)))
    six = width // 2
    middle = (grp != head).astype(jnp.int32)

    def window(j):
        return (middle ^ head ^ (j & 1)) * (third - six)

    def window_part(j):
        part = lax.dynamic_slice_in_dim(attn_qkv.T, window(j) + core * (six // 2), six // 2, 0)
        return jnp.concatenate([part, few], axis=0)

    own_window = lax.dynamic_slice_in_dim(attn_qkv.T, window(0), six, 0)
    partner_tokens = exchange(tokens_in, "head", 1)
    own_w = [to_member(window_part(j), j) for j in (1, 2, 3)]
    other_w = [exchange(part, "blk", 1) for part in own_w]
    proj_half = lax.dynamic_slice_in_dim(attn_proj.T, core * (quarter // 2), quarter // 2, 0)

    span = SFF // 2 // 4
    four = blk % 4
    down_t = shared_down.T
    piece = jnp.concatenate(
        [
            lax.dynamic_slice_in_dim(shared_gate_up, four * span, span, 1),
            lax.dynamic_slice_in_dim(down_t, four * span, span, 1),
            lax.dynamic_slice_in_dim(down_t, SFF // 2 + four * span, span, 1),
        ],
        axis=0,
    )

    def of_four(values):
        far = exchange(values, "blk", 2)
        return [values, exchange(values, "blk", 1), far, exchange(far, "blk", 1)]

    def sum_of_four(parts):
        near = exchange(jnp.stack([parts[1], parts[3]]), "blk", 1)
        far = (parts[2].astype(f32) + near[1].astype(f32)).astype(bf16)
        return parts[0].astype(f32) + near[0].astype(f32) + exchange(far, "blk", 2).astype(f32)

    def joined(own, part):
        return (own.astype(f32) + part.astype(f32)).astype(bf16)

    units = expert_gate_up.shape[2] // 4
    down_all = expert_down.T

    def unit_part(values, j):
        return lax.dynamic_slice_in_dim(values, (unit_me ^ UNIT_ORDER[j]) * units, units, 1)

    gate_send = [unit_part(expert_gate_up[0], j) for j in range(4)]
    up_send = [unit_part(expert_gate_up[1], j) for j in range(4)]
    down_send = [unit_part(down_all, j) for j in range(4)]

    def fetched(parts, after, *numbers):
        for j in numbers:
            parts[j] = to_member(tie(parts[j], after), j)

    expert_ids = jnp.arange(EXPERTS, dtype=jnp.int32)
    match = (routes[:, :, None] == expert_ids).astype(jnp.int32)
    flat = match.reshape(2 * rows, EXPERTS)
    rank = (jnp.sum(jnp.cumsum(flat, axis=0) * flat, axis=1) - 1).reshape(rows, 2)
    slots_all = 2 * blocks
    target = routes % 2 * blocks + routes // 2
    slots = jnp.where(
        rank < 16,
        rank // 8 * (8 * slots_all) + target * 8 + rank % 8,
        16 * slots_all + target * 4 + rank - 16,
    )
    per_half = 20 * slots_all
    slot_ids = jnp.arange(per_half, dtype=jnp.int32)[:, None]
    pick = ((slot_ids == slots[:, 0]) | (slot_ids == slots[:, 1])).astype(bf16)
    pack_shape = (slots_all, 8, 5 * width // 2)

    def over_line(values):
        return lax.all_to_all(values, line, 0, 0, tiled=True)

    def over_blocks(values):
        return lax.all_to_all(values, "blk", 0, 0, tiled=True)

    grad_sent = kernel_call(
        pack_kernel, [(pack_shape, bf16)], [], "pack_rows", mm(pick, out_grad).astype(bf16)
    )[0]
    grad_own = over_line(grad_sent)
    four_grads = of_four(out_grad)

    wait = lax.optimization_barrier
    own_w, other_w, partner_tokens, gate_send, up_send, down_send, piece, proj_half = wait(
        (own_w, other_w, partner_tokens, gate_send, up_send, down_send, piece, proj_half)
    )
    proj_own = [proj_half] * 4
    shared_parts = [piece] * 4
    steps = np.arange(DH // 2, dtype=np.float32)
    rates = np.power(np.float32(10000.0), np.float32(-2.0) * steps / np.float32(DH))
    angles = np.arange(prompt + cont, dtype=np.float32)[:, None] * rates[None, :].astype(np.float32)
    table = jnp.asarray(
        np.concatenate([np.cos(angles), np.sin(angles)], axis=1).astype(np.float32)
    )
    normed, head_send, gains, router_w, qkv_w = kernel_call(
        qkv_kernel,
        [
            ((2 * rows, width), bf16),
            ((blocks, rows, 6 * DH), bf16),
            ((2, width), f32),
            ((EXPERTS, width), bf16),
            ((3 * six, width), bf16),
        ],
        [((4, six, width), bf16), ((4, 16, width), f32), ((2, rows, width), bf16)],
        "qkv_rows",
        place, tokens_in, partner_tokens, table, own_window, few, *own_w, *other_w,
    )
    fetched(gate_send, own_w[2], 2, 1)
    head_send, gate_send, grad_own = wait((head_send, gate_send, grad_own))
    head_rows = over_blocks(head_send)
    fetched(gate_send, head_send, 3)
    fetched(up_send, head_send, 1, 2)
    head_rows, gate_send, up_send = wait((head_rows, gate_send, up_send))
    attn_heads = attention_forward(head_rows)
    fetched(up_send, head_rows, 3)
    attn_heads, up_send = wait((attn_heads, up_send))
    attn_got = over_blocks(attn_heads)
    all_normed = lax.all_gather(tie(normed, attn_heads), "blk", axis=0)
    fetched(proj_own, attn_heads, 1, 2, 3)
    proj_other = [exchange(part, "blk", 1) for part in proj_own]
    fetched(shared_parts, attn_heads, 1, 2)
    attn_got, proj_own, proj_other = wait((attn_got, proj_own, proj_other))
    head_half = HEADS // 2
    theirs = lax.dynamic_slice_in_dim(attn_got[:head_half], (1 - head) * prompt_dev, prompt_dev, 1)
    attn_partner = exchange(theirs, "head", 1)
    grad_other = exchange(tie(grad_own, attn_got), "grp", 1)
    residual, hidden, attn_tok, sent, proj_w = kernel_call(
        hidden_kernel,
        [
            ((rows, width), f32),
            ((rows, width), bf16),
            ((rows, width), bf16),
            (pack_shape, bf16),
            ((8, quarter // 2, width), bf16),
        ],
        [((2, rows, six), bf16)],
        "hidden_rows",
        place, attn_got, attn_partner, tokens_in, gains, pick, *proj_own, *proj_other,
    )

    sent, shared_parts = wait((sent, shared_parts))
    got_own = over_line(sent)
    shared_parts[3] = exchange(tie(shared_parts[2], sent), "head", 1)
    fetched(down_send, sent, 2)
    four_hidden = of_four(tie(hidden, sent))
    got_own, shared_parts, down_send, four_hidden, grad_other = wait(
        (got_own, shared_parts, down_send, four_hidden, grad_other)
    )
    got_other = exchange(got_own, "grp", 1)
    fetched(down_send, got_own, 1, 3)
    shared_out, shared_back, *shared_given = kernel_call(
        shared_kernel,
        [((4 * rows, width), bf16)] * 2 + [((width + 2 * quarter, span), bf16)] * 4,
        [
            ((width, 4 * span), bf16),
            ((width, 2 * span), bf16),
            ((width, 4 * span), f32),
            ((width, 2 * span), f32),
        ],
        "shared_rows",
        place, *tie(four_hidden, got_own), *four_grads, *shared_parts,
    )
    shared_back = sum_of_four([shared_back[i * rows : (i + 1) * rows] for i in range(4)])

    def quad_once(parts):
        middle = parts[0].shape[0] // 2
        upper, lower = [part[:middle] for part in parts], [part[middle:] for part in parts]
        crossed = exchange(jnp.stack([upper[2], upper[3]]), "grp", 1)
        turned = exchange(jnp.stack([lower[1], lower[3]]), "head", 1)
        return (
            (joined(upper[1], crossed[1]), joined(upper[0], crossed[0])),
            (joined(lower[2], turned[1]), joined(lower[0], turned[0])),
        )

    got_other, shared_given, down_send, all_normed = wait(
        (got_other, shared_given, down_send, all_normed)
    )
    summed_once = quad_once(shared_given)
    count = 2 * per_half
    g_own, g_part, e_own, e_part, egate, eup, e_mid, g_eout, g_router, got_rows = kernel_call(
        expert_kernel,
        [
            ((per_half, width), f32),
            ((per_half, width), bf16),
            ((per_half, width), f32),
            ((per_half, width), bf16),
            ((count, units), bf16),
            ((count, units), bf16),
            ((count, units), bf16),
            ((count, width), bf16),
            ((EXPERTS, width), f32),
            ((count, width), bf16),
        ],
        [((width, units), bf16)] * 3 + [((count, width), bf16)],
        "expert_rows",
        place, got_own, got_other, grad_own, grad_other, router_w,
        *gate_send, *up_send, *down_send,
        room=12,
    )

    def features(left, right):
        whole = mm(left, right, FIRST).astype(bf16)
        return [
            lax.dynamic_slice_in_dim(whole, (member ^ j) * quarter, quarter, 0) for j in range(4)
        ]

    def joined_rows(own, part):
        return kernel_call(join_kernel, [(pack_shape, bf16)], [], "join_rows", own, part)[0]

    gate_out, up_out, down_out = (
        features(got_rows, egate), features(got_rows, eup), features(g_eout, e_mid)
    )
    g_part, summed_once = wait((g_part, summed_once))
    g_other = exchange(g_part, "grp", 1)
    g_joined = joined_rows(g_own, g_other)
    g_back = over_line(g_joined)
    gate_out[2] = to_member(tie(gate_out[2], g_joined), 2)
    crossed, turned = summed_once[0], summed_once[1]
    shared_sum = jnp.concatenate(
        [
            joined(crossed[1], exchange(tie(crossed[0], g_joined), "head", 1)),
            joined(turned[1], exchange(tie(turned[0], g_joined), "grp", 1)),
        ]
    )
    cutting = 576

    def far_sum(values):
        return joined(values, exchange(values, "blk", 4))

    far_one = far_sum(shared_sum[:cutting])

    g_resid, g_branch, grad_mine, grad_theirs, g_second_gain = kernel_call(
        branch_kernel,
        [
            ((rows, width), f32),
            ((rows, width), bf16),
            ((head_half, prompt_dev, 2 * DH), bf16),
            ((head_half, prompt_dev, 2 * DH), bf16),
            ((1, width), f32),
        ],
        [((per_half, width), bf16), ((2, head_half, prompt_dev, 2 * DH), bf16)],
        "branch_rows",
        place, g_back, pick, shared_back, residual, gains, out_grad, proj_w,
    )
    grad_theirs = exchange(grad_theirs, "head", 1)
    grad_theirs, far_one, gate_out[2] = wait((grad_theirs, far_one, gate_out[2]))
    grad_send = jnp.where(
        head == 0,
        jnp.concatenate([grad_mine, grad_theirs], axis=1),
        jnp.concatenate([grad_theirs, grad_mine], axis=1),
    )
    grad_send = jnp.pad(grad_send, ((0, blocks - head_half), (0, 0), (0, 0)))
    grad_heads = over_blocks(grad_send)
    fetched(gate_out, grad_send, 1, 3)
    g_head_rows = attention_backward(head_rows, grad_heads, table)
    far_two = far_sum(tie(shared_sum[cutting:], grad_heads))
    fetched(up_out, grad_heads, 2, 1)
    g_got = over_blocks(g_head_rows)
    e_other = exchange(tie(e_part, g_head_rows), "grp", 1)
    fetched(up_out, g_head_rows, 3)
    g_proj = mm(g_branch, attn_tok, FIRST).astype(bf16).reshape(4, 4, quarter // 4, width)
    g_proj = sum_of_four(
        [
            lax.dynamic_index_in_dim(
                tie(g_proj, grad_heads), four ^ j, 1, keepdims=False
            ).reshape(quarter, width)
            for j in range(4)
        ]
    )
    g_proj = g_proj.astype(bf16)
    g_got, e_other, gate_out, g_proj = wait((g_got, e_other, gate_out, g_proj))
    g_normed, g_normed_theirs, g_first_gain = kernel_call(
        tokens_kernel,
        [((rows, width), f32), ((rows, width), bf16), ((1, width), f32)],
        [((2 * rows, 3 * six), bf16), ((2, rows, width), f32)],
        "token_parts",
        place, g_got, qkv_w, tokens_in, partner_tokens,
    )
    g_normed_theirs = exchange(g_normed_theirs, "head", 1)
    e_back = over_line(joined_rows(e_own, e_other))

    head_w = kernel_call(
        head_weight_kernel,
        [((3 * DH, width), bf16)],
        [((2 * rows * blocks, 3 * DH), bf16)],
        "head_weights",
        tie(g_head_rows, g_first_gain), all_normed,
    )[0].reshape(3, DH, width)

    def chunk_pair(side):
        kept_kind = 2 * side
        given_kind = jnp.where(head == 0, 1 + side, side)
        return jnp.stack([head_w[kept_kind], head_w[given_kind]])

    few = jnp.concatenate([g_first_gain, g_second_gain, g_router], axis=0)
    few = jnp.pad(few, ((0, FEW - few.shape[0]), (0, 0))).astype(bf16)
    own_pair = jnp.concatenate([*jnp.where(grp == 0, chunk_pair(0), chunk_pair(1)), few])
    other_pair = jnp.concatenate([*jnp.where(grp == 0, chunk_pair(1), chunk_pair(0)), few])
    own_pair = joined(own_pair, exchange(other_pair, "grp", 1))
    from_head = exchange(own_pair[DH:], "head", 1)
    own_pair = jnp.concatenate(
        [own_pair[:DH], from_head[:DH], joined(own_pair[2 * DH :], from_head[DH:])]
    )
    all_pairs = lax.all_gather(own_pair, "blk", axis=0)
    order = jnp.array(
        [
            [0, 2, 4, 6, 8, 10, 1, 3, 5],
            [6, 8, 10, 1, 3, 5, 7, 9, 11],
            [1, 3, 5, 7, 9, 11, 0, 2, 4],
            [7, 9, 11, 0, 2, 4, 6, 8, 10],
        ],
        jnp.int32,
    )[member]
    grad_qkv, few = kernel_call(
        chunk_kernel,
        [((third, width), f32), ((FEW, width), f32)],
        [],
        "chunk_rows",
        order, all_pairs,
    )
    grad_qkv = grad_qkv.T

    g_proj = g_proj.reshape(4, quarter // 4, width)
    proj_out = []
    for j in range(4):
        part = lax.dynamic_index_in_dim(g_proj, member ^ j, 0, keepdims=False)
        proj_out.append(
            jnp.concatenate([part[:, i * span : (i + 1) * span] for i in range(width // span)])
        )
    fetched(proj_out, g_normed, 1, 2, 3)
    proj_sum = sum(part.astype(f32) for part in proj_out).astype(bf16)
    grad_tokens = kernel_call(
        tokens_out_kernel,
        [((rows, width), f32)],
        [],
        "token_grads",
        g_normed, g_normed_theirs, tokens_in, gains, g_resid,
    )[0]
    four_shared = of_four(tie(jnp.concatenate([far_one, far_two]), g_normed))
    few = lax.dynamic_slice_in_dim(few, member * quarter, quarter, 1)
    shared_out = sum_of_four(
        [tie(shared_out, g_got)[i * rows : (i + 1) * rows] for i in range(4)]
    )
    fetched(down_out, from_head, 1, 2, 3)
    four_proj = of_four(far_sum(tie(proj_sum, g_normed)))
    layer_out = kernel_call(
        layer_kernel,
        [((rows, width), bf16)],
        [((per_half, width), bf16)],
        "layer_rows",
        e_back, pick, residual, shared_out,
    )[0]
    grad_expert_w = kernel_call(
        units_out_kernel,
        [((2, quarter, 4 * units), f32)],
        [],
        "units_out",
        place, *gate_out, *up_out,
    )[0]
    grad_expert_out = kernel_call(
        units_out_kernel, [((1, quarter, 4 * units), f32)], [], "down_out", place, *down_out
    )[0][0].T
    grad_shared_w, grad_shared_out, grad_proj = kernel_call(
        shared_out_kernel,
        [((width, 4 * span), f32), ((quarter, SFF), f32), ((quarter, width), f32)],
        [],
        "shared_grads",
        place, *four_shared, *four_proj,
    )
    grad_shared_out, grad_proj = grad_shared_out.T, grad_proj.T
    return (
        layer_out,
        grad_tokens,
        few[0:2],
        grad_qkv,
        grad_proj,
        few[2 : 2 + EXPERTS],
        grad_shared_w,
        grad_shared_out,
        grad_expert_w,
        grad_expert_out,
    )


def solution(mesh):
    whole = P(("grp", "head", "blk"), None)
    split = P(None, ("grp", "head"))
    sizes = dict(mesh.shape)
    quick = sizes["grp"] == 2 and sizes["head"] == 2 and sizes["blk"] == 8
    return jax.shard_map(
        quick_body if quick else body,
        mesh=mesh,
        in_specs=(
            whole, split, split, split, split, split, split,
            P(None, ("grp", "head"), "blk"), P("blk", ("grp", "head")), whole, whole,
        ),
        out_specs=(
            whole, whole, split, split, split, split, split, split,
            P(None, ("grp", "head"), "blk"), P("blk", ("grp", "head")),
        ),
        check_vma=False,
    )
```

```python
import math

import jax
import jax.numpy as jnp
import numpy as np
from jax import lax
from jax.experimental import pallas as pl
from jax.experimental.pallas import tpu as pltpu
from jax.sharding import PartitionSpec as P

HEADS = 12
DH = 64
EXPERTS = 16
FF = 2048
SFF = 2048
PROMPT_ROWS = 64
PROMPT_LEAST = 1024


EPSILON = 1e-06
NEGATIVE = -1e30


def norm_rows(values, gain):
    inverse = lax.rsqrt(jnp.mean(values * values, axis=-1, keepdims=True) + EPSILON)
    return (values * inverse * gain, inverse)


def norm_back(values, inverse, gain, upstream):
    scaled = upstream * gain
    inner_mean = jnp.mean(scaled * values, axis=-1, keepdims=True)
    return (
        inverse * scaled - values * inverse**3 * inner_mean,
        jnp.sum(upstream * values * inverse, axis=0),
    )


def angle_tables(positions):
    step_index = jnp.arange(DH // 2, dtype=jnp.float32)
    freq_rates = 10000.0 ** (-2.0 * step_index / DH)
    angles = positions.astype(jnp.float32)[:, None] * freq_rates[None, :]
    return (jnp.cos(angles)[:, None, :], jnp.sin(angles)[:, None, :])


def rotate(values, cosine, sine_table):
    half_size = values.shape[-1] // 2
    first_half = values[..., :half_size]
    second = values[..., half_size:]
    return jnp.concatenate(
        [first_half * cosine - second * sine_table, second * cosine + first_half * sine_table],
        axis=-1,
    )


def swish_parts(gate_value):
    sigmoid = jax.nn.sigmoid(gate_value)
    return (gate_value * sigmoid, sigmoid * (1.0 + gate_value * (1.0 - sigmoid)))


def row_layout(head_part, within, block_index, heads_axis, blocks_axis, row_count, prompt_dev):
    prompt_all = prompt_dev * heads_axis * blocks_axis
    is_prompt = within < prompt_dev
    prompt_index = (block_index * heads_axis + head_part) * prompt_dev + within
    cont_index = head_part * (row_count - prompt_dev) + within - prompt_dev
    positions = jnp.where(is_prompt, prompt_index, prompt_all + cont_index)
    return (is_prompt, prompt_index, cont_index, positions)


def fetch_weights(
    norm_gains,
    attn_qkv,
    attn_proj,
    router_rows,
    shared_gate_up,
    shared_down,
    expert_gate_up,
    expert_down,
):
    return (
        lax.all_gather(norm_gains, ("grp", "head"), axis=1, tiled=True),
        lax.all_gather(attn_qkv, ("grp", "head"), axis=1, tiled=True),
        lax.all_gather(attn_proj, ("grp", "head"), axis=1, tiled=True),
        lax.all_gather(router_rows, ("grp", "head"), axis=1, tiled=True),
        lax.all_gather(shared_gate_up, ("grp", "head"), axis=1, tiled=True),
        lax.all_gather(shared_down, ("grp", "head"), axis=1, tiled=True),
        lax.all_gather(expert_gate_up, ("grp", "head"), axis=1, tiled=True),
        lax.all_gather(expert_down, ("grp", "head"), axis=1, tiled=True),
    )


def masked_scores(queries, key_rows, visible):
    scores = jnp.einsum(
        "qhd,khd->hqk", queries, key_rows, preferred_element_type=jnp.float32
    ) * DH ** (-0.5)
    return jnp.where(visible[None], scores, NEGATIVE)


def add_stats(carry, scores, visible):
    row_peak, row_total = carry
    new_peak = jnp.maximum(row_peak, jnp.max(scores, axis=-1))
    terms = jnp.where(visible[None], jnp.exp(scores - new_peak[:, :, None]), 0.0)
    return (new_peak, row_total * jnp.exp(row_peak - new_peak) + jnp.sum(terms, axis=-1))


def block_probs(scores, visible, log_total):
    return jnp.where(visible[None], jnp.exp(scores - log_total[:, :, None]), 0.0)


def grad_block(queries, grad_out, log_total, delta, key_rows, value_rows, visible):
    scale_factor = DH ** (-0.5)
    soft_weights = block_probs(masked_scores(queries, key_rows, visible), visible, log_total)
    grad_weights = jnp.einsum(
        "qhd,khd->hqk", grad_out, value_rows, preferred_element_type=jnp.float32
    )
    grad_scores = (soft_weights * (grad_weights - delta[:, :, None])).astype(jnp.bfloat16)
    grad_query = (
        jnp.einsum("hqk,khd->qhd", grad_scores, key_rows, preferred_element_type=jnp.float32)
        * scale_factor
    )
    grad_key = (
        jnp.einsum("hqk,qhd->khd", grad_scores, queries, preferred_element_type=jnp.float32)
        * scale_factor
    )
    grad_value = jnp.einsum(
        "hqk,qhd->khd",
        soft_weights.astype(jnp.bfloat16),
        grad_out,
        preferred_element_type=jnp.float32,
    )
    return (grad_query, grad_key, grad_value)


def body(
    tokens_in,
    norm_gains,
    attn_qkv,
    attn_proj,
    router_rows,
    shared_gate_up,
    shared_down,
    expert_gate_up,
    expert_down,
    routes,
    out_grad,
):
    heads_axis = lax.axis_size("head")
    blocks_axis = lax.axis_size("blk")
    row_count = tokens_in.shape[0]
    width_all = tokens_in.shape[1]
    prompt_dev = max(PROMPT_ROWS, PROMPT_LEAST // (heads_axis * blocks_axis))
    prompt_all = prompt_dev * heads_axis * blocks_axis
    local_heads = HEADS // heads_axis
    query_rows = heads_axis * row_count
    key_block = min(512, prompt_all)
    block_count = prompt_all // key_block
    head_me = lax.axis_index("head")
    block_me = lax.axis_index("blk")
    gain_rows, qkv_w, proj_w, router_w, shared_w, shared_out_w, expert_w, expert_out_w = (
        fetch_weights(
            norm_gains,
            attn_qkv,
            attn_proj,
            router_rows,
            shared_gate_up,
            shared_down,
            expert_gate_up,
            expert_down,
        )
    )
    tokens = tokens_in.astype(jnp.float32)
    first_gain = gain_rows[0].astype(jnp.float32)
    second_gain = gain_rows[1].astype(jnp.float32)
    normed_f, first_inverse = norm_rows(tokens, first_gain)
    normed = normed_f.astype(jnp.bfloat16)
    mixed_qkv = jnp.dot(normed, qkv_w, preferred_element_type=jnp.float32)
    token_row = jnp.arange(row_count, dtype=jnp.int32)
    token_pos = row_layout(
        head_me, token_row, block_me, heads_axis, blocks_axis, row_count, prompt_dev
    )[3]
    token_cos, token_sin = angle_tables(token_pos)
    query_tok = (
        rotate(mixed_qkv[:, :width_all].reshape(row_count, HEADS, DH), token_cos, token_sin)
        .reshape(row_count, width_all)
        .astype(jnp.bfloat16)
    )
    key_tok = (
        rotate(
            mixed_qkv[:, width_all : 2 * width_all].reshape(row_count, HEADS, DH),
            token_cos,
            token_sin,
        )
        .reshape(row_count, width_all)
        .astype(jnp.bfloat16)
    )
    value_tok = mixed_qkv[:, 2 * width_all :].astype(jnp.bfloat16)
    query_head, key_head, value_head = (
        lax.all_to_all(query_tok, "head", split_axis=1, concat_axis=0, tiled=True),
        lax.all_to_all(key_tok, "head", split_axis=1, concat_axis=0, tiled=True),
        lax.all_to_all(value_tok, "head", split_axis=1, concat_axis=0, tiled=True),
    )
    local_index = jnp.arange(query_rows, dtype=jnp.int32)
    is_prompt, prompt_index, cont_index, head_pos = row_layout(
        local_index // row_count,
        local_index % row_count,
        block_me,
        heads_axis,
        blocks_axis,
        row_count,
        prompt_dev,
    )
    is_cont = jnp.logical_not(is_prompt)
    local_visible = (
        is_cont[:, None] & is_cont[None, :] & (cont_index[None, :] <= cont_index[:, None])
    )
    queries = query_head.reshape(query_rows, local_heads, DH)
    key_local = key_head.reshape(query_rows, local_heads, DH)
    value_local = value_head.reshape(query_rows, local_heads, DH)
    prompt_keys, prompt_values = (
        lax.all_gather(
            key_head.reshape(heads_axis, row_count, -1)[:, :prompt_dev].reshape(
                heads_axis * prompt_dev, -1
            ),
            "blk",
            axis=0,
            tiled=True,
        ),
        lax.all_gather(
            value_head.reshape(heads_axis, row_count, -1)[:, :prompt_dev].reshape(
                heads_axis * prompt_dev, -1
            ),
            "blk",
            axis=0,
            tiled=True,
        ),
    )
    key_blocks = prompt_keys.reshape(block_count, key_block, local_heads, DH)
    value_blocks = prompt_values.reshape(block_count, key_block, local_heads, DH)
    block_starts = jnp.arange(block_count, dtype=jnp.int32) * key_block
    key_offsets = jnp.arange(key_block, dtype=jnp.int32)

    def prompt_visible(start):
        return is_cont[:, None] | (start + key_offsets[None, :] <= prompt_index[:, None])

    def stats_step(carry, member):
        visible = prompt_visible(member[1])
        return (add_stats(carry, masked_scores(queries, member[0], visible), visible), None)

    start_stats = (
        jnp.full((local_heads, query_rows), NEGATIVE, jnp.float32),
        jnp.zeros((local_heads, query_rows), jnp.float32),
    )
    stats = lax.scan(stats_step, start_stats, (key_blocks, block_starts))[0]
    row_peak, row_total = add_stats(
        stats, masked_scores(queries, key_local, local_visible), local_visible
    )
    log_total = row_peak + jnp.log(row_total)

    def output_step(total_out, member):
        visible = prompt_visible(member[2])
        soft_weights = block_probs(
            masked_scores(queries, member[0], visible), visible, log_total
        ).astype(jnp.bfloat16)
        return (
            total_out
            + jnp.einsum(
                "hqk,khd->qhd", soft_weights, member[1], preferred_element_type=jnp.float32
            ),
            None,
        )

    attn_heads = lax.scan(
        output_step,
        jnp.zeros((query_rows, local_heads, DH), jnp.float32),
        (key_blocks, value_blocks, block_starts),
    )[0]
    local_weights = block_probs(
        masked_scores(queries, key_local, local_visible), local_visible, log_total
    ).astype(jnp.bfloat16)
    attn_heads = attn_heads + jnp.einsum(
        "hqk,khd->qhd", local_weights, value_local, preferred_element_type=jnp.float32
    )
    attn_tok = lax.all_to_all(
        attn_heads.reshape(query_rows, -1).astype(jnp.bfloat16),
        "head",
        split_axis=0,
        concat_axis=1,
        tiled=True,
    )
    residual = tokens + jnp.dot(attn_tok, proj_w, preferred_element_type=jnp.float32)
    hidden_f, second_inverse = norm_rows(residual, second_gain)
    hidden = hidden_f.astype(jnp.bfloat16)
    logits = jnp.einsum("td,ed->te", hidden, router_w, preferred_element_type=jnp.float32)
    soft_route = jax.nn.softmax(logits, axis=-1)
    expert_ids = jnp.arange(EXPERTS, dtype=jnp.int32)
    route_match = routes[:, :, None] == expert_ids[None, None, :]
    gate_values = jnp.sum(jnp.where(route_match, soft_route[:, None, :], 0.0), axis=-1)
    shared_pre = jnp.dot(hidden, shared_w, preferred_element_type=jnp.float32)
    shared_act, shared_slope = swish_parts(shared_pre[:, :SFF])
    shared_up = shared_pre[:, SFF:]
    shared_mid = (shared_act * shared_up).astype(jnp.bfloat16)
    shared_out = jnp.dot(shared_mid, shared_out_w, preferred_element_type=jnp.float32)
    unit_count = expert_w.shape[2]
    per_device = max(1, unit_count // FF)
    spread = max(1, FF // unit_count)
    unit_width = unit_count // per_device
    capacity = max(2, 5 * row_count // (2 * EXPERTS))
    slot_count = blocks_axis * per_device * capacity
    pair_expert = routes.reshape(-1)
    pair_match = route_match.reshape(2 * row_count, EXPERTS).astype(jnp.int32)
    pair_rank = jnp.sum(jnp.cumsum(pair_match, axis=0) * pair_match, axis=1) - 1
    slot_base = (
        pair_expert // per_device * spread * per_device * capacity
        + pair_expert % per_device * capacity
        + pair_rank
    )
    slot_index = (
        slot_base[None, :] + (jnp.arange(spread, dtype=jnp.int32) * per_device * capacity)[:, None]
    )
    pair_ids = jnp.arange(2 * row_count, dtype=jnp.int32)
    slot_pair = (
        jnp.full((slot_count,), 2 * row_count, jnp.int32)
        .at[slot_index.reshape(-1)]
        .set(jnp.tile(pair_ids, spread))
    )
    slot_token = slot_pair // 2
    hidden_pad = jnp.concatenate([hidden, jnp.zeros((1, width_all), jnp.bfloat16)], axis=0)
    send_rows = hidden_pad[slot_token].reshape(blocks_axis, per_device, capacity, width_all)
    received_rows = lax.all_to_all(send_rows, "blk", split_axis=0, concat_axis=0, tiled=True)
    gate_weight = expert_w[0].reshape(width_all, per_device, unit_width)
    up_weight = expert_w[1].reshape(width_all, per_device, unit_width)
    down_w = expert_out_w.reshape(per_device, unit_width, width_all)
    expert_gate = jnp.einsum(
        "tfoa,afw->tfow", received_rows, gate_weight, preferred_element_type=jnp.float32
    )
    expert_up_projection = jnp.einsum(
        "tfoa,afw->tfow", received_rows, up_weight, preferred_element_type=jnp.float32
    )
    expert_activation, expert_slope = swish_parts(expert_gate)
    expert_mid = (expert_activation * expert_up_projection).astype(jnp.bfloat16)
    expert_part = jnp.einsum(
        "secm,emd->secd", expert_mid, down_w, preferred_element_type=jnp.float32
    )
    returned = (
        lax.all_to_all(
            expert_part.astype(jnp.bfloat16), "blk", split_axis=0, concat_axis=0, tiled=True
        )
        .astype(expert_part.dtype)
        .reshape(slot_count, width_all)
    )
    pair_out = jnp.sum(returned[slot_index], axis=0).reshape(row_count, 2, width_all)
    expert_sum = jnp.sum(gate_values[:, :, None] * pair_out, axis=1)
    layer_out = (residual + shared_out + expert_sum).astype(jnp.bfloat16)
    gain_rows, qkv_w, proj_w, router_w, shared_w, shared_out_w, expert_w, expert_out_w = (
        fetch_weights(
            norm_gains,
            attn_qkv,
            attn_proj,
            router_rows,
            shared_gate_up,
            shared_down,
            expert_gate_up,
            expert_down,
        )
    )
    gate_weight = expert_w[0].reshape(width_all, per_device, unit_width)
    up_weight = expert_w[1].reshape(width_all, per_device, unit_width)
    down_w = expert_out_w.reshape(per_device, unit_width, width_all)
    grad_layer = out_grad.astype(jnp.float32)
    grad_smid = jnp.einsum("td,fd->tf", out_grad, shared_out_w, preferred_element_type=jnp.float32)
    shared_grads = jnp.concatenate(
        [grad_smid * shared_up * shared_slope, grad_smid * shared_act], axis=1
    ).astype(jnp.bfloat16)
    grad_hidden = jnp.einsum(
        "tf,df->td", shared_grads, shared_w, preferred_element_type=jnp.float32
    )
    grad_shared_w = jnp.einsum(
        "td,tf->df", hidden, shared_grads, preferred_element_type=jnp.float32
    )
    grad_shared_out = jnp.einsum(
        "tf,td->fd", shared_mid, out_grad, preferred_element_type=jnp.float32
    )
    grad_gates = jnp.sum(grad_layer[:, None, :] * pair_out, axis=-1)
    grad_pairs = (
        (gate_values[:, :, None] * grad_layer[:, None, :])
        .reshape(2 * row_count, width_all)
        .astype(jnp.bfloat16)
    )
    grad_pad = jnp.concatenate([grad_pairs, jnp.zeros((1, width_all), jnp.bfloat16)], axis=0)
    grad_recv = lax.all_to_all(
        grad_pad[slot_pair].reshape(blocks_axis, per_device, capacity, width_all),
        "blk",
        split_axis=0,
        concat_axis=0,
        tiled=True,
    )
    grad_expert_middle = jnp.einsum(
        "secd,emd->secm", grad_recv, down_w, preferred_element_type=jnp.float32
    )
    grad_expert_gate_branch = (grad_expert_middle * expert_up_projection * expert_slope).astype(
        jnp.bfloat16
    )
    grad_expert_up_branch = (grad_expert_middle * expert_activation).astype(jnp.bfloat16)
    grad_rows = jnp.einsum(
        "auwj,buj->auwb", grad_expert_gate_branch, gate_weight, preferred_element_type=jnp.float32
    ) + jnp.einsum(
        "auwj,buj->auwb", grad_expert_up_branch, up_weight, preferred_element_type=jnp.float32
    )
    grad_expert_w = jnp.stack(
        [
            jnp.einsum(
                "jgki,jgkt->igt",
                received_rows,
                grad_expert_gate_branch,
                preferred_element_type=jnp.float32,
            ).reshape(width_all, unit_count),
            jnp.einsum(
                "jgki,jgkt->igt",
                received_rows,
                grad_expert_up_branch,
                preferred_element_type=jnp.float32,
            ).reshape(width_all, unit_count),
        ]
    )
    grad_expert_out = jnp.einsum(
        "secm,secd->emd", expert_mid, grad_recv, preferred_element_type=jnp.float32
    ).reshape(unit_count, width_all)
    grad_back = (
        lax.all_to_all(
            grad_rows.astype(jnp.bfloat16), "blk", split_axis=0, concat_axis=0, tiled=True
        )
        .astype(grad_rows.dtype)
        .reshape(slot_count, width_all)
    )
    grad_hidden = grad_hidden + jnp.sum(
        jnp.sum(grad_back[slot_index], axis=0).reshape(row_count, 2, width_all), axis=1
    )
    grad_soft = jnp.sum(jnp.where(route_match, grad_gates[:, :, None], 0.0), axis=1)
    grad_logits = (
        soft_route * (grad_soft - jnp.sum(soft_route * grad_soft, axis=-1, keepdims=True))
    ).astype(jnp.bfloat16)
    grad_hidden = grad_hidden + jnp.einsum(
        "te,ed->td", grad_logits, router_w, preferred_element_type=jnp.float32
    )
    grad_router = jnp.einsum("te,td->ed", grad_logits, hidden, preferred_element_type=jnp.float32)
    grad_norm_two, grad_second_gain = norm_back(residual, second_inverse, second_gain, grad_hidden)
    grad_resid = grad_layer + grad_norm_two
    grad_branch = grad_resid.astype(jnp.bfloat16)
    grad_proj = jnp.einsum("td,te->de", attn_tok, grad_branch, preferred_element_type=jnp.float32)
    grad_attn_tok = jnp.einsum(
        "te,de->td", grad_branch, proj_w, preferred_element_type=jnp.float32
    ).astype(jnp.bfloat16)
    grad_heads = lax.all_to_all(
        grad_attn_tok, "head", split_axis=1, concat_axis=0, tiled=True
    ).reshape(query_rows, local_heads, DH)
    delta = jnp.transpose(jnp.sum(grad_heads * attn_heads, axis=-1))

    def back_step(grad_acc, member):
        visible = prompt_visible(member[2])
        step_query, step_key, step_value = grad_block(
            queries, grad_heads, log_total, delta, member[0], member[1], visible
        )
        return (grad_acc + step_query, (step_key, step_value))

    grad_query, prompt_grads = lax.scan(
        back_step,
        jnp.zeros((query_rows, local_heads, DH), jnp.float32),
        (key_blocks, value_blocks, block_starts),
    )
    local_query, local_key, local_value = grad_block(
        queries, grad_heads, log_total, delta, key_local, value_local, local_visible
    )
    grad_query = grad_query + local_query
    key_share, value_share = (
        lax.psum_scatter(
            prompt_grads[0].reshape(prompt_all, -1), "blk", scatter_dimension=0, tiled=True
        ),
        lax.psum_scatter(
            prompt_grads[1].reshape(prompt_all, -1), "blk", scatter_dimension=0, tiled=True
        ),
    )
    grad_key = (
        local_key.reshape(heads_axis, row_count, -1)
        .at[:, :prompt_dev]
        .add(key_share.reshape(heads_axis, prompt_dev, -1))
        .reshape(query_rows, local_heads, DH)
    )
    grad_value = (
        local_value.reshape(heads_axis, row_count, -1)
        .at[:, :prompt_dev]
        .add(value_share.reshape(heads_axis, prompt_dev, -1))
    )
    head_cos, head_sin = angle_tables(head_pos)
    grad_query = (
        rotate(grad_query, head_cos, -head_sin).reshape(query_rows, -1).astype(jnp.bfloat16)
    )
    grad_key = rotate(grad_key, head_cos, -head_sin).reshape(query_rows, -1).astype(jnp.bfloat16)
    grad_value = grad_value.reshape(query_rows, -1).astype(jnp.bfloat16)
    grad_q_tok, grad_k_tok, grad_v_tok = (
        lax.all_to_all(grad_query, "head", split_axis=0, concat_axis=1, tiled=True),
        lax.all_to_all(grad_key, "head", split_axis=0, concat_axis=1, tiled=True),
        lax.all_to_all(grad_value, "head", split_axis=0, concat_axis=1, tiled=True),
    )
    grad_qkv_rows = jnp.concatenate([grad_q_tok, grad_k_tok, grad_v_tok], axis=1)
    grad_normed = jnp.einsum("tf,df->td", grad_qkv_rows, qkv_w, preferred_element_type=jnp.float32)
    grad_qkv = jnp.einsum("td,tf->df", normed, grad_qkv_rows, preferred_element_type=jnp.float32)
    grad_norm_one, grad_first_gain = norm_back(tokens, first_inverse, first_gain, grad_normed)
    grad_tokens = grad_resid + grad_norm_one
    owned = (
        lax.psum_scatter(
            jnp.stack([grad_first_gain, grad_second_gain]).astype(jnp.bfloat16),
            ("grp", "head"),
            scatter_dimension=1,
            tiled=True,
        ).astype(jnp.float32),
        lax.psum_scatter(
            grad_qkv.astype(jnp.bfloat16), ("grp", "head"), scatter_dimension=1, tiled=True
        ).astype(jnp.float32),
        lax.psum_scatter(
            grad_proj.astype(jnp.bfloat16), ("grp", "head"), scatter_dimension=1, tiled=True
        ).astype(jnp.float32),
        lax.psum_scatter(
            grad_router.astype(jnp.bfloat16), ("grp", "head"), scatter_dimension=1, tiled=True
        ).astype(jnp.float32),
        lax.psum_scatter(
            grad_shared_w.astype(jnp.bfloat16), ("grp", "head"), scatter_dimension=1, tiled=True
        ).astype(jnp.float32),
        lax.psum_scatter(
            grad_shared_out.astype(jnp.bfloat16), ("grp", "head"), scatter_dimension=1, tiled=True
        ).astype(jnp.float32),
        lax.psum_scatter(
            grad_expert_w.astype(jnp.bfloat16), ("grp", "head"), scatter_dimension=1, tiled=True
        ).astype(jnp.float32),
        lax.psum_scatter(
            grad_expert_out.astype(jnp.bfloat16), ("grp", "head"), scatter_dimension=1, tiled=True
        ).astype(jnp.float32),
    )
    summed = lax.psum((owned[0], owned[1], owned[2], owned[3], owned[4], owned[5]), "blk")
    return (
        layer_out,
        grad_tokens,
        summed[0],
        summed[1],
        summed[2],
        summed[3],
        summed[4],
        summed[5],
        owned[6],
        owned[7],
    )


TRANSPOSED = (((1,), (1,)), ((), ()))
PLAIN = (((1,), (0,)), ((), ()))
FIRST = (((0,), (0,)), ((), ()))
FORWARD_VMEM = 14 * 1024 * 1024
BACKWARD_VMEM = 24 * 1024 * 1024
FEW = 32
UNIT_ORDER = (0, 2, 1, 3)


def mm(left, right, dims=PLAIN):
    return lax.dot_general(left, right, dims, preferred_element_type=jnp.float32)


def assemble(rows_ref, cut, parts, prompt_to, cont_to):
    blocks, half = rows_ref.shape[0], rows_ref.shape[1] // 2
    for block in range(blocks):
        for head_part in range(2):
            piece = rows_ref[block, head_part * half : (head_part + 1) * half, :]
            place = (block * 2 + head_part) * half
            for order in range(parts):
                prompt_to[order][place : place + half, :] = piece[
                    :, order * cut : (order + 1) * cut
                ]
                cont_to[order][place : place + half, :] = piece[
                    :, (parts + order) * cut : (parts + order + 1) * cut
                ]


def spread_out(target, prompt_parts, cont_parts, cut):
    blocks, half = target.shape[0], target.shape[1] // 2
    for block in range(blocks):
        for head_part in range(2):
            place = (block * 2 + head_part) * half
            pieces = [part[place : place + half, :] for part in prompt_parts]
            pieces += [part[place : place + half, :] for part in cont_parts]
            target[block, head_part * half : (head_part + 1) * half, :] = jnp.concatenate(
                pieces, axis=1
            ).astype(target.dtype)


def causal_mask(rows):
    keys = lax.broadcasted_iota(jnp.int32, (rows, rows), 0)
    query = lax.broadcasted_iota(jnp.int32, (rows, rows), 1)
    return keys <= query


def cont_mask(rows, cont):
    keys = lax.broadcasted_iota(jnp.int32, (rows, rows), 0)
    query = lax.broadcasted_iota(jnp.int32, (rows, rows), 1)
    return (keys // cont == query // cont) & (keys <= query)


def masked_block(keys, queries, mask):
    scores = mm(keys, queries, TRANSPOSED) * DH ** (-0.5)
    if mask is None:
        return scores
    return jnp.where(mask, scores, NEGATIVE)


def attention_kernel(rows_ref, out_ref, qp, kp, vp, qc, kc, vc, op, oc):
    block = 256
    prompt = qp.shape[0]
    assemble(rows_ref, DH, 3, (qp, kp, vp), (qc, kc, vc))
    cont = rows_ref.shape[1]
    for is_cont in range(2):
        source_q, source_k, source_v, result = (
            (qc, kc, vc, oc) if is_cont else (qp, kp, vp, op)
        )
        mask = cont_mask(block, cont) if is_cont else causal_mask(block)
        for step in range(prompt // block):
            rows = slice(step * block, (step + 1) * block)
            queries = source_q[rows, :]
            own = masked_block(source_k[rows, :], queries, mask)
            seen = prompt if is_cont else step * block
            peak = jnp.max(own, axis=0, keepdims=True)
            if seen:
                past = masked_block(kp[0:seen, :], queries, None)
                peak = jnp.maximum(peak, jnp.max(past, axis=0, keepdims=True))
            own = jnp.exp(own - peak)
            total = jnp.sum(own, axis=0, keepdims=True)
            gathered = mm(source_v[rows, :], own.astype(jnp.bfloat16), FIRST)
            if seen:
                past = jnp.exp(past - peak)
                total = total + jnp.sum(past, axis=0, keepdims=True)
                gathered = gathered + mm(vp[0:seen, :], past.astype(jnp.bfloat16), FIRST)
            result[rows, :] = jnp.transpose(gathered / total)
    spread_out(out_ref, (op,), (oc,), DH)


def attention_forward(rows):
    blocks, both, _ = rows.shape
    prompt = blocks * both
    small = pltpu.VMEM((prompt, DH), jnp.bfloat16)
    wide = pltpu.VMEM((prompt, DH), jnp.float32)
    return pl.pallas_call(
        attention_kernel,
        out_shape=jax.ShapeDtypeStruct((blocks, both, 2 * DH), jnp.bfloat16),
        in_specs=[pl.BlockSpec(memory_space=pltpu.VMEM)],
        out_specs=pl.BlockSpec(memory_space=pltpu.VMEM),
        scratch_shapes=[small] * 6 + [wide] * 2,
        compiler_params=pltpu.CompilerParams(vmem_limit_bytes=FORWARD_VMEM),
        cost_estimate=pl.CostEstimate(
            flops=2**20, bytes_accessed=2**16, transcendentals=0
        ),
        name="attention_forward",
    )(rows)


def turn_back(values, cosine, sine):
    half = DH // 2
    first, second = values[:, :half], values[:, half:]
    return jnp.concatenate(
        [first * cosine + second * sine, second * cosine - first * sine], axis=1
    )


def attention_back_kernel(
    rows_ref, grad_ref, table_ref, out_ref,
    qp, kp, vp, qc, kc, vc, gp, gc, dqp, dkp, dvp, dqc, dkc, dvc,
):
    block = 256
    prompt = qp.shape[0]
    scale = DH ** (-0.5)
    assemble(rows_ref, DH, 3, (qp, kp, vp), (qc, kc, vc))
    assemble(grad_ref, DH, 1, (gp,), (gc,))
    cont = rows_ref.shape[1]
    dkp[...] = jnp.zeros_like(dkp)
    dvp[...] = jnp.zeros_like(dvp)
    for is_cont in range(2):
        source_q, source_k, source_v, source_g = (
            (qc, kc, vc, gc) if is_cont else (qp, kp, vp, gp)
        )
        to_q, to_k, to_v = (dqc, dkc, dvc) if is_cont else (dqp, dkp, dvp)
        mask = cont_mask(block, cont) if is_cont else causal_mask(block)
        for step in range(prompt // block):
            rows = slice(step * block, (step + 1) * block)
            queries = source_q[rows, :]
            grads = source_g[rows, :]
            own_keys = source_k[rows, :]
            own = masked_block(own_keys, queries, mask)
            seen = prompt if is_cont else step * block
            peak = jnp.max(own, axis=0, keepdims=True)
            if seen:
                past = masked_block(kp[0:seen, :], queries, None)
                peak = jnp.maximum(peak, jnp.max(past, axis=0, keepdims=True))
            own = jnp.exp(own - peak)
            total = jnp.sum(own, axis=0, keepdims=True)
            if seen:
                past = jnp.exp(past - peak)
                total = total + jnp.sum(past, axis=0, keepdims=True)
            inverse = 1.0 / total
            own = own * inverse
            own_grad = mm(source_v[rows, :], grads, TRANSPOSED)
            delta = jnp.sum(own * own_grad, axis=0, keepdims=True)
            if seen:
                past = past * inverse
                past_grad = mm(vp[0:seen, :], grads, TRANSPOSED)
                delta = delta + jnp.sum(past * past_grad, axis=0, keepdims=True)
            own_scores = (own * (own_grad - delta)).astype(jnp.bfloat16)
            own_dv = mm(own.astype(jnp.bfloat16), grads)
            own_dk = mm(own_scores, queries) * scale
            turned = mm(own_keys, own_scores, FIRST)
            if is_cont:
                to_v[rows, :] = own_dv
                to_k[rows, :] = own_dk
            else:
                to_v[rows, :] += own_dv
                to_k[rows, :] += own_dk
            if seen:
                past_scores = (past * (past_grad - delta)).astype(jnp.bfloat16)
                dvp[0:seen, :] += mm(past.astype(jnp.bfloat16), grads)
                dkp[0:seen, :] += mm(past_scores, queries) * scale
                turned = turned + mm(kp[0:seen, :], past_scores, FIRST)
            to_q[rows, :] = jnp.transpose(turned) * scale
    turn = DH // 2
    cos_p, sin_p = table_ref[0:prompt, :turn], table_ref[0:prompt, turn:]
    dqp[...] = turn_back(dqp[...], cos_p, sin_p)
    dkp[...] = turn_back(dkp[...], cos_p, sin_p)
    for step in range(prompt // cont):
        rows = slice(step * cont, (step + 1) * cont)
        cos_c = table_ref[prompt : prompt + cont, :turn]
        sin_c = table_ref[prompt : prompt + cont, turn:]
        dqc[rows, :] = turn_back(dqc[rows, :], cos_c, sin_c)
        dkc[rows, :] = turn_back(dkc[rows, :], cos_c, sin_c)
    spread_out(out_ref, (dqp, dkp, dvp), (dqc, dkc, dvc), DH)


def attention_backward(rows, grads, table):
    blocks, both, wide = rows.shape
    prompt = blocks * both
    small = pltpu.VMEM((prompt, DH), jnp.bfloat16)
    large = pltpu.VMEM((prompt, DH), jnp.float32)
    return pl.pallas_call(
        attention_back_kernel,
        out_shape=jax.ShapeDtypeStruct((blocks, both, wide), jnp.bfloat16),
        in_specs=[pl.BlockSpec(memory_space=pltpu.VMEM)] * 3,
        out_specs=pl.BlockSpec(memory_space=pltpu.VMEM),
        scratch_shapes=[small] * 8 + [large] * 6,
        compiler_params=pltpu.CompilerParams(vmem_limit_bytes=BACKWARD_VMEM),
        cost_estimate=pl.CostEstimate(
            flops=2**20, bytes_accessed=2**16, transcendentals=0
        ),
        name="attention_backward",
    )(rows, grads, table)


def exchange(values, axis, mask):
    return lax.ppermute(values, axis, [(i, i ^ mask) for i in range(lax.axis_size(axis))])


def to_member(values, number):
    if number == 2:
        return exchange(values, "grp", 1)
    if number == 1:
        return exchange(values, "head", 1)
    return lax.ppermute(values, ("grp", "head"), [(i, i ^ number) for i in range(4)])


def tie(values, *after):
    return lax.optimization_barrier((values, *after))[0]


def padded_bytes(shape, kind):
    shape = (1,) * (2 - len(shape)) + tuple(shape)
    rows, lanes = -(-shape[-2] // 16) * 16, -(-shape[-1] // 128) * 128
    return math.prod(shape[:-2]) * rows * lanes * jnp.dtype(kind).itemsize


def kernel_call(body_of, outs, scratch, name, *inputs, room=6, alone=False):
    held = [*outs, *scratch, *((one.shape, one.dtype) for one in inputs)]
    limit = sum(padded_bytes(*one) for one in held) + room * 2**20
    limit = 56 * 2**20 if alone else limit
    spec = pl.BlockSpec(memory_space=pltpu.VMEM)
    return pl.pallas_call(
        body_of,
        out_shape=[jax.ShapeDtypeStruct(*out) for out in outs],
        in_specs=[
            pl.BlockSpec(memory_space=pltpu.SMEM) if one.dtype == jnp.int32 else spec
            for one in inputs
        ],
        out_specs=[spec] * len(outs),
        scratch_shapes=[pltpu.VMEM(*one) for one in scratch],
        compiler_params=pltpu.CompilerParams(vmem_limit_bytes=limit),
        cost_estimate=pl.CostEstimate(flops=2**20, bytes_accessed=2**16, transcendentals=0),
        name=name,
    )(*inputs)


def move_all(copies, sems):
    started = [
        pltpu.make_async_copy(source, target, sems.at[number])
        for number, (source, target) in enumerate(copies)
    ]
    for one in started:
        one.start()
    for one in started:
        one.wait()


def first_kernel(place, qkv_ref, few_ref, proj_ref, own_ref, *refs):
    given, sems = refs[0:3], refs[3]
    six = own_ref.shape[0]
    start, small = six // 2, few_ref.shape[0]
    half = given[0].shape[0] - start - small
    middle = (place[5] + place[4]) % 2
    shift = qkv_ref.shape[0] - six
    copies = []
    for j in range(4):
        window = ((middle + place[4] + j) % 2) * shift
        if j == 0:
            copies.append((qkv_ref.at[pl.ds(pl.multiple_of(window, 64), six), :], own_ref))
            continue
        at = pl.multiple_of(window + place[1] * start, 64)
        target = given[j - 1]
        copies.append((qkv_ref.at[pl.ds(at, start), :], target.at[pl.ds(0, start), :]))
        copies.append((few_ref, target.at[pl.ds(start, small), :]))
        copies.append(
            (
                proj_ref.at[pl.ds(pl.multiple_of(place[1] * half, 16), half), :],
                target.at[pl.ds(start + small, half), :],
            )
        )
    move_all(copies, sems)


def rest_kernel(place, wide_ref, shared_down_ref, both_ref, down_ref, *refs):
    outs, held, sems, out_sems = refs[0:9], refs[9:18], refs[18], refs[19]
    piece_ref, pairs, downs = held[0], held[1:5], held[5:9]
    width, span = wide_ref.shape[0], piece_ref.shape[1]
    quarter, units = downs[0].shape
    four = place[3] % 4
    copies = []
    for j in range(4):
        at = pl.ds(pl.multiple_of((place[6] ^ UNIT_ORDER[j]) * units, 128), units)
        copies.append((both_ref.at[0, :, at], pairs[j].at[0]))
        copies.append((both_ref.at[1, :, at], pairs[j].at[1]))
        copies.append((down_ref.at[:, at], downs[j]))
    at = pl.ds(pl.multiple_of(four * span, 128), span)
    copies.append((wide_ref.at[:, at], piece_ref.at[pl.ds(0, width), :]))
    copies.append((shared_down_ref.at[:, at], piece_ref.at[pl.ds(width, quarter), :]))
    at = pl.ds(pl.multiple_of((4 + four) * span, 128), span)
    copies.append((shared_down_ref.at[:, at], piece_ref.at[pl.ds(width + quarter, quarter), :]))
    move_all(copies, sems)
    move_all(list(zip(held, outs)), out_sems)


def copy_call(body_of, outs, count, name, place, *inputs, through=False):
    held = [pltpu.VMEM(shape, jnp.bfloat16) for shape in outs] if through else []
    sems = [pltpu.SemaphoreType.DMA((count,))]
    if through:
        sems.append(pltpu.SemaphoreType.DMA((len(outs),)))
    return pl.pallas_call(
        body_of,
        out_shape=[jax.ShapeDtypeStruct(shape, jnp.bfloat16) for shape in outs],
        in_specs=[pl.BlockSpec(memory_space=pltpu.SMEM)]
        + [pl.BlockSpec(memory_space=pl.ANY)] * len(inputs),
        out_specs=[pl.BlockSpec(memory_space=pl.ANY)] * len(outs),
        scratch_shapes=held + sems,
        compiler_params=pltpu.CompilerParams(vmem_limit_bytes=(56 if through else 1) * 2**20),
        cost_estimate=pl.CostEstimate(flops=2**20, bytes_accessed=2**16, transcendentals=0),
        name=name,
    )(place, *inputs)


def packed(rows):
    count, width = rows.shape
    blocks = count // 20
    last = rows[16 * blocks :]
    half = width // 2
    return jnp.concatenate(
        [
            rows[: 8 * blocks].reshape(blocks, 8, width),
            rows[8 * blocks : 16 * blocks].reshape(blocks, 8, width),
            jnp.concatenate(
                [last[:, :half].reshape(blocks, 4, half), last[:, half:].reshape(blocks, 4, half)],
                axis=1,
            ),
        ],
        axis=2,
    )


def unpack_to(target, at, source_ref):
    blocks = source_ref.shape[0]
    width = target.shape[1]
    half = width // 2
    target[at : at + 8 * blocks, :] = source_ref[:, :, 0:width].reshape(8 * blocks, width)
    target[at + 8 * blocks : at + 16 * blocks, :] = source_ref[:, :, width : 2 * width].reshape(
        8 * blocks, width
    )
    for block in range(blocks):
        place = at + 16 * blocks + 4 * block
        last = source_ref[block, :, 2 * width :]
        target[place : place + 4, 0:half] = last[0:4]
        target[place : place + 4, half:width] = last[4:8]


def pack_kernel(rows_ref, out_ref):
    out_ref[...] = packed(rows_ref[...].astype(jnp.float32)).astype(jnp.bfloat16)


def join_kernel(own_ref, part_ref, out_ref):
    rows = own_ref[...] + part_ref[...].astype(jnp.float32)
    out_ref[...] = packed(rows).astype(jnp.bfloat16)


def layer_kernel(got_ref, pick_ref, residual_ref, shared_ref, out_ref, rows):
    unpack_to(rows, 0, got_ref)
    out_ref[...] = (
        residual_ref[...] + shared_ref[...] + mm(pick_ref[...], rows[...], FIRST)
    ).astype(jnp.bfloat16)


def qkv_kernel(place, tokens_ref, partner_ref, table_ref, window_ref, few_ref, *refs):
    got, passed = refs[0:3], refs[3:6]
    normed_ref, rows_ref, gains_ref, router_ref, weight_ref, window, few, both = refs[6:]
    quad_me, core, head = place[0], place[1], place[4]
    rows, width = tokens_ref.shape
    half, quarter = rows // 2, width // 4
    per = window.shape[1] // 2
    window[quad_me] = window_ref[...]
    few[quad_me] = few_ref[...].astype(jnp.float32)
    for j in (1, 2, 3):
        k = quad_me ^ j
        few[k] = got[j - 1][per : per + 16, :].astype(jnp.float32)
        window[k, pl.ds(pl.multiple_of(core * per, 64), per), :] = got[j - 1][0:per, :]
        window[k, pl.ds(pl.multiple_of((1 - core) * per, 64), per), :] = passed[j - 1][0:per, :]
    span = 2 * per

    @pl.when(head == 0)
    def _():
        weight_ref[0:span, :] = window[0]
        weight_ref[span : 2 * span, :] = window[1]
        weight_ref[2 * span : 2 * span + per, :] = window[2, per:span, :]
        weight_ref[2 * span + per : 3 * span, :] = window[3, 0:per, :]

    @pl.when(head == 1)
    def _():
        weight_ref[0:per, :] = window[0, per:span, :]
        weight_ref[per:span, :] = window[1, 0:per, :]
        weight_ref[span : 2 * span, :] = window[2]
        weight_ref[2 * span : 3 * span, :] = window[3]

    def few_row(number):
        part, row = divmod(number, 5)
        return jnp.concatenate(
            [few[k, row : row + 1, part * quarter : (part + 1) * quarter] for k in range(4)],
            axis=1,
        )

    gains = jnp.concatenate([few_row(0), few_row(1)], axis=0)
    gains_ref[...] = gains
    router_ref[...] = jnp.concatenate(
        [few_row(2 + e) for e in range(EXPERTS)], axis=0
    ).astype(jnp.bfloat16)
    for where, source in ((head, tokens_ref), (1 - head, partner_ref)):
        tokens = source[...].astype(jnp.float32)
        both[where] = norm_rows(tokens, gains[0:1])[0].astype(jnp.bfloat16)
    normed = both[...].reshape(2 * rows, width)
    normed_ref[...] = normed
    mixed = mm(normed, weight_ref[...], TRANSPOSED)
    turn = DH // 2
    table = []
    for part in range(2):
        table.append(table_ref[pl.ds(pl.multiple_of((2 * place[3] + part) * half, 64), half), :])
        at = table_ref.shape[0] - 2 * half + part * half
        table.append(table_ref[at : at + half, :])
    table = jnp.concatenate(table, axis=0)
    cosine, sine = table[:, :turn], table[:, turn:]
    heads = HEADS // 2

    def chunk(number):
        return mixed[:, number * DH : (number + 1) * DH]

    rows_ref[...] = jnp.zeros_like(rows_ref)
    for one in range(heads):
        pieces = [
            turn_back(chunk(one), cosine, -sine),
            turn_back(chunk(heads + one), cosine, -sine),
            chunk(2 * heads + one),
        ]
        for part in range(2):
            at = part * rows
            rows_ref[one, part * half : (part + 1) * half, :] = jnp.concatenate(
                [piece[at : at + half] for piece in pieces]
                + [piece[at + half : at + rows] for piece in pieces],
                axis=1,
            ).astype(jnp.bfloat16)


def hidden_kernel(place, got_ref, partner_ref, tokens_ref, gains_ref, pick_ref, mine_ref, *refs):
    own, other = refs[0:3], refs[3:6]
    residual_ref, hidden_ref, attn_ref, sent_ref, proj_ref, attn = refs[6:]
    head = place[4]
    rows, width = tokens_ref.shape
    half = rows // 2
    per, start = proj_ref.shape[1], own[0].shape[0] - proj_ref.shape[1]
    for part in range(2):
        proj_ref[place[0] * 2 + part] = mine_ref[part * per : (part + 1) * per, :]
    for j in (1, 2, 3):
        for where, source in ((place[1], own[j - 1]), (1 - place[1], other[j - 1])):
            proj_ref[(place[0] ^ j) * 2 + where] = source[start : start + per, :]
    for one in range(HEADS // 2):
        at = slice(one * DH, (one + 1) * DH)
        mine = got_ref[one, pl.ds(pl.multiple_of(head * half, 64), half), :]
        for where, piece in ((head, mine), (1 - head, partner_ref[one])):
            attn[where, 0:half, at] = piece[:, 0:DH]
            attn[where, half:rows, at] = piece[:, DH : 2 * DH]
    attn_all = jnp.concatenate([attn[0], attn[1]], axis=1)
    attn_ref[...] = attn_all
    residual = tokens_ref[...].astype(jnp.float32) + mm(
        attn_all, proj_ref[...].reshape(width, width), TRANSPOSED
    )
    residual_ref[...] = residual
    hidden = norm_rows(residual, gains_ref[1:2, :])[0].astype(jnp.bfloat16)
    hidden_ref[...] = hidden
    sent_ref[...] = packed(mm(pick_ref[...], hidden)).astype(jnp.bfloat16)


def expert_kernel(place, own_ref, other_ref, own_grad, other_grad, router_ref, *refs):
    pairs, downs = refs[0:4], refs[4:8]
    (
        g_own, g_part, e_own, e_part, egate_ref, eup_ref, mid_ref, eout_ref, g_router_ref,
        rows_ref, gate_w, up_w, down_w, grad_ref,
    ) = refs[8:]
    quad_me, expert_me = place[0], place[2]
    half_count = rows_ref.shape[0] // 2
    unpack_to(rows_ref, 0, own_ref)
    unpack_to(rows_ref, half_count, other_ref)
    unpack_to(grad_ref, 0, own_grad)
    unpack_to(grad_ref, half_count, other_grad)
    quarter = downs[0].shape[0]
    for j in range(4):
        at = pl.ds(pl.multiple_of((quad_me ^ j) * quarter, 64), quarter)
        gate_w[at, :] = pairs[j][0]
        up_w[at, :] = pairs[j][1]
        down_w[at, :] = downs[j][...]
    count = rows_ref.shape[0]
    block = count // 4
    router = router_ref[...]
    mine = lax.broadcasted_iota(jnp.int32, (block, EXPERTS), 1) == expert_me
    mine = mine.astype(jnp.float32)
    g_router = jnp.zeros_like(g_router_ref)
    for step in range(4):
        at = slice(step * block, (step + 1) * block)
        rows, grads = rows_ref[at, :], grad_ref[at, :]
        logits = mm(rows, router, TRANSPOSED)
        logits = jnp.exp(logits - jnp.max(logits, axis=1, keepdims=True))
        soft = logits / jnp.sum(logits, axis=1, keepdims=True)
        gate = jnp.sum(soft * mine, axis=1, keepdims=True)
        e_up = mm(rows, up_w[...])
        e_act, e_slope = swish_parts(mm(rows, gate_w[...]))
        e_mid = e_act * e_up
        e_grad = mm(grads, down_w[...])
        g_gate = jnp.sum(e_mid * e_grad, axis=1, keepdims=True)
        g_mid = e_grad * gate
        egate = (g_mid * e_up * e_slope).astype(jnp.bfloat16)
        eup = (g_mid * e_act).astype(jnp.bfloat16)
        e_mid = e_mid.astype(jnp.bfloat16)
        g_logits = (g_gate * soft * (mine - gate)).astype(jnp.bfloat16)
        g_rows = (
            mm(egate, gate_w[...], TRANSPOSED)
            + mm(eup, up_w[...], TRANSPOSED)
            + mm(g_logits, router)
        )
        e_rows = gate * mm(e_mid, down_w[...], TRANSPOSED)
        if step < 2:
            g_own[at, :] = g_rows
            e_own[at, :] = e_rows
        else:
            there = slice((step - 2) * block, (step - 1) * block)
            g_part[there, :] = g_rows.astype(jnp.bfloat16)
            e_part[there, :] = e_rows.astype(jnp.bfloat16)
        egate_ref[at, :] = egate
        eup_ref[at, :] = eup
        mid_ref[at, :] = e_mid
        eout_ref[at, :] = (gate * grads.astype(jnp.float32)).astype(jnp.bfloat16)
        g_router = g_router + mm(g_logits, rows, FIRST)
    g_router_ref[...] = g_router


def expert_weight_kernel(place, rows_ref, eout_ref, egate_ref, eup_ref, mid_ref, *refs):
    pairs, downs, whole, turned = refs[0:4], refs[4:8], refs[8], refs[9]
    quarter = downs[0].shape[0]
    turned[...] = jnp.transpose(rows_ref[...])
    for number, right in enumerate((egate_ref, eup_ref, mid_ref)):
        if number == 2:
            turned[...] = jnp.transpose(eout_ref[...])
        whole[...] = mm(turned[...], right[...]).astype(jnp.bfloat16)
        for j in range(4):
            at = pl.ds(pl.multiple_of((place[0] ^ j) * quarter, 64), quarter)
            if number == 2:
                downs[j][...] = whole[at, :]
            else:
                pairs[j][number] = whole[at, :]


def branch_kernel(
    place, got_ref, pick_ref, shared_ref, residual_ref, gains_ref, grad_ref, proj_ref,
    resid_ref, branch_ref, mine_ref, theirs_ref, gain_ref, back, heads,
):
    rows, width = grad_ref.shape
    unpack_to(back, 0, got_ref)
    g_hidden = mm(pick_ref[...], back[...], FIRST) + shared_ref[...].astype(jnp.float32)
    residual = residual_ref[...]
    gain = gains_ref[1:2, :]
    inverse = norm_rows(residual, gain)[1]
    g_norm, g_gain = norm_back(residual, inverse, gain, g_hidden)
    gain_ref[...] = g_gain[None]
    g_resid = grad_ref[...].astype(jnp.float32) + g_norm
    resid_ref[...] = g_resid
    branch = g_resid.astype(jnp.bfloat16)
    branch_ref[...] = branch
    attn = mm(branch, proj_ref[...].reshape(width, width)).astype(jnp.bfloat16)
    half = rows // 2
    for one in range(HEADS):
        piece = attn[:, one * DH : (one + 1) * DH]
        heads[one // (HEADS // 2), one % (HEADS // 2)] = jnp.concatenate(
            [piece[:half], piece[half:]], axis=1
        )
    mine_ref[...] = heads[place[4]]
    theirs_ref[...] = heads[1 - place[4]]


def tokens_kernel(
    place, got_ref, qkv_ref, tokens_ref, partner_ref, mine_ref, theirs_ref, gain_ref, parts, grads
):
    half = got_ref.shape[1] // 2
    rows = 2 * half
    heads = HEADS // 2
    for one in range(heads):
        for part in range(2):
            piece = got_ref[one, part * half : (part + 1) * half, :]
            at = part * rows
            for kind in range(3):
                there = slice((kind * heads + one) * DH, (kind * heads + one + 1) * DH)
                parts[at : at + half, there] = piece[:, kind * DH : (kind + 1) * DH]
                parts[at + half : at + rows, there] = piece[:, (3 + kind) * DH : (4 + kind) * DH]
    g_normed = mm(parts[...], qkv_ref[...])
    grads[0] = g_normed[:rows]
    grads[1] = g_normed[rows:]
    mine_ref[...] = grads[place[4]]
    theirs_ref[...] = grads[1 - place[4]].astype(jnp.bfloat16)
    gain = 0.0
    for source, where in ((tokens_ref, place[4]), (partner_ref, 1 - place[4])):
        tokens = source[...].astype(jnp.float32)
        inverse = norm_rows(tokens, 1.0)[1]
        gain = gain + jnp.sum(grads[where] * tokens * inverse, axis=0, keepdims=True)
    gain_ref[...] = gain


def tokens_out_kernel(mine_ref, partner_ref, tokens_ref, gains_ref, resid_ref, out_ref):
    g_normed = mine_ref[...] + partner_ref[...].astype(jnp.float32)
    tokens = tokens_ref[...].astype(jnp.float32)
    gain = gains_ref[0:1, :]
    inverse = norm_rows(tokens, gain)[1]
    out_ref[...] = resid_ref[...] + norm_back(tokens, inverse, gain, g_normed)[0]


def head_weight_kernel(rows_ref, normed_ref, out_ref, left):
    blocks, both, wide = rows_ref.shape
    half = both // 2
    for block in range(blocks):
        for part in range(2):
            at = (block * 2 + part) * both
            piece = rows_ref[block, part * half : (part + 1) * half, :]
            left[at : at + half, :] = piece[:, 0 : wide // 2]
            left[at + half : at + both, :] = piece[:, wide // 2 : wide]
    right = normed_ref[...].reshape(2 * both * blocks, normed_ref.shape[2])
    out_ref[...] = mm(left[...], right, FIRST).astype(jnp.bfloat16)


def chunk_kernel(order, got_ref, out_ref, few_ref):
    few = jnp.zeros_like(few_ref)
    for source in range(got_ref.shape[0]):
        few = few + got_ref[source, 2 * DH : 2 * DH + FEW, :].astype(jnp.float32)
    few_ref[...] = few
    for number in range(order.shape[0]):
        which = order[number]
        at = pl.ds(pl.multiple_of(which % 2 * DH, DH), DH)
        out_ref[number * DH : (number + 1) * DH, :] = got_ref[which // 2, at, :].astype(
            jnp.float32
        )


def shared_kernel(place, *refs):
    hidden_refs, grads_refs, pieces = refs[0:4], refs[4:8], refs[8:12]
    out_ref, back_ref = refs[12:14]
    given = refs[14:18]
    both_w, down_w, g_both, g_down = refs[18:]
    quad_me = place[0]
    width, span = both_w.shape[0], both_w.shape[1] // 4
    quarter = width // 4
    block = hidden_refs[0].shape[0]
    for j in range(4):
        k = quad_me ^ j
        both_w[:, pl.ds(pl.multiple_of(k * span, 128), span)] = pieces[j][0:width, :]
        at = pl.ds(pl.multiple_of(k * quarter, 64), quarter)
        down_w[at, 0:span] = pieces[j][width : width + quarter, :]
        down_w[at, span : 2 * span] = pieces[j][width + quarter : width + 2 * quarter, :]
    for step in range(2):
        rows = slice(step * 2 * block, (step + 1) * 2 * block)
        hidden = jnp.concatenate([hidden_refs[2 * step][...], hidden_refs[2 * step + 1][...]])
        grads = jnp.concatenate([grads_refs[2 * step][...], grads_refs[2 * step + 1][...]])
        pre = mm(hidden, both_w[...])
        act, slope = swish_parts(pre[:, : 2 * span])
        up = pre[:, 2 * span :]
        mid = (act * up).astype(jnp.bfloat16)
        out_ref[rows, :] = mm(mid, down_w[...], TRANSPOSED).astype(jnp.bfloat16)
        g_mid = mm(grads, down_w[...])
        g_pre = jnp.concatenate([g_mid * up * slope, g_mid * act], axis=1).astype(jnp.bfloat16)
        back_ref[rows, :] = mm(g_pre, both_w[...], TRANSPOSED).astype(jnp.bfloat16)
        new_both = mm(hidden, g_pre, FIRST)
        new_down = mm(grads, mid, FIRST)
        if step == 0:
            g_both[...] = new_both
            g_down[...] = new_down
        else:
            g_both[...] += new_both
            g_down[...] += new_down
    for j in range(4):
        k = quad_me ^ j
        at = pl.ds(pl.multiple_of(k * quarter, 64), quarter)
        given[j][0:width, :] = g_both[:, pl.ds(pl.multiple_of(k * span, 128), span)].astype(
            jnp.bfloat16
        )
        given[j][width : width + quarter, :] = g_down[at, 0:span].astype(jnp.bfloat16)
        given[j][width + quarter : width + 2 * quarter, :] = g_down[at, span : 2 * span].astype(
            jnp.bfloat16
        )


def shared_out_kernel(place, *refs):
    parts, wide_ref, down_ref, proj_ref = refs[0:4], refs[4], refs[5], refs[6]
    width, span = wide_ref.shape[0], parts[0].shape[1]
    quarter = down_ref.shape[0]
    last, per = width + 2 * quarter, quarter // 4
    for j in range(4):
        k = (place[3] % 4) ^ j
        at = pl.ds(pl.multiple_of(k * span, 128), span)
        wide_ref[:, at] = parts[j][0:width, :].astype(jnp.float32)
        down_ref[:, at] = parts[j][width : width + quarter, :].astype(jnp.float32)
        at = pl.ds(pl.multiple_of((4 + k) * span, 128), span)
        down_ref[:, at] = parts[j][width + quarter : last, :].astype(jnp.float32)
        at = pl.ds(pl.multiple_of(k * per, 16), per)
        for i in range(width // span):
            proj_ref[at, i * span : (i + 1) * span] = parts[j][
                last + i * per : last + (i + 1) * per, :
            ].astype(jnp.float32)


def units_out_kernel(place, *refs):
    parts, out_ref = refs[:-1], refs[-1]
    units = parts[0].shape[-1]
    for j in range(4):
        at = pl.ds(pl.multiple_of((place[6] ^ UNIT_ORDER[j]) * units, 128), units)
        if len(out_ref.shape) == 3:
            out_ref[0, :, at] = parts[j][0].astype(jnp.float32)
            out_ref[1, :, at] = parts[j][1].astype(jnp.float32)
        else:
            out_ref[:, at] = parts[j][...].astype(jnp.float32)


def quick_body(
    tokens_in,
    norm_gains,
    attn_qkv,
    attn_proj,
    router_rows,
    shared_gate_up,
    shared_down,
    expert_gate_up,
    expert_down,
    routes,
    out_grad,
):
    quad = ("grp", "head")
    line = ("head", "blk")
    blocks = lax.axis_size("blk")
    rows, width = tokens_in.shape
    grp, head, blk = lax.axis_index("grp"), lax.axis_index("head"), lax.axis_index("blk")
    core = blk % 2
    quarter = width // 4
    prompt_dev = max(PROMPT_ROWS, PROMPT_LEAST // (2 * blocks))
    prompt = prompt_dev * 2 * blocks
    cont = 2 * (rows - prompt_dev)
    bf16, f32 = jnp.bfloat16, jnp.float32

    member = 2 * grp + head
    unit_me = 2 * head + grp
    place = jnp.stack([member, core, 2 * blk + head, blk, head, grp, unit_me])
    third = attn_qkv.shape[1]
    few = jnp.concatenate([norm_gains, router_rows], axis=0)
    few = jnp.pad(few, ((0, 20 - few.shape[0]), (0, 0)))
    few = jnp.concatenate([few[5 * i : 5 * i + 5] for i in range(4)], axis=1)
    few = jnp.pad(few, ((0, 11), (0, 0)))
    six = width // 2
    own_window, *window_parts = copy_call(
        first_kernel,
        [(six, width)] + [(six // 2 + 16 + quarter // 2, width)] * 3,
        10,
        "first_parts",
        place, attn_qkv.T, few, attn_proj.T,
    )
    partner_tokens = exchange(tokens_in, "head", 1)
    own_w = [to_member(window_parts[j - 1], j) for j in (1, 2, 3)]
    other_w = [exchange(part, "blk", 1) for part in own_w]

    span = SFF // 2 // 4
    four = blk % 4
    units = expert_gate_up.shape[2] // 4
    piece, *unit_parts = copy_call(
        rest_kernel,
        [(width + 2 * quarter, span)] + [(2, quarter, units)] * 4 + [(quarter, units)] * 4,
        15,
        "rest_parts",
        place, shared_gate_up, shared_down.T, expert_gate_up, expert_down.T,
        through=True,
    )
    pair_send, down_send = unit_parts[0:4], unit_parts[4:8]

    def of_four(values):
        far = exchange(values, "blk", 2)
        return [values, exchange(values, "blk", 1), far, exchange(far, "blk", 1)]

    def sum_of_four(parts):
        near = exchange(jnp.stack([parts[1], parts[3]]), "blk", 1)
        far = (parts[2].astype(f32) + near[1].astype(f32)).astype(bf16)
        return parts[0].astype(f32) + near[0].astype(f32) + exchange(far, "blk", 2).astype(f32)

    def joined(own, part):
        return (own.astype(f32) + part.astype(f32)).astype(bf16)

    def fetched(parts, after, *numbers):
        for j in numbers:
            parts[j] = to_member(tie(parts[j], after), j)

    expert_ids = jnp.arange(EXPERTS, dtype=jnp.int32)
    match = (routes[:, :, None] == expert_ids).astype(jnp.int32)
    flat = match.reshape(2 * rows, EXPERTS)
    rank = (jnp.sum(jnp.cumsum(flat, axis=0) * flat, axis=1) - 1).reshape(rows, 2)
    slots_all = 2 * blocks
    target = routes % 2 * blocks + routes // 2
    slots = jnp.where(
        rank < 16,
        rank // 8 * (8 * slots_all) + target * 8 + rank % 8,
        16 * slots_all + target * 4 + rank - 16,
    )
    per_half = 20 * slots_all
    slot_ids = jnp.arange(per_half, dtype=jnp.int32)[:, None]
    pick = ((slot_ids == slots[:, 0]) | (slot_ids == slots[:, 1])).astype(bf16)
    pack_shape = (slots_all, 8, 5 * width // 2)

    def over_line(values):
        return lax.all_to_all(values, line, 0, 0, tiled=True)

    def over_blocks(values):
        return lax.all_to_all(values, "blk", 0, 0, tiled=True)

    grad_sent = kernel_call(
        pack_kernel, [(pack_shape, bf16)], [], "pack_rows", mm(pick, tie(out_grad, own_w[0])).astype(bf16)
    )[0]
    grad_own = over_line(grad_sent)
    four_grads = of_four(out_grad)

    wait = lax.optimization_barrier
    own_w, other_w, partner_tokens, pair_send, down_send, piece = wait(
        (own_w, other_w, partner_tokens, pair_send, down_send, piece)
    )
    shared_parts = [piece] * 4
    steps = np.arange(DH // 2, dtype=np.float32)
    rates = np.power(np.float32(10000.0), np.float32(-2.0) * steps / np.float32(DH))
    angles = np.arange(prompt + cont, dtype=np.float32)[:, None] * rates[None, :].astype(np.float32)
    table = jnp.asarray(
        np.concatenate([np.cos(angles), np.sin(angles)], axis=1).astype(np.float32)
    )
    normed, head_send, gains, router_w, qkv_w = kernel_call(
        qkv_kernel,
        [
            ((2 * rows, width), bf16),
            ((blocks, rows, 6 * DH), bf16),
            ((2, width), f32),
            ((EXPERTS, width), bf16),
            ((3 * six, width), bf16),
        ],
        [((4, six, width), bf16), ((4, 16, width), f32), ((2, rows, width), bf16)],
        "qkv_rows",
        place, tokens_in, partner_tokens, table, own_window, few, *own_w, *other_w,
        alone=True,
    )
    head_send, grad_own = wait((head_send, grad_own))
    head_rows = over_blocks(head_send)
    fetched(pair_send, head_send, 1, 2)
    head_rows, pair_send = wait((head_rows, pair_send))
    attn_heads = attention_forward(head_rows)
    fetched(pair_send, head_rows, 3)
    attn_got = over_blocks(attn_heads)
    all_normed = lax.all_gather(tie(normed, attn_heads), "blk", axis=0)
    fetched(shared_parts, attn_heads, 1, 2)
    grad_other = exchange(tie(grad_own, attn_heads), "grp", 1)
    attn_got, pair_send = wait((attn_got, pair_send))
    head_half = HEADS // 2
    theirs = lax.dynamic_slice_in_dim(attn_got[:head_half], (1 - head) * prompt_dev, prompt_dev, 1)
    attn_partner = exchange(theirs, "head", 1)
    shared_parts[3] = exchange(tie(shared_parts[2], attn_partner), "head", 1)
    residual, hidden, attn_tok, sent, proj_w = kernel_call(
        hidden_kernel,
        [
            ((rows, width), f32),
            ((rows, width), bf16),
            ((rows, width), bf16),
            (pack_shape, bf16),
            ((8, quarter // 2, width), bf16),
        ],
        [((2, rows, six), bf16)],
        "hidden_rows",
        place, attn_got, attn_partner, tokens_in, gains, pick, attn_proj.T, *own_w, *other_w,
        alone=True,
    )

    sent, grad_other, shared_parts[1], shared_parts[2] = wait(
        (sent, grad_other, shared_parts[1], shared_parts[2])
    )
    got_own = over_line(sent)
    fetched(down_send, sent, 2, 3, 1)
    four_hidden = of_four(tie(hidden, sent))
    got_own, shared_parts, down_send[3], four_hidden = wait(
        (got_own, shared_parts, down_send[3], four_hidden)
    )
    got_other = exchange(got_own, "grp", 1)
    shared_out, shared_back, *shared_given = kernel_call(
        shared_kernel,
        [((4 * rows, width), bf16)] * 2 + [((width + 2 * quarter, span), bf16)] * 4,
        [
            ((width, 4 * span), bf16),
            ((width, 2 * span), bf16),
            ((width, 4 * span), f32),
            ((width, 2 * span), f32),
        ],
        "shared_rows",
        place, *tie(four_hidden, got_own), *four_grads, *shared_parts,
        alone=True,
    )
    shared_back = sum_of_four([shared_back[i * rows : (i + 1) * rows] for i in range(4)])

    got_other, shared_given, down_send, all_normed = wait(
        (got_other, shared_given, down_send, all_normed)
    )
    middle = shared_given[0].shape[0] // 2
    upper = [part[:middle] for part in shared_given]
    lower = [part[middle:] for part in shared_given]
    count = 2 * per_half
    g_own, g_part, e_own, e_part, egate, eup, e_mid, g_eout, g_router, got_rows = kernel_call(
        expert_kernel,
        [
            ((per_half, width), f32),
            ((per_half, width), bf16),
            ((per_half, width), f32),
            ((per_half, width), bf16),
            ((count, units), bf16),
            ((count, units), bf16),
            ((count, units), bf16),
            ((count, width), bf16),
            ((EXPERTS, width), f32),
            ((count, width), bf16),
        ],
        [((width, units), bf16)] * 3 + [((count, width), bf16)],
        "expert_rows",
        place, got_own, got_other, grad_own, grad_other, router_w,
        *pair_send, *down_send,
        alone=True,
    )

    def joined_rows(own, part):
        return kernel_call(join_kernel, [(pack_shape, bf16)], [], "join_rows", own, part)[0]

    weight_parts = kernel_call(
        expert_weight_kernel,
        [((2, quarter, units), bf16)] * 4 + [((quarter, units), bf16)] * 4,
        [((width, units), bf16), ((width, count), bf16)],
        "expert_weights",
        place, got_rows, g_eout, egate, eup, e_mid,
        alone=True,
    )
    pair_out, down_out = list(weight_parts[0:4]), list(weight_parts[4:8])
    g_other = exchange(g_part, "grp", 1)
    turned = exchange(tie(jnp.stack([lower[1], lower[3]]), g_part), "head", 1)
    g_other, pair_out, down_out = wait((g_other, pair_out, down_out))
    crossed = exchange(tie(jnp.stack([upper[2], upper[3]]), g_other), "grp", 1)
    g_joined, shared_back, turned = wait((joined_rows(g_own, g_other), shared_back, turned))
    crossed = joined(upper[1], crossed[1]), joined(upper[0], crossed[0])
    turned = joined(lower[2], turned[1]), joined(lower[0], turned[0])
    g_back = over_line(g_joined)
    shared_sum = jnp.concatenate(
        [
            joined(crossed[1], exchange(tie(crossed[0], g_joined), "head", 1)),
            joined(turned[1], exchange(tie(turned[0], g_joined), "grp", 1)),
        ]
    )
    cutting = 576

    def far_sum(values):
        return joined(values, exchange(values, "blk", 4))


    g_resid, g_branch, grad_mine, grad_theirs, g_second_gain = kernel_call(
        branch_kernel,
        [
            ((rows, width), f32),
            ((rows, width), bf16),
            ((head_half, prompt_dev, 2 * DH), bf16),
            ((head_half, prompt_dev, 2 * DH), bf16),
            ((1, width), f32),
        ],
        [((per_half, width), bf16), ((2, head_half, prompt_dev, 2 * DH), bf16)],
        "branch_rows",
        place, g_back, pick, shared_back, residual, gains, out_grad, proj_w,
    )
    grad_theirs = exchange(grad_theirs, "head", 1)
    grad_theirs, shared_sum = wait((grad_theirs, shared_sum))
    g_proj = mm(g_branch, attn_tok, FIRST).astype(bf16).reshape(4, 4, quarter // 4, width)
    g_proj = sum_of_four(
        [
            lax.dynamic_index_in_dim(g_proj, four ^ j, 1, keepdims=False).reshape(quarter, width)
            for j in range(4)
        ]
    )
    g_proj = g_proj.astype(bf16)
    grad_send = jnp.where(
        head == 0,
        jnp.concatenate([grad_mine, grad_theirs], axis=1),
        jnp.concatenate([grad_theirs, grad_mine], axis=1),
    )
    grad_send = jnp.pad(grad_send, ((0, blocks - head_half), (0, 0), (0, 0)))
    grad_heads = over_blocks(grad_send)
    fetched(pair_out, grad_send, 1, 2)
    far_one = far_sum(tie(shared_sum[:cutting], grad_heads))
    g_head_rows = attention_backward(head_rows, grad_heads, table)
    g_proj = g_proj.reshape(4, quarter // 4, width)
    proj_out = []
    for j in range(4):
        part = lax.dynamic_index_in_dim(g_proj, member ^ j, 0, keepdims=False)
        proj_out.append(
            jnp.concatenate([part[:, i * span : (i + 1) * span] for i in range(width // span)])
        )
    fetched(proj_out, g_head_rows, 1, 2, 3)
    proj_sum = sum(part.astype(f32) for part in proj_out).astype(bf16)
    far_two = far_sum(tie(shared_sum[cutting:], g_head_rows))
    far_proj = far_sum(tie(proj_sum, g_head_rows))
    fetched(pair_out, grad_heads, 3)
    g_head_rows, far_one = wait((g_head_rows, far_one))
    g_got = over_blocks(g_head_rows)
    e_other = exchange(tie(e_part, g_head_rows), "grp", 1)
    g_got, pair_out, e_joined = wait((g_got, pair_out, joined_rows(e_own, e_other)))
    g_normed, g_normed_theirs, g_first_gain = kernel_call(
        tokens_kernel,
        [((rows, width), f32), ((rows, width), bf16), ((1, width), f32)],
        [((2 * rows, 3 * six), bf16), ((2, rows, width), f32)],
        "token_parts",
        place, g_got, qkv_w, tokens_in, partner_tokens,
    )
    g_normed_theirs = exchange(g_normed_theirs, "head", 1)

    head_w = kernel_call(
        head_weight_kernel,
        [((3 * DH, width), bf16)],
        [((2 * rows * blocks, 3 * DH), bf16)],
        "head_weights",
        tie(g_head_rows, g_first_gain), all_normed,
    )[0].reshape(3, DH, width)

    def chunk_pair(side):
        kept_kind = 2 * side
        given_kind = jnp.where(head == 0, 1 + side, side)
        return jnp.stack([head_w[kept_kind], head_w[given_kind]])

    few = jnp.concatenate([g_first_gain, g_second_gain, g_router], axis=0)
    few = jnp.pad(few, ((0, FEW - few.shape[0]), (0, 0))).astype(bf16)
    own_pair = jnp.concatenate([*jnp.where(grp == 0, chunk_pair(0), chunk_pair(1)), few])
    other_pair = jnp.concatenate([*jnp.where(grp == 0, chunk_pair(1), chunk_pair(0)), few])
    own_pair = joined(own_pair, exchange(other_pair, "grp", 1))
    from_head = exchange(own_pair[DH:], "head", 1)
    own_pair = jnp.concatenate(
        [own_pair[:DH], from_head[:DH], joined(own_pair[2 * DH :], from_head[DH:])]
    )
    own_pair, far_two, far_proj = wait((own_pair, far_two, far_proj))
    all_pairs = lax.all_gather(own_pair, "blk", axis=0)
    order = jnp.array(
        [
            [0, 2, 4, 6, 8, 10, 1, 3, 5],
            [6, 8, 10, 1, 3, 5, 7, 9, 11],
            [1, 3, 5, 7, 9, 11, 0, 2, 4],
            [7, 9, 11, 0, 2, 4, 6, 8, 10],
        ],
        jnp.int32,
    )[member]
    grad_tokens = kernel_call(
        tokens_out_kernel,
        [((rows, width), f32)],
        [],
        "token_grads",
        g_normed, g_normed_theirs, tokens_in, gains, g_resid,
    )[0]
    grad_expert_w = kernel_call(
        units_out_kernel,
        [((2, quarter, 4 * units), f32)],
        [],
        "units_out",
        place, *pair_out,
        alone=True,
    )[0]
    shared_out = sum_of_four(
        [tie(shared_out, g_got)[i * rows : (i + 1) * rows] for i in range(4)]
    )
    fetched(down_out, from_head, 1, 2, 3)
    e_joined, down_out = wait((e_joined, down_out))
    e_back = over_line(e_joined)
    layer_out = kernel_call(
        layer_kernel,
        [((rows, width), bf16)],
        [((per_half, width), bf16)],
        "layer_rows",
        e_back, pick, residual, shared_out,
    )[0]
    four_shared = of_four(
        tie(jnp.concatenate([far_one, far_two, far_proj]), grad_expert_w)
    )
    grad_expert_out = kernel_call(
        units_out_kernel,
        [((quarter, 4 * units), f32)],
        [],
        "down_out",
        place, *down_out,
        alone=True,
    )[0].T
    grad_shared_w, grad_shared_out, grad_proj = kernel_call(
        shared_out_kernel,
        [((width, 4 * span), f32), ((quarter, SFF), f32), ((quarter, width), f32)],
        [],
        "shared_grads",
        place, *four_shared,
        alone=True,
    )
    all_pairs, grad_expert_w, grad_expert_out, layer_out, grad_shared_w = wait(
        (all_pairs, grad_expert_w, grad_expert_out, layer_out, grad_shared_w)
    )
    grad_qkv, few = kernel_call(
        chunk_kernel,
        [((third, width), f32), ((FEW, width), f32)],
        [],
        "chunk_rows",
        order, all_pairs,
    )
    grad_qkv = grad_qkv.T

    few = lax.dynamic_slice_in_dim(few, member * quarter, quarter, 1)
    grad_shared_out, grad_proj = grad_shared_out.T, grad_proj.T
    return (
        layer_out,
        grad_tokens,
        few[0:2],
        grad_qkv,
        grad_proj,
        few[2 : 2 + EXPERTS],
        grad_shared_w,
        grad_shared_out,
        grad_expert_w,
        grad_expert_out,
    )


def solution(mesh):
    whole = P(("grp", "head", "blk"), None)
    split = P(None, ("grp", "head"))
    sizes = dict(mesh.shape)
    quick = sizes["grp"] == 2 and sizes["head"] == 2 and sizes["blk"] == 8
    return jax.shard_map(
        quick_body if quick else body,
        mesh=mesh,
        in_specs=(
            whole, split, split, split, split, split, split,
            P(None, ("grp", "head"), "blk"), P("blk", ("grp", "head")), whole, whole,
        ),
        out_specs=(
            whole, whole, split, split, split, split, split, split,
            P(None, ("grp", "head"), "blk"), P("blk", ("grp", "head")),
        ),
        check_vma=False,
    )
```

```python
import math

import jax
import jax.numpy as jnp
import numpy as np
from jax import lax
from jax.experimental import pallas as pl
from jax.experimental.pallas import tpu as pltpu
from jax.sharding import PartitionSpec as P

HEADS = 12
DH = 64
EXPERTS = 16
FF = 2048
SFF = 2048
PROMPT_ROWS = 64
PROMPT_LEAST = 1024


EPSILON = 1e-06
NEGATIVE = -1e30


def norm_rows(values, gain):
    inverse = lax.rsqrt(jnp.mean(values * values, axis=-1, keepdims=True) + EPSILON)
    return (values * inverse * gain, inverse)


def norm_back(values, inverse, gain, upstream):
    scaled = upstream * gain
    inner_mean = jnp.mean(scaled * values, axis=-1, keepdims=True)
    return (
        inverse * scaled - values * inverse**3 * inner_mean,
        jnp.sum(upstream * values * inverse, axis=0),
    )


def angle_tables(positions):
    step_index = jnp.arange(DH // 2, dtype=jnp.float32)
    freq_rates = 10000.0 ** (-2.0 * step_index / DH)
    angles = positions.astype(jnp.float32)[:, None] * freq_rates[None, :]
    return (jnp.cos(angles)[:, None, :], jnp.sin(angles)[:, None, :])


def rotate(values, cosine, sine_table):
    half_size = values.shape[-1] // 2
    first_half = values[..., :half_size]
    second = values[..., half_size:]
    return jnp.concatenate(
        [first_half * cosine - second * sine_table, second * cosine + first_half * sine_table],
        axis=-1,
    )


def swish_parts(gate_value):
    sigmoid = jax.nn.sigmoid(gate_value)
    return (gate_value * sigmoid, sigmoid * (1.0 + gate_value * (1.0 - sigmoid)))


def row_layout(head_part, within, block_index, heads_axis, blocks_axis, row_count, prompt_dev):
    prompt_all = prompt_dev * heads_axis * blocks_axis
    is_prompt = within < prompt_dev
    prompt_index = (block_index * heads_axis + head_part) * prompt_dev + within
    cont_index = head_part * (row_count - prompt_dev) + within - prompt_dev
    positions = jnp.where(is_prompt, prompt_index, prompt_all + cont_index)
    return (is_prompt, prompt_index, cont_index, positions)


def fetch_weights(
    norm_gains,
    attn_qkv,
    attn_proj,
    router_rows,
    shared_gate_up,
    shared_down,
    expert_gate_up,
    expert_down,
):
    return (
        lax.all_gather(norm_gains, ("grp", "head"), axis=1, tiled=True),
        lax.all_gather(attn_qkv, ("grp", "head"), axis=1, tiled=True),
        lax.all_gather(attn_proj, ("grp", "head"), axis=1, tiled=True),
        lax.all_gather(router_rows, ("grp", "head"), axis=1, tiled=True),
        lax.all_gather(shared_gate_up, ("grp", "head"), axis=1, tiled=True),
        lax.all_gather(shared_down, ("grp", "head"), axis=1, tiled=True),
        lax.all_gather(expert_gate_up, ("grp", "head"), axis=1, tiled=True),
        lax.all_gather(expert_down, ("grp", "head"), axis=1, tiled=True),
    )


def masked_scores(queries, key_rows, visible):
    scores = jnp.einsum(
        "qhd,khd->hqk", queries, key_rows, preferred_element_type=jnp.float32
    ) * DH ** (-0.5)
    return jnp.where(visible[None], scores, NEGATIVE)


def add_stats(carry, scores, visible):
    row_peak, row_total = carry
    new_peak = jnp.maximum(row_peak, jnp.max(scores, axis=-1))
    terms = jnp.where(visible[None], jnp.exp(scores - new_peak[:, :, None]), 0.0)
    return (new_peak, row_total * jnp.exp(row_peak - new_peak) + jnp.sum(terms, axis=-1))


def block_probs(scores, visible, log_total):
    return jnp.where(visible[None], jnp.exp(scores - log_total[:, :, None]), 0.0)


def grad_block(queries, grad_out, log_total, delta, key_rows, value_rows, visible):
    scale_factor = DH ** (-0.5)
    soft_weights = block_probs(masked_scores(queries, key_rows, visible), visible, log_total)
    grad_weights = jnp.einsum(
        "qhd,khd->hqk", grad_out, value_rows, preferred_element_type=jnp.float32
    )
    grad_scores = (soft_weights * (grad_weights - delta[:, :, None])).astype(jnp.bfloat16)
    grad_query = (
        jnp.einsum("hqk,khd->qhd", grad_scores, key_rows, preferred_element_type=jnp.float32)
        * scale_factor
    )
    grad_key = (
        jnp.einsum("hqk,qhd->khd", grad_scores, queries, preferred_element_type=jnp.float32)
        * scale_factor
    )
    grad_value = jnp.einsum(
        "hqk,qhd->khd",
        soft_weights.astype(jnp.bfloat16),
        grad_out,
        preferred_element_type=jnp.float32,
    )
    return (grad_query, grad_key, grad_value)


def body(
    tokens_in,
    norm_gains,
    attn_qkv,
    attn_proj,
    router_rows,
    shared_gate_up,
    shared_down,
    expert_gate_up,
    expert_down,
    routes,
    out_grad,
):
    heads_axis = lax.axis_size("head")
    blocks_axis = lax.axis_size("blk")
    row_count = tokens_in.shape[0]
    width_all = tokens_in.shape[1]
    prompt_dev = max(PROMPT_ROWS, PROMPT_LEAST // (heads_axis * blocks_axis))
    prompt_all = prompt_dev * heads_axis * blocks_axis
    local_heads = HEADS // heads_axis
    query_rows = heads_axis * row_count
    key_block = min(512, prompt_all)
    block_count = prompt_all // key_block
    head_me = lax.axis_index("head")
    block_me = lax.axis_index("blk")
    gain_rows, qkv_w, proj_w, router_w, shared_w, shared_out_w, expert_w, expert_out_w = (
        fetch_weights(
            norm_gains,
            attn_qkv,
            attn_proj,
            router_rows,
            shared_gate_up,
            shared_down,
            expert_gate_up,
            expert_down,
        )
    )
    tokens = tokens_in.astype(jnp.float32)
    first_gain = gain_rows[0].astype(jnp.float32)
    second_gain = gain_rows[1].astype(jnp.float32)
    normed_f, first_inverse = norm_rows(tokens, first_gain)
    normed = normed_f.astype(jnp.bfloat16)
    mixed_qkv = jnp.dot(normed, qkv_w, preferred_element_type=jnp.float32)
    token_row = jnp.arange(row_count, dtype=jnp.int32)
    token_pos = row_layout(
        head_me, token_row, block_me, heads_axis, blocks_axis, row_count, prompt_dev
    )[3]
    token_cos, token_sin = angle_tables(token_pos)
    query_tok = (
        rotate(mixed_qkv[:, :width_all].reshape(row_count, HEADS, DH), token_cos, token_sin)
        .reshape(row_count, width_all)
        .astype(jnp.bfloat16)
    )
    key_tok = (
        rotate(
            mixed_qkv[:, width_all : 2 * width_all].reshape(row_count, HEADS, DH),
            token_cos,
            token_sin,
        )
        .reshape(row_count, width_all)
        .astype(jnp.bfloat16)
    )
    value_tok = mixed_qkv[:, 2 * width_all :].astype(jnp.bfloat16)
    query_head, key_head, value_head = (
        lax.all_to_all(query_tok, "head", split_axis=1, concat_axis=0, tiled=True),
        lax.all_to_all(key_tok, "head", split_axis=1, concat_axis=0, tiled=True),
        lax.all_to_all(value_tok, "head", split_axis=1, concat_axis=0, tiled=True),
    )
    local_index = jnp.arange(query_rows, dtype=jnp.int32)
    is_prompt, prompt_index, cont_index, head_pos = row_layout(
        local_index // row_count,
        local_index % row_count,
        block_me,
        heads_axis,
        blocks_axis,
        row_count,
        prompt_dev,
    )
    is_cont = jnp.logical_not(is_prompt)
    local_visible = (
        is_cont[:, None] & is_cont[None, :] & (cont_index[None, :] <= cont_index[:, None])
    )
    queries = query_head.reshape(query_rows, local_heads, DH)
    key_local = key_head.reshape(query_rows, local_heads, DH)
    value_local = value_head.reshape(query_rows, local_heads, DH)
    prompt_keys, prompt_values = (
        lax.all_gather(
            key_head.reshape(heads_axis, row_count, -1)[:, :prompt_dev].reshape(
                heads_axis * prompt_dev, -1
            ),
            "blk",
            axis=0,
            tiled=True,
        ),
        lax.all_gather(
            value_head.reshape(heads_axis, row_count, -1)[:, :prompt_dev].reshape(
                heads_axis * prompt_dev, -1
            ),
            "blk",
            axis=0,
            tiled=True,
        ),
    )
    key_blocks = prompt_keys.reshape(block_count, key_block, local_heads, DH)
    value_blocks = prompt_values.reshape(block_count, key_block, local_heads, DH)
    block_starts = jnp.arange(block_count, dtype=jnp.int32) * key_block
    key_offsets = jnp.arange(key_block, dtype=jnp.int32)

    def prompt_visible(start):
        return is_cont[:, None] | (start + key_offsets[None, :] <= prompt_index[:, None])

    def stats_step(carry, member):
        visible = prompt_visible(member[1])
        return (add_stats(carry, masked_scores(queries, member[0], visible), visible), None)

    start_stats = (
        jnp.full((local_heads, query_rows), NEGATIVE, jnp.float32),
        jnp.zeros((local_heads, query_rows), jnp.float32),
    )
    stats = lax.scan(stats_step, start_stats, (key_blocks, block_starts))[0]
    row_peak, row_total = add_stats(
        stats, masked_scores(queries, key_local, local_visible), local_visible
    )
    log_total = row_peak + jnp.log(row_total)

    def output_step(total_out, member):
        visible = prompt_visible(member[2])
        soft_weights = block_probs(
            masked_scores(queries, member[0], visible), visible, log_total
        ).astype(jnp.bfloat16)
        return (
            total_out
            + jnp.einsum(
                "hqk,khd->qhd", soft_weights, member[1], preferred_element_type=jnp.float32
            ),
            None,
        )

    attn_heads = lax.scan(
        output_step,
        jnp.zeros((query_rows, local_heads, DH), jnp.float32),
        (key_blocks, value_blocks, block_starts),
    )[0]
    local_weights = block_probs(
        masked_scores(queries, key_local, local_visible), local_visible, log_total
    ).astype(jnp.bfloat16)
    attn_heads = attn_heads + jnp.einsum(
        "hqk,khd->qhd", local_weights, value_local, preferred_element_type=jnp.float32
    )
    attn_tok = lax.all_to_all(
        attn_heads.reshape(query_rows, -1).astype(jnp.bfloat16),
        "head",
        split_axis=0,
        concat_axis=1,
        tiled=True,
    )
    residual = tokens + jnp.dot(attn_tok, proj_w, preferred_element_type=jnp.float32)
    hidden_f, second_inverse = norm_rows(residual, second_gain)
    hidden = hidden_f.astype(jnp.bfloat16)
    logits = jnp.einsum("td,ed->te", hidden, router_w, preferred_element_type=jnp.float32)
    soft_route = jax.nn.softmax(logits, axis=-1)
    expert_ids = jnp.arange(EXPERTS, dtype=jnp.int32)
    route_match = routes[:, :, None] == expert_ids[None, None, :]
    gate_values = jnp.sum(jnp.where(route_match, soft_route[:, None, :], 0.0), axis=-1)
    shared_pre = jnp.dot(hidden, shared_w, preferred_element_type=jnp.float32)
    shared_act, shared_slope = swish_parts(shared_pre[:, :SFF])
    shared_up = shared_pre[:, SFF:]
    shared_mid = (shared_act * shared_up).astype(jnp.bfloat16)
    shared_out = jnp.dot(shared_mid, shared_out_w, preferred_element_type=jnp.float32)
    unit_count = expert_w.shape[2]
    per_device = max(1, unit_count // FF)
    spread = max(1, FF // unit_count)
    unit_width = unit_count // per_device
    capacity = max(2, 5 * row_count // (2 * EXPERTS))
    slot_count = blocks_axis * per_device * capacity
    pair_expert = routes.reshape(-1)
    pair_match = route_match.reshape(2 * row_count, EXPERTS).astype(jnp.int32)
    pair_rank = jnp.sum(jnp.cumsum(pair_match, axis=0) * pair_match, axis=1) - 1
    slot_base = (
        pair_expert // per_device * spread * per_device * capacity
        + pair_expert % per_device * capacity
        + pair_rank
    )
    slot_index = (
        slot_base[None, :] + (jnp.arange(spread, dtype=jnp.int32) * per_device * capacity)[:, None]
    )
    pair_ids = jnp.arange(2 * row_count, dtype=jnp.int32)
    slot_pair = (
        jnp.full((slot_count,), 2 * row_count, jnp.int32)
        .at[slot_index.reshape(-1)]
        .set(jnp.tile(pair_ids, spread))
    )
    slot_token = slot_pair // 2
    hidden_pad = jnp.concatenate([hidden, jnp.zeros((1, width_all), jnp.bfloat16)], axis=0)
    send_rows = hidden_pad[slot_token].reshape(blocks_axis, per_device, capacity, width_all)
    received_rows = lax.all_to_all(send_rows, "blk", split_axis=0, concat_axis=0, tiled=True)
    gate_weight = expert_w[0].reshape(width_all, per_device, unit_width)
    up_weight = expert_w[1].reshape(width_all, per_device, unit_width)
    down_w = expert_out_w.reshape(per_device, unit_width, width_all)
    expert_gate = jnp.einsum(
        "tfoa,afw->tfow", received_rows, gate_weight, preferred_element_type=jnp.float32
    )
    expert_up_projection = jnp.einsum(
        "tfoa,afw->tfow", received_rows, up_weight, preferred_element_type=jnp.float32
    )
    expert_activation, expert_slope = swish_parts(expert_gate)
    expert_mid = (expert_activation * expert_up_projection).astype(jnp.bfloat16)
    expert_part = jnp.einsum(
        "secm,emd->secd", expert_mid, down_w, preferred_element_type=jnp.float32
    )
    returned = (
        lax.all_to_all(
            expert_part.astype(jnp.bfloat16), "blk", split_axis=0, concat_axis=0, tiled=True
        )
        .astype(expert_part.dtype)
        .reshape(slot_count, width_all)
    )
    pair_out = jnp.sum(returned[slot_index], axis=0).reshape(row_count, 2, width_all)
    expert_sum = jnp.sum(gate_values[:, :, None] * pair_out, axis=1)
    layer_out = (residual + shared_out + expert_sum).astype(jnp.bfloat16)
    gain_rows, qkv_w, proj_w, router_w, shared_w, shared_out_w, expert_w, expert_out_w = (
        fetch_weights(
            norm_gains,
            attn_qkv,
            attn_proj,
            router_rows,
            shared_gate_up,
            shared_down,
            expert_gate_up,
            expert_down,
        )
    )
    gate_weight = expert_w[0].reshape(width_all, per_device, unit_width)
    up_weight = expert_w[1].reshape(width_all, per_device, unit_width)
    down_w = expert_out_w.reshape(per_device, unit_width, width_all)
    grad_layer = out_grad.astype(jnp.float32)
    grad_smid = jnp.einsum("td,fd->tf", out_grad, shared_out_w, preferred_element_type=jnp.float32)
    shared_grads = jnp.concatenate(
        [grad_smid * shared_up * shared_slope, grad_smid * shared_act], axis=1
    ).astype(jnp.bfloat16)
    grad_hidden = jnp.einsum(
        "tf,df->td", shared_grads, shared_w, preferred_element_type=jnp.float32
    )
    grad_shared_w = jnp.einsum(
        "td,tf->df", hidden, shared_grads, preferred_element_type=jnp.float32
    )
    grad_shared_out = jnp.einsum(
        "tf,td->fd", shared_mid, out_grad, preferred_element_type=jnp.float32
    )
    grad_gates = jnp.sum(grad_layer[:, None, :] * pair_out, axis=-1)
    grad_pairs = (
        (gate_values[:, :, None] * grad_layer[:, None, :])
        .reshape(2 * row_count, width_all)
        .astype(jnp.bfloat16)
    )
    grad_pad = jnp.concatenate([grad_pairs, jnp.zeros((1, width_all), jnp.bfloat16)], axis=0)
    grad_recv = lax.all_to_all(
        grad_pad[slot_pair].reshape(blocks_axis, per_device, capacity, width_all),
        "blk",
        split_axis=0,
        concat_axis=0,
        tiled=True,
    )
    grad_expert_middle = jnp.einsum(
        "secd,emd->secm", grad_recv, down_w, preferred_element_type=jnp.float32
    )
    grad_expert_gate_branch = (grad_expert_middle * expert_up_projection * expert_slope).astype(
        jnp.bfloat16
    )
    grad_expert_up_branch = (grad_expert_middle * expert_activation).astype(jnp.bfloat16)
    grad_rows = jnp.einsum(
        "auwj,buj->auwb", grad_expert_gate_branch, gate_weight, preferred_element_type=jnp.float32
    ) + jnp.einsum(
        "auwj,buj->auwb", grad_expert_up_branch, up_weight, preferred_element_type=jnp.float32
    )
    grad_expert_w = jnp.stack(
        [
            jnp.einsum(
                "jgki,jgkt->igt",
                received_rows,
                grad_expert_gate_branch,
                preferred_element_type=jnp.float32,
            ).reshape(width_all, unit_count),
            jnp.einsum(
                "jgki,jgkt->igt",
                received_rows,
                grad_expert_up_branch,
                preferred_element_type=jnp.float32,
            ).reshape(width_all, unit_count),
        ]
    )
    grad_expert_out = jnp.einsum(
        "secm,secd->emd", expert_mid, grad_recv, preferred_element_type=jnp.float32
    ).reshape(unit_count, width_all)
    grad_back = (
        lax.all_to_all(
            grad_rows.astype(jnp.bfloat16), "blk", split_axis=0, concat_axis=0, tiled=True
        )
        .astype(grad_rows.dtype)
        .reshape(slot_count, width_all)
    )
    grad_hidden = grad_hidden + jnp.sum(
        jnp.sum(grad_back[slot_index], axis=0).reshape(row_count, 2, width_all), axis=1
    )
    grad_soft = jnp.sum(jnp.where(route_match, grad_gates[:, :, None], 0.0), axis=1)
    grad_logits = (
        soft_route * (grad_soft - jnp.sum(soft_route * grad_soft, axis=-1, keepdims=True))
    ).astype(jnp.bfloat16)
    grad_hidden = grad_hidden + jnp.einsum(
        "te,ed->td", grad_logits, router_w, preferred_element_type=jnp.float32
    )
    grad_router = jnp.einsum("te,td->ed", grad_logits, hidden, preferred_element_type=jnp.float32)
    grad_norm_two, grad_second_gain = norm_back(residual, second_inverse, second_gain, grad_hidden)
    grad_resid = grad_layer + grad_norm_two
    grad_branch = grad_resid.astype(jnp.bfloat16)
    grad_proj = jnp.einsum("td,te->de", attn_tok, grad_branch, preferred_element_type=jnp.float32)
    grad_attn_tok = jnp.einsum(
        "te,de->td", grad_branch, proj_w, preferred_element_type=jnp.float32
    ).astype(jnp.bfloat16)
    grad_heads = lax.all_to_all(
        grad_attn_tok, "head", split_axis=1, concat_axis=0, tiled=True
    ).reshape(query_rows, local_heads, DH)
    delta = jnp.transpose(jnp.sum(grad_heads * attn_heads, axis=-1))

    def back_step(grad_acc, member):
        visible = prompt_visible(member[2])
        step_query, step_key, step_value = grad_block(
            queries, grad_heads, log_total, delta, member[0], member[1], visible
        )
        return (grad_acc + step_query, (step_key, step_value))

    grad_query, prompt_grads = lax.scan(
        back_step,
        jnp.zeros((query_rows, local_heads, DH), jnp.float32),
        (key_blocks, value_blocks, block_starts),
    )
    local_query, local_key, local_value = grad_block(
        queries, grad_heads, log_total, delta, key_local, value_local, local_visible
    )
    grad_query = grad_query + local_query
    key_share, value_share = (
        lax.psum_scatter(
            prompt_grads[0].reshape(prompt_all, -1), "blk", scatter_dimension=0, tiled=True
        ),
        lax.psum_scatter(
            prompt_grads[1].reshape(prompt_all, -1), "blk", scatter_dimension=0, tiled=True
        ),
    )
    grad_key = (
        local_key.reshape(heads_axis, row_count, -1)
        .at[:, :prompt_dev]
        .add(key_share.reshape(heads_axis, prompt_dev, -1))
        .reshape(query_rows, local_heads, DH)
    )
    grad_value = (
        local_value.reshape(heads_axis, row_count, -1)
        .at[:, :prompt_dev]
        .add(value_share.reshape(heads_axis, prompt_dev, -1))
    )
    head_cos, head_sin = angle_tables(head_pos)
    grad_query = (
        rotate(grad_query, head_cos, -head_sin).reshape(query_rows, -1).astype(jnp.bfloat16)
    )
    grad_key = rotate(grad_key, head_cos, -head_sin).reshape(query_rows, -1).astype(jnp.bfloat16)
    grad_value = grad_value.reshape(query_rows, -1).astype(jnp.bfloat16)
    grad_q_tok, grad_k_tok, grad_v_tok = (
        lax.all_to_all(grad_query, "head", split_axis=0, concat_axis=1, tiled=True),
        lax.all_to_all(grad_key, "head", split_axis=0, concat_axis=1, tiled=True),
        lax.all_to_all(grad_value, "head", split_axis=0, concat_axis=1, tiled=True),
    )
    grad_qkv_rows = jnp.concatenate([grad_q_tok, grad_k_tok, grad_v_tok], axis=1)
    grad_normed = jnp.einsum("tf,df->td", grad_qkv_rows, qkv_w, preferred_element_type=jnp.float32)
    grad_qkv = jnp.einsum("td,tf->df", normed, grad_qkv_rows, preferred_element_type=jnp.float32)
    grad_norm_one, grad_first_gain = norm_back(tokens, first_inverse, first_gain, grad_normed)
    grad_tokens = grad_resid + grad_norm_one
    owned = (
        lax.psum_scatter(
            jnp.stack([grad_first_gain, grad_second_gain]).astype(jnp.bfloat16),
            ("grp", "head"),
            scatter_dimension=1,
            tiled=True,
        ).astype(jnp.float32),
        lax.psum_scatter(
            grad_qkv.astype(jnp.bfloat16), ("grp", "head"), scatter_dimension=1, tiled=True
        ).astype(jnp.float32),
        lax.psum_scatter(
            grad_proj.astype(jnp.bfloat16), ("grp", "head"), scatter_dimension=1, tiled=True
        ).astype(jnp.float32),
        lax.psum_scatter(
            grad_router.astype(jnp.bfloat16), ("grp", "head"), scatter_dimension=1, tiled=True
        ).astype(jnp.float32),
        lax.psum_scatter(
            grad_shared_w.astype(jnp.bfloat16), ("grp", "head"), scatter_dimension=1, tiled=True
        ).astype(jnp.float32),
        lax.psum_scatter(
            grad_shared_out.astype(jnp.bfloat16), ("grp", "head"), scatter_dimension=1, tiled=True
        ).astype(jnp.float32),
        lax.psum_scatter(
            grad_expert_w.astype(jnp.bfloat16), ("grp", "head"), scatter_dimension=1, tiled=True
        ).astype(jnp.float32),
        lax.psum_scatter(
            grad_expert_out.astype(jnp.bfloat16), ("grp", "head"), scatter_dimension=1, tiled=True
        ).astype(jnp.float32),
    )
    summed = lax.psum((owned[0], owned[1], owned[2], owned[3], owned[4], owned[5]), "blk")
    return (
        layer_out,
        grad_tokens,
        summed[0],
        summed[1],
        summed[2],
        summed[3],
        summed[4],
        summed[5],
        owned[6],
        owned[7],
    )


TRANSPOSED = (((1,), (1,)), ((), ()))
PLAIN = (((1,), (0,)), ((), ()))
FIRST = (((0,), (0,)), ((), ()))
FORWARD_VMEM = 14 * 1024 * 1024
BACKWARD_VMEM = 24 * 1024 * 1024
FEW = 32
UNIT_ORDER = (0, 2, 1, 3)


def mm(left, right, dims=PLAIN):
    return lax.dot_general(left, right, dims, preferred_element_type=jnp.float32)


def assemble(rows_ref, cut, parts, prompt_to, cont_to):
    blocks, half = rows_ref.shape[0], rows_ref.shape[1] // 2
    for block in range(blocks):
        for head_part in range(2):
            piece = rows_ref[block, head_part * half : (head_part + 1) * half, :]
            place = (block * 2 + head_part) * half
            for order in range(parts):
                prompt_to[order][place : place + half, :] = piece[
                    :, order * cut : (order + 1) * cut
                ]
                cont_to[order][place : place + half, :] = piece[
                    :, (parts + order) * cut : (parts + order + 1) * cut
                ]


def spread_out(target, prompt_parts, cont_parts, cut):
    blocks, half = target.shape[0], target.shape[1] // 2
    for block in range(blocks):
        for head_part in range(2):
            place = (block * 2 + head_part) * half
            pieces = [part[place : place + half, :] for part in prompt_parts]
            pieces += [part[place : place + half, :] for part in cont_parts]
            target[block, head_part * half : (head_part + 1) * half, :] = jnp.concatenate(
                pieces, axis=1
            ).astype(target.dtype)


def causal_mask(rows):
    keys = lax.broadcasted_iota(jnp.int32, (rows, rows), 0)
    query = lax.broadcasted_iota(jnp.int32, (rows, rows), 1)
    return keys <= query


def cont_mask(rows, cont):
    keys = lax.broadcasted_iota(jnp.int32, (rows, rows), 0)
    query = lax.broadcasted_iota(jnp.int32, (rows, rows), 1)
    return (keys // cont == query // cont) & (keys <= query)


def masked_block(keys, queries, mask):
    scores = mm(keys, queries, TRANSPOSED) * DH ** (-0.5)
    if mask is None:
        return scores
    return jnp.where(mask, scores, NEGATIVE)


def attention_kernel(rows_ref, out_ref, qp, kp, vp, qc, kc, vc, op, oc):
    block = 256
    prompt = qp.shape[0]
    assemble(rows_ref, DH, 3, (qp, kp, vp), (qc, kc, vc))
    cont = rows_ref.shape[1]
    for is_cont in range(2):
        source_q, source_k, source_v, result = (
            (qc, kc, vc, oc) if is_cont else (qp, kp, vp, op)
        )
        mask = cont_mask(block, cont) if is_cont else causal_mask(block)
        for step in range(prompt // block):
            rows = slice(step * block, (step + 1) * block)
            queries = source_q[rows, :]
            own = masked_block(source_k[rows, :], queries, mask)
            seen = prompt if is_cont else step * block
            peak = jnp.max(own, axis=0, keepdims=True)
            if seen:
                past = masked_block(kp[0:seen, :], queries, None)
                peak = jnp.maximum(peak, jnp.max(past, axis=0, keepdims=True))
            own = jnp.exp(own - peak)
            total = jnp.sum(own, axis=0, keepdims=True)
            gathered = mm(source_v[rows, :], own.astype(jnp.bfloat16), FIRST)
            if seen:
                past = jnp.exp(past - peak)
                total = total + jnp.sum(past, axis=0, keepdims=True)
                gathered = gathered + mm(vp[0:seen, :], past.astype(jnp.bfloat16), FIRST)
            result[rows, :] = jnp.transpose(gathered / total)
    spread_out(out_ref, (op,), (oc,), DH)


def attention_forward(rows):
    blocks, both, _ = rows.shape
    prompt = blocks * both
    small = pltpu.VMEM((prompt, DH), jnp.bfloat16)
    wide = pltpu.VMEM((prompt, DH), jnp.float32)
    return pl.pallas_call(
        attention_kernel,
        out_shape=jax.ShapeDtypeStruct((blocks, both, 2 * DH), jnp.bfloat16),
        in_specs=[pl.BlockSpec(memory_space=pltpu.VMEM)],
        out_specs=pl.BlockSpec(memory_space=pltpu.VMEM),
        scratch_shapes=[small] * 6 + [wide] * 2,
        compiler_params=pltpu.CompilerParams(vmem_limit_bytes=FORWARD_VMEM),
        cost_estimate=pl.CostEstimate(
            flops=2**20, bytes_accessed=2**16, transcendentals=0
        ),
        name="attention_forward",
    )(rows)


def turn_back(values, cosine, sine):
    half = DH // 2
    first, second = values[:, :half], values[:, half:]
    return jnp.concatenate(
        [first * cosine + second * sine, second * cosine - first * sine], axis=1
    )


def attention_back_kernel(
    rows_ref, grad_ref, table_ref, out_ref,
    qp, kp, vp, qc, kc, vc, gp, gc, dqp, dkp, dvp, dqc, dkc, dvc,
):
    block = 256
    prompt = qp.shape[0]
    scale = DH ** (-0.5)
    assemble(rows_ref, DH, 3, (qp, kp, vp), (qc, kc, vc))
    assemble(grad_ref, DH, 1, (gp,), (gc,))
    cont = rows_ref.shape[1]
    dkp[...] = jnp.zeros_like(dkp)
    dvp[...] = jnp.zeros_like(dvp)
    for is_cont in range(2):
        source_q, source_k, source_v, source_g = (
            (qc, kc, vc, gc) if is_cont else (qp, kp, vp, gp)
        )
        to_q, to_k, to_v = (dqc, dkc, dvc) if is_cont else (dqp, dkp, dvp)
        mask = cont_mask(block, cont) if is_cont else causal_mask(block)
        for step in range(prompt // block):
            rows = slice(step * block, (step + 1) * block)
            queries = source_q[rows, :]
            grads = source_g[rows, :]
            own_keys = source_k[rows, :]
            own = masked_block(own_keys, queries, mask)
            seen = prompt if is_cont else step * block
            peak = jnp.max(own, axis=0, keepdims=True)
            if seen:
                past = masked_block(kp[0:seen, :], queries, None)
                peak = jnp.maximum(peak, jnp.max(past, axis=0, keepdims=True))
            own = jnp.exp(own - peak)
            total = jnp.sum(own, axis=0, keepdims=True)
            if seen:
                past = jnp.exp(past - peak)
                total = total + jnp.sum(past, axis=0, keepdims=True)
            inverse = 1.0 / total
            own = own * inverse
            own_grad = mm(source_v[rows, :], grads, TRANSPOSED)
            delta = jnp.sum(own * own_grad, axis=0, keepdims=True)
            if seen:
                past = past * inverse
                past_grad = mm(vp[0:seen, :], grads, TRANSPOSED)
                delta = delta + jnp.sum(past * past_grad, axis=0, keepdims=True)
            own_scores = (own * (own_grad - delta)).astype(jnp.bfloat16)
            own_dv = mm(own.astype(jnp.bfloat16), grads)
            own_dk = mm(own_scores, queries) * scale
            turned = mm(own_keys, own_scores, FIRST)
            if is_cont:
                to_v[rows, :] = own_dv
                to_k[rows, :] = own_dk
            else:
                to_v[rows, :] += own_dv
                to_k[rows, :] += own_dk
            if seen:
                past_scores = (past * (past_grad - delta)).astype(jnp.bfloat16)
                dvp[0:seen, :] += mm(past.astype(jnp.bfloat16), grads)
                dkp[0:seen, :] += mm(past_scores, queries) * scale
                turned = turned + mm(kp[0:seen, :], past_scores, FIRST)
            to_q[rows, :] = jnp.transpose(turned) * scale
    turn = DH // 2
    cos_p, sin_p = table_ref[0:prompt, :turn], table_ref[0:prompt, turn:]
    dqp[...] = turn_back(dqp[...], cos_p, sin_p)
    dkp[...] = turn_back(dkp[...], cos_p, sin_p)
    for step in range(prompt // cont):
        rows = slice(step * cont, (step + 1) * cont)
        cos_c = table_ref[prompt : prompt + cont, :turn]
        sin_c = table_ref[prompt : prompt + cont, turn:]
        dqc[rows, :] = turn_back(dqc[rows, :], cos_c, sin_c)
        dkc[rows, :] = turn_back(dkc[rows, :], cos_c, sin_c)
    spread_out(out_ref, (dqp, dkp, dvp), (dqc, dkc, dvc), DH)


def attention_backward(rows, grads, table):
    blocks, both, wide = rows.shape
    prompt = blocks * both
    small = pltpu.VMEM((prompt, DH), jnp.bfloat16)
    large = pltpu.VMEM((prompt, DH), jnp.float32)
    return pl.pallas_call(
        attention_back_kernel,
        out_shape=jax.ShapeDtypeStruct((blocks, both, wide), jnp.bfloat16),
        in_specs=[pl.BlockSpec(memory_space=pltpu.VMEM)] * 3,
        out_specs=pl.BlockSpec(memory_space=pltpu.VMEM),
        scratch_shapes=[small] * 8 + [large] * 6,
        compiler_params=pltpu.CompilerParams(vmem_limit_bytes=BACKWARD_VMEM),
        cost_estimate=pl.CostEstimate(
            flops=2**20, bytes_accessed=2**16, transcendentals=0
        ),
        name="attention_backward",
    )(rows, grads, table)


def exchange(values, axis, mask):
    return lax.ppermute(values, axis, [(i, i ^ mask) for i in range(lax.axis_size(axis))])


def to_member(values, number):
    if number == 2:
        return exchange(values, "grp", 1)
    if number == 1:
        return exchange(values, "head", 1)
    return lax.ppermute(values, ("grp", "head"), [(i, i ^ number) for i in range(4)])


def tie(values, *after):
    return lax.optimization_barrier((values, *after))[0]


def padded_bytes(shape, kind):
    shape = (1,) * (2 - len(shape)) + tuple(shape)
    rows, lanes = -(-shape[-2] // 16) * 16, -(-shape[-1] // 128) * 128
    return math.prod(shape[:-2]) * rows * lanes * jnp.dtype(kind).itemsize


def kernel_call(body_of, outs, scratch, name, *inputs, room=6, alone=False, flops=2**20):
    held = [*outs, *scratch, *((one.shape, one.dtype) for one in inputs)]
    limit = sum(padded_bytes(*one) for one in held) + room * 2**20
    limit = 56 * 2**20 if alone else limit
    spec = pl.BlockSpec(memory_space=pltpu.VMEM)
    return pl.pallas_call(
        body_of,
        out_shape=[jax.ShapeDtypeStruct(*out) for out in outs],
        in_specs=[
            pl.BlockSpec(memory_space=pltpu.SMEM) if one.dtype == jnp.int32 else spec
            for one in inputs
        ],
        out_specs=[spec] * len(outs),
        scratch_shapes=[pltpu.VMEM(*one) for one in scratch],
        compiler_params=pltpu.CompilerParams(vmem_limit_bytes=limit),
        cost_estimate=pl.CostEstimate(flops=flops, bytes_accessed=2**16, transcendentals=0),
        name=name,
    )(*inputs)


def move_all(copies, sems):
    started = [
        pltpu.make_async_copy(source, target, sems.at[number])
        for number, (source, target) in enumerate(copies)
    ]
    for one in started:
        one.start()
    for one in started:
        one.wait()


def first_kernel(place, qkv_ref, few_ref, proj_ref, own_ref, *refs):
    given, sems = refs[0:3], refs[3]
    six = own_ref.shape[0]
    start, small = six // 2, few_ref.shape[0]
    half = given[0].shape[0] - start - small
    middle = (place[5] + place[4]) % 2
    shift = qkv_ref.shape[0] - six
    copies = []
    for j in range(4):
        window = ((middle + place[4] + j) % 2) * shift
        if j == 0:
            copies.append((qkv_ref.at[pl.ds(pl.multiple_of(window, 64), six), :], own_ref))
            continue
        at = pl.multiple_of(window + place[1] * start, 64)
        target = given[j - 1]
        copies.append((qkv_ref.at[pl.ds(at, start), :], target.at[pl.ds(0, start), :]))
        copies.append((few_ref, target.at[pl.ds(start, small), :]))
        copies.append(
            (
                proj_ref.at[pl.ds(pl.multiple_of(place[1] * half, 16), half), :],
                target.at[pl.ds(start + small, half), :],
            )
        )
    move_all(copies, sems)


def rest_kernel(place, wide_ref, shared_down_ref, both_ref, down_ref, *refs):
    outs, held, sems, out_sems = refs[0:9], refs[9:18], refs[18], refs[19]
    piece_ref, pairs, downs = held[0], held[1:5], held[5:9]
    width, span = wide_ref.shape[0], piece_ref.shape[1]
    quarter, units = downs[0].shape
    four = place[3] % 4
    copies = []
    for j in range(4):
        at = pl.ds(pl.multiple_of((place[6] ^ UNIT_ORDER[j]) * units, 128), units)
        copies.append((both_ref.at[0, :, at], pairs[j].at[0]))
        copies.append((both_ref.at[1, :, at], pairs[j].at[1]))
        copies.append((down_ref.at[:, at], downs[j]))
    at = pl.ds(pl.multiple_of(four * span, 128), span)
    copies.append((wide_ref.at[:, at], piece_ref.at[pl.ds(0, width), :]))
    copies.append((shared_down_ref.at[:, at], piece_ref.at[pl.ds(width, quarter), :]))
    at = pl.ds(pl.multiple_of((4 + four) * span, 128), span)
    copies.append((shared_down_ref.at[:, at], piece_ref.at[pl.ds(width + quarter, quarter), :]))
    move_all(copies, sems)
    move_all(list(zip(held, outs)), out_sems)


def copy_call(body_of, outs, count, name, place, *inputs, through=False):
    held = [pltpu.VMEM(shape, jnp.bfloat16) for shape in outs] if through else []
    sems = [pltpu.SemaphoreType.DMA((count,))]
    if through:
        sems.append(pltpu.SemaphoreType.DMA((len(outs),)))
    return pl.pallas_call(
        body_of,
        out_shape=[jax.ShapeDtypeStruct(shape, jnp.bfloat16) for shape in outs],
        in_specs=[pl.BlockSpec(memory_space=pltpu.SMEM)]
        + [pl.BlockSpec(memory_space=pl.ANY)] * len(inputs),
        out_specs=[pl.BlockSpec(memory_space=pl.ANY)] * len(outs),
        scratch_shapes=held + sems,
        compiler_params=pltpu.CompilerParams(vmem_limit_bytes=(56 if through else 1) * 2**20),
        cost_estimate=pl.CostEstimate(flops=2**20, bytes_accessed=2**16, transcendentals=0),
        name=name,
    )(place, *inputs)


def packed(rows):
    count, width = rows.shape
    blocks = count // 20
    last = rows[16 * blocks :]
    half = width // 2
    return jnp.concatenate(
        [
            rows[: 8 * blocks].reshape(blocks, 8, width),
            rows[8 * blocks : 16 * blocks].reshape(blocks, 8, width),
            jnp.concatenate(
                [last[:, :half].reshape(blocks, 4, half), last[:, half:].reshape(blocks, 4, half)],
                axis=1,
            ),
        ],
        axis=2,
    )


def unpack_to(target, at, source_ref):
    blocks = source_ref.shape[0]
    width = target.shape[1]
    half = width // 2
    target[at : at + 8 * blocks, :] = source_ref[:, :, 0:width].reshape(8 * blocks, width)
    target[at + 8 * blocks : at + 16 * blocks, :] = source_ref[:, :, width : 2 * width].reshape(
        8 * blocks, width
    )
    for block in range(blocks):
        place = at + 16 * blocks + 4 * block
        last = source_ref[block, :, 2 * width :]
        target[place : place + 4, 0:half] = last[0:4]
        target[place : place + 4, half:width] = last[4:8]


def pack_kernel(rows_ref, out_ref):
    out_ref[...] = packed(rows_ref[...].astype(jnp.float32)).astype(jnp.bfloat16)


def join_kernel(own_ref, part_ref, out_ref):
    rows = own_ref[...] + part_ref[...].astype(jnp.float32)
    out_ref[...] = packed(rows).astype(jnp.bfloat16)


def layer_kernel(got_ref, pick_ref, residual_ref, shared_ref, out_ref, rows):
    unpack_to(rows, 0, got_ref)
    out_ref[...] = (
        residual_ref[...] + shared_ref[...] + mm(pick_ref[...], rows[...], FIRST)
    ).astype(jnp.bfloat16)


def qkv_kernel(place, tokens_ref, partner_ref, table_ref, window_ref, few_ref, *refs):
    got, passed = refs[0:3], refs[3:6]
    normed_ref, rows_ref, gains_ref, router_ref, weight_ref, window, few, both = refs[6:]
    quad_me, core, head = place[0], place[1], place[4]
    rows, width = tokens_ref.shape
    half, quarter = rows // 2, width // 4
    per = window.shape[1] // 2
    window[quad_me] = window_ref[...]
    few[quad_me] = few_ref[...].astype(jnp.float32)
    for j in (1, 2, 3):
        k = quad_me ^ j
        few[k] = got[j - 1][per : per + 16, :].astype(jnp.float32)
        window[k, pl.ds(pl.multiple_of(core * per, 64), per), :] = got[j - 1][0:per, :]
        window[k, pl.ds(pl.multiple_of((1 - core) * per, 64), per), :] = passed[j - 1][0:per, :]
    span = 2 * per

    @pl.when(head == 0)
    def _():
        weight_ref[0:span, :] = window[0]
        weight_ref[span : 2 * span, :] = window[1]
        weight_ref[2 * span : 2 * span + per, :] = window[2, per:span, :]
        weight_ref[2 * span + per : 3 * span, :] = window[3, 0:per, :]

    @pl.when(head == 1)
    def _():
        weight_ref[0:per, :] = window[0, per:span, :]
        weight_ref[per:span, :] = window[1, 0:per, :]
        weight_ref[span : 2 * span, :] = window[2]
        weight_ref[2 * span : 3 * span, :] = window[3]

    def few_row(number):
        part, row = divmod(number, 5)
        return jnp.concatenate(
            [few[k, row : row + 1, part * quarter : (part + 1) * quarter] for k in range(4)],
            axis=1,
        )

    gains = jnp.concatenate([few_row(0), few_row(1)], axis=0)
    gains_ref[...] = gains
    router_ref[...] = jnp.concatenate(
        [few_row(2 + e) for e in range(EXPERTS)], axis=0
    ).astype(jnp.bfloat16)
    for where, source in ((head, tokens_ref), (1 - head, partner_ref)):
        tokens = source[...].astype(jnp.float32)
        both[where] = norm_rows(tokens, gains[0:1])[0].astype(jnp.bfloat16)
    normed = both[...].reshape(2 * rows, width)
    normed_ref[...] = normed
    mixed = mm(normed, weight_ref[...], TRANSPOSED)
    turn = DH // 2
    table = []
    for part in range(2):
        table.append(table_ref[pl.ds(pl.multiple_of((2 * place[3] + part) * half, 64), half), :])
        at = table_ref.shape[0] - 2 * half + part * half
        table.append(table_ref[at : at + half, :])
    table = jnp.concatenate(table, axis=0)
    cosine, sine = table[:, :turn], table[:, turn:]
    heads = HEADS // 2

    def chunk(number):
        return mixed[:, number * DH : (number + 1) * DH]

    rows_ref[...] = jnp.zeros_like(rows_ref)
    for one in range(heads):
        pieces = [
            turn_back(chunk(one), cosine, -sine),
            turn_back(chunk(heads + one), cosine, -sine),
            chunk(2 * heads + one),
        ]
        for part in range(2):
            at = part * rows
            rows_ref[one, part * half : (part + 1) * half, :] = jnp.concatenate(
                [piece[at : at + half] for piece in pieces]
                + [piece[at + half : at + rows] for piece in pieces],
                axis=1,
            ).astype(jnp.bfloat16)


def hidden_kernel(place, got_ref, partner_ref, tokens_ref, gains_ref, pick_ref, mine_ref, *refs):
    own, other = refs[0:3], refs[3:6]
    residual_ref, hidden_ref, attn_ref, sent_ref, proj_ref, attn = refs[6:]
    head = place[4]
    rows, width = tokens_ref.shape
    half = rows // 2
    per, start = proj_ref.shape[1], own[0].shape[0] - proj_ref.shape[1]
    for part in range(2):
        proj_ref[place[0] * 2 + part] = mine_ref[part * per : (part + 1) * per, :]
    for j in (1, 2, 3):
        for where, source in ((place[1], own[j - 1]), (1 - place[1], other[j - 1])):
            proj_ref[(place[0] ^ j) * 2 + where] = source[start : start + per, :]
    for one in range(HEADS // 2):
        at = slice(one * DH, (one + 1) * DH)
        mine = got_ref[one, pl.ds(pl.multiple_of(head * half, 64), half), :]
        for where, piece in ((head, mine), (1 - head, partner_ref[one])):
            attn[where, 0:half, at] = piece[:, 0:DH]
            attn[where, half:rows, at] = piece[:, DH : 2 * DH]
    attn_all = jnp.concatenate([attn[0], attn[1]], axis=1)
    attn_ref[...] = attn_all
    residual = tokens_ref[...].astype(jnp.float32) + mm(
        attn_all, proj_ref[...].reshape(width, width), TRANSPOSED
    )
    residual_ref[...] = residual
    hidden = norm_rows(residual, gains_ref[1:2, :])[0].astype(jnp.bfloat16)
    hidden_ref[...] = hidden
    sent_ref[...] = packed(mm(pick_ref[...], hidden)).astype(jnp.bfloat16)


def expert_kernel(place, own_ref, other_ref, own_grad, other_grad, router_ref, *refs):
    pairs, downs = refs[0:4], refs[4:8]
    (
        g_own, g_part, e_own, e_part, egate_ref, eup_ref, mid_ref, eout_ref, g_router_ref,
        rows_ref, gate_w, up_w, down_w, grad_ref,
    ) = refs[8:]
    quad_me, expert_me = place[0], place[2]
    half_count = rows_ref.shape[0] // 2
    unpack_to(rows_ref, 0, own_ref)
    unpack_to(rows_ref, half_count, other_ref)
    unpack_to(grad_ref, 0, own_grad)
    unpack_to(grad_ref, half_count, other_grad)
    quarter = downs[0].shape[0]
    for j in range(4):
        at = pl.ds(pl.multiple_of((quad_me ^ j) * quarter, 64), quarter)
        gate_w[at, :] = pairs[j][0]
        up_w[at, :] = pairs[j][1]
        down_w[at, :] = downs[j][...]
    count = rows_ref.shape[0]
    block = count // 4
    router = router_ref[...]
    mine = lax.broadcasted_iota(jnp.int32, (block, EXPERTS), 1) == expert_me
    mine = mine.astype(jnp.float32)
    g_router = jnp.zeros_like(g_router_ref)
    for step in range(4):
        at = slice(step * block, (step + 1) * block)
        rows, grads = rows_ref[at, :], grad_ref[at, :]
        logits = mm(rows, router, TRANSPOSED)
        logits = jnp.exp(logits - jnp.max(logits, axis=1, keepdims=True))
        soft = logits / jnp.sum(logits, axis=1, keepdims=True)
        gate = jnp.sum(soft * mine, axis=1, keepdims=True)
        e_up = mm(rows, up_w[...])
        e_act, e_slope = swish_parts(mm(rows, gate_w[...]))
        e_mid = e_act * e_up
        e_grad = mm(grads, down_w[...])
        g_gate = jnp.sum(e_mid * e_grad, axis=1, keepdims=True)
        g_mid = e_grad * gate
        egate = (g_mid * e_up * e_slope).astype(jnp.bfloat16)
        eup = (g_mid * e_act).astype(jnp.bfloat16)
        e_mid = e_mid.astype(jnp.bfloat16)
        g_logits = (g_gate * soft * (mine - gate)).astype(jnp.bfloat16)
        g_rows = (
            mm(egate, gate_w[...], TRANSPOSED)
            + mm(eup, up_w[...], TRANSPOSED)
            + mm(g_logits, router)
        )
        e_rows = gate * mm(e_mid, down_w[...], TRANSPOSED)
        if step < 2:
            g_own[at, :] = g_rows
            e_own[at, :] = e_rows
        else:
            there = slice((step - 2) * block, (step - 1) * block)
            g_part[there, :] = g_rows.astype(jnp.bfloat16)
            e_part[there, :] = e_rows.astype(jnp.bfloat16)
        egate_ref[at, :] = egate
        eup_ref[at, :] = eup
        mid_ref[at, :] = e_mid
        eout_ref[at, :] = (gate * grads.astype(jnp.float32)).astype(jnp.bfloat16)
        g_router = g_router + mm(g_logits, rows, FIRST)
    g_router_ref[...] = g_router


def expert_weight_kernel(place, rows_ref, eout_ref, egate_ref, eup_ref, mid_ref, *refs):
    pairs, downs, whole, turned = refs[0:4], refs[4:8], refs[8], refs[9]
    quarter = downs[0].shape[0]
    turned[...] = jnp.transpose(rows_ref[...])
    for number, right in enumerate((egate_ref, eup_ref, mid_ref)):
        if number == 2:
            turned[...] = jnp.transpose(eout_ref[...])
        whole[...] = mm(turned[...], right[...]).astype(jnp.bfloat16)
        for j in range(4):
            at = pl.ds(pl.multiple_of((place[0] ^ j) * quarter, 64), quarter)
            if number == 2:
                downs[j][...] = whole[at, :]
            else:
                pairs[j][number] = whole[at, :]


def branch_kernel(
    place, got_ref, pick_ref, shared_ref, residual_ref, gains_ref, grad_ref, proj_ref,
    resid_ref, branch_ref, mine_ref, theirs_ref, gain_ref, back, heads,
):
    rows, width = grad_ref.shape
    unpack_to(back, 0, got_ref)
    g_hidden = mm(pick_ref[...], back[...], FIRST) + shared_ref[...].astype(jnp.float32)
    residual = residual_ref[...]
    gain = gains_ref[1:2, :]
    inverse = norm_rows(residual, gain)[1]
    g_norm, g_gain = norm_back(residual, inverse, gain, g_hidden)
    gain_ref[...] = g_gain[None]
    g_resid = grad_ref[...].astype(jnp.float32) + g_norm
    resid_ref[...] = g_resid
    branch = g_resid.astype(jnp.bfloat16)
    branch_ref[...] = branch
    attn = mm(branch, proj_ref[...].reshape(width, width)).astype(jnp.bfloat16)
    half = rows // 2
    for one in range(HEADS):
        piece = attn[:, one * DH : (one + 1) * DH]
        heads[one // (HEADS // 2), one % (HEADS // 2)] = jnp.concatenate(
            [piece[:half], piece[half:]], axis=1
        )
    mine_ref[...] = heads[place[4]]
    theirs_ref[...] = heads[1 - place[4]]


def tokens_kernel(
    place, got_ref, qkv_ref, tokens_ref, partner_ref, mine_ref, theirs_ref, gain_ref, parts, grads
):
    half = got_ref.shape[1] // 2
    rows = 2 * half
    heads = HEADS // 2
    for one in range(heads):
        for part in range(2):
            piece = got_ref[one, part * half : (part + 1) * half, :]
            at = part * rows
            for kind in range(3):
                there = slice((kind * heads + one) * DH, (kind * heads + one + 1) * DH)
                parts[at : at + half, there] = piece[:, kind * DH : (kind + 1) * DH]
                parts[at + half : at + rows, there] = piece[:, (3 + kind) * DH : (4 + kind) * DH]
    g_normed = mm(parts[...], qkv_ref[...])
    grads[0] = g_normed[:rows]
    grads[1] = g_normed[rows:]
    mine_ref[...] = grads[place[4]]
    theirs_ref[...] = grads[1 - place[4]].astype(jnp.bfloat16)
    gain = 0.0
    for source, where in ((tokens_ref, place[4]), (partner_ref, 1 - place[4])):
        tokens = source[...].astype(jnp.float32)
        inverse = norm_rows(tokens, 1.0)[1]
        gain = gain + jnp.sum(grads[where] * tokens * inverse, axis=0, keepdims=True)
    gain_ref[...] = gain


def tokens_out_kernel(mine_ref, partner_ref, tokens_ref, gains_ref, resid_ref, out_ref):
    g_normed = mine_ref[...] + partner_ref[...].astype(jnp.float32)
    tokens = tokens_ref[...].astype(jnp.float32)
    gain = gains_ref[0:1, :]
    inverse = norm_rows(tokens, gain)[1]
    out_ref[...] = resid_ref[...] + norm_back(tokens, inverse, gain, g_normed)[0]


def head_weight_kernel(rows_ref, normed_ref, out_ref, left):
    blocks, both, wide = rows_ref.shape
    half = both // 2
    for block in range(blocks):
        for part in range(2):
            at = (block * 2 + part) * both
            piece = rows_ref[block, part * half : (part + 1) * half, :]
            left[at : at + half, :] = piece[:, 0 : wide // 2]
            left[at + half : at + both, :] = piece[:, wide // 2 : wide]
    right = normed_ref[...].reshape(2 * both * blocks, normed_ref.shape[2])
    out_ref[...] = mm(left[...], right, FIRST).astype(jnp.bfloat16)


def chunk_kernel(order, got_ref, out_ref, few_ref):
    few = jnp.zeros_like(few_ref)
    for source in range(got_ref.shape[0]):
        few = few + got_ref[source, 2 * DH : 2 * DH + FEW, :].astype(jnp.float32)
    few_ref[...] = few
    for number in range(order.shape[0]):
        which = order[number]
        at = pl.ds(pl.multiple_of(which % 2 * DH, DH), DH)
        out_ref[number * DH : (number + 1) * DH, :] = got_ref[which // 2, at, :].astype(
            jnp.float32
        )


def shared_kernel(place, *refs):
    hidden_refs, grads_refs, pieces = refs[0:4], refs[4:8], refs[8:12]
    out_ref, back_ref = refs[12:14]
    given = refs[14:18]
    both_w, down_w, g_both, g_down = refs[18:]
    quad_me = place[0]
    width, span = both_w.shape[0], both_w.shape[1] // 4
    quarter = width // 4
    block = hidden_refs[0].shape[0]
    for j in range(4):
        k = quad_me ^ j
        both_w[:, pl.ds(pl.multiple_of(k * span, 128), span)] = pieces[j][0:width, :]
        at = pl.ds(pl.multiple_of(k * quarter, 64), quarter)
        down_w[at, 0:span] = pieces[j][width : width + quarter, :]
        down_w[at, span : 2 * span] = pieces[j][width + quarter : width + 2 * quarter, :]
    for step in range(2):
        rows = slice(step * 2 * block, (step + 1) * 2 * block)
        hidden = jnp.concatenate([hidden_refs[2 * step][...], hidden_refs[2 * step + 1][...]])
        grads = jnp.concatenate([grads_refs[2 * step][...], grads_refs[2 * step + 1][...]])
        pre = mm(hidden, both_w[...])
        act, slope = swish_parts(pre[:, : 2 * span])
        up = pre[:, 2 * span :]
        mid = (act * up).astype(jnp.bfloat16)
        out_ref[rows, :] = mm(mid, down_w[...], TRANSPOSED).astype(jnp.bfloat16)
        g_mid = mm(grads, down_w[...])
        g_pre = jnp.concatenate([g_mid * up * slope, g_mid * act], axis=1).astype(jnp.bfloat16)
        back_ref[rows, :] = mm(g_pre, both_w[...], TRANSPOSED).astype(jnp.bfloat16)
        new_both = mm(hidden, g_pre, FIRST)
        new_down = mm(grads, mid, FIRST)
        if step == 0:
            g_both[...] = new_both
            g_down[...] = new_down
        else:
            g_both[...] += new_both
            g_down[...] += new_down
    for j in range(4):
        k = quad_me ^ j
        at = pl.ds(pl.multiple_of(k * quarter, 64), quarter)
        given[j][0:width, :] = g_both[:, pl.ds(pl.multiple_of(k * span, 128), span)].astype(
            jnp.bfloat16
        )
        given[j][width : width + quarter, :] = g_down[at, 0:span].astype(jnp.bfloat16)
        given[j][width + quarter : width + 2 * quarter, :] = g_down[at, span : 2 * span].astype(
            jnp.bfloat16
        )


def shared_out_kernel(place, *refs):
    parts, wide_ref, down_ref, proj_ref = refs[0:4], refs[4], refs[5], refs[6]
    width, span = wide_ref.shape[0], parts[0].shape[1]
    quarter = down_ref.shape[0]
    last, per = width + 2 * quarter, quarter // 4
    for j in range(4):
        k = (place[3] % 4) ^ j
        at = pl.ds(pl.multiple_of(k * span, 128), span)
        wide_ref[:, at] = parts[j][0:width, :].astype(jnp.float32)
        down_ref[:, at] = parts[j][width : width + quarter, :].astype(jnp.float32)
        at = pl.ds(pl.multiple_of((4 + k) * span, 128), span)
        down_ref[:, at] = parts[j][width + quarter : last, :].astype(jnp.float32)
        at = pl.ds(pl.multiple_of(k * per, 16), per)
        for i in range(width // span):
            proj_ref[at, i * span : (i + 1) * span] = parts[j][
                last + i * per : last + (i + 1) * per, :
            ].astype(jnp.float32)


def units_out_kernel(place, *refs):
    parts, out_ref = refs[:-1], refs[-1]
    units = parts[0].shape[-1]
    for j in range(4):
        at = pl.ds(pl.multiple_of((place[6] ^ UNIT_ORDER[j]) * units, 128), units)
        if len(out_ref.shape) == 3:
            out_ref[0, :, at] = parts[j][0].astype(jnp.float32)
            out_ref[1, :, at] = parts[j][1].astype(jnp.float32)
        else:
            out_ref[:, at] = parts[j][...].astype(jnp.float32)


def quick_body(
    tokens_in,
    norm_gains,
    attn_qkv,
    attn_proj,
    router_rows,
    shared_gate_up,
    shared_down,
    expert_gate_up,
    expert_down,
    routes,
    out_grad,
):
    quad = ("grp", "head")
    line = ("head", "blk")
    blocks = lax.axis_size("blk")
    rows, width = tokens_in.shape
    grp, head, blk = lax.axis_index("grp"), lax.axis_index("head"), lax.axis_index("blk")
    core = blk % 2
    quarter = width // 4
    prompt_dev = max(PROMPT_ROWS, PROMPT_LEAST // (2 * blocks))
    prompt = prompt_dev * 2 * blocks
    cont = 2 * (rows - prompt_dev)
    bf16, f32 = jnp.bfloat16, jnp.float32

    member = 2 * grp + head
    unit_me = 2 * head + grp
    place = jnp.stack([member, core, 2 * blk + head, blk, head, grp, unit_me])
    third = attn_qkv.shape[1]
    few = jnp.concatenate([norm_gains, router_rows], axis=0)
    few = jnp.pad(few, ((0, 20 - few.shape[0]), (0, 0)))
    few = jnp.concatenate([few[5 * i : 5 * i + 5] for i in range(4)], axis=1)
    few = jnp.pad(few, ((0, 11), (0, 0)))
    six = width // 2
    own_window, *window_parts = copy_call(
        first_kernel,
        [(six, width)] + [(six // 2 + 16 + quarter // 2, width)] * 3,
        10,
        "first_parts",
        place, attn_qkv.T, few, attn_proj.T,
    )
    partner_tokens = exchange(tokens_in, "head", 1)
    own_w = [to_member(window_parts[j - 1], j) for j in (1, 2, 3)]
    other_w = [exchange(part, "blk", 1) for part in own_w]

    span = SFF // 2 // 4
    four = blk % 4
    units = expert_gate_up.shape[2] // 4
    piece, *unit_parts = copy_call(
        rest_kernel,
        [(width + 2 * quarter, span)] + [(2, quarter, units)] * 4 + [(quarter, units)] * 4,
        15,
        "rest_parts",
        place, shared_gate_up, shared_down.T, expert_gate_up, expert_down.T,
        through=True,
    )
    pair_send, down_send = unit_parts[0:4], unit_parts[4:8]

    def of_four(values):
        far = exchange(values, "blk", 2)
        return [values, exchange(values, "blk", 1), far, exchange(far, "blk", 1)]

    def sum_of_four(parts):
        near = exchange(jnp.stack([parts[1], parts[3]]), "blk", 1)
        far = (parts[2].astype(f32) + near[1].astype(f32)).astype(bf16)
        return parts[0].astype(f32) + near[0].astype(f32) + exchange(far, "blk", 2).astype(f32)

    def joined(own, part):
        return (own.astype(f32) + part.astype(f32)).astype(bf16)

    def fetched(parts, after, *numbers):
        for j in numbers:
            parts[j] = to_member(tie(parts[j], after), j)

    expert_ids = jnp.arange(EXPERTS, dtype=jnp.int32)
    match = (routes[:, :, None] == expert_ids).astype(jnp.int32)
    flat = match.reshape(2 * rows, EXPERTS)
    rank = (jnp.sum(jnp.cumsum(flat, axis=0) * flat, axis=1) - 1).reshape(rows, 2)
    slots_all = 2 * blocks
    target = routes % 2 * blocks + routes // 2
    slots = jnp.where(
        rank < 16,
        rank // 8 * (8 * slots_all) + target * 8 + rank % 8,
        16 * slots_all + target * 4 + rank - 16,
    )
    per_half = 20 * slots_all
    slot_ids = jnp.arange(per_half, dtype=jnp.int32)[:, None]
    pick = ((slot_ids == slots[:, 0]) | (slot_ids == slots[:, 1])).astype(bf16)
    pack_shape = (slots_all, 8, 5 * width // 2)

    def over_line(values):
        return lax.all_to_all(values, line, 0, 0, tiled=True)

    def over_blocks(values):
        return lax.all_to_all(values, "blk", 0, 0, tiled=True)

    grad_sent = kernel_call(
        pack_kernel, [(pack_shape, bf16)], [], "pack_rows", mm(pick, tie(out_grad, own_w[0])).astype(bf16)
    )[0]
    grad_own = over_line(grad_sent)
    four_grads = of_four(out_grad)

    wait = lax.optimization_barrier
    own_w, other_w, partner_tokens, pair_send, down_send, piece = wait(
        (own_w, other_w, partner_tokens, pair_send, down_send, piece)
    )
    shared_parts = [piece] * 4
    steps = np.arange(DH // 2, dtype=np.float32)
    rates = np.power(np.float32(10000.0), np.float32(-2.0) * steps / np.float32(DH))
    angles = np.arange(prompt + cont, dtype=np.float32)[:, None] * rates[None, :].astype(np.float32)
    table = jnp.asarray(
        np.concatenate([np.cos(angles), np.sin(angles)], axis=1).astype(np.float32)
    )
    normed, head_send, gains, router_w, qkv_w = kernel_call(
        qkv_kernel,
        [
            ((2 * rows, width), bf16),
            ((blocks, rows, 6 * DH), bf16),
            ((2, width), f32),
            ((EXPERTS, width), bf16),
            ((3 * six, width), bf16),
        ],
        [((4, six, width), bf16), ((4, 16, width), f32), ((2, rows, width), bf16)],
        "qkv_rows",
        place, tokens_in, partner_tokens, table, own_window, few, *own_w, *other_w,
        alone=True,
    )
    head_send, grad_own = wait((head_send, grad_own))
    head_rows = over_blocks(head_send)
    fetched(pair_send, head_send, 1, 2)
    head_rows, pair_send = wait((head_rows, pair_send))
    attn_heads = attention_forward(head_rows)
    fetched(pair_send, head_rows, 3)
    attn_got = over_blocks(attn_heads)
    all_normed = lax.all_gather(tie(normed, attn_heads), "blk", axis=0)
    fetched(shared_parts, attn_heads, 1, 2)
    grad_other = exchange(tie(grad_own, attn_heads), "grp", 1)
    attn_got, pair_send = wait((attn_got, pair_send))
    head_half = HEADS // 2
    theirs = lax.dynamic_slice_in_dim(attn_got[:head_half], (1 - head) * prompt_dev, prompt_dev, 1)
    attn_partner = exchange(theirs, "head", 1)
    shared_parts[3] = exchange(tie(shared_parts[2], attn_partner), "head", 1)
    residual, hidden, attn_tok, sent, proj_w = kernel_call(
        hidden_kernel,
        [
            ((rows, width), f32),
            ((rows, width), bf16),
            ((rows, width), bf16),
            (pack_shape, bf16),
            ((8, quarter // 2, width), bf16),
        ],
        [((2, rows, six), bf16)],
        "hidden_rows",
        place, attn_got, attn_partner, tokens_in, gains, pick, attn_proj.T, *own_w, *other_w,
        alone=True,
    )

    sent, grad_other, shared_parts[1], shared_parts[2] = wait(
        (sent, grad_other, shared_parts[1], shared_parts[2])
    )
    got_own = over_line(sent)
    fetched(down_send, sent, 2, 3, 1)
    four_hidden = of_four(tie(hidden, sent))
    got_own, down_send[2], four_hidden = wait((got_own, down_send[2], four_hidden))
    got_other = exchange(got_own, "grp", 1)
    shared_out, shared_back, *shared_given = kernel_call(
        shared_kernel,
        [((4 * rows, width), bf16)] * 2 + [((width + 2 * quarter, span), bf16)] * 4,
        [
            ((width, 4 * span), bf16),
            ((width, 2 * span), bf16),
            ((width, 4 * span), f32),
            ((width, 2 * span), f32),
        ],
        "shared_rows",
        place, *tie(four_hidden, got_own), *four_grads, *shared_parts,
        alone=True,
    )
    shared_back = sum_of_four([shared_back[i * rows : (i + 1) * rows] for i in range(4)])

    got_other, shared_given, down_send, all_normed = wait(
        (got_other, shared_given, down_send, all_normed)
    )
    middle = shared_given[0].shape[0] // 2
    upper = [part[:middle] for part in shared_given]
    lower = [part[middle:] for part in shared_given]
    count = 2 * per_half
    g_own, g_part, e_own, e_part, egate, eup, e_mid, g_eout, g_router, got_rows = kernel_call(
        expert_kernel,
        [
            ((per_half, width), f32),
            ((per_half, width), bf16),
            ((per_half, width), f32),
            ((per_half, width), bf16),
            ((count, units), bf16),
            ((count, units), bf16),
            ((count, units), bf16),
            ((count, width), bf16),
            ((EXPERTS, width), f32),
            ((count, width), bf16),
        ],
        [((width, units), bf16)] * 3 + [((count, width), bf16)],
        "expert_rows",
        place, got_own, got_other, grad_own, grad_other, router_w,
        *pair_send, *down_send,
        alone=True,
        flops=15 * 10**9,
    )

    def joined_rows(own, part):
        return kernel_call(join_kernel, [(pack_shape, bf16)], [], "join_rows", own, part)[0]

    weight_parts = kernel_call(
        expert_weight_kernel,
        [((2, quarter, units), bf16)] * 4 + [((quarter, units), bf16)] * 4,
        [((width, units), bf16), ((width, count), bf16)],
        "expert_weights",
        place, got_rows, g_eout, egate, eup, e_mid,
        alone=True,
    )
    pair_out, down_out = list(weight_parts[0:4]), list(weight_parts[4:8])
    g_other = exchange(g_part, "grp", 1)
    turned = exchange(tie(jnp.stack([lower[1], lower[3]]), g_part), "head", 1)
    g_other, pair_out, down_out = wait((g_other, pair_out, down_out))
    crossed = exchange(tie(jnp.stack([upper[2], upper[3]]), g_other), "grp", 1)
    g_joined, shared_back, turned = wait((joined_rows(g_own, g_other), shared_back, turned))
    crossed = joined(upper[1], crossed[1]), joined(upper[0], crossed[0])
    turned = joined(lower[2], turned[1]), joined(lower[0], turned[0])
    g_back = over_line(g_joined)
    shared_sum = jnp.concatenate(
        [
            joined(crossed[1], exchange(tie(crossed[0], g_joined), "head", 1)),
            joined(turned[1], exchange(tie(turned[0], g_joined), "grp", 1)),
        ]
    )
    shared_out = sum_of_four(
        [tie(shared_out, g_joined)[i * rows : (i + 1) * rows] for i in range(4)]
    )
    cutting = 576

    def far_sum(values):
        return joined(values, exchange(values, "blk", 4))


    g_resid, g_branch, grad_mine, grad_theirs, g_second_gain = kernel_call(
        branch_kernel,
        [
            ((rows, width), f32),
            ((rows, width), bf16),
            ((head_half, prompt_dev, 2 * DH), bf16),
            ((head_half, prompt_dev, 2 * DH), bf16),
            ((1, width), f32),
        ],
        [((per_half, width), bf16), ((2, head_half, prompt_dev, 2 * DH), bf16)],
        "branch_rows",
        place, g_back, pick, shared_back, residual, gains, out_grad, proj_w,
    )
    grad_theirs = exchange(grad_theirs, "head", 1)
    grad_theirs, shared_sum = wait((grad_theirs, shared_sum))
    g_proj = mm(g_branch, attn_tok, FIRST).astype(bf16).reshape(4, 4, quarter // 4, width)
    g_proj = sum_of_four(
        [
            lax.dynamic_index_in_dim(g_proj, four ^ j, 1, keepdims=False).reshape(quarter, width)
            for j in range(4)
        ]
    )
    g_proj = g_proj.astype(bf16)
    grad_send = jnp.where(
        head == 0,
        jnp.concatenate([grad_mine, grad_theirs], axis=1),
        jnp.concatenate([grad_theirs, grad_mine], axis=1),
    )
    grad_send = jnp.pad(grad_send, ((0, blocks - head_half), (0, 0), (0, 0)))
    grad_heads = over_blocks(grad_send)
    grad_heads, shared_out = wait((grad_heads, shared_out))
    fetched(pair_out, grad_send, 1, 2)
    far_one = far_sum(tie(shared_sum[:cutting], grad_heads))
    g_head_rows = attention_backward(head_rows, grad_heads, table)
    g_proj = g_proj.reshape(4, quarter // 4, width)
    proj_out = []
    for j in range(4):
        part = lax.dynamic_index_in_dim(g_proj, member ^ j, 0, keepdims=False)
        proj_out.append(
            jnp.concatenate([part[:, i * span : (i + 1) * span] for i in range(width // span)])
        )
    fetched(proj_out, g_head_rows, 1, 2, 3)
    proj_sum = sum(part.astype(f32) for part in proj_out).astype(bf16)
    far_two = far_sum(tie(shared_sum[cutting:], g_head_rows))
    far_proj = far_sum(tie(proj_sum, g_head_rows))
    fetched(pair_out, grad_heads, 3)
    g_head_rows, far_one = wait((g_head_rows, far_one))
    g_got = over_blocks(g_head_rows)
    e_other = exchange(tie(e_part, g_head_rows), "grp", 1)
    g_got, pair_out, e_joined = wait((g_got, pair_out, joined_rows(e_own, e_other)))
    g_normed, g_normed_theirs, g_first_gain = kernel_call(
        tokens_kernel,
        [((rows, width), f32), ((rows, width), bf16), ((1, width), f32)],
        [((2 * rows, 3 * six), bf16), ((2, rows, width), f32)],
        "token_parts",
        place, g_got, qkv_w, tokens_in, partner_tokens,
    )
    g_normed_theirs = exchange(g_normed_theirs, "head", 1)

    head_w = kernel_call(
        head_weight_kernel,
        [((3 * DH, width), bf16)],
        [((2 * rows * blocks, 3 * DH), bf16)],
        "head_weights",
        tie(g_head_rows, g_first_gain), all_normed,
    )[0].reshape(3, DH, width)

    def chunk_pair(side):
        kept_kind = 2 * side
        given_kind = jnp.where(head == 0, 1 + side, side)
        return jnp.stack([head_w[kept_kind], head_w[given_kind]])

    few = jnp.concatenate([g_first_gain, g_second_gain, g_router], axis=0)
    few = jnp.pad(few, ((0, FEW - few.shape[0]), (0, 0))).astype(bf16)
    own_pair = jnp.concatenate([*jnp.where(grp == 0, chunk_pair(0), chunk_pair(1)), few])
    other_pair = jnp.concatenate([*jnp.where(grp == 0, chunk_pair(1), chunk_pair(0)), few])
    own_pair = joined(own_pair, exchange(other_pair, "grp", 1))
    from_head = exchange(own_pair[DH:], "head", 1)
    own_pair = jnp.concatenate(
        [own_pair[:DH], from_head[:DH], joined(own_pair[2 * DH :], from_head[DH:])]
    )
    own_pair, far_two, far_proj = wait((own_pair, far_two, far_proj))
    all_pairs = lax.all_gather(own_pair, "blk", axis=0)
    order = jnp.array(
        [
            [0, 2, 4, 6, 8, 10, 1, 3, 5],
            [6, 8, 10, 1, 3, 5, 7, 9, 11],
            [1, 3, 5, 7, 9, 11, 0, 2, 4],
            [7, 9, 11, 0, 2, 4, 6, 8, 10],
        ],
        jnp.int32,
    )[member]
    grad_tokens = kernel_call(
        tokens_out_kernel,
        [((rows, width), f32)],
        [],
        "token_grads",
        g_normed, g_normed_theirs, tokens_in, gains, g_resid,
    )[0]
    grad_expert_w = kernel_call(
        units_out_kernel,
        [((2, quarter, 4 * units), f32)],
        [],
        "units_out",
        place, *pair_out,
        alone=True,
    )[0]
    fetched(down_out, from_head, 1, 2, 3)
    e_joined, down_out = wait((e_joined, down_out))
    grad_expert_out = kernel_call(
        units_out_kernel,
        [((quarter, 4 * units), f32)],
        [],
        "down_out",
        place, *down_out,
        alone=True,
    )[0].T
    e_joined, grad_expert_out = wait((e_joined, grad_expert_out))
    e_back = over_line(e_joined)
    layer_out = kernel_call(
        layer_kernel,
        [((rows, width), bf16)],
        [((per_half, width), bf16)],
        "layer_rows",
        e_back, pick, residual, shared_out,
    )[0]
    four_shared = of_four(
        tie(jnp.concatenate([far_one, far_two, far_proj]), from_head)
    )
    grad_shared_w, grad_shared_out, grad_proj = kernel_call(
        shared_out_kernel,
        [((width, 4 * span), f32), ((quarter, SFF), f32), ((quarter, width), f32)],
        [],
        "shared_grads",
        place, *four_shared,
        alone=True,
    )
    all_pairs, grad_expert_w = wait((all_pairs, grad_expert_w))
    grad_qkv, few = kernel_call(
        chunk_kernel,
        [((third, width), f32), ((FEW, width), f32)],
        [],
        "chunk_rows",
        order, all_pairs,
    )
    grad_qkv = grad_qkv.T

    few = lax.dynamic_slice_in_dim(few, member * quarter, quarter, 1)
    grad_shared_out, grad_proj = grad_shared_out.T, grad_proj.T
    return (
        layer_out,
        grad_tokens,
        few[0:2],
        grad_qkv,
        grad_proj,
        few[2 : 2 + EXPERTS],
        grad_shared_w,
        grad_shared_out,
        grad_expert_w,
        grad_expert_out,
    )


def solution(mesh):
    whole = P(("grp", "head", "blk"), None)
    split = P(None, ("grp", "head"))
    sizes = dict(mesh.shape)
    quick = sizes["grp"] == 2 and sizes["head"] == 2 and sizes["blk"] == 8
    return jax.shard_map(
        quick_body if quick else body,
        mesh=mesh,
        in_specs=(
            whole, split, split, split, split, split, split,
            P(None, ("grp", "head"), "blk"), P("blk", ("grp", "head")), whole, whole,
        ),
        out_specs=(
            whole, whole, split, split, split, split, split, split,
            P(None, ("grp", "head"), "blk"), P("blk", ("grp", "head")),
        ),
        check_vma=False,
    )
```

```python
import math

import jax
import jax.numpy as jnp
import numpy as np
from jax import lax
from jax.experimental import pallas as pl
from jax.experimental.pallas import tpu as pltpu
from jax.sharding import PartitionSpec as P

HEADS = 12
DH = 64
EXPERTS = 16
FF = 2048
SFF = 2048
PROMPT_ROWS = 64
PROMPT_LEAST = 1024


EPSILON = 1e-06
NEGATIVE = -1e30


def norm_rows(values, gain):
    inverse = lax.rsqrt(jnp.mean(values * values, axis=-1, keepdims=True) + EPSILON)
    return (values * inverse * gain, inverse)


def norm_back(values, inverse, gain, upstream):
    scaled = upstream * gain
    inner_mean = jnp.mean(scaled * values, axis=-1, keepdims=True)
    return (
        inverse * scaled - values * inverse**3 * inner_mean,
        jnp.sum(upstream * values * inverse, axis=0),
    )


def angle_tables(positions):
    step_index = jnp.arange(DH // 2, dtype=jnp.float32)
    freq_rates = 10000.0 ** (-2.0 * step_index / DH)
    angles = positions.astype(jnp.float32)[:, None] * freq_rates[None, :]
    return (jnp.cos(angles)[:, None, :], jnp.sin(angles)[:, None, :])


def rotate(values, cosine, sine_table):
    half_size = values.shape[-1] // 2
    first_half = values[..., :half_size]
    second = values[..., half_size:]
    return jnp.concatenate(
        [first_half * cosine - second * sine_table, second * cosine + first_half * sine_table],
        axis=-1,
    )


def swish_parts(gate_value):
    sigmoid = jax.nn.sigmoid(gate_value)
    return (gate_value * sigmoid, sigmoid * (1.0 + gate_value * (1.0 - sigmoid)))


def row_layout(head_part, within, block_index, heads_axis, blocks_axis, row_count, prompt_dev):
    prompt_all = prompt_dev * heads_axis * blocks_axis
    is_prompt = within < prompt_dev
    prompt_index = (block_index * heads_axis + head_part) * prompt_dev + within
    cont_index = head_part * (row_count - prompt_dev) + within - prompt_dev
    positions = jnp.where(is_prompt, prompt_index, prompt_all + cont_index)
    return (is_prompt, prompt_index, cont_index, positions)


def fetch_weights(
    norm_gains,
    attn_qkv,
    attn_proj,
    router_rows,
    shared_gate_up,
    shared_down,
    expert_gate_up,
    expert_down,
):
    return (
        lax.all_gather(norm_gains, ("grp", "head"), axis=1, tiled=True),
        lax.all_gather(attn_qkv, ("grp", "head"), axis=1, tiled=True),
        lax.all_gather(attn_proj, ("grp", "head"), axis=1, tiled=True),
        lax.all_gather(router_rows, ("grp", "head"), axis=1, tiled=True),
        lax.all_gather(shared_gate_up, ("grp", "head"), axis=1, tiled=True),
        lax.all_gather(shared_down, ("grp", "head"), axis=1, tiled=True),
        lax.all_gather(expert_gate_up, ("grp", "head"), axis=1, tiled=True),
        lax.all_gather(expert_down, ("grp", "head"), axis=1, tiled=True),
    )


def masked_scores(queries, key_rows, visible):
    scores = jnp.einsum(
        "qhd,khd->hqk", queries, key_rows, preferred_element_type=jnp.float32
    ) * DH ** (-0.5)
    return jnp.where(visible[None], scores, NEGATIVE)


def add_stats(carry, scores, visible):
    row_peak, row_total = carry
    new_peak = jnp.maximum(row_peak, jnp.max(scores, axis=-1))
    terms = jnp.where(visible[None], jnp.exp(scores - new_peak[:, :, None]), 0.0)
    return (new_peak, row_total * jnp.exp(row_peak - new_peak) + jnp.sum(terms, axis=-1))


def block_probs(scores, visible, log_total):
    return jnp.where(visible[None], jnp.exp(scores - log_total[:, :, None]), 0.0)


def grad_block(queries, grad_out, log_total, delta, key_rows, value_rows, visible):
    scale_factor = DH ** (-0.5)
    soft_weights = block_probs(masked_scores(queries, key_rows, visible), visible, log_total)
    grad_weights = jnp.einsum(
        "qhd,khd->hqk", grad_out, value_rows, preferred_element_type=jnp.float32
    )
    grad_scores = (soft_weights * (grad_weights - delta[:, :, None])).astype(jnp.bfloat16)
    grad_query = (
        jnp.einsum("hqk,khd->qhd", grad_scores, key_rows, preferred_element_type=jnp.float32)
        * scale_factor
    )
    grad_key = (
        jnp.einsum("hqk,qhd->khd", grad_scores, queries, preferred_element_type=jnp.float32)
        * scale_factor
    )
    grad_value = jnp.einsum(
        "hqk,qhd->khd",
        soft_weights.astype(jnp.bfloat16),
        grad_out,
        preferred_element_type=jnp.float32,
    )
    return (grad_query, grad_key, grad_value)


def body(
    tokens_in,
    norm_gains,
    attn_qkv,
    attn_proj,
    router_rows,
    shared_gate_up,
    shared_down,
    expert_gate_up,
    expert_down,
    routes,
    out_grad,
):
    heads_axis = lax.axis_size("head")
    blocks_axis = lax.axis_size("blk")
    row_count = tokens_in.shape[0]
    width_all = tokens_in.shape[1]
    prompt_dev = max(PROMPT_ROWS, PROMPT_LEAST // (heads_axis * blocks_axis))
    prompt_all = prompt_dev * heads_axis * blocks_axis
    local_heads = HEADS // heads_axis
    query_rows = heads_axis * row_count
    key_block = min(512, prompt_all)
    block_count = prompt_all // key_block
    head_me = lax.axis_index("head")
    block_me = lax.axis_index("blk")
    gain_rows, qkv_w, proj_w, router_w, shared_w, shared_out_w, expert_w, expert_out_w = (
        fetch_weights(
            norm_gains,
            attn_qkv,
            attn_proj,
            router_rows,
            shared_gate_up,
            shared_down,
            expert_gate_up,
            expert_down,
        )
    )
    tokens = tokens_in.astype(jnp.float32)
    first_gain = gain_rows[0].astype(jnp.float32)
    second_gain = gain_rows[1].astype(jnp.float32)
    normed_f, first_inverse = norm_rows(tokens, first_gain)
    normed = normed_f.astype(jnp.bfloat16)
    mixed_qkv = jnp.dot(normed, qkv_w, preferred_element_type=jnp.float32)
    token_row = jnp.arange(row_count, dtype=jnp.int32)
    token_pos = row_layout(
        head_me, token_row, block_me, heads_axis, blocks_axis, row_count, prompt_dev
    )[3]
    token_cos, token_sin = angle_tables(token_pos)
    query_tok = (
        rotate(mixed_qkv[:, :width_all].reshape(row_count, HEADS, DH), token_cos, token_sin)
        .reshape(row_count, width_all)
        .astype(jnp.bfloat16)
    )
    key_tok = (
        rotate(
            mixed_qkv[:, width_all : 2 * width_all].reshape(row_count, HEADS, DH),
            token_cos,
            token_sin,
        )
        .reshape(row_count, width_all)
        .astype(jnp.bfloat16)
    )
    value_tok = mixed_qkv[:, 2 * width_all :].astype(jnp.bfloat16)
    query_head, key_head, value_head = (
        lax.all_to_all(query_tok, "head", split_axis=1, concat_axis=0, tiled=True),
        lax.all_to_all(key_tok, "head", split_axis=1, concat_axis=0, tiled=True),
        lax.all_to_all(value_tok, "head", split_axis=1, concat_axis=0, tiled=True),
    )
    local_index = jnp.arange(query_rows, dtype=jnp.int32)
    is_prompt, prompt_index, cont_index, head_pos = row_layout(
        local_index // row_count,
        local_index % row_count,
        block_me,
        heads_axis,
        blocks_axis,
        row_count,
        prompt_dev,
    )
    is_cont = jnp.logical_not(is_prompt)
    local_visible = (
        is_cont[:, None] & is_cont[None, :] & (cont_index[None, :] <= cont_index[:, None])
    )
    queries = query_head.reshape(query_rows, local_heads, DH)
    key_local = key_head.reshape(query_rows, local_heads, DH)
    value_local = value_head.reshape(query_rows, local_heads, DH)
    prompt_keys, prompt_values = (
        lax.all_gather(
            key_head.reshape(heads_axis, row_count, -1)[:, :prompt_dev].reshape(
                heads_axis * prompt_dev, -1
            ),
            "blk",
            axis=0,
            tiled=True,
        ),
        lax.all_gather(
            value_head.reshape(heads_axis, row_count, -1)[:, :prompt_dev].reshape(
                heads_axis * prompt_dev, -1
            ),
            "blk",
            axis=0,
            tiled=True,
        ),
    )
    key_blocks = prompt_keys.reshape(block_count, key_block, local_heads, DH)
    value_blocks = prompt_values.reshape(block_count, key_block, local_heads, DH)
    block_starts = jnp.arange(block_count, dtype=jnp.int32) * key_block
    key_offsets = jnp.arange(key_block, dtype=jnp.int32)

    def prompt_visible(start):
        return is_cont[:, None] | (start + key_offsets[None, :] <= prompt_index[:, None])

    def stats_step(carry, member):
        visible = prompt_visible(member[1])
        return (add_stats(carry, masked_scores(queries, member[0], visible), visible), None)

    start_stats = (
        jnp.full((local_heads, query_rows), NEGATIVE, jnp.float32),
        jnp.zeros((local_heads, query_rows), jnp.float32),
    )
    stats = lax.scan(stats_step, start_stats, (key_blocks, block_starts))[0]
    row_peak, row_total = add_stats(
        stats, masked_scores(queries, key_local, local_visible), local_visible
    )
    log_total = row_peak + jnp.log(row_total)

    def output_step(total_out, member):
        visible = prompt_visible(member[2])
        soft_weights = block_probs(
            masked_scores(queries, member[0], visible), visible, log_total
        ).astype(jnp.bfloat16)
        return (
            total_out
            + jnp.einsum(
                "hqk,khd->qhd", soft_weights, member[1], preferred_element_type=jnp.float32
            ),
            None,
        )

    attn_heads = lax.scan(
        output_step,
        jnp.zeros((query_rows, local_heads, DH), jnp.float32),
        (key_blocks, value_blocks, block_starts),
    )[0]
    local_weights = block_probs(
        masked_scores(queries, key_local, local_visible), local_visible, log_total
    ).astype(jnp.bfloat16)
    attn_heads = attn_heads + jnp.einsum(
        "hqk,khd->qhd", local_weights, value_local, preferred_element_type=jnp.float32
    )
    attn_tok = lax.all_to_all(
        attn_heads.reshape(query_rows, -1).astype(jnp.bfloat16),
        "head",
        split_axis=0,
        concat_axis=1,
        tiled=True,
    )
    residual = tokens + jnp.dot(attn_tok, proj_w, preferred_element_type=jnp.float32)
    hidden_f, second_inverse = norm_rows(residual, second_gain)
    hidden = hidden_f.astype(jnp.bfloat16)
    logits = jnp.einsum("td,ed->te", hidden, router_w, preferred_element_type=jnp.float32)
    soft_route = jax.nn.softmax(logits, axis=-1)
    expert_ids = jnp.arange(EXPERTS, dtype=jnp.int32)
    route_match = routes[:, :, None] == expert_ids[None, None, :]
    gate_values = jnp.sum(jnp.where(route_match, soft_route[:, None, :], 0.0), axis=-1)
    shared_pre = jnp.dot(hidden, shared_w, preferred_element_type=jnp.float32)
    shared_act, shared_slope = swish_parts(shared_pre[:, :SFF])
    shared_up = shared_pre[:, SFF:]
    shared_mid = (shared_act * shared_up).astype(jnp.bfloat16)
    shared_out = jnp.dot(shared_mid, shared_out_w, preferred_element_type=jnp.float32)
    unit_count = expert_w.shape[2]
    per_device = max(1, unit_count // FF)
    spread = max(1, FF // unit_count)
    unit_width = unit_count // per_device
    capacity = max(2, 5 * row_count // (2 * EXPERTS))
    slot_count = blocks_axis * per_device * capacity
    pair_expert = routes.reshape(-1)
    pair_match = route_match.reshape(2 * row_count, EXPERTS).astype(jnp.int32)
    pair_rank = jnp.sum(jnp.cumsum(pair_match, axis=0) * pair_match, axis=1) - 1
    slot_base = (
        pair_expert // per_device * spread * per_device * capacity
        + pair_expert % per_device * capacity
        + pair_rank
    )
    slot_index = (
        slot_base[None, :] + (jnp.arange(spread, dtype=jnp.int32) * per_device * capacity)[:, None]
    )
    pair_ids = jnp.arange(2 * row_count, dtype=jnp.int32)
    slot_pair = (
        jnp.full((slot_count,), 2 * row_count, jnp.int32)
        .at[slot_index.reshape(-1)]
        .set(jnp.tile(pair_ids, spread))
    )
    slot_token = slot_pair // 2
    hidden_pad = jnp.concatenate([hidden, jnp.zeros((1, width_all), jnp.bfloat16)], axis=0)
    send_rows = hidden_pad[slot_token].reshape(blocks_axis, per_device, capacity, width_all)
    received_rows = lax.all_to_all(send_rows, "blk", split_axis=0, concat_axis=0, tiled=True)
    gate_weight = expert_w[0].reshape(width_all, per_device, unit_width)
    up_weight = expert_w[1].reshape(width_all, per_device, unit_width)
    down_w = expert_out_w.reshape(per_device, unit_width, width_all)
    expert_gate = jnp.einsum(
        "tfoa,afw->tfow", received_rows, gate_weight, preferred_element_type=jnp.float32
    )
    expert_up_projection = jnp.einsum(
        "tfoa,afw->tfow", received_rows, up_weight, preferred_element_type=jnp.float32
    )
    expert_activation, expert_slope = swish_parts(expert_gate)
    expert_mid = (expert_activation * expert_up_projection).astype(jnp.bfloat16)
    expert_part = jnp.einsum(
        "secm,emd->secd", expert_mid, down_w, preferred_element_type=jnp.float32
    )
    returned = (
        lax.all_to_all(
            expert_part.astype(jnp.bfloat16), "blk", split_axis=0, concat_axis=0, tiled=True
        )
        .astype(expert_part.dtype)
        .reshape(slot_count, width_all)
    )
    pair_out = jnp.sum(returned[slot_index], axis=0).reshape(row_count, 2, width_all)
    expert_sum = jnp.sum(gate_values[:, :, None] * pair_out, axis=1)
    layer_out = (residual + shared_out + expert_sum).astype(jnp.bfloat16)
    gain_rows, qkv_w, proj_w, router_w, shared_w, shared_out_w, expert_w, expert_out_w = (
        fetch_weights(
            norm_gains,
            attn_qkv,
            attn_proj,
            router_rows,
            shared_gate_up,
            shared_down,
            expert_gate_up,
            expert_down,
        )
    )
    gate_weight = expert_w[0].reshape(width_all, per_device, unit_width)
    up_weight = expert_w[1].reshape(width_all, per_device, unit_width)
    down_w = expert_out_w.reshape(per_device, unit_width, width_all)
    grad_layer = out_grad.astype(jnp.float32)
    grad_smid = jnp.einsum("td,fd->tf", out_grad, shared_out_w, preferred_element_type=jnp.float32)
    shared_grads = jnp.concatenate(
        [grad_smid * shared_up * shared_slope, grad_smid * shared_act], axis=1
    ).astype(jnp.bfloat16)
    grad_hidden = jnp.einsum(
        "tf,df->td", shared_grads, shared_w, preferred_element_type=jnp.float32
    )
    grad_shared_w = jnp.einsum(
        "td,tf->df", hidden, shared_grads, preferred_element_type=jnp.float32
    )
    grad_shared_out = jnp.einsum(
        "tf,td->fd", shared_mid, out_grad, preferred_element_type=jnp.float32
    )
    grad_gates = jnp.sum(grad_layer[:, None, :] * pair_out, axis=-1)
    grad_pairs = (
        (gate_values[:, :, None] * grad_layer[:, None, :])
        .reshape(2 * row_count, width_all)
        .astype(jnp.bfloat16)
    )
    grad_pad = jnp.concatenate([grad_pairs, jnp.zeros((1, width_all), jnp.bfloat16)], axis=0)
    grad_recv = lax.all_to_all(
        grad_pad[slot_pair].reshape(blocks_axis, per_device, capacity, width_all),
        "blk",
        split_axis=0,
        concat_axis=0,
        tiled=True,
    )
    grad_expert_middle = jnp.einsum(
        "secd,emd->secm", grad_recv, down_w, preferred_element_type=jnp.float32
    )
    grad_expert_gate_branch = (grad_expert_middle * expert_up_projection * expert_slope).astype(
        jnp.bfloat16
    )
    grad_expert_up_branch = (grad_expert_middle * expert_activation).astype(jnp.bfloat16)
    grad_rows = jnp.einsum(
        "auwj,buj->auwb", grad_expert_gate_branch, gate_weight, preferred_element_type=jnp.float32
    ) + jnp.einsum(
        "auwj,buj->auwb", grad_expert_up_branch, up_weight, preferred_element_type=jnp.float32
    )
    grad_expert_w = jnp.stack(
        [
            jnp.einsum(
                "jgki,jgkt->igt",
                received_rows,
                grad_expert_gate_branch,
                preferred_element_type=jnp.float32,
            ).reshape(width_all, unit_count),
            jnp.einsum(
                "jgki,jgkt->igt",
                received_rows,
                grad_expert_up_branch,
                preferred_element_type=jnp.float32,
            ).reshape(width_all, unit_count),
        ]
    )
    grad_expert_out = jnp.einsum(
        "secm,secd->emd", expert_mid, grad_recv, preferred_element_type=jnp.float32
    ).reshape(unit_count, width_all)
    grad_back = (
        lax.all_to_all(
            grad_rows.astype(jnp.bfloat16), "blk", split_axis=0, concat_axis=0, tiled=True
        )
        .astype(grad_rows.dtype)
        .reshape(slot_count, width_all)
    )
    grad_hidden = grad_hidden + jnp.sum(
        jnp.sum(grad_back[slot_index], axis=0).reshape(row_count, 2, width_all), axis=1
    )
    grad_soft = jnp.sum(jnp.where(route_match, grad_gates[:, :, None], 0.0), axis=1)
    grad_logits = (
        soft_route * (grad_soft - jnp.sum(soft_route * grad_soft, axis=-1, keepdims=True))
    ).astype(jnp.bfloat16)
    grad_hidden = grad_hidden + jnp.einsum(
        "te,ed->td", grad_logits, router_w, preferred_element_type=jnp.float32
    )
    grad_router = jnp.einsum("te,td->ed", grad_logits, hidden, preferred_element_type=jnp.float32)
    grad_norm_two, grad_second_gain = norm_back(residual, second_inverse, second_gain, grad_hidden)
    grad_resid = grad_layer + grad_norm_two
    grad_branch = grad_resid.astype(jnp.bfloat16)
    grad_proj = jnp.einsum("td,te->de", attn_tok, grad_branch, preferred_element_type=jnp.float32)
    grad_attn_tok = jnp.einsum(
        "te,de->td", grad_branch, proj_w, preferred_element_type=jnp.float32
    ).astype(jnp.bfloat16)
    grad_heads = lax.all_to_all(
        grad_attn_tok, "head", split_axis=1, concat_axis=0, tiled=True
    ).reshape(query_rows, local_heads, DH)
    delta = jnp.transpose(jnp.sum(grad_heads * attn_heads, axis=-1))

    def back_step(grad_acc, member):
        visible = prompt_visible(member[2])
        step_query, step_key, step_value = grad_block(
            queries, grad_heads, log_total, delta, member[0], member[1], visible
        )
        return (grad_acc + step_query, (step_key, step_value))

    grad_query, prompt_grads = lax.scan(
        back_step,
        jnp.zeros((query_rows, local_heads, DH), jnp.float32),
        (key_blocks, value_blocks, block_starts),
    )
    local_query, local_key, local_value = grad_block(
        queries, grad_heads, log_total, delta, key_local, value_local, local_visible
    )
    grad_query = grad_query + local_query
    key_share, value_share = (
        lax.psum_scatter(
            prompt_grads[0].reshape(prompt_all, -1), "blk", scatter_dimension=0, tiled=True
        ),
        lax.psum_scatter(
            prompt_grads[1].reshape(prompt_all, -1), "blk", scatter_dimension=0, tiled=True
        ),
    )
    grad_key = (
        local_key.reshape(heads_axis, row_count, -1)
        .at[:, :prompt_dev]
        .add(key_share.reshape(heads_axis, prompt_dev, -1))
        .reshape(query_rows, local_heads, DH)
    )
    grad_value = (
        local_value.reshape(heads_axis, row_count, -1)
        .at[:, :prompt_dev]
        .add(value_share.reshape(heads_axis, prompt_dev, -1))
    )
    head_cos, head_sin = angle_tables(head_pos)
    grad_query = (
        rotate(grad_query, head_cos, -head_sin).reshape(query_rows, -1).astype(jnp.bfloat16)
    )
    grad_key = rotate(grad_key, head_cos, -head_sin).reshape(query_rows, -1).astype(jnp.bfloat16)
    grad_value = grad_value.reshape(query_rows, -1).astype(jnp.bfloat16)
    grad_q_tok, grad_k_tok, grad_v_tok = (
        lax.all_to_all(grad_query, "head", split_axis=0, concat_axis=1, tiled=True),
        lax.all_to_all(grad_key, "head", split_axis=0, concat_axis=1, tiled=True),
        lax.all_to_all(grad_value, "head", split_axis=0, concat_axis=1, tiled=True),
    )
    grad_qkv_rows = jnp.concatenate([grad_q_tok, grad_k_tok, grad_v_tok], axis=1)
    grad_normed = jnp.einsum("tf,df->td", grad_qkv_rows, qkv_w, preferred_element_type=jnp.float32)
    grad_qkv = jnp.einsum("td,tf->df", normed, grad_qkv_rows, preferred_element_type=jnp.float32)
    grad_norm_one, grad_first_gain = norm_back(tokens, first_inverse, first_gain, grad_normed)
    grad_tokens = grad_resid + grad_norm_one
    owned = (
        lax.psum_scatter(
            jnp.stack([grad_first_gain, grad_second_gain]).astype(jnp.bfloat16),
            ("grp", "head"),
            scatter_dimension=1,
            tiled=True,
        ).astype(jnp.float32),
        lax.psum_scatter(
            grad_qkv.astype(jnp.bfloat16), ("grp", "head"), scatter_dimension=1, tiled=True
        ).astype(jnp.float32),
        lax.psum_scatter(
            grad_proj.astype(jnp.bfloat16), ("grp", "head"), scatter_dimension=1, tiled=True
        ).astype(jnp.float32),
        lax.psum_scatter(
            grad_router.astype(jnp.bfloat16), ("grp", "head"), scatter_dimension=1, tiled=True
        ).astype(jnp.float32),
        lax.psum_scatter(
            grad_shared_w.astype(jnp.bfloat16), ("grp", "head"), scatter_dimension=1, tiled=True
        ).astype(jnp.float32),
        lax.psum_scatter(
            grad_shared_out.astype(jnp.bfloat16), ("grp", "head"), scatter_dimension=1, tiled=True
        ).astype(jnp.float32),
        lax.psum_scatter(
            grad_expert_w.astype(jnp.bfloat16), ("grp", "head"), scatter_dimension=1, tiled=True
        ).astype(jnp.float32),
        lax.psum_scatter(
            grad_expert_out.astype(jnp.bfloat16), ("grp", "head"), scatter_dimension=1, tiled=True
        ).astype(jnp.float32),
    )
    summed = lax.psum((owned[0], owned[1], owned[2], owned[3], owned[4], owned[5]), "blk")
    return (
        layer_out,
        grad_tokens,
        summed[0],
        summed[1],
        summed[2],
        summed[3],
        summed[4],
        summed[5],
        owned[6],
        owned[7],
    )


TRANSPOSED = (((1,), (1,)), ((), ()))
PLAIN = (((1,), (0,)), ((), ()))
FIRST = (((0,), (0,)), ((), ()))
FORWARD_VMEM = 14 * 1024 * 1024
BACKWARD_VMEM = 24 * 1024 * 1024
FEW = 32
UNIT_ORDER = (0, 2, 1, 3)


def mm(left, right, dims=PLAIN):
    return lax.dot_general(left, right, dims, preferred_element_type=jnp.float32)


def assemble(rows_ref, cut, parts, prompt_to, cont_to):
    blocks, half = rows_ref.shape[0], rows_ref.shape[1] // 2
    for block in range(blocks):
        for head_part in range(2):
            piece = rows_ref[block, head_part * half : (head_part + 1) * half, :]
            place = (block * 2 + head_part) * half
            for order in range(parts):
                prompt_to[order][place : place + half, :] = piece[
                    :, order * cut : (order + 1) * cut
                ]
                cont_to[order][place : place + half, :] = piece[
                    :, (parts + order) * cut : (parts + order + 1) * cut
                ]


def spread_out(target, prompt_parts, cont_parts, cut):
    blocks, half = target.shape[0], target.shape[1] // 2
    for block in range(blocks):
        for head_part in range(2):
            place = (block * 2 + head_part) * half
            pieces = [part[place : place + half, :] for part in prompt_parts]
            pieces += [part[place : place + half, :] for part in cont_parts]
            target[block, head_part * half : (head_part + 1) * half, :] = jnp.concatenate(
                pieces, axis=1
            ).astype(target.dtype)


def causal_mask(rows):
    keys = lax.broadcasted_iota(jnp.int32, (rows, rows), 0)
    query = lax.broadcasted_iota(jnp.int32, (rows, rows), 1)
    return keys <= query


def cont_mask(rows, cont):
    keys = lax.broadcasted_iota(jnp.int32, (rows, rows), 0)
    query = lax.broadcasted_iota(jnp.int32, (rows, rows), 1)
    return (keys // cont == query // cont) & (keys <= query)


def masked_block(keys, queries, mask):
    scores = mm(keys, queries, TRANSPOSED) * DH ** (-0.5)
    if mask is None:
        return scores
    return jnp.where(mask, scores, NEGATIVE)


def attention_kernel(rows_ref, out_ref, qp, kp, vp, qc, kc, vc, op, oc):
    block = 256
    prompt = qp.shape[0]
    assemble(rows_ref, DH, 3, (qp, kp, vp), (qc, kc, vc))
    cont = rows_ref.shape[1]
    for is_cont in range(2):
        source_q, source_k, source_v, result = (
            (qc, kc, vc, oc) if is_cont else (qp, kp, vp, op)
        )
        mask = cont_mask(block, cont) if is_cont else causal_mask(block)
        for step in range(prompt // block):
            rows = slice(step * block, (step + 1) * block)
            queries = source_q[rows, :]
            own = masked_block(source_k[rows, :], queries, mask)
            seen = prompt if is_cont else step * block
            peak = jnp.max(own, axis=0, keepdims=True)
            if seen:
                past = masked_block(kp[0:seen, :], queries, None)
                peak = jnp.maximum(peak, jnp.max(past, axis=0, keepdims=True))
            own = jnp.exp(own - peak)
            total = jnp.sum(own, axis=0, keepdims=True)
            gathered = mm(source_v[rows, :], own.astype(jnp.bfloat16), FIRST)
            if seen:
                past = jnp.exp(past - peak)
                total = total + jnp.sum(past, axis=0, keepdims=True)
                gathered = gathered + mm(vp[0:seen, :], past.astype(jnp.bfloat16), FIRST)
            result[rows, :] = jnp.transpose(gathered / total)
    spread_out(out_ref, (op,), (oc,), DH)


def attention_forward(rows):
    blocks, both, _ = rows.shape
    prompt = blocks * both
    small = pltpu.VMEM((prompt, DH), jnp.bfloat16)
    wide = pltpu.VMEM((prompt, DH), jnp.float32)
    return pl.pallas_call(
        attention_kernel,
        out_shape=jax.ShapeDtypeStruct((blocks, both, 2 * DH), jnp.bfloat16),
        in_specs=[pl.BlockSpec(memory_space=pltpu.VMEM)],
        out_specs=pl.BlockSpec(memory_space=pltpu.VMEM),
        scratch_shapes=[small] * 6 + [wide] * 2,
        compiler_params=pltpu.CompilerParams(vmem_limit_bytes=FORWARD_VMEM),
        cost_estimate=pl.CostEstimate(
            flops=2**20, bytes_accessed=2**16, transcendentals=0
        ),
        name="attention_forward",
    )(rows)


def turn_back(values, cosine, sine):
    half = DH // 2
    first, second = values[:, :half], values[:, half:]
    return jnp.concatenate(
        [first * cosine + second * sine, second * cosine - first * sine], axis=1
    )


def attention_back_kernel(
    rows_ref, grad_ref, table_ref, out_ref,
    qp, kp, vp, qc, kc, vc, gp, gc, dqp, dkp, dvp, dqc, dkc, dvc,
):
    block = 256
    prompt = qp.shape[0]
    scale = DH ** (-0.5)
    assemble(rows_ref, DH, 3, (qp, kp, vp), (qc, kc, vc))
    assemble(grad_ref, DH, 1, (gp,), (gc,))
    cont = rows_ref.shape[1]
    dkp[...] = jnp.zeros_like(dkp)
    dvp[...] = jnp.zeros_like(dvp)
    for is_cont in range(2):
        source_q, source_k, source_v, source_g = (
            (qc, kc, vc, gc) if is_cont else (qp, kp, vp, gp)
        )
        to_q, to_k, to_v = (dqc, dkc, dvc) if is_cont else (dqp, dkp, dvp)
        mask = cont_mask(block, cont) if is_cont else causal_mask(block)
        for step in range(prompt // block):
            rows = slice(step * block, (step + 1) * block)
            queries = source_q[rows, :]
            grads = source_g[rows, :]
            own_keys = source_k[rows, :]
            own = masked_block(own_keys, queries, mask)
            seen = prompt if is_cont else step * block
            peak = jnp.max(own, axis=0, keepdims=True)
            if seen:
                past = masked_block(kp[0:seen, :], queries, None)
                peak = jnp.maximum(peak, jnp.max(past, axis=0, keepdims=True))
            own = jnp.exp(own - peak)
            total = jnp.sum(own, axis=0, keepdims=True)
            if seen:
                past = jnp.exp(past - peak)
                total = total + jnp.sum(past, axis=0, keepdims=True)
            inverse = 1.0 / total
            own = own * inverse
            own_grad = mm(source_v[rows, :], grads, TRANSPOSED)
            delta = jnp.sum(own * own_grad, axis=0, keepdims=True)
            if seen:
                past = past * inverse
                past_grad = mm(vp[0:seen, :], grads, TRANSPOSED)
                delta = delta + jnp.sum(past * past_grad, axis=0, keepdims=True)
            own_scores = (own * (own_grad - delta)).astype(jnp.bfloat16)
            own_dv = mm(own.astype(jnp.bfloat16), grads)
            own_dk = mm(own_scores, queries) * scale
            turned = mm(own_keys, own_scores, FIRST)
            if is_cont:
                to_v[rows, :] = own_dv
                to_k[rows, :] = own_dk
            else:
                to_v[rows, :] += own_dv
                to_k[rows, :] += own_dk
            if seen:
                past_scores = (past * (past_grad - delta)).astype(jnp.bfloat16)
                dvp[0:seen, :] += mm(past.astype(jnp.bfloat16), grads)
                dkp[0:seen, :] += mm(past_scores, queries) * scale
                turned = turned + mm(kp[0:seen, :], past_scores, FIRST)
            to_q[rows, :] = jnp.transpose(turned) * scale
    turn = DH // 2
    cos_p, sin_p = table_ref[0:prompt, :turn], table_ref[0:prompt, turn:]
    dqp[...] = turn_back(dqp[...], cos_p, sin_p)
    dkp[...] = turn_back(dkp[...], cos_p, sin_p)
    for step in range(prompt // cont):
        rows = slice(step * cont, (step + 1) * cont)
        cos_c = table_ref[prompt : prompt + cont, :turn]
        sin_c = table_ref[prompt : prompt + cont, turn:]
        dqc[rows, :] = turn_back(dqc[rows, :], cos_c, sin_c)
        dkc[rows, :] = turn_back(dkc[rows, :], cos_c, sin_c)
    spread_out(out_ref, (dqp, dkp, dvp), (dqc, dkc, dvc), DH)


def attention_backward(rows, grads, table):
    blocks, both, wide = rows.shape
    prompt = blocks * both
    small = pltpu.VMEM((prompt, DH), jnp.bfloat16)
    large = pltpu.VMEM((prompt, DH), jnp.float32)
    return pl.pallas_call(
        attention_back_kernel,
        out_shape=jax.ShapeDtypeStruct((blocks, both, wide), jnp.bfloat16),
        in_specs=[pl.BlockSpec(memory_space=pltpu.VMEM)] * 3,
        out_specs=pl.BlockSpec(memory_space=pltpu.VMEM),
        scratch_shapes=[small] * 8 + [large] * 6,
        compiler_params=pltpu.CompilerParams(vmem_limit_bytes=BACKWARD_VMEM),
        cost_estimate=pl.CostEstimate(
            flops=2**20, bytes_accessed=2**16, transcendentals=0
        ),
        name="attention_backward",
    )(rows, grads, table)


def exchange(values, axis, mask):
    return lax.ppermute(values, axis, [(i, i ^ mask) for i in range(lax.axis_size(axis))])


def to_member(values, number):
    if number == 2:
        return exchange(values, "grp", 1)
    if number == 1:
        return exchange(values, "head", 1)
    return lax.ppermute(values, ("grp", "head"), [(i, i ^ number) for i in range(4)])


def tie(values, *after):
    return lax.optimization_barrier((values, *after))[0]


def padded_bytes(shape, kind):
    shape = (1,) * (2 - len(shape)) + tuple(shape)
    rows, lanes = -(-shape[-2] // 16) * 16, -(-shape[-1] // 128) * 128
    return math.prod(shape[:-2]) * rows * lanes * jnp.dtype(kind).itemsize


def kernel_call(body_of, outs, scratch, name, *inputs, room=6, alone=False, flops=2**20):
    held = [*outs, *scratch, *((one.shape, one.dtype) for one in inputs)]
    limit = sum(padded_bytes(*one) for one in held) + room * 2**20
    limit = 56 * 2**20 if alone else limit
    spec = pl.BlockSpec(memory_space=pltpu.VMEM)
    return pl.pallas_call(
        body_of,
        out_shape=[jax.ShapeDtypeStruct(*out) for out in outs],
        in_specs=[
            pl.BlockSpec(memory_space=pltpu.SMEM) if one.dtype == jnp.int32 else spec
            for one in inputs
        ],
        out_specs=[spec] * len(outs),
        scratch_shapes=[pltpu.VMEM(*one) for one in scratch],
        compiler_params=pltpu.CompilerParams(vmem_limit_bytes=limit),
        cost_estimate=pl.CostEstimate(flops=flops, bytes_accessed=2**16, transcendentals=0),
        name=name,
    )(*inputs)


def move_all(copies, sems):
    started = [
        pltpu.make_async_copy(source, target, sems.at[number])
        for number, (source, target) in enumerate(copies)
    ]
    for one in started:
        one.start()
    for one in started:
        one.wait()


def first_kernel(place, qkv_ref, few_ref, proj_ref, own_ref, *refs):
    given, sems = refs[0:3], refs[3]
    six = own_ref.shape[0]
    start, small = six // 2, few_ref.shape[0]
    half = given[0].shape[0] - start - small
    middle = (place[5] + place[4]) % 2
    shift = qkv_ref.shape[0] - six
    copies = []
    for j in range(4):
        window = ((middle + place[4] + j) % 2) * shift
        if j == 0:
            copies.append((qkv_ref.at[pl.ds(pl.multiple_of(window, 64), six), :], own_ref))
            continue
        at = pl.multiple_of(window + place[1] * start, 64)
        target = given[j - 1]
        copies.append((qkv_ref.at[pl.ds(at, start), :], target.at[pl.ds(0, start), :]))
        copies.append((few_ref, target.at[pl.ds(start, small), :]))
        copies.append(
            (
                proj_ref.at[pl.ds(pl.multiple_of(place[1] * half, 16), half), :],
                target.at[pl.ds(start + small, half), :],
            )
        )
    move_all(copies, sems)


def rest_kernel(place, wide_ref, shared_down_ref, both_ref, down_ref, *refs):
    outs, held, sems, out_sems = refs[0:9], refs[9:18], refs[18], refs[19]
    piece_ref, pairs, downs = held[0], held[1:5], held[5:9]
    width, span = wide_ref.shape[0], piece_ref.shape[1]
    quarter, units = downs[0].shape
    four = place[3] % 4
    copies = []
    for j in range(4):
        at = pl.ds(pl.multiple_of((place[6] ^ UNIT_ORDER[j]) * units, 128), units)
        copies.append((both_ref.at[0, :, at], pairs[j].at[0]))
        copies.append((both_ref.at[1, :, at], pairs[j].at[1]))
        copies.append((down_ref.at[:, at], downs[j]))
    at = pl.ds(pl.multiple_of(four * span, 128), span)
    copies.append((wide_ref.at[:, at], piece_ref.at[pl.ds(0, width), :]))
    copies.append((shared_down_ref.at[:, at], piece_ref.at[pl.ds(width, quarter), :]))
    at = pl.ds(pl.multiple_of((4 + four) * span, 128), span)
    copies.append((shared_down_ref.at[:, at], piece_ref.at[pl.ds(width + quarter, quarter), :]))
    move_all(copies, sems)
    move_all(list(zip(held, outs)), out_sems)


def copy_call(body_of, outs, count, name, place, *inputs, through=False):
    held = [pltpu.VMEM(shape, jnp.bfloat16) for shape in outs] if through else []
    sems = [pltpu.SemaphoreType.DMA((count,))]
    if through:
        sems.append(pltpu.SemaphoreType.DMA((len(outs),)))
    return pl.pallas_call(
        body_of,
        out_shape=[jax.ShapeDtypeStruct(shape, jnp.bfloat16) for shape in outs],
        in_specs=[pl.BlockSpec(memory_space=pltpu.SMEM)]
        + [pl.BlockSpec(memory_space=pl.ANY)] * len(inputs),
        out_specs=[pl.BlockSpec(memory_space=pl.ANY)] * len(outs),
        scratch_shapes=held + sems,
        compiler_params=pltpu.CompilerParams(vmem_limit_bytes=(56 if through else 1) * 2**20),
        cost_estimate=pl.CostEstimate(flops=2**20, bytes_accessed=2**16, transcendentals=0),
        name=name,
    )(place, *inputs)


def packed(rows):
    count, width = rows.shape
    blocks = count // 20
    last = rows[16 * blocks :]
    half = width // 2
    return jnp.concatenate(
        [
            rows[: 8 * blocks].reshape(blocks, 8, width),
            rows[8 * blocks : 16 * blocks].reshape(blocks, 8, width),
            jnp.concatenate(
                [last[:, :half].reshape(blocks, 4, half), last[:, half:].reshape(blocks, 4, half)],
                axis=1,
            ),
        ],
        axis=2,
    )


def unpack_to(target, at, source_ref):
    blocks = source_ref.shape[0]
    width = target.shape[1]
    half = width // 2
    target[at : at + 8 * blocks, :] = source_ref[:, :, 0:width].reshape(8 * blocks, width)
    target[at + 8 * blocks : at + 16 * blocks, :] = source_ref[:, :, width : 2 * width].reshape(
        8 * blocks, width
    )
    for block in range(blocks):
        place = at + 16 * blocks + 4 * block
        last = source_ref[block, :, 2 * width :]
        target[place : place + 4, 0:half] = last[0:4]
        target[place : place + 4, half:width] = last[4:8]


def pack_kernel(rows_ref, out_ref):
    out_ref[...] = packed(rows_ref[...].astype(jnp.float32)).astype(jnp.bfloat16)


def join_kernel(own_ref, part_ref, out_ref):
    rows = own_ref[...] + part_ref[...].astype(jnp.float32)
    out_ref[...] = packed(rows).astype(jnp.bfloat16)


def layer_kernel(got_ref, pick_ref, residual_ref, shared_ref, out_ref, rows):
    unpack_to(rows, 0, got_ref)
    out_ref[...] = (
        residual_ref[...] + shared_ref[...] + mm(pick_ref[...], rows[...], FIRST)
    ).astype(jnp.bfloat16)


def qkv_kernel(place, tokens_ref, partner_ref, table_ref, window_ref, few_ref, *refs):
    got, passed = refs[0:3], refs[3:6]
    normed_ref, rows_ref, gains_ref, router_ref, weight_ref, window, few, both = refs[6:]
    quad_me, core, head = place[0], place[1], place[4]
    rows, width = tokens_ref.shape
    half, quarter = rows // 2, width // 4
    per = window.shape[1] // 2
    window[quad_me] = window_ref[...]
    few[quad_me] = few_ref[...].astype(jnp.float32)
    for j in (1, 2, 3):
        k = quad_me ^ j
        few[k] = got[j - 1][per : per + 16, :].astype(jnp.float32)
        window[k, pl.ds(pl.multiple_of(core * per, 64), per), :] = got[j - 1][0:per, :]
        window[k, pl.ds(pl.multiple_of((1 - core) * per, 64), per), :] = passed[j - 1][0:per, :]
    span = 2 * per

    @pl.when(head == 0)
    def _():
        weight_ref[0:span, :] = window[0]
        weight_ref[span : 2 * span, :] = window[1]
        weight_ref[2 * span : 2 * span + per, :] = window[2, per:span, :]
        weight_ref[2 * span + per : 3 * span, :] = window[3, 0:per, :]

    @pl.when(head == 1)
    def _():
        weight_ref[0:per, :] = window[0, per:span, :]
        weight_ref[per:span, :] = window[1, 0:per, :]
        weight_ref[span : 2 * span, :] = window[2]
        weight_ref[2 * span : 3 * span, :] = window[3]

    def few_row(number):
        part, row = divmod(number, 5)
        return jnp.concatenate(
            [few[k, row : row + 1, part * quarter : (part + 1) * quarter] for k in range(4)],
            axis=1,
        )

    gains = jnp.concatenate([few_row(0), few_row(1)], axis=0)
    gains_ref[...] = gains
    router_ref[...] = jnp.concatenate(
        [few_row(2 + e) for e in range(EXPERTS)], axis=0
    ).astype(jnp.bfloat16)
    for where, source in ((head, tokens_ref), (1 - head, partner_ref)):
        tokens = source[...].astype(jnp.float32)
        both[where] = norm_rows(tokens, gains[0:1])[0].astype(jnp.bfloat16)
    normed = both[...].reshape(2 * rows, width)
    normed_ref[...] = normed
    mixed = mm(normed, weight_ref[...], TRANSPOSED)
    turn = DH // 2
    table = []
    for part in range(2):
        table.append(table_ref[pl.ds(pl.multiple_of((2 * place[3] + part) * half, 64), half), :])
        at = table_ref.shape[0] - 2 * half + part * half
        table.append(table_ref[at : at + half, :])
    table = jnp.concatenate(table, axis=0)
    cosine, sine = table[:, :turn], table[:, turn:]
    heads = HEADS // 2

    def chunk(number):
        return mixed[:, number * DH : (number + 1) * DH]

    rows_ref[...] = jnp.zeros_like(rows_ref)
    for one in range(heads):
        pieces = [
            turn_back(chunk(one), cosine, -sine),
            turn_back(chunk(heads + one), cosine, -sine),
            chunk(2 * heads + one),
        ]
        for part in range(2):
            at = part * rows
            rows_ref[one, part * half : (part + 1) * half, :] = jnp.concatenate(
                [piece[at : at + half] for piece in pieces]
                + [piece[at + half : at + rows] for piece in pieces],
                axis=1,
            ).astype(jnp.bfloat16)


def hidden_kernel(place, got_ref, partner_ref, tokens_ref, gains_ref, pick_ref, mine_ref, *refs):
    own, other = refs[0:3], refs[3:6]
    residual_ref, hidden_ref, attn_ref, sent_ref, proj_ref, attn = refs[6:]
    head = place[4]
    rows, width = tokens_ref.shape
    half = rows // 2
    per, start = proj_ref.shape[1], own[0].shape[0] - proj_ref.shape[1]
    for part in range(2):
        proj_ref[place[0] * 2 + part] = mine_ref[part * per : (part + 1) * per, :]
    for j in (1, 2, 3):
        for where, source in ((place[1], own[j - 1]), (1 - place[1], other[j - 1])):
            proj_ref[(place[0] ^ j) * 2 + where] = source[start : start + per, :]
    for one in range(HEADS // 2):
        at = slice(one * DH, (one + 1) * DH)
        mine = got_ref[one, pl.ds(pl.multiple_of(head * half, 64), half), :]
        for where, piece in ((head, mine), (1 - head, partner_ref[one])):
            attn[where, 0:half, at] = piece[:, 0:DH]
            attn[where, half:rows, at] = piece[:, DH : 2 * DH]
    attn_all = jnp.concatenate([attn[0], attn[1]], axis=1)
    attn_ref[...] = attn_all
    residual = tokens_ref[...].astype(jnp.float32) + mm(
        attn_all, proj_ref[...].reshape(width, width), TRANSPOSED
    )
    residual_ref[...] = residual
    hidden = norm_rows(residual, gains_ref[1:2, :])[0].astype(jnp.bfloat16)
    hidden_ref[...] = hidden
    sent_ref[...] = packed(mm(pick_ref[...], hidden)).astype(jnp.bfloat16)


def expert_kernel(place, own_ref, other_ref, own_grad, other_grad, router_ref, *refs):
    pairs, downs = refs[0:4], refs[4:8]
    (
        g_own, g_part, e_own, e_part, egate_ref, eup_ref, mid_ref, eout_ref, g_router_ref,
        rows_ref, gate_w, up_w, down_w, grad_ref,
    ) = refs[8:]
    quad_me, expert_me = place[0], place[2]
    half_count = rows_ref.shape[0] // 2
    unpack_to(rows_ref, 0, own_ref)
    unpack_to(rows_ref, half_count, other_ref)
    unpack_to(grad_ref, 0, own_grad)
    unpack_to(grad_ref, half_count, other_grad)
    quarter = downs[0].shape[0]
    for j in range(4):
        at = pl.ds(pl.multiple_of((quad_me ^ j) * quarter, 64), quarter)
        gate_w[at, :] = pairs[j][0]
        up_w[at, :] = pairs[j][1]
        down_w[at, :] = downs[j][...]
    count = rows_ref.shape[0]
    block = count // 4
    router = router_ref[...]
    mine = lax.broadcasted_iota(jnp.int32, (block, EXPERTS), 1) == expert_me
    mine = mine.astype(jnp.float32)
    g_router = jnp.zeros_like(g_router_ref)
    for step in range(4):
        at = slice(step * block, (step + 1) * block)
        rows, grads = rows_ref[at, :], grad_ref[at, :]
        logits = mm(rows, router, TRANSPOSED)
        logits = jnp.exp(logits - jnp.max(logits, axis=1, keepdims=True))
        soft = logits / jnp.sum(logits, axis=1, keepdims=True)
        gate = jnp.sum(soft * mine, axis=1, keepdims=True)
        e_up = mm(rows, up_w[...])
        e_act, e_slope = swish_parts(mm(rows, gate_w[...]))
        e_mid = e_act * e_up
        e_grad = mm(grads, down_w[...])
        g_gate = jnp.sum(e_mid * e_grad, axis=1, keepdims=True)
        g_mid = e_grad * gate
        egate = (g_mid * e_up * e_slope).astype(jnp.bfloat16)
        eup = (g_mid * e_act).astype(jnp.bfloat16)
        e_mid = e_mid.astype(jnp.bfloat16)
        g_logits = (g_gate * soft * (mine - gate)).astype(jnp.bfloat16)
        g_rows = (
            mm(egate, gate_w[...], TRANSPOSED)
            + mm(eup, up_w[...], TRANSPOSED)
            + mm(g_logits, router)
        )
        e_rows = gate * mm(e_mid, down_w[...], TRANSPOSED)
        if step < 2:
            g_own[at, :] = g_rows
            e_own[at, :] = e_rows
        else:
            there = slice((step - 2) * block, (step - 1) * block)
            g_part[there, :] = g_rows.astype(jnp.bfloat16)
            e_part[there, :] = e_rows.astype(jnp.bfloat16)
        egate_ref[at, :] = egate
        eup_ref[at, :] = eup
        mid_ref[at, :] = e_mid
        eout_ref[at, :] = (gate * grads.astype(jnp.float32)).astype(jnp.bfloat16)
        g_router = g_router + mm(g_logits, rows, FIRST)
    g_router_ref[...] = g_router


def expert_weight_kernel(place, rows_ref, eout_ref, egate_ref, eup_ref, mid_ref, *refs):
    pairs, downs, whole, turned = refs[0:4], refs[4:8], refs[8], refs[9]
    quarter = downs[0].shape[0]
    turned[...] = jnp.transpose(rows_ref[...])
    for number, right in enumerate((egate_ref, eup_ref, mid_ref)):
        if number == 2:
            turned[...] = jnp.transpose(eout_ref[...])
        whole[...] = mm(turned[...], right[...]).astype(jnp.bfloat16)
        for j in range(4):
            at = pl.ds(pl.multiple_of((place[0] ^ j) * quarter, 64), quarter)
            if number == 2:
                downs[j][...] = whole[at, :]
            else:
                pairs[j][number] = whole[at, :]


def branch_kernel(
    place, got_ref, pick_ref, shared_ref, residual_ref, gains_ref, grad_ref, proj_ref,
    resid_ref, branch_ref, mine_ref, theirs_ref, gain_ref, back, heads,
):
    rows, width = grad_ref.shape
    unpack_to(back, 0, got_ref)
    g_hidden = mm(pick_ref[...], back[...], FIRST) + shared_ref[...].astype(jnp.float32)
    residual = residual_ref[...]
    gain = gains_ref[1:2, :]
    inverse = norm_rows(residual, gain)[1]
    g_norm, g_gain = norm_back(residual, inverse, gain, g_hidden)
    gain_ref[...] = g_gain[None]
    g_resid = grad_ref[...].astype(jnp.float32) + g_norm
    resid_ref[...] = g_resid
    branch = g_resid.astype(jnp.bfloat16)
    branch_ref[...] = branch
    attn = mm(branch, proj_ref[...].reshape(width, width)).astype(jnp.bfloat16)
    half = rows // 2
    for one in range(HEADS):
        piece = attn[:, one * DH : (one + 1) * DH]
        heads[one // (HEADS // 2), one % (HEADS // 2)] = jnp.concatenate(
            [piece[:half], piece[half:]], axis=1
        )
    mine_ref[...] = heads[place[4]]
    theirs_ref[...] = heads[1 - place[4]]


def tokens_kernel(
    place, got_ref, qkv_ref, tokens_ref, partner_ref, mine_ref, theirs_ref, gain_ref, parts, grads
):
    half = got_ref.shape[1] // 2
    rows = 2 * half
    heads = HEADS // 2
    for one in range(heads):
        for part in range(2):
            piece = got_ref[one, part * half : (part + 1) * half, :]
            at = part * rows
            for kind in range(3):
                there = slice((kind * heads + one) * DH, (kind * heads + one + 1) * DH)
                parts[at : at + half, there] = piece[:, kind * DH : (kind + 1) * DH]
                parts[at + half : at + rows, there] = piece[:, (3 + kind) * DH : (4 + kind) * DH]
    g_normed = mm(parts[...], qkv_ref[...])
    grads[0] = g_normed[:rows]
    grads[1] = g_normed[rows:]
    mine_ref[...] = grads[place[4]]
    theirs_ref[...] = grads[1 - place[4]].astype(jnp.bfloat16)
    gain = 0.0
    for source, where in ((tokens_ref, place[4]), (partner_ref, 1 - place[4])):
        tokens = source[...].astype(jnp.float32)
        inverse = norm_rows(tokens, 1.0)[1]
        gain = gain + jnp.sum(grads[where] * tokens * inverse, axis=0, keepdims=True)
    gain_ref[...] = gain


def tokens_out_kernel(mine_ref, partner_ref, tokens_ref, gains_ref, resid_ref, out_ref):
    g_normed = mine_ref[...] + partner_ref[...].astype(jnp.float32)
    tokens = tokens_ref[...].astype(jnp.float32)
    gain = gains_ref[0:1, :]
    inverse = norm_rows(tokens, gain)[1]
    out_ref[...] = resid_ref[...] + norm_back(tokens, inverse, gain, g_normed)[0]


def head_weight_kernel(rows_ref, normed_ref, out_ref, left):
    blocks, both, wide = rows_ref.shape
    half = both // 2
    for block in range(blocks):
        for part in range(2):
            at = (block * 2 + part) * both
            piece = rows_ref[block, part * half : (part + 1) * half, :]
            left[at : at + half, :] = piece[:, 0 : wide // 2]
            left[at + half : at + both, :] = piece[:, wide // 2 : wide]
    right = normed_ref[...].reshape(2 * both * blocks, normed_ref.shape[2])
    out_ref[...] = mm(left[...], right, FIRST).astype(jnp.bfloat16)


def chunk_kernel(order, got_ref, out_ref, few_ref):
    few = jnp.zeros_like(few_ref)
    for source in range(got_ref.shape[0]):
        few = few + got_ref[source, 2 * DH : 2 * DH + FEW, :].astype(jnp.float32)
    few_ref[...] = few
    for number in range(order.shape[0]):
        which = order[number]
        at = pl.ds(pl.multiple_of(which % 2 * DH, DH), DH)
        out_ref[number * DH : (number + 1) * DH, :] = got_ref[which // 2, at, :].astype(
            jnp.float32
        )


def shared_kernel(place, *refs):
    hidden_refs, grads_refs, pieces = refs[0:4], refs[4:8], refs[8:12]
    out_ref, back_ref = refs[12:14]
    given = refs[14:18]
    both_w, down_w, g_both, g_down = refs[18:]
    quad_me = place[0]
    width, span = both_w.shape[0], both_w.shape[1] // 4
    quarter = width // 4
    block = hidden_refs[0].shape[0]
    for j in range(4):
        k = quad_me ^ j
        both_w[:, pl.ds(pl.multiple_of(k * span, 128), span)] = pieces[j][0:width, :]
        at = pl.ds(pl.multiple_of(k * quarter, 64), quarter)
        down_w[at, 0:span] = pieces[j][width : width + quarter, :]
        down_w[at, span : 2 * span] = pieces[j][width + quarter : width + 2 * quarter, :]
    for step in range(2):
        rows = slice(step * 2 * block, (step + 1) * 2 * block)
        hidden = jnp.concatenate([hidden_refs[2 * step][...], hidden_refs[2 * step + 1][...]])
        grads = jnp.concatenate([grads_refs[2 * step][...], grads_refs[2 * step + 1][...]])
        pre = mm(hidden, both_w[...])
        act, slope = swish_parts(pre[:, : 2 * span])
        up = pre[:, 2 * span :]
        mid = (act * up).astype(jnp.bfloat16)
        out_ref[rows, :] = mm(mid, down_w[...], TRANSPOSED).astype(jnp.bfloat16)
        g_mid = mm(grads, down_w[...])
        g_pre = jnp.concatenate([g_mid * up * slope, g_mid * act], axis=1).astype(jnp.bfloat16)
        back_ref[rows, :] = mm(g_pre, both_w[...], TRANSPOSED).astype(jnp.bfloat16)
        new_both = mm(hidden, g_pre, FIRST)
        new_down = mm(grads, mid, FIRST)
        if step == 0:
            g_both[...] = new_both
            g_down[...] = new_down
        else:
            g_both[...] += new_both
            g_down[...] += new_down
    for j in range(4):
        k = quad_me ^ j
        at = pl.ds(pl.multiple_of(k * quarter, 64), quarter)
        given[j][0:width, :] = g_both[:, pl.ds(pl.multiple_of(k * span, 128), span)].astype(
            jnp.bfloat16
        )
        given[j][width : width + quarter, :] = g_down[at, 0:span].astype(jnp.bfloat16)
        given[j][width + quarter : width + 2 * quarter, :] = g_down[at, span : 2 * span].astype(
            jnp.bfloat16
        )


def shared_out_kernel(place, *refs):
    parts, wide_ref, down_ref, proj_ref = refs[0:4], refs[4], refs[5], refs[6]
    width, span = wide_ref.shape[0], parts[0].shape[1]
    quarter = down_ref.shape[0]
    last, per = width + 2 * quarter, quarter // 4
    for j in range(4):
        k = (place[3] % 4) ^ j
        at = pl.ds(pl.multiple_of(k * span, 128), span)
        wide_ref[:, at] = parts[j][0:width, :].astype(jnp.float32)
        down_ref[:, at] = parts[j][width : width + quarter, :].astype(jnp.float32)
        at = pl.ds(pl.multiple_of((4 + k) * span, 128), span)
        down_ref[:, at] = parts[j][width + quarter : last, :].astype(jnp.float32)
        at = pl.ds(pl.multiple_of(k * per, 16), per)
        for i in range(width // span):
            proj_ref[at, i * span : (i + 1) * span] = parts[j][
                last + i * per : last + (i + 1) * per, :
            ].astype(jnp.float32)


def units_out_kernel(place, *refs):
    parts, out_ref = refs[:-1], refs[-1]
    units = parts[0].shape[-1]
    for j in range(4):
        at = pl.ds(pl.multiple_of((place[6] ^ UNIT_ORDER[j]) * units, 128), units)
        if len(out_ref.shape) == 3:
            out_ref[0, :, at] = parts[j][0].astype(jnp.float32)
            out_ref[1, :, at] = parts[j][1].astype(jnp.float32)
        else:
            out_ref[:, at] = parts[j][...].astype(jnp.float32)


def quick_body(
    tokens_in,
    norm_gains,
    attn_qkv,
    attn_proj,
    router_rows,
    shared_gate_up,
    shared_down,
    expert_gate_up,
    expert_down,
    routes,
    out_grad,
):
    quad = ("grp", "head")
    line = ("head", "blk")
    blocks = lax.axis_size("blk")
    rows, width = tokens_in.shape
    grp, head, blk = lax.axis_index("grp"), lax.axis_index("head"), lax.axis_index("blk")
    core = blk % 2
    quarter = width // 4
    prompt_dev = max(PROMPT_ROWS, PROMPT_LEAST // (2 * blocks))
    prompt = prompt_dev * 2 * blocks
    cont = 2 * (rows - prompt_dev)
    bf16, f32 = jnp.bfloat16, jnp.float32

    member = 2 * grp + head
    unit_me = 2 * head + grp
    place = jnp.stack([member, core, 2 * blk + head, blk, head, grp, unit_me])
    third = attn_qkv.shape[1]
    few = jnp.concatenate([norm_gains, router_rows], axis=0)
    few = jnp.pad(few, ((0, 20 - few.shape[0]), (0, 0)))
    few = jnp.concatenate([few[5 * i : 5 * i + 5] for i in range(4)], axis=1)
    few = jnp.pad(few, ((0, 11), (0, 0)))
    six = width // 2
    own_window, *window_parts = copy_call(
        first_kernel,
        [(six, width)] + [(six // 2 + 16 + quarter // 2, width)] * 3,
        10,
        "first_parts",
        place, attn_qkv.T, few, attn_proj.T,
    )
    partner_tokens = exchange(tokens_in, "head", 1)
    own_w = [to_member(window_parts[j - 1], j) for j in (1, 2, 3)]
    other_w = [exchange(part, "blk", 1) for part in own_w]

    span = SFF // 2 // 4
    four = blk % 4
    units = expert_gate_up.shape[2] // 4
    piece, *unit_parts = copy_call(
        rest_kernel,
        [(width + 2 * quarter, span)] + [(2, quarter, units)] * 4 + [(quarter, units)] * 4,
        15,
        "rest_parts",
        place, shared_gate_up, shared_down.T, expert_gate_up, expert_down.T,
        through=True,
    )
    pair_send, down_send = unit_parts[0:4], unit_parts[4:8]

    def of_four(values):
        far = exchange(values, "blk", 2)
        return [values, exchange(values, "blk", 1), far, exchange(far, "blk", 1)]

    def sum_of_four(parts):
        near = exchange(jnp.stack([parts[1], parts[3]]), "blk", 1)
        far = (parts[2].astype(f32) + near[1].astype(f32)).astype(bf16)
        return parts[0].astype(f32) + near[0].astype(f32) + exchange(far, "blk", 2).astype(f32)

    def joined(own, part):
        return (own.astype(f32) + part.astype(f32)).astype(bf16)

    def fetched(parts, after, *numbers):
        for j in numbers:
            parts[j] = to_member(tie(parts[j], after), j)

    expert_ids = jnp.arange(EXPERTS, dtype=jnp.int32)
    match = (routes[:, :, None] == expert_ids).astype(jnp.int32)
    flat = match.reshape(2 * rows, EXPERTS)
    rank = (jnp.sum(jnp.cumsum(flat, axis=0) * flat, axis=1) - 1).reshape(rows, 2)
    slots_all = 2 * blocks
    target = routes % 2 * blocks + routes // 2
    slots = jnp.where(
        rank < 16,
        rank // 8 * (8 * slots_all) + target * 8 + rank % 8,
        16 * slots_all + target * 4 + rank - 16,
    )
    per_half = 20 * slots_all
    slot_ids = jnp.arange(per_half, dtype=jnp.int32)[:, None]
    pick = ((slot_ids == slots[:, 0]) | (slot_ids == slots[:, 1])).astype(bf16)
    pack_shape = (slots_all, 8, 5 * width // 2)

    def over_line(values):
        return lax.all_to_all(values, line, 0, 0, tiled=True)

    def over_blocks(values):
        return lax.all_to_all(values, "blk", 0, 0, tiled=True)

    grad_sent = kernel_call(
        pack_kernel, [(pack_shape, bf16)], [], "pack_rows", mm(pick, tie(out_grad, own_w[0])).astype(bf16)
    )[0]
    grad_own = over_line(grad_sent)
    four_grads = of_four(out_grad)

    wait = lax.optimization_barrier
    own_w, other_w, partner_tokens, pair_send, down_send, piece = wait(
        (own_w, other_w, partner_tokens, pair_send, down_send, piece)
    )
    shared_parts = [piece] * 4
    steps = np.arange(DH // 2, dtype=np.float32)
    rates = np.power(np.float32(10000.0), np.float32(-2.0) * steps / np.float32(DH))
    angles = np.arange(prompt + cont, dtype=np.float32)[:, None] * rates[None, :].astype(np.float32)
    table = jnp.asarray(
        np.concatenate([np.cos(angles), np.sin(angles)], axis=1).astype(np.float32)
    )
    normed, head_send, gains, router_w, qkv_w = kernel_call(
        qkv_kernel,
        [
            ((2 * rows, width), bf16),
            ((blocks, rows, 6 * DH), bf16),
            ((2, width), f32),
            ((EXPERTS, width), bf16),
            ((3 * six, width), bf16),
        ],
        [((4, six, width), bf16), ((4, 16, width), f32), ((2, rows, width), bf16)],
        "qkv_rows",
        place, tokens_in, partner_tokens, table, own_window, few, *own_w, *other_w,
        alone=True,
    )
    head_send, grad_own = wait((head_send, grad_own))
    head_rows = over_blocks(head_send)
    fetched(pair_send, head_send, 1, 2)
    head_rows, pair_send = wait((head_rows, pair_send))
    attn_heads = attention_forward(head_rows)
    fetched(pair_send, head_rows, 3)
    attn_got = over_blocks(attn_heads)
    all_normed = lax.all_gather(tie(normed, head_rows), "blk", axis=0)
    fetched(shared_parts, attn_heads, 1, 2)
    grad_other = exchange(tie(grad_own, attn_heads), "grp", 1)
    attn_got, pair_send = wait((attn_got, pair_send))
    head_half = HEADS // 2
    theirs = lax.dynamic_slice_in_dim(attn_got[:head_half], (1 - head) * prompt_dev, prompt_dev, 1)
    attn_partner = exchange(theirs, "head", 1)
    shared_parts[3] = exchange(tie(shared_parts[2], attn_partner), "head", 1)
    residual, hidden, attn_tok, sent, proj_w = kernel_call(
        hidden_kernel,
        [
            ((rows, width), f32),
            ((rows, width), bf16),
            ((rows, width), bf16),
            (pack_shape, bf16),
            ((8, quarter // 2, width), bf16),
        ],
        [((2, rows, six), bf16)],
        "hidden_rows",
        place, attn_got, attn_partner, tokens_in, gains, pick, attn_proj.T, *own_w, *other_w,
        alone=True,
    )

    sent, grad_other, shared_parts[1], shared_parts[2] = wait(
        (sent, grad_other, shared_parts[1], shared_parts[2])
    )
    got_own = over_line(sent)
    fetched(down_send, sent, 2, 3, 1)
    four_hidden = of_four(tie(hidden, sent))
    got_own, down_send[2], four_hidden = wait((got_own, down_send[2], four_hidden))
    got_other = exchange(got_own, "grp", 1)
    shared_out, shared_back, *shared_given = kernel_call(
        shared_kernel,
        [((4 * rows, width), bf16)] * 2 + [((width + 2 * quarter, span), bf16)] * 4,
        [
            ((width, 4 * span), bf16),
            ((width, 2 * span), bf16),
            ((width, 4 * span), f32),
            ((width, 2 * span), f32),
        ],
        "shared_rows",
        place, *tie(four_hidden, got_own), *four_grads, *shared_parts,
        alone=True,
    )
    shared_back = sum_of_four([shared_back[i * rows : (i + 1) * rows] for i in range(4)])

    got_other, shared_given, down_send, all_normed = wait(
        (got_other, shared_given, down_send, all_normed)
    )
    middle = shared_given[0].shape[0] // 2
    upper = [part[:middle] for part in shared_given]
    lower = [part[middle:] for part in shared_given]
    count = 2 * per_half
    g_own, g_part, e_own, e_part, egate, eup, e_mid, g_eout, g_router, got_rows = kernel_call(
        expert_kernel,
        [
            ((per_half, width), f32),
            ((per_half, width), bf16),
            ((per_half, width), f32),
            ((per_half, width), bf16),
            ((count, units), bf16),
            ((count, units), bf16),
            ((count, units), bf16),
            ((count, width), bf16),
            ((EXPERTS, width), f32),
            ((count, width), bf16),
        ],
        [((width, units), bf16)] * 3 + [((count, width), bf16)],
        "expert_rows",
        place, got_own, got_other, grad_own, grad_other, router_w,
        *pair_send, *down_send,
        alone=True,
        flops=15 * 10**9,
    )

    def joined_rows(own, part):
        return kernel_call(join_kernel, [(pack_shape, bf16)], [], "join_rows", own, part)[0]

    weight_parts = kernel_call(
        expert_weight_kernel,
        [((2, quarter, units), bf16)] * 4 + [((quarter, units), bf16)] * 4,
        [((width, units), bf16), ((width, count), bf16)],
        "expert_weights",
        place, got_rows, g_eout, egate, eup, e_mid,
        alone=True,
    )
    pair_out, down_out = list(weight_parts[0:4]), list(weight_parts[4:8])
    g_other = exchange(g_part, "grp", 1)
    turned = exchange(tie(jnp.stack([lower[1], lower[3]]), g_part), "head", 1)
    g_other, pair_out, down_out = wait((g_other, pair_out, down_out))
    crossed = exchange(tie(jnp.stack([upper[2], upper[3]]), g_other), "grp", 1)
    g_joined, shared_back, turned = wait((joined_rows(g_own, g_other), shared_back, turned))
    crossed = joined(upper[1], crossed[1]), joined(upper[0], crossed[0])
    turned = joined(lower[2], turned[1]), joined(lower[0], turned[0])
    g_back = over_line(g_joined)
    shared_sum = jnp.concatenate(
        [
            joined(crossed[1], exchange(tie(crossed[0], g_joined), "head", 1)),
            joined(turned[1], exchange(tie(turned[0], g_joined), "grp", 1)),
        ]
    )
    shared_out = sum_of_four(
        [tie(shared_out, g_joined)[i * rows : (i + 1) * rows] for i in range(4)]
    )
    cutting = 576

    def far_sum(values):
        return joined(values, exchange(values, "blk", 4))


    g_resid, g_branch, grad_mine, grad_theirs, g_second_gain = kernel_call(
        branch_kernel,
        [
            ((rows, width), f32),
            ((rows, width), bf16),
            ((head_half, prompt_dev, 2 * DH), bf16),
            ((head_half, prompt_dev, 2 * DH), bf16),
            ((1, width), f32),
        ],
        [((per_half, width), bf16), ((2, head_half, prompt_dev, 2 * DH), bf16)],
        "branch_rows",
        place, g_back, pick, shared_back, residual, gains, out_grad, proj_w,
    )
    grad_theirs = exchange(grad_theirs, "head", 1)
    grad_theirs, shared_sum = wait((grad_theirs, shared_sum))
    g_proj = mm(g_branch, attn_tok, FIRST).astype(bf16).reshape(4, 4, quarter // 4, width)
    g_proj = sum_of_four(
        [
            lax.dynamic_index_in_dim(g_proj, four ^ j, 1, keepdims=False).reshape(quarter, width)
            for j in range(4)
        ]
    )
    g_proj = g_proj.astype(bf16)
    grad_send = jnp.where(
        head == 0,
        jnp.concatenate([grad_mine, grad_theirs], axis=1),
        jnp.concatenate([grad_theirs, grad_mine], axis=1),
    )
    grad_send = jnp.pad(grad_send, ((0, blocks - head_half), (0, 0), (0, 0)))
    grad_heads = over_blocks(grad_send)
    grad_heads, shared_out = wait((grad_heads, shared_out))
    fetched(pair_out, grad_send, 1, 2)
    far_one = far_sum(tie(shared_sum[:cutting], grad_heads))
    g_head_rows = attention_backward(head_rows, grad_heads, table)
    g_proj = g_proj.reshape(4, quarter // 4, width)
    proj_out = []
    for j in range(4):
        part = lax.dynamic_index_in_dim(g_proj, member ^ j, 0, keepdims=False)
        proj_out.append(
            jnp.concatenate([part[:, i * span : (i + 1) * span] for i in range(width // span)])
        )
    fetched(proj_out, g_head_rows, 1, 2, 3)
    proj_sum = sum(part.astype(f32) for part in proj_out).astype(bf16)
    far_two = far_sum(tie(shared_sum[cutting:], g_head_rows))
    far_proj = far_sum(tie(proj_sum, g_head_rows))
    fetched(pair_out, grad_heads, 3)
    g_head_rows, far_one = wait((g_head_rows, far_one))
    g_got = over_blocks(g_head_rows)
    e_other = exchange(tie(e_part, g_head_rows), "grp", 1)
    g_got, pair_out, e_joined = wait((g_got, pair_out, joined_rows(e_own, e_other)))
    g_normed, g_normed_theirs, g_first_gain = kernel_call(
        tokens_kernel,
        [((rows, width), f32), ((rows, width), bf16), ((1, width), f32)],
        [((2 * rows, 3 * six), bf16), ((2, rows, width), f32)],
        "token_parts",
        place, g_got, qkv_w, tokens_in, partner_tokens,
    )
    g_normed_theirs = exchange(g_normed_theirs, "head", 1)

    head_w = kernel_call(
        head_weight_kernel,
        [((3 * DH, width), bf16)],
        [((2 * rows * blocks, 3 * DH), bf16)],
        "head_weights",
        tie(g_head_rows, g_first_gain), all_normed,
    )[0].reshape(3, DH, width)

    def chunk_pair(side):
        kept_kind = 2 * side
        given_kind = jnp.where(head == 0, 1 + side, side)
        return jnp.stack([head_w[kept_kind], head_w[given_kind]])

    few = jnp.concatenate([g_first_gain, g_second_gain, g_router], axis=0)
    few = jnp.pad(few, ((0, FEW - few.shape[0]), (0, 0))).astype(bf16)
    own_pair = jnp.concatenate([*jnp.where(grp == 0, chunk_pair(0), chunk_pair(1)), few])
    other_pair = jnp.concatenate([*jnp.where(grp == 0, chunk_pair(1), chunk_pair(0)), few])
    own_pair = joined(own_pair, exchange(other_pair, "grp", 1))
    from_head = exchange(own_pair[DH:], "head", 1)
    own_pair = jnp.concatenate(
        [own_pair[:DH], from_head[:DH], joined(own_pair[2 * DH :], from_head[DH:])]
    )
    own_pair, far_two, far_proj = wait((own_pair, far_two, far_proj))
    all_pairs = lax.all_gather(own_pair, "blk", axis=0)
    order = jnp.array(
        [
            [0, 2, 4, 6, 8, 10, 1, 3, 5],
            [6, 8, 10, 1, 3, 5, 7, 9, 11],
            [1, 3, 5, 7, 9, 11, 0, 2, 4],
            [7, 9, 11, 0, 2, 4, 6, 8, 10],
        ],
        jnp.int32,
    )[member]
    grad_tokens = kernel_call(
        tokens_out_kernel,
        [((rows, width), f32)],
        [],
        "token_grads",
        g_normed, g_normed_theirs, tokens_in, gains, g_resid,
    )[0]
    grad_expert_w = kernel_call(
        units_out_kernel,
        [((2, quarter, 4 * units), f32)],
        [],
        "units_out",
        place, *pair_out,
        alone=True,
    )[0]
    fetched(down_out, from_head, 1, 2, 3)
    e_joined, down_out = wait((e_joined, down_out))
    grad_expert_out = kernel_call(
        units_out_kernel,
        [((quarter, 4 * units), f32)],
        [],
        "down_out",
        place, *down_out,
        alone=True,
    )[0].T
    e_joined, grad_expert_out = wait((e_joined, grad_expert_out))
    e_back = over_line(e_joined)
    layer_out = kernel_call(
        layer_kernel,
        [((rows, width), bf16)],
        [((per_half, width), bf16)],
        "layer_rows",
        e_back, pick, residual, shared_out,
    )[0]
    four_shared = of_four(
        tie(jnp.concatenate([far_one, far_two, far_proj]), from_head)
    )
    grad_shared_w, grad_shared_out, grad_proj = kernel_call(
        shared_out_kernel,
        [((width, 4 * span), f32), ((quarter, SFF), f32), ((quarter, width), f32)],
        [],
        "shared_grads",
        place, *four_shared,
        alone=True,
    )
    all_pairs, grad_expert_w = wait((all_pairs, grad_expert_w))
    grad_qkv, few = kernel_call(
        chunk_kernel,
        [((third, width), f32), ((FEW, width), f32)],
        [],
        "chunk_rows",
        order, all_pairs,
    )
    grad_qkv = grad_qkv.T

    few = lax.dynamic_slice_in_dim(few, member * quarter, quarter, 1)
    grad_shared_out, grad_proj = grad_shared_out.T, grad_proj.T
    return (
        layer_out,
        grad_tokens,
        few[0:2],
        grad_qkv,
        grad_proj,
        few[2 : 2 + EXPERTS],
        grad_shared_w,
        grad_shared_out,
        grad_expert_w,
        grad_expert_out,
    )


def solution(mesh):
    whole = P(("grp", "head", "blk"), None)
    split = P(None, ("grp", "head"))
    sizes = dict(mesh.shape)
    quick = sizes["grp"] == 2 and sizes["head"] == 2 and sizes["blk"] == 8
    return jax.shard_map(
        quick_body if quick else body,
        mesh=mesh,
        in_specs=(
            whole, split, split, split, split, split, split,
            P(None, ("grp", "head"), "blk"), P("blk", ("grp", "head")), whole, whole,
        ),
        out_specs=(
            whole, whole, split, split, split, split, split, split,
            P(None, ("grp", "head"), "blk"), P("blk", ("grp", "head")),
        ),
        check_vma=False,
    )
```
